32 devices in a mesh: lat: 4 (over x, core), lon: 8 (over z, y).
Axes of the slice: x: 2, y: 2, z: 4, core: 2. Of those that a mesh axis runs over, the one named last changes fastest.
Arguments:
- latent_field: float32 [32, 8, 64, 1024], P(None, None, 'lat', 'lon'), may hold values from -6 to 6
- east_courant: float32 [8, 64, 1024], P(None, 'lat', 'lon'), may hold values from -0.45 to 0.45
- north_courant: float32 [8, 64, 1024], P(None, 'lat', 'lon'), may hold values from -0.45 to 0.45
- mixing: float32 [7, 64, 1024], P(None, 'lat', 'lon'), may hold values from 0.2 to 5
- sunlit: int32 [4, 64], P('lat', 'lon'), may hold values from 0 to 1, as said below
- decode_w: bfloat16 [224, 32], replicated, may hold values from -1 to 1
- react_a: bfloat16 [256, 224], replicated, may hold values from -0.375 to 0.375
- react_b: bfloat16 [256, 224], replicated, may hold values from -0.375 to 0.375
- stoich: bfloat16 [224, 256], replicated, may hold values from -0.375 to 0.375
- encode_w: bfloat16 [32, 224], replicated, may hold values from -0.375 to 0.375
- rate_const: float32 [256], replicated, may hold values from 0.05 to 0.5
Outputs:
- advanced: float32 [32, 8, 64, 1024], P(None, None, 'lat', 'lon')
The draws below stay inside these ranges and needn't reach their ends.
Inputs may be any that keep to these rules, and one draw needn't show every extreme that they name: In each row of blocks the sunlit blocks form one run, periodic in longitude, of 16 to 48 blocks.
All inputs are finite; a program needn't handle non-finite values.
Results may differ from the reference program's by a relative error of at most 0.0035.
Values may be sent and summed in bfloat16 or wider, within the bound.
No kernel may reach another device: no remote copies, remote signals or barrier semaphores. Data moves between devices by JAX's collectives and lax.ppermute only.
A program may use at most 128 MiB of HBM per device.

```python
import math
import jax
import jax.numpy as jnp
from jax import lax

S = 32
NSP = 224
NR = 256
LEV = 8
BLOCK = 16
SUBSTEPS = 2
STEPS = 2
NLAT = 64
NLON = 1024
BLOCK_ROWS = 4
BLOCK_COLS = 64


def draw_sunlit(key, part):
    centre_key, width_key = jax.random.split(key)
    centres = jax.random.randint(centre_key, (BLOCK_ROWS, 1), 0, BLOCK_COLS)
    widths = jax.random.randint(width_key, (BLOCK_ROWS, 1), BLOCK_COLS // 4, 3 * BLOCK_COLS // 4 + 1)
    columns = jnp.arange(BLOCK_COLS)[None, :]
    return ((columns - centres) % BLOCK_COLS < widths).astype(jnp.int32)


def block_levels(key, shape, cuts, smallest, top_value):
    gain, own = 1.0, jax.random.fold_in(key, 6)
    for axis_at, blocks in cuts:
        draws = jnp.exp(jax.random.uniform(jax.random.fold_in(own, axis_at), (blocks,), jnp.float32, smallest / len(cuts), top_value / len(cuts)))
        gain = gain * jnp.repeat(draws, shape[axis_at] // blocks).reshape([-1 if axis == axis_at else 1 for axis in range(len(shape))])
    return gain


def noise(rng, dims, spread, reach, cuts=(), kind=jnp.bfloat16):
    array = jax.random.normal(rng, dims, jnp.float32) * spread
    if len(cuts) > 0:
        array = block_levels(rng, dims, cuts, -0.22, 0.18) * array
    return jnp.clip(array, min=-reach, max=reach).astype(kind)


def setup_inputs(seed: int = 0) -> dict:
    streams_of = jax.random.split(jax.random.key(seed), 12)
    latent_field = noise(streams_of[0], (S, LEV, NLAT, NLON), 1.0, 6.0, ((2, 4), (3, 8)), jnp.float32)
    east_courant = jnp.clip(jax.random.uniform(streams_of[1], (LEV, NLAT, NLON), jnp.float32, -0.45, 0.45) * block_levels(streams_of[1], (LEV, NLAT, NLON), ((1, 4), (2, 8)), -0.4, 0.0), -0.45, 0.45)
    north_courant = jnp.clip(jax.random.uniform(streams_of[2], (LEV, NLAT, NLON), jnp.float32, -0.45, 0.45) * block_levels(streams_of[2], (LEV, NLAT, NLON), ((1, 4), (2, 8)), -0.4, 0.0), -0.45, 0.45)
    mixing = jnp.clip(jnp.exp(math.log(5.0) - 3.218876 * jax.random.uniform(streams_of[3], (LEV - 1, NLAT, NLON), jnp.float32) ** block_levels(streams_of[3], (LEV - 1, NLAT, NLON), ((1, 4), (2, 8)), -0.2, 0.2)), 0.2, 5.0)
    sunlit = draw_sunlit(jax.random.fold_in(streams_of[11], 71), 0)
    decode_w = noise(streams_of[5], (NSP, S), S ** -0.5, 1.0)
    react_a = noise(streams_of[6], (NR, NSP), NSP ** -0.5, 0.375)
    react_b = noise(streams_of[7], (NR, NSP), NSP ** -0.5, 0.375)
    stoich = noise(streams_of[8], (NSP, NR), NR ** -0.5, 0.375)
    encode_w = noise(streams_of[9], (S, NSP), NSP ** -0.5, 0.375)
    rate_const = jnp.clip(jnp.exp(jax.random.uniform(streams_of[10], (NR,), jnp.float32, math.log(0.05), math.log(0.5))), 0.05, 0.5)
    return dict(latent_field=latent_field, east_courant=east_courant, north_courant=north_courant, mixing=mixing, sunlit=sunlit, decode_w=decode_w, react_a=react_a, react_b=react_b, stoich=stoich, encode_w=encode_w, rate_const=rate_const)


def advect(latent_field, east_courant, north_courant):
    lat_cells = latent_field.shape[2]
    east_speed = east_courant[None]
    north_speed = north_courant[None]
    east_face = jnp.maximum(east_speed, 0.0) * latent_field + jnp.minimum(jnp.roll(east_speed, -1, 3), 0.0) * jnp.roll(latent_field, -1, 3)
    north_face = jnp.maximum(north_speed, 0.0) * latent_field + jnp.minimum(jnp.roll(north_speed, -1, 2), 0.0) * jnp.roll(latent_field, -1, 2)
    north_open = jnp.arange(lat_cells) < lat_cells - 1
    north_face = jnp.where(north_open[:, None], north_face, 0.0)
    return latent_field - (east_face - jnp.roll(east_face, 1, 3)) - (north_face - jnp.roll(north_face, 1, 2))


def diffuse(tracers, mixing):
    n_levels = tracers.shape[1]
    sweep_upper = []
    sweep_right = []
    for level_index in range(n_levels):
        below_mix = mixing[level_index - 1][None] if level_index > 0 else 0.0
        above_mix = mixing[level_index][None] if level_index < n_levels - 1 else 0.0
        diagonal = 1.0 + below_mix + above_mix
        if level_index > 0:
            pivot_value = diagonal + below_mix * sweep_upper[-1]
            right_side = tracers[:, level_index] + below_mix * sweep_right[-1]
        else:
            pivot_value = diagonal
            right_side = tracers[:, 0]
        sweep_upper.append(-above_mix / pivot_value)
        sweep_right.append(right_side / pivot_value)
    solved = [sweep_right[-1]]
    for level_index in range(n_levels - 2, -1, -1):
        solved.insert(0, sweep_right[level_index] - sweep_upper[level_index] * solved[0])
    return jnp.stack(solved, 1)


def chemistry(latent_in, species_in, decode_w, react_a, react_b, stoich, encode_w, rate_const):
    current = latent_in.astype(jnp.float32)
    summed = jnp.zeros(current.shape, jnp.float32)
    species = species_in
    for substep in range(SUBSTEPS):
        if substep > 0:
            species = jnp.dot(decode_w, current.astype(jnp.bfloat16), preferred_element_type=jnp.float32).astype(jnp.bfloat16)
        react_first = jnp.dot(react_a, species, preferred_element_type=jnp.float32)
        react_second = jnp.dot(react_b, species, preferred_element_type=jnp.float32)
        rate_values = (rate_const[:, None] * react_first * react_second).astype(jnp.bfloat16)
        tendency = jnp.dot(stoich, rate_values, preferred_element_type=jnp.float32).astype(jnp.bfloat16)
        increment = jnp.dot(encode_w, tendency, preferred_element_type=jnp.float32).astype(jnp.bfloat16)
        increment = lax.optimization_barrier(increment).astype(jnp.float32)
        summed = summed + increment
        current = current + increment
    return summed.astype(jnp.bfloat16)


def reference(latent_field, east_courant, north_courant, mixing, sunlit, decode_w, react_a, react_b, stoich, encode_w, rate_const):
    n_species, n_levels, lat_cells, lon_cells = latent_field.shape
    block_rows = lat_cells // BLOCK
    block_cols = lon_cells // BLOCK
    sun_flags = sunlit.reshape(-1)

    def react_block(pieces):
        block_data, sun_flag = pieces

        def lit_branch(values):
            latent_in = values.astype(jnp.bfloat16)
            species = jnp.dot(decode_w, latent_in, preferred_element_type=jnp.float32).astype(jnp.bfloat16)
            return chemistry(latent_in, species, decode_w, react_a, react_b, stoich, encode_w, rate_const)

        def dark_branch(values):
            return jnp.zeros(values.shape, jnp.bfloat16)

        return lax.cond(sun_flag > 0, lit_branch, dark_branch, block_data)

    for step_index in range(STEPS):
        tracers = diffuse(advect(latent_field, east_courant, north_courant), mixing)
        blocks = tracers.reshape(n_species, n_levels, block_rows, BLOCK, block_cols, BLOCK).transpose(2, 4, 0, 1, 3, 5).reshape(block_rows * block_cols, n_species, n_levels * BLOCK * BLOCK)
        increments = lax.map(react_block, (blocks, sun_flags))
        blocks = blocks + increments.astype(jnp.float32)
        latent_field = blocks.reshape(block_rows, block_cols, n_species, n_levels, BLOCK, BLOCK).transpose(2, 3, 0, 4, 1, 5).reshape(n_species, n_levels, lat_cells, lon_cells)
    return latent_field
```

```python
import functools

import jax
import jax.numpy as jnp
from jax import lax
from jax.experimental import pallas as pl
from jax.experimental.pallas import tpu as pltpu
from jax.sharding import PartitionSpec as P

BLOCK = 16
SUBSTEPS = 2
STEPS = 2

F32 = jnp.float32
BF16 = jnp.bfloat16
VMEM_BYTES = 48 * 1024 * 1024


def lane_ids(shape):
    return lax.broadcasted_iota(jnp.int32, shape, len(shape) - 1)


def fold_kernel(decode_t, react_a_t, react_b_t, stoich, encode, rate, linear_out, encode_out):
    n_reactions = react_a_t.shape[1]
    contract = (((0,), (1,)), ((), ()))
    for part, react in enumerate((react_a_t, react_b_t)):
        product = lax.dot_general(
            react[...], decode_t[...], contract, preferred_element_type=F32
        )
        linear_out[part * n_reactions : (part + 1) * n_reactions, :] = product.astype(BF16)
    folded = jnp.dot(encode[...], stoich[...], preferred_element_type=F32)
    encode_out[...] = (folded * rate[...]).astype(BF16)


def fold_weights(decode_w, react_a, react_b, stoich, encode_w, rate_const):
    n_reactions, n_species = react_a.shape[0], decode_w.shape[1]
    return pl.pallas_call(
        fold_kernel,
        out_shape=(
            jax.ShapeDtypeStruct((2 * n_reactions, n_species), BF16),
            jax.ShapeDtypeStruct((n_species, n_reactions), BF16),
        ),
        cost_estimate=pl.CostEstimate(flops=20_000_000, bytes_accessed=500_000, transcendentals=0),
        name="fold_weights",
    )(decode_w.T, react_a.T, react_b.T, stoich, encode_w, rate_const[None])


def pack_sides(value, coef, at, west, east):
    lanes = lane_ids(value.shape)
    size = value.shape[-1]
    turned = pltpu.roll(value * coef, at, 1)
    west = jnp.where(lanes == at, turned, west)
    east = jnp.where(lanes == (at + size - 1) % size, turned, east)
    return west, east


def edge_kernel(n_levels, n_rows, latent, east_c, north_c, moved_out, west, east, south, north):
    n_species, n_cols = west.shape
    cells = n_levels * n_rows
    lanes = lane_ids((1, n_cols))

    def row(r, sides):
        for level in range(n_levels):
            at = level * n_rows + r
            value = latent[pl.ds(at, n_species, stride=cells), :]
            moved_out[level, r] = value
            speed = east_c[level, pl.ds(r, 1), :]
            coef = jnp.where(lanes == 0, jnp.minimum(speed, 0.0), jnp.maximum(speed, 0.0))
            sides = pack_sides(value, coef, at, *sides)
        return sides

    zeros = jnp.zeros((n_species, n_cols), F32)
    west[...], east[...] = lax.fori_loop(0, n_rows, row, (zeros, zeros))
    for level in range(n_levels):
        for edge, out, clip in ((0, south, jnp.minimum), (n_rows - 1, north, jnp.maximum)):
            speed = clip(north_c[level, edge : edge + 1, :], 0.0)
            out[level] = (moved_out[level, edge] * speed).astype(BF16)


def step_kernel(
    n_levels,
    n_rows,
    last,
    sun,
    place,
    field,
    east_c,
    north_c,
    mixing,
    linear,
    encode,
    west_in,
    east_in,
    south_in,
    north_in,
    *refs,
):
    coefs = refs[-1]
    n_species, n_cols = west_in.shape
    n_reactions = encode.shape[1]
    cells = n_levels * n_rows
    lanes = lane_ids((1, n_cols))
    row_ids = lax.broadcasted_iota(jnp.int32, (n_rows, n_cols), 0)
    is_first, is_last = place[0] > 0, place[1] > 0
    CENTRE, EAST, WEST, NORTH, SOUTH, SCALE, LOWER, UPPER = range(8)

    upper = None
    for level in range(n_levels):
        ce, cn = east_c[level], north_c[level]
        east, west = jnp.maximum(ce, 0.0), jnp.minimum(ce, 0.0)
        north = jnp.where((row_ids == n_rows - 1) & is_last, 0.0, jnp.maximum(cn, 0.0))
        south = jnp.where((row_ids == 0) & is_first, 0.0, jnp.minimum(cn, 0.0))
        coefs[CENTRE, level] = 1.0 - east + west - north + south
        coefs[EAST, level] = east
        coefs[WEST, level] = west
        coefs[NORTH, level] = north
        coefs[SOUTH, level] = south
        pivot = 1.0
        if level > 0:
            below = mixing[level - 1]
            pivot = pivot + below - below * upper
        if level < n_levels - 1:
            pivot = pivot + mixing[level]
        scale = 1.0 / pivot
        coefs[SCALE, level] = scale
        if level > 0:
            coefs[LOWER, level] = below * scale
        if level < n_levels - 1:
            upper = mixing[level] * scale
            coefs[UPPER, level] = upper

    lit = jnp.zeros((1, n_cols), jnp.int32)
    for block in range(n_cols // BLOCK):
        lit = jnp.where(lanes // BLOCK == block, sun[0, block], lit)
    lit = lit > 0

    def coef(kind, level, r):
        return coefs[kind, level, pl.ds(r, 1), :]

    def transported(r):
        before, after = jnp.maximum(r - 1, 0), jnp.minimum(r + 1, n_rows - 1)
        swept = []
        for level in range(n_levels):
            at = level * n_rows + r
            value = field[level, r]
            from_west = jnp.where(
                lanes == 0,
                pltpu.roll(west_in[...], (n_cols + 1 - at) % n_cols, 1),
                pltpu.roll(value * coef(EAST, level, r), 1, 1),
            )
            from_east = jnp.where(
                lanes == n_cols - 1,
                pltpu.roll(east_in[...], n_cols - 1 - at, 1),
                pltpu.roll(value * coef(WEST, level, r), n_cols - 1, 1),
            )
            from_south = jnp.where(
                r == 0,
                south_in[level].astype(F32),
                field[level, before] * coef(NORTH, level, before),
            )
            from_north = jnp.where(
                r == n_rows - 1,
                north_in[level].astype(F32),
                field[level, after] * coef(SOUTH, level, after),
            )
            moved = value * coef(CENTRE, level, r) + (from_west - from_east) + (from_south - from_north)
            right = moved * coef(SCALE, level, r)
            if level > 0:
                right = right + coef(LOWER, level, r) * swept[-1]
            swept.append(right)
        for level in range(n_levels - 2, -1, -1):
            swept[level] = swept[level] + coef(UPPER, level, r) * swept[level + 1]
        return swept

    def increment_of(latent):
        rounded = latent.astype(BF16)
        current = rounded.astype(F32)
        summed = None
        for substep in range(SUBSTEPS):
            both = jnp.dot(linear[...], rounded, preferred_element_type=F32)
            rates = (both[:n_reactions] * both[n_reactions:]).astype(BF16)
            change = jnp.dot(encode[...], rates, preferred_element_type=F32)
            summed = change if summed is None else summed + change
            if substep < SUBSTEPS - 1:
                current = current + change
                rounded = current.astype(BF16)
        return summed

    def row(r, sides):
        diffused = transported(r)
        for level in range(0, n_levels, 2):
            tile = jnp.concatenate(diffused[level : level + 2], axis=1)
            tile = tile + jnp.where(
                jnp.concatenate([lit, lit], axis=1), increment_of(tile), 0.0
            )
            for half in range(2):
                value = tile[:, half * n_cols : (half + 1) * n_cols]
                at = (level + half) * n_rows + r
                if last:
                    refs[0][pl.ds(at, n_species, stride=cells), :] = value
                else:
                    refs[0][level + half, r] = value
                    speed = east_c[level + half, pl.ds(r, 1), :]
                    side = jnp.where(
                        lanes == 0, jnp.minimum(speed, 0.0), jnp.maximum(speed, 0.0)
                    )
                    sides = pack_sides(value, side, at, *sides)
        return sides

    if last:
        lax.fori_loop(0, n_rows, lambda r, c: row(r, c), 0)
        return
    out, west, east, south, north = refs[:5]
    zeros = jnp.zeros((n_species, n_cols), F32)
    west[...], east[...] = lax.fori_loop(0, n_rows, row, (zeros, zeros))
    for level in range(n_levels):
        for edge, send, clip in ((0, south, jnp.minimum), (n_rows - 1, north, jnp.maximum)):
            speed = clip(north_c[level, edge : edge + 1, :], 0.0)
            send[level] = (out[level, edge] * speed).astype(BF16)


def vmem(count):
    return [pl.BlockSpec(memory_space=pltpu.VMEM)] * count


def exchanged(west, east, south, north):
    lon, lat = lax.axis_size("lon"), lax.axis_size("lat")
    up = [(i, (i + 1) % lon) for i in range(lon)]
    down = [(j, i) for i, j in up]
    climb = [(i, i + 1) for i in range(lat - 1)]
    descend = [(j, i) for i, j in climb]
    from_south = lax.ppermute(north, "lat", climb)
    from_north = lax.ppermute(south, "lat", descend)
    from_west = lax.ppermute(east, "lon", up)
    from_east = lax.ppermute(west, "lon", down)
    return from_west, from_east, from_south, from_north


def on_device(
    latent_field,
    east_courant,
    north_courant,
    mixing,
    sunlit,
    decode_w,
    react_a,
    react_b,
    stoich,
    encode_w,
    rate_const,
):
    n_species, n_levels, n_rows, n_cols = latent_field.shape
    flat = (n_species * n_levels * n_rows, n_cols)
    layered = jax.ShapeDtypeStruct((n_levels, n_rows, n_species, n_cols), F32)
    side = jax.ShapeDtypeStruct((n_species, n_cols), F32)
    edge = jax.ShapeDtypeStruct((n_levels, n_species, n_cols), BF16)
    params = pltpu.CompilerParams(vmem_limit_bytes=VMEM_BYTES)
    field, *edges = pl.pallas_call(
        functools.partial(edge_kernel, n_levels, n_rows),
        out_shape=(layered, side, side, edge, edge),
        in_specs=vmem(3),
        out_specs=tuple(vmem(5)),
        compiler_params=params,
        name="edges",
    )(latent_field.reshape(flat), east_courant, north_courant)
    linear, encode = fold_weights(decode_w, react_a, react_b, stoich, encode_w, rate_const)
    lat_index = lax.axis_index("lat")
    place = jnp.stack([lat_index == 0, lat_index == lax.axis_size("lat") - 1]).astype(jnp.int32)
    for step in range(STEPS):
        last = step == STEPS - 1
        halos = exchanged(*edges)
        outs = pl.pallas_call(
            functools.partial(step_kernel, n_levels, n_rows, last),
            out_shape=(jax.ShapeDtypeStruct(flat, F32),)
            if last
            else (layered, side, side, edge, edge),
            in_specs=[pl.BlockSpec(memory_space=pltpu.SMEM)] * 2 + vmem(10),
            out_specs=tuple(vmem(1 if last else 5)),
            scratch_shapes=[pltpu.VMEM((8, n_levels, n_rows, n_cols), F32)],
            compiler_params=params,
            name="splitting_step",
        )(sunlit, place, field, east_courant, north_courant, mixing, linear, encode, *halos)
        field, edges = outs[0], outs[1:]
    return field.reshape(latent_field.shape)


def solution(mesh):
    placed = (
        P(None, None, "lat", "lon"),
        P(None, "lat", "lon"),
        P(None, "lat", "lon"),
        P(None, "lat", "lon"),
        P("lat", "lon"),
        P(),
        P(),
        P(),
        P(),
        P(),
        P(),
    )
    return jax.shard_map(
        on_device,
        mesh=mesh,
        in_specs=placed,
        out_specs=P(None, None, "lat", "lon"),
        check_vma=False,
    )
```

```python
import functools

import jax
import jax.numpy as jnp
from jax import lax
from jax.experimental import pallas as pl
from jax.experimental.pallas import tpu as pltpu
from jax.sharding import PartitionSpec as P

BLOCK = 16
SUBSTEPS = 2
STEPS = 2
GROUP = 16
ROWS_AT_ONCE = 2

F32 = jnp.float32
BF16 = jnp.bfloat16
VMEM_BYTES = 48 * 1024 * 1024


def lane_ids(shape):
    return lax.broadcasted_iota(jnp.int32, shape, len(shape) - 1)


def fold_kernel(decode_t, react_a_t, react_b_t, stoich, encode, rate, linear_out, encode_out):
    n_reactions = react_a_t.shape[1]
    contract = (((0,), (1,)), ((), ()))
    for part, react in enumerate((react_a_t, react_b_t)):
        product = lax.dot_general(
            react[...], decode_t[...], contract, preferred_element_type=F32
        )
        for group in range(n_reactions // GROUP):
            at = (2 * group + part) * GROUP
            linear_out[at : at + GROUP, :] = product[
                group * GROUP : (group + 1) * GROUP
            ].astype(BF16)
    folded = jnp.dot(encode[...], stoich[...], preferred_element_type=F32)
    encode_out[...] = (folded * rate[...]).astype(BF16)


def fold_weights(decode_w, react_a, react_b, stoich, encode_w, rate_const):
    n_reactions, n_species = react_a.shape[0], decode_w.shape[1]
    return pl.pallas_call(
        fold_kernel,
        out_shape=(
            jax.ShapeDtypeStruct((2 * n_reactions, n_species), BF16),
            jax.ShapeDtypeStruct((n_species, n_reactions), BF16),
        ),
        cost_estimate=pl.CostEstimate(flops=20_000_000, bytes_accessed=500_000, transcendentals=0),
        name="fold_weights",
    )(decode_w.T, react_a.T, react_b.T, stoich, encode_w, rate_const[None])


def pack_sides(value, coef, at, west, east):
    lanes = lane_ids(value.shape)
    size = value.shape[-1]
    turned = pltpu.roll(value * coef, at, 1)
    west = jnp.where(lanes == at, turned, west)
    east = jnp.where(lanes == (at + size - 1) % size, turned, east)
    return west, east


def edge_kernel(n_levels, n_rows, latent, east_c, north_c, moved_out, west, east, south, north):
    n_species, n_cols = west.shape
    cells = n_levels * n_rows
    lanes = lane_ids((1, n_cols))

    def row(r, sides):
        for level in range(n_levels):
            at = level * n_rows + r
            value = latent[pl.ds(at, n_species, stride=cells), :]
            moved_out[level, r] = value
            speed = east_c[level, pl.ds(r, 1), :]
            coef = jnp.where(lanes == 0, jnp.minimum(speed, 0.0), jnp.maximum(speed, 0.0))
            sides = pack_sides(value, coef, at, *sides)
        return sides

    zeros = jnp.zeros((n_species, n_cols), F32)
    west[...], east[...] = lax.fori_loop(0, n_rows, row, (zeros, zeros))
    for level in range(n_levels):
        for edge, out, clip in ((0, south, jnp.minimum), (n_rows - 1, north, jnp.maximum)):
            speed = clip(north_c[level, edge : edge + 1, :], 0.0)
            out[level] = (moved_out[level, edge] * speed).astype(BF16)


def step_kernel(
    n_levels,
    n_rows,
    last,
    sun,
    place,
    field,
    east_c,
    north_c,
    mixing,
    linear,
    encode,
    west_in,
    east_in,
    south_in,
    north_in,
    *refs,
):
    coefs, diffused = refs[-2:]
    n_species, n_cols = west_in.shape
    n_reactions = encode.shape[1]
    cells = n_levels * n_rows
    lanes = lane_ids((1, n_cols))
    row_ids = lax.broadcasted_iota(jnp.int32, (n_rows, n_cols), 0)
    is_first, is_last = place[0] > 0, place[1] > 0
    CENTRE, EAST, WEST, NORTH, SOUTH, SCALE, LOWER, UPPER = range(8)

    upper = None
    for level in range(n_levels):
        ce, cn = east_c[level], north_c[level]
        east, west = jnp.maximum(ce, 0.0), jnp.minimum(ce, 0.0)
        north = jnp.where((row_ids == n_rows - 1) & is_last, 0.0, jnp.maximum(cn, 0.0))
        south = jnp.where((row_ids == 0) & is_first, 0.0, jnp.minimum(cn, 0.0))
        coefs[CENTRE, level] = 1.0 - east + west - north + south
        coefs[EAST, level] = east
        coefs[WEST, level] = west
        coefs[NORTH, level] = north
        coefs[SOUTH, level] = south
        pivot = 1.0
        if level > 0:
            below = mixing[level - 1]
            pivot = pivot + below - below * upper
        if level < n_levels - 1:
            pivot = pivot + mixing[level]
        scale = 1.0 / pivot
        coefs[SCALE, level] = scale
        if level > 0:
            coefs[LOWER, level] = below * scale
        if level < n_levels - 1:
            upper = mixing[level] * scale
            coefs[UPPER, level] = upper

    lit = jnp.zeros((1, n_cols), jnp.int32)
    for block in range(n_cols // BLOCK):
        lit = jnp.where(lanes // BLOCK == block, sun[0, block], lit)
    lit = lit > 0

    def coef(kind, level, r):
        return coefs[kind, level, pl.ds(r, 1), :]

    def transported(r):
        before, after = jnp.maximum(r - 1, 0), jnp.minimum(r + 1, n_rows - 1)
        swept = []
        for level in range(n_levels):
            at = level * n_rows + r
            value = field[level, r]
            from_west = jnp.where(
                lanes == 0,
                pltpu.roll(west_in[...], (n_cols + 1 - at) % n_cols, 1),
                pltpu.roll(value * coef(EAST, level, r), 1, 1),
            )
            from_east = jnp.where(
                lanes == n_cols - 1,
                pltpu.roll(east_in[...], n_cols - 1 - at, 1),
                pltpu.roll(value * coef(WEST, level, r), n_cols - 1, 1),
            )
            from_south = jnp.where(
                r == 0,
                south_in[level].astype(F32),
                field[level, before] * coef(NORTH, level, before),
            )
            from_north = jnp.where(
                r == n_rows - 1,
                north_in[level].astype(F32),
                field[level, after] * coef(SOUTH, level, after),
            )
            moved = value * coef(CENTRE, level, r) + (from_west - from_east) + (from_south - from_north)
            right = moved * coef(SCALE, level, r)
            if level > 0:
                right = right + coef(LOWER, level, r) * swept[-1]
            swept.append(right)
        for level in range(n_levels - 2, -1, -1):
            swept[level] = swept[level] + coef(UPPER, level, r) * swept[level + 1]
        return swept

    def product_of(rounded):
        both = jnp.dot(linear[...], rounded, preferred_element_type=F32)
        parts = [
            both[at : at + GROUP] * both[at + GROUP : at + 2 * GROUP]
            for at in range(0, 2 * n_reactions, 2 * GROUP)
        ]
        return jnp.concatenate(parts, axis=0).astype(BF16)

    def increments(tiles):
        rounded = [tile.astype(BF16) for tile in tiles]
        current = [value.astype(F32) for value in rounded]
        summed = [None] * len(tiles)
        units = [(substep, tile) for substep in range(SUBSTEPS) for tile in range(len(tiles))]
        rates = {}
        for at in range(len(units) + 1):
            if at < len(units):
                rates[at] = product_of(rounded[units[at][1]])
            if at > 0:
                substep, tile = units[at - 1]
                change = jnp.dot(encode[...], rates.pop(at - 1), preferred_element_type=F32)
                if substep == 0:
                    summed[tile] = change
                else:
                    summed[tile] = summed[tile] + change
                if substep < SUBSTEPS - 1:
                    current[tile] = current[tile] + change
                    rounded[tile] = current[tile].astype(BF16)
        return summed

    def transport_row(r, carry):
        for level, value in enumerate(transported(r)):
            diffused[level, r] = value
        return carry

    lax.fori_loop(0, n_rows, transport_row, 0)
    lit_pair = jnp.concatenate([lit, lit], axis=1)

    def rows(group, sides):
        places = [
            (level, group * ROWS_AT_ONCE + extra)
            for extra in range(ROWS_AT_ONCE)
            for level in range(0, n_levels, 2)
        ]
        tiles = [
            jnp.concatenate([diffused[level, r], diffused[level + 1, r]], axis=1)
            for level, r in places
        ]
        for (level, r), tile, change in zip(places, tiles, increments(tiles)):
            tile = tile + jnp.where(lit_pair, change, 0.0)
            for half in range(2):
                value = tile[:, half * n_cols : (half + 1) * n_cols]
                at = (level + half) * n_rows + r
                if last:
                    refs[0][pl.ds(at, n_species, stride=cells), :] = value
                else:
                    refs[0][level + half, r] = value
                    speed = east_c[level + half, pl.ds(r, 1), :]
                    side = jnp.where(
                        lanes == 0, jnp.minimum(speed, 0.0), jnp.maximum(speed, 0.0)
                    )
                    sides = pack_sides(value, side, at, *sides)
        return sides

    n_groups = n_rows // ROWS_AT_ONCE
    if last:
        lax.fori_loop(0, n_groups, rows, 0)
        return
    out, west, east, south, north = refs[:5]
    zeros = jnp.zeros((n_species, n_cols), F32)
    west[...], east[...] = lax.fori_loop(0, n_groups, rows, (zeros, zeros))
    for level in range(n_levels):
        for edge, send, clip in ((0, south, jnp.minimum), (n_rows - 1, north, jnp.maximum)):
            speed = clip(north_c[level, edge : edge + 1, :], 0.0)
            send[level] = (out[level, edge] * speed).astype(BF16)


def vmem(count):
    return [pl.BlockSpec(memory_space=pltpu.VMEM)] * count


def exchanged(west, east, south, north):
    lon, lat = lax.axis_size("lon"), lax.axis_size("lat")
    up = [(i, (i + 1) % lon) for i in range(lon)]
    down = [(j, i) for i, j in up]
    climb = [(i, i + 1) for i in range(lat - 1)]
    descend = [(j, i) for i, j in climb]
    from_south = lax.ppermute(north, "lat", climb)
    from_north = lax.ppermute(south, "lat", descend)
    from_west = lax.ppermute(east, "lon", up)
    from_east = lax.ppermute(west, "lon", down)
    return from_west, from_east, from_south, from_north


def on_device(
    latent_field,
    east_courant,
    north_courant,
    mixing,
    sunlit,
    decode_w,
    react_a,
    react_b,
    stoich,
    encode_w,
    rate_const,
):
    n_species, n_levels, n_rows, n_cols = latent_field.shape
    flat = (n_species * n_levels * n_rows, n_cols)
    layered = jax.ShapeDtypeStruct((n_levels, n_rows, n_species, n_cols), F32)
    side = jax.ShapeDtypeStruct((n_species, n_cols), F32)
    edge = jax.ShapeDtypeStruct((n_levels, n_species, n_cols), BF16)
    params = pltpu.CompilerParams(vmem_limit_bytes=VMEM_BYTES)
    field, *edges = pl.pallas_call(
        functools.partial(edge_kernel, n_levels, n_rows),
        out_shape=(layered, side, side, edge, edge),
        in_specs=vmem(3),
        out_specs=tuple(vmem(5)),
        compiler_params=params,
        name="edges",
    )(latent_field.reshape(flat), east_courant, north_courant)
    linear, encode = fold_weights(decode_w, react_a, react_b, stoich, encode_w, rate_const)
    lat_index = lax.axis_index("lat")
    place = jnp.stack([lat_index == 0, lat_index == lax.axis_size("lat") - 1]).astype(jnp.int32)
    for step in range(STEPS):
        last = step == STEPS - 1
        halos = exchanged(*edges)
        outs = pl.pallas_call(
            functools.partial(step_kernel, n_levels, n_rows, last),
            out_shape=(jax.ShapeDtypeStruct(flat, F32),)
            if last
            else (layered, side, side, edge, edge),
            in_specs=[pl.BlockSpec(memory_space=pltpu.SMEM)] * 2 + vmem(10),
            out_specs=tuple(vmem(1 if last else 5)),
            scratch_shapes=[
                pltpu.VMEM((8, n_levels, n_rows, n_cols), F32),
                pltpu.VMEM(layered.shape, F32),
            ],
            compiler_params=params,
            name="splitting_step",
        )(sunlit, place, field, east_courant, north_courant, mixing, linear, encode, *halos)
        field, edges = outs[0], outs[1:]
    return field.reshape(latent_field.shape)


def solution(mesh):
    placed = (
        P(None, None, "lat", "lon"),
        P(None, "lat", "lon"),
        P(None, "lat", "lon"),
        P(None, "lat", "lon"),
        P("lat", "lon"),
        P(),
        P(),
        P(),
        P(),
        P(),
        P(),
    )
    return jax.shard_map(
        on_device,
        mesh=mesh,
        in_specs=placed,
        out_specs=P(None, None, "lat", "lon"),
        check_vma=False,
    )
```

```python
import functools

import jax
import jax.numpy as jnp
from jax import lax
from jax.experimental import pallas as pl
from jax.experimental.pallas import tpu as pltpu
from jax.sharding import PartitionSpec as P

BLOCK = 16
SUBSTEPS = 2
STEPS = 2
GROUP = 16
ROWS_AT_ONCE = 2
LEVELS_AT_ONCE = 8

F32 = jnp.float32
BF16 = jnp.bfloat16
VMEM_BYTES = 48 * 1024 * 1024


def lane_ids(shape):
    return lax.broadcasted_iota(jnp.int32, shape, len(shape) - 1)


def fold_kernel(decode_t, react_a_t, react_b_t, stoich, encode, rate, linear_out, encode_out):
    n_reactions = react_a_t.shape[1]
    contract = (((0,), (1,)), ((), ()))
    for part, react in enumerate((react_a_t, react_b_t)):
        product = lax.dot_general(
            react[...], decode_t[...], contract, preferred_element_type=F32
        )
        for group in range(n_reactions // GROUP):
            at = (2 * group + part) * GROUP
            linear_out[at : at + GROUP, :] = product[
                group * GROUP : (group + 1) * GROUP
            ].astype(BF16)
    folded = jnp.dot(encode[...], stoich[...], preferred_element_type=F32)
    encode_out[...] = (folded * rate[...]).astype(BF16)


def fold_weights(decode_w, react_a, react_b, stoich, encode_w, rate_const):
    n_reactions, n_species = react_a.shape[0], decode_w.shape[1]
    return pl.pallas_call(
        fold_kernel,
        out_shape=(
            jax.ShapeDtypeStruct((2 * n_reactions, n_species), BF16),
            jax.ShapeDtypeStruct((n_species, n_reactions), BF16),
        ),
        out_specs=tuple(vmem(2)),
        compiler_params=pltpu.CompilerParams(vmem_limit_bytes=VMEM_BYTES),
        cost_estimate=pl.CostEstimate(flops=20_000_000, bytes_accessed=500_000, transcendentals=0),
        name="fold_weights",
    )(decode_w.T, react_a.T, react_b.T, stoich, encode_w, rate_const[None])


def pack_sides(value, coef, at, west, east):
    lanes = lane_ids(value.shape)
    size = value.shape[-1]
    turned = pltpu.roll(value * coef, at, 1)
    west = jnp.where(lanes == at, turned, west)
    east = jnp.where(lanes == (at + size - 1) % size, turned, east)
    return west, east


def edge_kernel(place, latent, east_c, north_c, moved_out, west, east, south, north, *scratch):
    tiles, east_v, north_v, sems = scratch
    n_levels, n_species, n_rows, n_cols = tiles.shape
    lanes = lane_ids((1, n_cols))
    copies = [
        pltpu.make_async_copy(east_c, east_v, sems.at[n_levels]),
        pltpu.make_async_copy(north_c, north_v, sems.at[n_levels + 1]),
    ]
    for level in range(n_levels):
        copies.append(
            pltpu.make_async_copy(latent.at[:, level], tiles.at[level], sems.at[level])
        )
    for copy in copies:
        copy.start()
    copies[0].wait()
    copies[1].wait()
    sides = (jnp.zeros((n_species, n_cols), F32),) * 2
    for level in range(n_levels):
        copies[2 + level].wait()
        tile = tiles.at[level].reshape(n_species * n_rows, n_cols)
        for r in range(n_rows):
            at = level * n_rows + r
            value = tile[pl.ds(r, n_species, stride=n_rows), :]
            moved_out[level, r] = value
            speed = east_v[level, r : r + 1, :]
            coef = jnp.where(lanes == 0, jnp.minimum(speed, 0.0), jnp.maximum(speed, 0.0))
            sides = pack_sides(value, coef, at, *sides)
        low = jnp.minimum(north_v[level, :1, :], 0.0)
        south[level] = (moved_out[level, 0] * jnp.where(place[0] > 0, 0.0, low)).astype(BF16)
        high = jnp.maximum(north_v[level, n_rows - 1 :, :], 0.0)
        north[level] = (moved_out[level, n_rows - 1] * jnp.where(place[1] > 0, 0.0, high)).astype(BF16)
    west[...], east[...] = sides


def step_kernel(
    n_levels,
    n_rows,
    last,
    sun,
    place,
    field,
    east_c,
    north_c,
    mixing,
    linear,
    encode,
    west_in,
    east_in,
    south_in,
    north_in,
    *refs,
):
    coefs, diffused = refs[-2:]
    n_species, n_cols = west_in.shape
    n_reactions = encode.shape[1]
    cells = n_levels * n_rows
    lanes = lane_ids((1, n_cols))
    row_ids = lax.broadcasted_iota(jnp.int32, (n_rows, n_cols), 0)
    is_first, is_last = place[0] > 0, place[1] > 0
    CENTRE, EAST, WEST, NORTH, SOUTH, SCALE, LOWER, UPPER = range(8)

    upper = None
    for level in range(n_levels):
        ce, cn = east_c[level], north_c[level]
        east, west = jnp.maximum(ce, 0.0), jnp.minimum(ce, 0.0)
        north = jnp.where((row_ids == n_rows - 1) & is_last, 0.0, jnp.maximum(cn, 0.0))
        south = jnp.where((row_ids == 0) & is_first, 0.0, jnp.minimum(cn, 0.0))
        coefs[CENTRE, level] = 1.0 - east + west - north + south
        coefs[EAST, level] = east
        coefs[WEST, level] = west
        coefs[NORTH, level] = north
        coefs[SOUTH, level] = south
        pivot = 1.0
        if level > 0:
            below = mixing[level - 1]
            pivot = pivot + below - below * upper
        if level < n_levels - 1:
            pivot = pivot + mixing[level]
        scale = 1.0 / pivot
        coefs[SCALE, level] = scale
        if level > 0:
            coefs[LOWER, level] = below * scale
        if level < n_levels - 1:
            upper = mixing[level] * scale
            coefs[UPPER, level] = upper

    lit = jnp.zeros((1, n_cols), jnp.int32)
    for block in range(n_cols // BLOCK):
        lit = jnp.where(lanes // BLOCK == block, sun[0, block], lit)
    lit = lit > 0

    def coef(kind, level, r):
        return coefs[kind, level, pl.ds(r, 1), :]

    def transported(r):
        before, after = jnp.maximum(r - 1, 0), jnp.minimum(r + 1, n_rows - 1)
        swept = []
        for level in range(n_levels):
            at = level * n_rows + r
            value = field[level, r]
            from_west = jnp.where(
                lanes == 0,
                pltpu.roll(west_in[...], (n_cols + 1 - at) % n_cols, 1),
                pltpu.roll(value * coef(EAST, level, r), 1, 1),
            )
            from_east = jnp.where(
                lanes == n_cols - 1,
                pltpu.roll(east_in[...], n_cols - 1 - at, 1),
                pltpu.roll(value * coef(WEST, level, r), n_cols - 1, 1),
            )
            from_south = jnp.where(
                r == 0,
                south_in[level].astype(F32),
                field[level, before] * coef(NORTH, level, before),
            )
            from_north = jnp.where(
                r == n_rows - 1,
                north_in[level].astype(F32),
                field[level, after] * coef(SOUTH, level, after),
            )
            moved = value * coef(CENTRE, level, r) + (from_west - from_east) + (from_south - from_north)
            right = moved * coef(SCALE, level, r)
            if level > 0:
                right = right + coef(LOWER, level, r) * swept[-1]
            swept.append(right)
        for level in range(n_levels - 2, -1, -1):
            swept[level] = swept[level] + coef(UPPER, level, r) * swept[level + 1]
        return swept

    def product_of(rounded):
        both = jnp.dot(linear[...], rounded, preferred_element_type=F32)
        parts = [
            both[at : at + GROUP] * both[at + GROUP : at + 2 * GROUP]
            for at in range(0, 2 * n_reactions, 2 * GROUP)
        ]
        return jnp.concatenate(parts, axis=0).astype(BF16)

    def increments(tiles):
        rounded = [tile.astype(BF16) for tile in tiles]
        current = [value.astype(F32) for value in rounded]
        summed = [None] * len(tiles)
        units = [(substep, tile) for substep in range(SUBSTEPS) for tile in range(len(tiles))]
        rates = {}
        for at in range(len(units) + 1):
            if at < len(units):
                rates[at] = product_of(rounded[units[at][1]])
            if at > 0:
                substep, tile = units[at - 1]
                change = jnp.dot(encode[...], rates.pop(at - 1), preferred_element_type=F32)
                if substep == 0:
                    summed[tile] = change
                else:
                    summed[tile] = summed[tile] + change
                if substep < SUBSTEPS - 1:
                    current[tile] = current[tile] + change
                    rounded[tile] = current[tile].astype(BF16)
        return summed

    def transport_row(r, carry):
        for level, value in enumerate(transported(r)):
            diffused[level, r] = value
        return carry

    lax.fori_loop(0, n_rows, transport_row, 0)
    lit_tile = jnp.concatenate([lit] * LEVELS_AT_ONCE, axis=1)

    def rows(group, sides):
        places = [
            (level, group * ROWS_AT_ONCE + extra)
            for extra in range(ROWS_AT_ONCE)
            for level in range(0, n_levels, LEVELS_AT_ONCE)
        ]
        tiles = [
            jnp.concatenate(
                [diffused[level + extra, r] for extra in range(LEVELS_AT_ONCE)], axis=1
            )
            for level, r in places
        ]
        for (level, r), tile, change in zip(places, tiles, increments(tiles)):
            tile = tile + jnp.where(lit_tile, change, 0.0)
            for half in range(LEVELS_AT_ONCE):
                value = tile[:, half * n_cols : (half + 1) * n_cols]
                at = (level + half) * n_rows + r
                if last:
                    refs[0][pl.ds(at, n_species, stride=cells), :] = value
                else:
                    refs[0][level + half, r] = value
                    speed = east_c[level + half, pl.ds(r, 1), :]
                    side = jnp.where(
                        lanes == 0, jnp.minimum(speed, 0.0), jnp.maximum(speed, 0.0)
                    )
                    sides = pack_sides(value, side, at, *sides)
        return sides

    n_groups = n_rows // ROWS_AT_ONCE
    if last:
        lax.fori_loop(0, n_groups, rows, 0)
        return
    out, west, east, south, north = refs[:5]
    zeros = jnp.zeros((n_species, n_cols), F32)
    west[...], east[...] = lax.fori_loop(0, n_groups, rows, (zeros, zeros))
    for level in range(n_levels):
        for edge, send, kind in ((0, south, SOUTH), (n_rows - 1, north, NORTH)):
            send[level] = (out[level, edge] * coefs[kind, level, edge : edge + 1]).astype(BF16)


def vmem(count):
    return [pl.BlockSpec(memory_space=pltpu.VMEM)] * count


def exchanged(west, east, south, north):
    lon, lat = lax.axis_size("lon"), lax.axis_size("lat")
    up = [(i, (i + 1) % lon) for i in range(lon)]
    down = [(j, i) for i, j in up]
    climb = [(i, (i + 1) % lat) for i in range(lat)]
    descend = [(j, i) for i, j in climb]
    from_south = lax.ppermute(north, "lat", climb)
    from_north = lax.ppermute(south, "lat", descend)
    from_west = lax.ppermute(east, "lon", up)
    from_east = lax.ppermute(west, "lon", down)
    return from_west, from_east, from_south, from_north


def on_device(
    latent_field,
    east_courant,
    north_courant,
    mixing,
    sunlit,
    decode_w,
    react_a,
    react_b,
    stoich,
    encode_w,
    rate_const,
):
    n_species, n_levels, n_rows, n_cols = latent_field.shape
    flat = (n_species * n_levels * n_rows, n_cols)
    layered = jax.ShapeDtypeStruct((n_levels, n_rows, n_species, n_cols), F32)
    side = jax.ShapeDtypeStruct((n_species, n_cols), F32)
    edge = jax.ShapeDtypeStruct((n_levels, n_species, n_cols), BF16)
    params = pltpu.CompilerParams(vmem_limit_bytes=VMEM_BYTES)
    lat_index = lax.axis_index("lat")
    place = jnp.stack([lat_index == 0, lat_index == lax.axis_size("lat") - 1]).astype(jnp.int32)
    smem = pl.BlockSpec(memory_space=pltpu.SMEM)
    hbm = pl.BlockSpec(memory_space=pltpu.HBM)
    field, *edges = pl.pallas_call(
        edge_kernel,
        out_shape=(layered, side, side, edge, edge),
        in_specs=[smem, hbm, hbm, hbm],
        out_specs=tuple(vmem(5)),
        scratch_shapes=[
            pltpu.VMEM((n_levels, n_species, n_rows, n_cols), F32),
            pltpu.VMEM((n_levels, n_rows, n_cols), F32),
            pltpu.VMEM((n_levels, n_rows, n_cols), F32),
            pltpu.SemaphoreType.DMA((n_levels + 2,)),
        ],
        compiler_params=params,
        name="edges",
    )(place, latent_field, east_courant, north_courant)
    linear, encode = fold_weights(decode_w, react_a, react_b, stoich, encode_w, rate_const)
    for step in range(STEPS):
        last = step == STEPS - 1
        halos = exchanged(*edges)
        outs = pl.pallas_call(
            functools.partial(step_kernel, n_levels, n_rows, last),
            out_shape=(jax.ShapeDtypeStruct(flat, F32),)
            if last
            else (layered, side, side, edge, edge),
            in_specs=[smem] * 2 + vmem(10),
            out_specs=tuple(vmem(1 if last else 5)),
            scratch_shapes=[
                pltpu.VMEM((8, n_levels, n_rows, n_cols), F32),
                pltpu.VMEM(layered.shape, F32),
            ],
            compiler_params=params,
            name="splitting_step",
        )(sunlit, place, field, east_courant, north_courant, mixing, linear, encode, *halos)
        field, edges = outs[0], outs[1:]
    return field.reshape(latent_field.shape)


def solution(mesh):
    placed = (
        P(None, None, "lat", "lon"),
        P(None, "lat", "lon"),
        P(None, "lat", "lon"),
        P(None, "lat", "lon"),
        P("lat", "lon"),
        P(),
        P(),
        P(),
        P(),
        P(),
        P(),
    )
    return jax.shard_map(
        on_device,
        mesh=mesh,
        in_specs=placed,
        out_specs=P(None, None, "lat", "lon"),
        check_vma=False,
    )
```

```python
import functools
import itertools

import jax
import jax.numpy as jnp
from jax import lax
from jax.experimental import pallas as pl
from jax.experimental.pallas import tpu as pltpu
from jax.sharding import PartitionSpec as P

BLOCK = 16
SUBSTEPS = 2
STEPS = 2
GROUP = 16
ROWS_AT_ONCE = 2
LEVELS_AT_ONCE = 4

F32 = jnp.float32
BF16 = jnp.bfloat16
VMEM_BYTES = 48 * 1024 * 1024
FIRST_VMEM_BYTES = 56 * 1024 * 1024


def lane_ids(shape):
    return lax.broadcasted_iota(jnp.int32, shape, len(shape) - 1)


def fold_weights(decode_t, react_a_t, react_b_t, stoich, encode, rate, linear_out, encode_out):
    n_reactions = react_a_t.shape[1]
    contract = (((0,), (1,)), ((), ()))
    for part, react in enumerate((react_a_t, react_b_t)):
        product = lax.dot_general(
            react[...], decode_t[...], contract, preferred_element_type=F32
        )
        for group in range(n_reactions // GROUP):
            at = (2 * group + part) * GROUP
            linear_out[at : at + GROUP, :] = product[
                group * GROUP : (group + 1) * GROUP
            ].astype(BF16)
    folded = jnp.dot(encode[...], stoich[...], preferred_element_type=F32)
    encode_out[...] = (folded * rate[...]).astype(BF16)


def pack_sides(value, coef, at, west, east):
    lanes = lane_ids(value.shape)
    size = value.shape[-1]
    turned = pltpu.roll(value * coef, at, 1)
    west = jnp.where(lanes == at, turned, west)
    east = jnp.where(lanes == (at + size - 1) % size, turned, east)
    return west, east


def first_kernel(place, latent, *refs):
    arrays, refs = refs[:8], refs[8:]
    west, east, south, north, linear, encode = refs[:6]
    tiles, held, sems = refs[6], refs[7:15], refs[15]
    east_v, north_v = held[:2]
    n_levels, n_species, n_rows, n_cols = tiles.shape
    lanes = lane_ids((1, n_cols))
    copies = [
        pltpu.make_async_copy(array, place_of, sems.at[n_levels + at])
        for at, (array, place_of) in enumerate(zip(arrays, held))
    ]
    levels = [
        pltpu.make_async_copy(latent.at[:, level], tiles.at[level], sems.at[level])
        for level in range(n_levels)
    ]
    for copy in copies + levels:
        copy.start()
    for copy in copies:
        copy.wait()
    fold_weights(*held[2:], linear, encode)
    sides = (jnp.zeros((n_species, n_cols), F32),) * 2
    for level in range(n_levels):
        levels[level].wait()
        tile = tiles.at[level].reshape(n_species * n_rows, n_cols)
        for r in range(n_rows):
            at = level * n_rows + r
            value = tile[pl.ds(r, n_species, stride=n_rows), :]
            speed = east_v[level, r : r + 1, :]
            coef = jnp.where(lanes == 0, jnp.minimum(speed, 0.0), jnp.maximum(speed, 0.0))
            sides = pack_sides(value, coef, at, *sides)
        for r, out, clip in ((0, south, jnp.minimum), (n_rows - 1, north, jnp.maximum)):
            speed = clip(north_v[level, r : r + 1, :], 0.0)
            speed = jnp.where(place[0 if r == 0 else 1] > 0, 0.0, speed)
            out[level] = (tile[pl.ds(r, n_species, stride=n_rows), :] * speed).astype(BF16)
    west[...], east[...] = sides


def step_kernel(
    n_levels,
    n_rows,
    first,
    last,
    sun,
    place,
    field,
    east_c,
    north_c,
    mixing,
    linear,
    encode,
    west_in,
    east_in,
    south_in,
    north_in,
    *refs,
):
    half_rows = n_rows // 2
    if last:
        coefs, diffused, staged, sems = refs[-4:]
    else:
        coefs, diffused = refs[-2:]
    n_species, n_cols = west_in.shape
    n_reactions = encode.shape[1]
    cells = n_levels * n_rows
    lanes = lane_ids((1, n_cols))
    row_ids = lax.broadcasted_iota(jnp.int32, (n_rows, n_cols), 0)
    is_first, is_last = place[0] > 0, place[1] > 0
    if first:
        latent, field, refs = field, refs[-3], refs[:-3] + refs[-2:]

        def gather(r, carry):
            for level in range(n_levels):
                at = level * n_rows + r
                field[level, r] = latent[pl.ds(at, n_species, stride=cells), :]
            return carry

        lax.fori_loop(0, n_rows, gather, 0)
    CENTRE, EAST, WEST, NORTH, SOUTH, SCALE, LOWER, UPPER = range(8)

    upper = None
    for level in range(n_levels):
        ce, cn = east_c[level], north_c[level]
        east, west = jnp.maximum(ce, 0.0), jnp.minimum(ce, 0.0)
        north = jnp.where((row_ids == n_rows - 1) & is_last, 0.0, jnp.maximum(cn, 0.0))
        south = jnp.where((row_ids == 0) & is_first, 0.0, jnp.minimum(cn, 0.0))
        coefs[CENTRE, level] = 1.0 - east + west - north + south
        coefs[EAST, level] = east
        coefs[WEST, level] = west
        coefs[NORTH, level] = north
        coefs[SOUTH, level] = south
        pivot = 1.0
        if level > 0:
            below = mixing[level - 1]
            pivot = pivot + below - below * upper
        if level < n_levels - 1:
            pivot = pivot + mixing[level]
        scale = 1.0 / pivot
        coefs[SCALE, level] = scale
        if level > 0:
            coefs[LOWER, level] = below * scale
        if level < n_levels - 1:
            upper = mixing[level] * scale
            coefs[UPPER, level] = upper

    lit = jnp.zeros((1, n_cols), jnp.int32)
    for block in range(n_cols // BLOCK):
        lit = jnp.where(lanes // BLOCK == block, sun[0, block], lit)
    lit = lit > 0

    def coef(kind, level, r):
        return coefs[kind, level, pl.ds(r, 1), :]

    def transport(slot):
        r = jnp.minimum(slot, n_rows - 1)
        before, after = jnp.maximum(r - 1, 0), jnp.minimum(r + 1, n_rows - 1)
        right = None
        for level in range(n_levels):
            at = level * n_rows + r
            value = field[level, r]
            from_west = jnp.where(
                lanes == 0,
                pltpu.roll(west_in[...], (n_cols + 1 - at) % n_cols, 1),
                pltpu.roll(value * coef(EAST, level, r), 1, 1),
            )
            from_east = jnp.where(
                lanes == n_cols - 1,
                pltpu.roll(east_in[...], n_cols - 1 - at, 1),
                pltpu.roll(value * coef(WEST, level, r), n_cols - 1, 1),
            )
            from_south = jnp.where(
                r == 0,
                south_in[level].astype(F32),
                field[level, before] * coef(NORTH, level, before),
            )
            from_north = jnp.where(
                r == n_rows - 1,
                north_in[level].astype(F32),
                field[level, after] * coef(SOUTH, level, after),
            )
            moved = value * coef(CENTRE, level, r) + (from_west - from_east) + (from_south - from_north)
            scaled = moved * coef(SCALE, level, r)
            right = scaled if level == 0 else scaled + coef(LOWER, level, r) * right
            diffused[level, slot] = right
            yield
        for level in range(n_levels - 2, -1, -1):
            right = diffused[level, slot] + coef(UPPER, level, r) * right
            diffused[level, slot] = right
            yield

    def product_of(rounded):
        both = jnp.dot(linear[...], rounded, preferred_element_type=F32)
        parts = [
            both[at : at + GROUP] * both[at + GROUP : at + 2 * GROUP]
            for at in range(0, 2 * n_reactions, 2 * GROUP)
        ]
        return jnp.concatenate(parts, axis=0).astype(BF16)

    def increments(rounded, beside):
        current = [value.astype(F32) for value in rounded]
        summed = [None] * len(rounded)
        units = [(substep, tile) for substep in range(SUBSTEPS) for tile in range(len(rounded))]
        rates = {}
        for at in range(len(units) + 1):
            if at < len(units):
                rates[at] = product_of(rounded[units[at][1]])
                beside()
            if at > 0:
                substep, tile = units[at - 1]
                change = jnp.dot(encode[...], rates.pop(at - 1), preferred_element_type=F32)
                if substep == 0:
                    summed[tile] = change
                else:
                    summed[tile] = summed[tile] + change
                if substep < SUBSTEPS - 1:
                    current[tile] = current[tile] + change
                    rounded[tile] = current[tile].astype(BF16)
        return summed

    for r in range(ROWS_AT_ONCE):
        for _ in transport(r):
            pass
    lit_tile = jnp.concatenate([lit] * LEVELS_AT_ONCE, axis=1)

    def rows(group, sides):
        places = [
            (level, group * ROWS_AT_ONCE + extra)
            for extra in range(ROWS_AT_ONCE)
            for level in range(0, n_levels, LEVELS_AT_ONCE)
        ]

        def tile_at(level, r):
            return jnp.concatenate(
                [diffused[level + extra, r] for extra in range(LEVELS_AT_ONCE)], axis=1
            )

        rounded = [tile_at(*place).astype(BF16) for place in places]
        ahead = itertools.chain(
            *[transport((group + 1) * ROWS_AT_ONCE + extra) for extra in range(ROWS_AT_ONCE)]
        )
        steps = (2 * n_levels - 1) * ROWS_AT_ONCE
        share = -(-steps // (SUBSTEPS * len(places) - 1))

        def beside():
            for _ in itertools.islice(ahead, share):
                pass

        changes = increments(rounded, beside)
        for _ in ahead:
            pass
        for (level, r), change in zip(places, changes):
            tile = tile_at(level, r) + jnp.where(lit_tile, change, 0.0)
            for half in range(LEVELS_AT_ONCE):
                value = tile[:, half * n_cols : (half + 1) * n_cols]
                at = (level + half) * n_rows + r
                if last:
                    at = (level + half) * half_rows + r % half_rows
                    staged[r // half_rows, pl.ds(at, n_species, stride=cells // 2), :] = value
                else:
                    refs[0][level + half, r] = value
                    speed = east_c[level + half, pl.ds(r, 1), :]
                    side = jnp.where(
                        lanes == 0, jnp.minimum(speed, 0.0), jnp.maximum(speed, 0.0)
                    )
                    sides = pack_sides(value, side, at, *sides)
        return sides

    n_groups = n_rows // ROWS_AT_ONCE
    if last:
        copies = []
        for half in range(2):
            lax.fori_loop(half * n_groups // 2, (half + 1) * n_groups // 2, rows, 0)
            copies.append(
                pltpu.make_async_copy(
                    staged.at[half].reshape(n_species, n_levels, half_rows, n_cols),
                    refs[0].at[:, :, half * half_rows : (half + 1) * half_rows],
                    sems.at[half],
                )
            )
            copies[-1].start()
        for copy in copies:
            copy.wait()
        return
    out, west, east, south, north = refs[:5]
    zeros = jnp.zeros((n_species, n_cols), F32)
    west[...], east[...] = lax.fori_loop(0, n_groups, rows, (zeros, zeros))
    for level in range(n_levels):
        for edge, send, kind in ((0, south, SOUTH), (n_rows - 1, north, NORTH)):
            send[level] = (out[level, edge] * coefs[kind, level, edge : edge + 1]).astype(BF16)


def vmem(count):
    return [pl.BlockSpec(memory_space=pltpu.VMEM)] * count


def exchanged(west, east, south, north):
    lon, lat = lax.axis_size("lon"), lax.axis_size("lat")
    up = [(i, (i + 1) % lon) for i in range(lon)]
    down = [(j, i) for i, j in up]
    climb = [(i, (i + 1) % lat) for i in range(lat)]
    descend = [(j, i) for i, j in climb]
    from_south = lax.ppermute(north, "lat", climb)
    from_north = lax.ppermute(south, "lat", descend)
    from_west = lax.ppermute(east, "lon", up)
    from_east = lax.ppermute(west, "lon", down)
    return from_west, from_east, from_south, from_north


def on_device(
    latent_field,
    east_courant,
    north_courant,
    mixing,
    sunlit,
    decode_w,
    react_a,
    react_b,
    stoich,
    encode_w,
    rate_const,
):
    n_species, n_levels, n_rows, n_cols = latent_field.shape
    layered = jax.ShapeDtypeStruct((n_levels, n_rows, n_species, n_cols), F32)
    side = jax.ShapeDtypeStruct((n_species, n_cols), F32)
    edge = jax.ShapeDtypeStruct((n_levels, n_species, n_cols), BF16)
    params = pltpu.CompilerParams(vmem_limit_bytes=VMEM_BYTES)
    lat_index = lax.axis_index("lat")
    place = jnp.stack([lat_index == 0, lat_index == lax.axis_size("lat") - 1]).astype(jnp.int32)
    smem = pl.BlockSpec(memory_space=pltpu.SMEM)
    hbm = pl.BlockSpec(memory_space=pltpu.HBM)
    n_reactions = react_a.shape[0]
    arrays = (
        east_courant,
        north_courant,
        decode_w.T,
        react_a.T,
        react_b.T,
        stoich,
        encode_w,
        rate_const[None],
    )
    *edges, linear, encode = pl.pallas_call(
        first_kernel,
        out_shape=(
            side,
            side,
            edge,
            edge,
            jax.ShapeDtypeStruct((2 * n_reactions, n_species), BF16),
            jax.ShapeDtypeStruct((n_species, n_reactions), BF16),
        ),
        in_specs=[smem] + [hbm] * (1 + len(arrays)),
        out_specs=tuple(vmem(6)),
        scratch_shapes=[pltpu.VMEM((n_levels, n_species, n_rows, n_cols), F32)]
        + [pltpu.VMEM(array.shape, array.dtype) for array in arrays]
        + [pltpu.SemaphoreType.DMA((n_levels + len(arrays),))],
        compiler_params=pltpu.CompilerParams(vmem_limit_bytes=FIRST_VMEM_BYTES),
        name="first_sends",
    )(place, latent_field, *arrays)
    field = latent_field.reshape(n_species * n_levels * n_rows, n_cols)
    for step in range(STEPS):
        first, last = step == 0, step == STEPS - 1
        halos = exchanged(*edges)
        scratch = [pltpu.VMEM(layered.shape, F32)] if first else []
        scratch += [
            pltpu.VMEM((8, n_levels, n_rows, n_cols), F32),
            pltpu.VMEM((n_levels, n_rows + ROWS_AT_ONCE, n_species, n_cols), F32),
        ]
        if last:
            scratch += [
                pltpu.VMEM((2, n_species * n_levels * n_rows // 2, n_cols), F32),
                pltpu.SemaphoreType.DMA((2,)),
            ]
        outs = pl.pallas_call(
            functools.partial(step_kernel, n_levels, n_rows, first, last),
            out_shape=(jax.ShapeDtypeStruct(latent_field.shape, F32),)
            if last
            else (layered, side, side, edge, edge),
            in_specs=[smem] * 2 + vmem(10),
            out_specs=(hbm,) if last else tuple(vmem(5)),
            scratch_shapes=scratch,
            compiler_params=params,
            name="splitting_step",
        )(sunlit, place, field, east_courant, north_courant, mixing, linear, encode, *halos)
        field, edges = outs[0], outs[1:]
    return field


def solution(mesh):
    placed = (
        P(None, None, "lat", "lon"),
        P(None, "lat", "lon"),
        P(None, "lat", "lon"),
        P(None, "lat", "lon"),
        P("lat", "lon"),
        P(),
        P(),
        P(),
        P(),
        P(),
        P(),
    )
    return jax.shard_map(
        on_device,
        mesh=mesh,
        in_specs=placed,
        out_specs=P(None, None, "lat", "lon"),
        check_vma=False,
    )
```

```python
import functools
import itertools

import jax
import jax.numpy as jnp
from jax import lax
from jax.experimental import pallas as pl
from jax.experimental.pallas import tpu as pltpu
from jax.sharding import PartitionSpec as P

BLOCK = 16
SUBSTEPS = 2
STEPS = 2
GROUP = 16
ROWS_AT_ONCE = 4
LEVELS_AT_ONCE = 4
LAG = 2

F32 = jnp.float32
BF16 = jnp.bfloat16
VMEM_BYTES = 48 * 1024 * 1024
FIRST_VMEM_BYTES = 56 * 1024 * 1024


def lane_ids(shape):
    return lax.broadcasted_iota(jnp.int32, shape, len(shape) - 1)


def fold_weights(decode_t, react_a_t, react_b_t, stoich, encode, rate, linear_out, encode_out):
    n_reactions = react_a_t.shape[1]
    contract = (((0,), (1,)), ((), ()))
    for part, react in enumerate((react_a_t, react_b_t)):
        product = lax.dot_general(
            react[...], decode_t[...], contract, preferred_element_type=F32
        )
        for group in range(n_reactions // GROUP):
            at = (2 * group + part) * GROUP
            linear_out[at : at + GROUP, :] = product[
                group * GROUP : (group + 1) * GROUP
            ].astype(BF16)
    folded = jnp.dot(encode[...], stoich[...], preferred_element_type=F32)
    encode_out[...] = (folded * rate[...]).astype(BF16)


def at_ends():
    index = lax.axis_index("lat")
    return index == 0, index == lax.axis_size("lat") - 1


def pack_sides(value, coef, at, west, east):
    lanes = lane_ids(value.shape)
    size = value.shape[-1]
    turned = pltpu.roll(value * coef, at, 1)
    west = jnp.where(lanes == at, turned, west)
    east = jnp.where(lanes == (at + size - 1) % size, turned, east)
    return west, east


def first_kernel(latent, east_c, north_c, west, east, south, north, *scratch):
    tiles, east_v, north_v, sems = scratch
    n_levels, n_species, n_rows, n_cols = tiles.shape
    lanes = lane_ids((1, n_cols))
    is_first, is_last = at_ends()
    copies = [
        pltpu.make_async_copy(east_c, east_v, sems.at[n_levels]),
        pltpu.make_async_copy(north_c, north_v, sems.at[n_levels + 1]),
    ]
    levels = [
        pltpu.make_async_copy(latent.at[:, level], tiles.at[level], sems.at[level])
        for level in range(n_levels)
    ]
    for copy in copies + levels:
        copy.start()
    for copy in copies:
        copy.wait()
    sides = (jnp.zeros((n_species, n_cols), F32),) * 2
    for level in range(n_levels):
        levels[level].wait()
        tile = jnp.transpose(tiles[level], (1, 0, 2))
        for r in range(n_rows):
            at = level * n_rows + r
            value = tile[r]
            speed = east_v[level, r : r + 1, :]
            coef = jnp.where(lanes == 0, jnp.minimum(speed, 0.0), jnp.maximum(speed, 0.0))
            sides = pack_sides(value, coef, at, *sides)
        for r, out, clip in ((0, south, jnp.minimum), (n_rows - 1, north, jnp.maximum)):
            speed = clip(north_v[level, r : r + 1, :], 0.0)
            speed = jnp.where(is_first if r == 0 else is_last, 0.0, speed)
            out[level] = (tile[r] * speed).astype(BF16)
    west[...], east[...] = sides


def step_kernel(
    n_levels,
    n_rows,
    first,
    last,
    sun,
    field,
    east_c,
    north_c,
    mixing,
    west_in,
    east_in,
    south_in,
    north_in,
    *refs,
):
    if first:
        weights, refs = refs[:6], refs[6:]
        linear, encode = refs[5:7]
    else:
        (linear, encode), refs = refs[:2], refs[2:]
    half_rows = n_rows // 2
    if last:
        coefs, diffused, staged, sems = refs[-4:]
    else:
        coefs, diffused = refs[-2:]
    n_species, n_cols = west_in.shape
    n_reactions = encode.shape[1]
    cells = n_levels * n_rows
    lanes = lane_ids((1, n_cols))
    row_ids = lax.broadcasted_iota(jnp.int32, (n_rows, n_cols), 0)
    is_first, is_last = at_ends()
    if first:
        latent, field = field, refs[-3]
        fold_weights(*weights, linear, encode)
        for level in range(n_levels):
            field[level] = jnp.transpose(latent[:, level], (1, 0, 2))
    CENTRE, EAST, WEST, NORTH, SOUTH, SCALE, LOWER, UPPER = range(8)

    upper = None
    for level in range(n_levels):
        ce, cn = east_c[level], north_c[level]
        east, west = jnp.maximum(ce, 0.0), jnp.minimum(ce, 0.0)
        north = jnp.where((row_ids == n_rows - 1) & is_last, 0.0, jnp.maximum(cn, 0.0))
        south = jnp.where((row_ids == 0) & is_first, 0.0, jnp.minimum(cn, 0.0))
        coefs[CENTRE, level] = 1.0 - east + west - north + south
        coefs[EAST, level] = east
        coefs[WEST, level] = west
        coefs[NORTH, level] = north
        coefs[SOUTH, level] = south
        pivot = 1.0
        if level > 0:
            below = mixing[level - 1]
            pivot = pivot + below - below * upper
        if level < n_levels - 1:
            pivot = pivot + mixing[level]
        scale = 1.0 / pivot
        coefs[SCALE, level] = scale
        if level > 0:
            coefs[LOWER, level] = below * scale
        if level < n_levels - 1:
            upper = mixing[level] * scale
            coefs[UPPER, level] = upper

    lit = jnp.zeros((1, n_cols), jnp.int32)
    for block in range(n_cols // BLOCK):
        lit = jnp.where(lanes // BLOCK == block, sun[0, block], lit)
    lit = lit > 0

    def coef(kind, level, r):
        return coefs[kind, level, pl.ds(r, 1), :]

    def transport(slot):
        r = jnp.minimum(slot, n_rows - 1)
        before, after = jnp.maximum(r - 1, 0), jnp.minimum(r + 1, n_rows - 1)
        right = None
        for level in range(n_levels):
            at = level * n_rows + r
            value = field[level, r]
            from_west = jnp.where(
                lanes == 0,
                pltpu.roll(west_in[...], (n_cols + 1 - at) % n_cols, 1),
                pltpu.roll(value * coef(EAST, level, r), 1, 1),
            )
            from_east = jnp.where(
                lanes == n_cols - 1,
                pltpu.roll(east_in[...], n_cols - 1 - at, 1),
                pltpu.roll(value * coef(WEST, level, r), n_cols - 1, 1),
            )
            from_south = jnp.where(
                r == 0,
                south_in[level].astype(F32),
                field[level, before] * coef(NORTH, level, before),
            )
            from_north = jnp.where(
                r == n_rows - 1,
                north_in[level].astype(F32),
                field[level, after] * coef(SOUTH, level, after),
            )
            moved = value * coef(CENTRE, level, r) + (from_west - from_east) + (from_south - from_north)
            scaled = moved * coef(SCALE, level, r)
            right = scaled if level == 0 else scaled + coef(LOWER, level, r) * right
            diffused[level, slot] = right
            yield
        for level in range(n_levels - 2, -1, -1):
            right = diffused[level, slot] + coef(UPPER, level, r) * right
            diffused[level, slot] = right
            yield

    def product_of(rounded):
        both = jnp.dot(linear[...], rounded, preferred_element_type=F32)
        parts = [
            both[at : at + GROUP] * both[at + GROUP : at + 2 * GROUP]
            for at in range(0, 2 * n_reactions, 2 * GROUP)
        ]
        return jnp.concatenate(parts, axis=0).astype(BF16)

    def increments(rounded, beside):
        current = [value.astype(F32) for value in rounded]
        summed = [None] * len(rounded)
        units = [(substep, tile) for substep in range(SUBSTEPS) for tile in range(len(rounded))]
        rates = {}
        for at in range(len(units) + LAG):
            if at < len(units):
                rates[at] = product_of(rounded[units[at][1]])
                beside()
            if at >= LAG:
                substep, tile = units[at - LAG]
                change = jnp.dot(encode[...], rates.pop(at - LAG), preferred_element_type=F32)
                if substep == 0:
                    summed[tile] = change
                else:
                    summed[tile] = summed[tile] + change
                if substep < SUBSTEPS - 1:
                    current[tile] = current[tile] + change
                    rounded[tile] = current[tile].astype(BF16)
        return summed

    for r in range(ROWS_AT_ONCE):
        for _ in transport(r):
            pass
    lit_tile = jnp.concatenate([lit] * LEVELS_AT_ONCE, axis=1)

    def rows(group, sides):
        places = [
            (level, group * ROWS_AT_ONCE + extra)
            for extra in range(ROWS_AT_ONCE)
            for level in range(0, n_levels, LEVELS_AT_ONCE)
        ]

        def tile_at(level, r):
            return jnp.concatenate(
                [diffused[level + extra, r] for extra in range(LEVELS_AT_ONCE)], axis=1
            )

        rounded = [tile_at(*place).astype(BF16) for place in places]
        ahead = itertools.chain(
            *[transport((group + 1) * ROWS_AT_ONCE + extra) for extra in range(ROWS_AT_ONCE)]
        )
        steps = (2 * n_levels - 1) * ROWS_AT_ONCE
        share = -(-steps // (SUBSTEPS * len(places) - 1))

        def beside():
            for _ in itertools.islice(ahead, share):
                pass

        changes = increments(rounded, beside)
        for _ in ahead:
            pass
        for (level, r), change in zip(places, changes):
            tile = tile_at(level, r) + jnp.where(lit_tile, change, 0.0)
            for half in range(LEVELS_AT_ONCE):
                value = tile[:, half * n_cols : (half + 1) * n_cols]
                at = (level + half) * n_rows + r
                if last:
                    diffused[level + half, r] = value
                else:
                    refs[0][level + half, r] = value
                    speed = east_c[level + half, pl.ds(r, 1), :]
                    side = jnp.where(
                        lanes == 0, jnp.minimum(speed, 0.0), jnp.maximum(speed, 0.0)
                    )
                    sides = pack_sides(value, side, at, *sides)
        return sides

    n_groups = n_rows // ROWS_AT_ONCE
    if last:
        copies = []
        for half in range(2):
            lax.fori_loop(half * n_groups // 2, (half + 1) * n_groups // 2, rows, 0)
            within = slice(half * half_rows, (half + 1) * half_rows)
            for level in range(n_levels):
                staged[half, level] = jnp.transpose(diffused[level, within], (1, 0, 2))
                copies.append(
                    pltpu.make_async_copy(
                        staged.at[half, level],
                        refs[0].at[:, level, within],
                        sems.at[half, level],
                    )
                )
                copies[-1].start()
        for copy in copies:
            copy.wait()
        return
    out, west, east, south, north = refs[:5]
    zeros = jnp.zeros((n_species, n_cols), F32)
    west[...], east[...] = lax.fori_loop(0, n_groups, rows, (zeros, zeros))
    for level in range(n_levels):
        for edge, send, kind in ((0, south, SOUTH), (n_rows - 1, north, NORTH)):
            send[level] = (out[level, edge] * coefs[kind, level, edge : edge + 1]).astype(BF16)


def vmem(count):
    return [pl.BlockSpec(memory_space=pltpu.VMEM)] * count


def exchanged(west, east, south, north):
    lon, lat = lax.axis_size("lon"), lax.axis_size("lat")
    up = [(i, (i + 1) % lon) for i in range(lon)]
    down = [(j, i) for i, j in up]
    climb = [(i, (i + 1) % lat) for i in range(lat)]
    descend = [(j, i) for i, j in climb]
    from_south = lax.ppermute(north, "lat", climb)
    from_north = lax.ppermute(south, "lat", descend)
    from_west = lax.ppermute(east, "lon", up)
    from_east = lax.ppermute(west, "lon", down)
    return from_west, from_east, from_south, from_north


def on_device(
    latent_field,
    east_courant,
    north_courant,
    mixing,
    sunlit,
    decode_w,
    react_a,
    react_b,
    stoich,
    encode_w,
    rate_const,
):
    n_species, n_levels, n_rows, n_cols = latent_field.shape
    layered = jax.ShapeDtypeStruct((n_levels, n_rows, n_species, n_cols), F32)
    side = jax.ShapeDtypeStruct((n_species, n_cols), F32)
    edge = jax.ShapeDtypeStruct((n_levels, n_species, n_cols), BF16)
    params = pltpu.CompilerParams(vmem_limit_bytes=VMEM_BYTES)
    smem = pl.BlockSpec(memory_space=pltpu.SMEM)
    hbm = pl.BlockSpec(memory_space=pltpu.HBM)
    n_reactions = react_a.shape[0]
    edges = pl.pallas_call(
        first_kernel,
        out_shape=(side, side, edge, edge),
        in_specs=[hbm] * 3,
        out_specs=tuple(vmem(4)),
        scratch_shapes=[
            pltpu.VMEM((n_levels, n_species, n_rows, n_cols), F32),
            pltpu.VMEM((n_levels, n_rows, n_cols), F32),
            pltpu.VMEM((n_levels, n_rows, n_cols), F32),
            pltpu.SemaphoreType.DMA((n_levels + 2,)),
        ],
        compiler_params=pltpu.CompilerParams(vmem_limit_bytes=FIRST_VMEM_BYTES),
        name="first_sends",
        cost_estimate=pl.CostEstimate(flops=4_000_000_000, bytes_accessed=2_000_000, transcendentals=0),
    )(latent_field, east_courant, north_courant)
    weights = (decode_w.T, react_a.T, react_b.T, stoich, encode_w, rate_const[None])
    folded = (
        jax.ShapeDtypeStruct((2 * n_reactions, n_species), BF16),
        jax.ShapeDtypeStruct((n_species, n_reactions), BF16),
    )
    field = latent_field
    for step in range(STEPS):
        first, last = step == 0, step == STEPS - 1
        halos = exchanged(*edges)
        scratch = [pltpu.VMEM(layered.shape, F32)] if first else []
        scratch += [
            pltpu.VMEM((8, n_levels, n_rows, n_cols), F32),
            pltpu.VMEM((n_levels, n_rows + ROWS_AT_ONCE, n_species, n_cols), F32),
        ]
        if last:
            scratch += [
                pltpu.VMEM((2, n_levels, n_species, n_rows // 2, n_cols), F32),
                pltpu.SemaphoreType.DMA((2, n_levels)),
            ]
        outs = pl.pallas_call(
            functools.partial(step_kernel, n_levels, n_rows, first, last),
            out_shape=(jax.ShapeDtypeStruct(latent_field.shape, F32),)
            if last
            else (layered, side, side, edge, edge, *folded),
            in_specs=[smem] + vmem(8 + len(weights)),
            out_specs=(hbm,) if last else tuple(vmem(7)),
            scratch_shapes=scratch,
            compiler_params=params,
            name="splitting_step",
            cost_estimate=pl.CostEstimate(flops=20_000_000_000, bytes_accessed=1, transcendentals=0),
        )(sunlit, field, east_courant, north_courant, mixing, *halos, *weights)
        field, edges, weights = outs[0], outs[1:5], outs[5:]
    return field


def solution(mesh):
    placed = (
        P(None, None, "lat", "lon"),
        P(None, "lat", "lon"),
        P(None, "lat", "lon"),
        P(None, "lat", "lon"),
        P("lat", "lon"),
        P(),
        P(),
        P(),
        P(),
        P(),
        P(),
    )
    return jax.shard_map(
        on_device,
        mesh=mesh,
        in_specs=placed,
        out_specs=P(None, None, "lat", "lon"),
        check_vma=False,
    )
```

```python
import functools
import itertools

import jax
import jax.numpy as jnp
from jax import lax
from jax.experimental import pallas as pl
from jax.experimental.pallas import tpu as pltpu
from jax.sharding import PartitionSpec as P

BLOCK = 16
SUBSTEPS = 2
STEPS = 2
GROUP = 16
ROWS_AT_ONCE = 4
LEVELS_AT_ONCE = 4
LAG = 2

F32 = jnp.float32
BF16 = jnp.bfloat16
VMEM_BYTES = 48 * 1024 * 1024
FIRST_VMEM_BYTES = 56 * 1024 * 1024


def lane_ids(shape):
    return lax.broadcasted_iota(jnp.int32, shape, len(shape) - 1)


def fold_weights(decode_t, react_a_t, react_b_t, stoich, encode, rate, linear_out, encode_out):
    n_reactions = react_a_t.shape[1]
    contract = (((0,), (1,)), ((), ()))
    for part, react in enumerate((react_a_t, react_b_t)):
        product = lax.dot_general(
            react[...], decode_t[...], contract, preferred_element_type=F32
        )
        for group in range(n_reactions // GROUP):
            at = (2 * group + part) * GROUP
            linear_out[at : at + GROUP, :] = product[
                group * GROUP : (group + 1) * GROUP
            ].astype(BF16)
    folded = jnp.dot(encode[...], stoich[...], preferred_element_type=F32)
    encode_out[...] = (folded * rate[...]).astype(BF16)


def at_ends():
    index = lax.axis_index("lat")
    return index == 0, index == lax.axis_size("lat") - 1


def is_even(axis):
    return lax.axis_index(axis) % 2 == 0


def by_parity(axis, up, down, into_first, into_second):
    even = is_even(axis)
    into_first[...] = jnp.where(even, up, down)
    into_second[...] = jnp.where(even, down, up)


def pack_sides(value, coef, at, west, east):
    lanes = lane_ids(value.shape)
    size = value.shape[-1]
    turned = pltpu.roll(value * coef, at, 1)
    west = jnp.where(lanes == at, turned, west)
    east = jnp.where(lanes == (at + size - 1) % size, turned, east)
    return west, east


def first_kernel(latent, east_c, north_c, lon_a, lon_b, lat_a, lat_b, *scratch):
    tiles, east_v, north_v, sems = scratch
    n_levels, n_species, n_rows, n_cols = tiles.shape
    lanes = lane_ids((1, n_cols))
    is_first, is_last = at_ends()
    copies = [
        pltpu.make_async_copy(east_c, east_v, sems.at[n_levels]),
        pltpu.make_async_copy(north_c, north_v, sems.at[n_levels + 1]),
    ]
    levels = [
        pltpu.make_async_copy(latent.at[:, level], tiles.at[level], sems.at[level])
        for level in range(n_levels)
    ]
    for copy in copies + levels:
        copy.start()
    for copy in copies:
        copy.wait()
    sides = (jnp.zeros((n_species, n_cols), F32),) * 2
    for level in range(n_levels):
        levels[level].wait()
        tile = jnp.transpose(tiles[level], (1, 0, 2))
        for r in range(n_rows):
            at = level * n_rows + r
            value = tile[r]
            speed = east_v[level, r : r + 1, :]
            coef = jnp.where(lanes == 0, jnp.minimum(speed, 0.0), jnp.maximum(speed, 0.0))
            sides = pack_sides(value, coef, at, *sides)
        ends = []
        for r, closed, clip in ((0, is_first, jnp.minimum), (n_rows - 1, is_last, jnp.maximum)):
            speed = clip(north_v[level, r : r + 1, :], 0.0)
            ends.append((tile[r] * jnp.where(closed, 0.0, speed)).astype(BF16))
        by_parity("lat", ends[1], ends[0], lat_a.at[level], lat_b.at[level])
    by_parity("lon", sides[1], sides[0], lon_a, lon_b)


def step_kernel(
    n_levels,
    n_rows,
    first,
    last,
    sun,
    field,
    east_c,
    north_c,
    mixing,
    lon_a_in,
    lon_b_in,
    lat_a_in,
    lat_b_in,
    *refs,
):
    if first:
        weights, refs = refs[:6], refs[6:]
        linear, encode = refs[5:7]
    else:
        (linear, encode), refs = refs[:2], refs[2:]
    half_rows = n_rows // 2
    south_in, north_in, west_in, east_in, coefs, diffused = refs[-6:]
    if last:
        staged, sems = refs[-8:-6]
    by_parity("lon", lon_a_in[...], lon_b_in[...], east_in, west_in)
    by_parity("lat", lat_a_in[...], lat_b_in[...], north_in, south_in)
    n_species, n_cols = west_in.shape
    n_reactions = encode.shape[1]
    cells = n_levels * n_rows
    lanes = lane_ids((1, n_cols))
    row_ids = lax.broadcasted_iota(jnp.int32, (n_rows, n_cols), 0)
    is_first, is_last = at_ends()
    if first:
        latent, field = field, refs[-7]
        fold_weights(*weights, linear, encode)
        for level in range(n_levels):
            field[level] = jnp.transpose(latent[:, level], (1, 0, 2))
    CENTRE, EAST, WEST, NORTH, SOUTH, SCALE, LOWER, UPPER = range(8)

    upper = None
    for level in range(n_levels):
        ce, cn = east_c[level], north_c[level]
        east, west = jnp.maximum(ce, 0.0), jnp.minimum(ce, 0.0)
        north = jnp.where((row_ids == n_rows - 1) & is_last, 0.0, jnp.maximum(cn, 0.0))
        south = jnp.where((row_ids == 0) & is_first, 0.0, jnp.minimum(cn, 0.0))
        coefs[CENTRE, level] = 1.0 - east + west - north + south
        coefs[EAST, level] = east
        coefs[WEST, level] = west
        coefs[NORTH, level] = north
        coefs[SOUTH, level] = south
        pivot = 1.0
        if level > 0:
            below = mixing[level - 1]
            pivot = pivot + below - below * upper
        if level < n_levels - 1:
            pivot = pivot + mixing[level]
        scale = 1.0 / pivot
        coefs[SCALE, level] = scale
        if level > 0:
            coefs[LOWER, level] = below * scale
        if level < n_levels - 1:
            upper = mixing[level] * scale
            coefs[UPPER, level] = upper

    lit = jnp.zeros((1, n_cols), jnp.int32)
    for block in range(n_cols // BLOCK):
        lit = jnp.where(lanes // BLOCK == block, sun[0, block], lit)
    lit = lit > 0

    def coef(kind, level, r):
        return coefs[kind, level, pl.ds(r, 1), :]

    def transport(slot):
        r = jnp.minimum(slot, n_rows - 1)
        before, after = jnp.maximum(r - 1, 0), jnp.minimum(r + 1, n_rows - 1)
        right = None
        for level in range(n_levels):
            at = level * n_rows + r
            value = field[level, r]
            from_west = jnp.where(
                lanes == 0,
                pltpu.roll(west_in[...], (n_cols + 1 - at) % n_cols, 1),
                pltpu.roll(value * coef(EAST, level, r), 1, 1),
            )
            from_east = jnp.where(
                lanes == n_cols - 1,
                pltpu.roll(east_in[...], n_cols - 1 - at, 1),
                pltpu.roll(value * coef(WEST, level, r), n_cols - 1, 1),
            )
            from_south = jnp.where(
                r == 0,
                south_in[level].astype(F32),
                field[level, before] * coef(NORTH, level, before),
            )
            from_north = jnp.where(
                r == n_rows - 1,
                north_in[level].astype(F32),
                field[level, after] * coef(SOUTH, level, after),
            )
            moved = value * coef(CENTRE, level, r) + (from_west - from_east) + (from_south - from_north)
            scaled = moved * coef(SCALE, level, r)
            right = scaled if level == 0 else scaled + coef(LOWER, level, r) * right
            diffused[level, slot] = right
            yield
        for level in range(n_levels - 2, -1, -1):
            right = diffused[level, slot] + coef(UPPER, level, r) * right
            diffused[level, slot] = right
            yield

    def product_of(rounded):
        both = jnp.dot(linear[...], rounded, preferred_element_type=F32)
        parts = [
            both[at : at + GROUP] * both[at + GROUP : at + 2 * GROUP]
            for at in range(0, 2 * n_reactions, 2 * GROUP)
        ]
        return jnp.concatenate(parts, axis=0).astype(BF16)

    def increments(rounded, beside):
        current = [value.astype(F32) for value in rounded]
        summed = [None] * len(rounded)
        units = [(substep, tile) for substep in range(SUBSTEPS) for tile in range(len(rounded))]
        rates = {}
        for at in range(len(units) + LAG):
            if at < len(units):
                rates[at] = product_of(rounded[units[at][1]])
                beside()
            if at >= LAG:
                substep, tile = units[at - LAG]
                change = jnp.dot(encode[...], rates.pop(at - LAG), preferred_element_type=F32)
                if substep == 0:
                    summed[tile] = change
                else:
                    summed[tile] = summed[tile] + change
                if substep < SUBSTEPS - 1:
                    current[tile] = current[tile] + change
                    rounded[tile] = current[tile].astype(BF16)
        return summed

    for r in range(ROWS_AT_ONCE):
        for _ in transport(r):
            pass
    lit_tile = jnp.concatenate([lit] * LEVELS_AT_ONCE, axis=1)

    def rows(group, sides):
        places = [
            (level, group * ROWS_AT_ONCE + extra)
            for extra in range(ROWS_AT_ONCE)
            for level in range(0, n_levels, LEVELS_AT_ONCE)
        ]

        def tile_at(level, r):
            return jnp.concatenate(
                [diffused[level + extra, r] for extra in range(LEVELS_AT_ONCE)], axis=1
            )

        rounded = [tile_at(*place).astype(BF16) for place in places]
        ahead = itertools.chain(
            *[transport((group + 1) * ROWS_AT_ONCE + extra) for extra in range(ROWS_AT_ONCE)]
        )
        steps = (2 * n_levels - 1) * ROWS_AT_ONCE
        share = -(-steps // (SUBSTEPS * len(places) - 1))

        def beside():
            for _ in itertools.islice(ahead, share):
                pass

        changes = increments(rounded, beside)
        for _ in ahead:
            pass
        for (level, r), change in zip(places, changes):
            tile = tile_at(level, r) + jnp.where(lit_tile, change, 0.0)
            for half in range(LEVELS_AT_ONCE):
                value = tile[:, half * n_cols : (half + 1) * n_cols]
                at = (level + half) * n_rows + r
                if last:
                    diffused[level + half, r] = value
                else:
                    refs[0][level + half, r] = value
                    speed = east_c[level + half, pl.ds(r, 1), :]
                    side = jnp.where(
                        lanes == 0, jnp.minimum(speed, 0.0), jnp.maximum(speed, 0.0)
                    )
                    sides = pack_sides(value, side, at, *sides)
        return sides

    n_groups = n_rows // ROWS_AT_ONCE
    if last:
        copies = []
        for half in range(2):
            lax.fori_loop(half * n_groups // 2, (half + 1) * n_groups // 2, rows, 0)
            within = slice(half * half_rows, (half + 1) * half_rows)
            for level in range(n_levels):
                staged[half, level] = jnp.transpose(diffused[level, within], (1, 0, 2))
                copies.append(
                    pltpu.make_async_copy(
                        staged.at[half, level],
                        refs[0].at[:, level, within],
                        sems.at[half, level],
                    )
                )
                copies[-1].start()
        for copy in copies:
            copy.wait()
        return
    out, lon_a, lon_b, lat_a, lat_b = refs[:5]
    zeros = jnp.zeros((n_species, n_cols), F32)
    west, east = lax.fori_loop(0, n_groups, rows, (zeros, zeros))
    by_parity("lon", east, west, lon_a, lon_b)
    for level in range(n_levels):
        south = (out[level, 0] * coefs[SOUTH, level, :1]).astype(BF16)
        north = (out[level, n_rows - 1] * coefs[NORTH, level, n_rows - 1 :]).astype(BF16)
        by_parity("lat", north, south, lat_a.at[level], lat_b.at[level])


def vmem(count):
    return [pl.BlockSpec(memory_space=pltpu.VMEM)] * count


def exchanged(lon_a, lon_b, lat_a, lat_b):
    def swapped(array, axis, first):
        size = lax.axis_size(axis)
        pairs = [(i % size, (i + 1) % size) for i in range(first, size + first, 2)]
        return lax.ppermute(array, axis, pairs + [(j, i) for i, j in pairs])

    lat_a, lat_b = swapped(lat_a, "lat", 0), swapped(lat_b, "lat", 1)
    return swapped(lon_a, "lon", 0), swapped(lon_b, "lon", 1), lat_a, lat_b


def on_device(
    latent_field,
    east_courant,
    north_courant,
    mixing,
    sunlit,
    decode_w,
    react_a,
    react_b,
    stoich,
    encode_w,
    rate_const,
):
    n_species, n_levels, n_rows, n_cols = latent_field.shape
    layered = jax.ShapeDtypeStruct((n_levels, n_rows, n_species, n_cols), F32)
    side = jax.ShapeDtypeStruct((n_species, n_cols), F32)
    edge = jax.ShapeDtypeStruct((n_levels, n_species, n_cols), BF16)
    params = pltpu.CompilerParams(vmem_limit_bytes=VMEM_BYTES)
    smem = pl.BlockSpec(memory_space=pltpu.SMEM)
    hbm = pl.BlockSpec(memory_space=pltpu.HBM)
    n_reactions = react_a.shape[0]
    edges = pl.pallas_call(
        first_kernel,
        out_shape=(side, side, edge, edge),
        in_specs=[hbm] * 3,
        out_specs=tuple(vmem(4)),
        scratch_shapes=[
            pltpu.VMEM((n_levels, n_species, n_rows, n_cols), F32),
            pltpu.VMEM((n_levels, n_rows, n_cols), F32),
            pltpu.VMEM((n_levels, n_rows, n_cols), F32),
            pltpu.SemaphoreType.DMA((n_levels + 2,)),
        ],
        compiler_params=pltpu.CompilerParams(vmem_limit_bytes=FIRST_VMEM_BYTES),
        name="first_sends",
        cost_estimate=pl.CostEstimate(flops=4_000_000_000, bytes_accessed=2_000_000, transcendentals=0),
    )(latent_field, east_courant, north_courant)
    weights = (decode_w.T, react_a.T, react_b.T, stoich, encode_w, rate_const[None])
    folded = (
        jax.ShapeDtypeStruct((2 * n_reactions, n_species), BF16),
        jax.ShapeDtypeStruct((n_species, n_reactions), BF16),
    )
    field = latent_field
    for step in range(STEPS):
        first, last = step == 0, step == STEPS - 1
        halos = exchanged(*edges)
        scratch = [pltpu.VMEM(layered.shape, F32)] if first else []
        if last:
            scratch += [
                pltpu.VMEM((2, n_levels, n_species, n_rows // 2, n_cols), F32),
                pltpu.SemaphoreType.DMA((2, n_levels)),
            ]
        scratch += [pltpu.VMEM(array.shape, array.dtype) for array in (edge, edge, side, side)]
        scratch += [
            pltpu.VMEM((8, n_levels, n_rows, n_cols), F32),
            pltpu.VMEM((n_levels, n_rows + ROWS_AT_ONCE, n_species, n_cols), F32),
        ]
        outs = pl.pallas_call(
            functools.partial(step_kernel, n_levels, n_rows, first, last),
            out_shape=(jax.ShapeDtypeStruct(latent_field.shape, F32),)
            if last
            else (layered, side, side, edge, edge, *folded),
            in_specs=[smem] + vmem(8 + len(weights)),
            out_specs=(hbm,) if last else tuple(vmem(7)),
            scratch_shapes=scratch,
            compiler_params=params,
            name="splitting_step",
            cost_estimate=pl.CostEstimate(flops=20_000_000_000, bytes_accessed=1, transcendentals=0),
        )(sunlit, field, east_courant, north_courant, mixing, *halos, *weights)
        field, edges, weights = outs[0], outs[1:5], outs[5:]
    return field


def solution(mesh):
    placed = (
        P(None, None, "lat", "lon"),
        P(None, "lat", "lon"),
        P(None, "lat", "lon"),
        P(None, "lat", "lon"),
        P("lat", "lon"),
        P(),
        P(),
        P(),
        P(),
        P(),
        P(),
    )
    return jax.shard_map(
        on_device,
        mesh=mesh,
        in_specs=placed,
        out_specs=P(None, None, "lat", "lon"),
        check_vma=False,
    )
```

```python
import functools
import itertools

import jax
import jax.numpy as jnp
from jax import lax
from jax.experimental import pallas as pl
from jax.experimental.pallas import tpu as pltpu
from jax.sharding import PartitionSpec as P

BLOCK = 16
SUBSTEPS = 2
STEPS = 2
GROUP = 16
ROWS_AT_ONCE = 8
LEVELS_AT_ONCE = 4
LAG = 2

F32 = jnp.float32
BF16 = jnp.bfloat16
VMEM_BYTES = 48 * 1024 * 1024
FIRST_VMEM_BYTES = 56 * 1024 * 1024


def lane_ids(shape):
    return lax.broadcasted_iota(jnp.int32, shape, len(shape) - 1)


def fold_weights(decode_t, react_a_t, react_b_t, stoich, encode, rate, linear_out, encode_out):
    n_reactions = react_a_t.shape[1]
    contract = (((0,), (1,)), ((), ()))
    for part, react in enumerate((react_a_t, react_b_t)):
        product = lax.dot_general(
            react[...], decode_t[...], contract, preferred_element_type=F32
        )
        for group in range(n_reactions // GROUP):
            at = (2 * group + part) * GROUP
            linear_out[at : at + GROUP, :] = product[
                group * GROUP : (group + 1) * GROUP
            ].astype(BF16)
    folded = jnp.dot(encode[...], stoich[...], preferred_element_type=F32)
    encode_out[...] = (folded * rate[...]).astype(BF16)


def at_ends():
    index = lax.axis_index("lat")
    return index == 0, index == lax.axis_size("lat") - 1


def is_even(axis):
    return lax.axis_index(axis) % 2 == 0


def by_parity(axis, up, down, into_first, into_second):
    even = is_even(axis)
    into_first[...] = jnp.where(even, up, down)
    into_second[...] = jnp.where(even, down, up)


def pack_sides(value, coef, at, west, east):
    lanes = lane_ids(value.shape)
    size = value.shape[-1]
    turned = pltpu.roll(value * coef, at, 1)
    west = jnp.where(lanes == at, turned, west)
    east = jnp.where(lanes == (at + size - 1) % size, turned, east)
    return west, east


def first_kernel(latent, east_c, north_c, lon_a, lon_b, lat_a, lat_b, *scratch):
    tiles, east_v, north_v, sems = scratch
    n_levels, n_species, n_rows, n_cols = tiles.shape
    lanes = lane_ids((1, n_cols))
    is_first, is_last = at_ends()
    copies = [
        pltpu.make_async_copy(east_c, east_v, sems.at[n_levels]),
        pltpu.make_async_copy(north_c, north_v, sems.at[n_levels + 1]),
    ]
    levels = [
        pltpu.make_async_copy(latent.at[:, level], tiles.at[level], sems.at[level])
        for level in range(n_levels)
    ]
    for copy in copies + levels:
        copy.start()
    for copy in copies:
        copy.wait()
    sides = (jnp.zeros((n_species, n_cols), F32),) * 2
    for level in range(n_levels):
        levels[level].wait()
        tile = jnp.transpose(tiles[level], (1, 0, 2))
        for r in range(n_rows):
            at = level * n_rows + r
            value = tile[r]
            speed = east_v[level, r : r + 1, :]
            coef = jnp.where(lanes == 0, jnp.minimum(speed, 0.0), jnp.maximum(speed, 0.0))
            sides = pack_sides(value, coef, at, *sides)
        ends = []
        for r, closed, clip in ((0, is_first, jnp.minimum), (n_rows - 1, is_last, jnp.maximum)):
            speed = clip(north_v[level, r : r + 1, :], 0.0)
            ends.append((tile[r] * jnp.where(closed, 0.0, speed)).astype(BF16))
        by_parity("lat", ends[1], ends[0], lat_a.at[level], lat_b.at[level])
    by_parity("lon", sides[1], sides[0], lon_a, lon_b)


def step_kernel(
    n_levels,
    n_rows,
    first,
    last,
    sun,
    field,
    east_c,
    north_c,
    mixing,
    lon_a_in,
    lon_b_in,
    lat_a_in,
    lat_b_in,
    *refs,
):
    if first:
        weights, refs = refs[:6], refs[6:]
        linear, encode = refs[5:7]
    else:
        (linear, encode), refs = refs[:2], refs[2:]
    half_rows = n_rows // 2
    south_in, north_in, west_in, east_in, coefs, diffused = refs[-6:]
    if last:
        staged, sems = refs[-8:-6]
    by_parity("lon", lon_a_in[...], lon_b_in[...], east_in, west_in)
    by_parity("lat", lat_a_in[...], lat_b_in[...], north_in, south_in)
    n_species, n_cols = west_in.shape
    n_reactions = encode.shape[1]
    cells = n_levels * n_rows
    lanes = lane_ids((1, n_cols))
    row_ids = lax.broadcasted_iota(jnp.int32, (n_rows, n_cols), 0)
    is_first, is_last = at_ends()
    if first:
        latent, field = field, refs[-7]
        fold_weights(*weights, linear, encode)
        for level in range(n_levels):
            field[level] = jnp.transpose(latent[:, level], (1, 0, 2))
    CENTRE, EAST, WEST, NORTH, SOUTH, SCALE, LOWER, UPPER = range(8)

    upper = None
    for level in range(n_levels):
        ce, cn = east_c[level], north_c[level]
        east, west = jnp.maximum(ce, 0.0), jnp.minimum(ce, 0.0)
        north = jnp.where((row_ids == n_rows - 1) & is_last, 0.0, jnp.maximum(cn, 0.0))
        south = jnp.where((row_ids == 0) & is_first, 0.0, jnp.minimum(cn, 0.0))
        coefs[CENTRE, level] = 1.0 - east + west - north + south
        coefs[EAST, level] = east
        coefs[WEST, level] = west
        coefs[NORTH, level] = north
        coefs[SOUTH, level] = south
        pivot = 1.0
        if level > 0:
            below = mixing[level - 1]
            pivot = pivot + below - below * upper
        if level < n_levels - 1:
            pivot = pivot + mixing[level]
        scale = 1.0 / pivot
        coefs[SCALE, level] = scale
        if level > 0:
            coefs[LOWER, level] = below * scale
        if level < n_levels - 1:
            upper = mixing[level] * scale
            coefs[UPPER, level] = upper

    lit = jnp.zeros((1, n_cols), jnp.int32)
    for block in range(n_cols // BLOCK):
        lit = jnp.where(lanes // BLOCK == block, sun[0, block], lit)
    lit = lit > 0

    def coef(kind, level, r):
        return coefs[kind, level, pl.ds(r, 1), :]

    def transport(slot):
        r = jnp.minimum(slot, n_rows - 1)
        before, after = jnp.maximum(r - 1, 0), jnp.minimum(r + 1, n_rows - 1)
        right = None
        for level in range(n_levels):
            at = level * n_rows + r
            value = field[level, r]
            from_west = jnp.where(
                lanes == 0,
                pltpu.roll(west_in[...], (n_cols + 1 - at) % n_cols, 1),
                pltpu.roll(value * coef(EAST, level, r), 1, 1),
            )
            from_east = jnp.where(
                lanes == n_cols - 1,
                pltpu.roll(east_in[...], n_cols - 1 - at, 1),
                pltpu.roll(value * coef(WEST, level, r), n_cols - 1, 1),
            )
            from_south = jnp.where(
                r == 0,
                south_in[level].astype(F32),
                field[level, before] * coef(NORTH, level, before),
            )
            from_north = jnp.where(
                r == n_rows - 1,
                north_in[level].astype(F32),
                field[level, after] * coef(SOUTH, level, after),
            )
            moved = value * coef(CENTRE, level, r) + (from_west - from_east) + (from_south - from_north)
            scaled = moved * coef(SCALE, level, r)
            right = scaled if level == 0 else scaled + coef(LOWER, level, r) * right
            diffused[level, slot] = right
            yield
        for level in range(n_levels - 2, -1, -1):
            right = diffused[level, slot] + coef(UPPER, level, r) * right
            diffused[level, slot] = right
            yield

    def product_of(rounded):
        both = jnp.dot(linear[...], rounded, preferred_element_type=F32)
        parts = [
            both[at : at + GROUP] * both[at + GROUP : at + 2 * GROUP]
            for at in range(0, 2 * n_reactions, 2 * GROUP)
        ]
        return jnp.concatenate(parts, axis=0).astype(BF16)

    def increments(rounded, beside):
        current = [value.astype(F32) for value in rounded]
        summed = [None] * len(rounded)
        units = [(substep, tile) for substep in range(SUBSTEPS) for tile in range(len(rounded))]
        rates = {}
        for at in range(len(units) + LAG):
            if at < len(units):
                rates[at] = product_of(rounded[units[at][1]])
                beside()
            if at >= LAG:
                substep, tile = units[at - LAG]
                change = jnp.dot(encode[...], rates.pop(at - LAG), preferred_element_type=F32)
                if substep == 0:
                    summed[tile] = change
                else:
                    summed[tile] = summed[tile] + change
                if substep < SUBSTEPS - 1:
                    current[tile] = current[tile] + change
                    rounded[tile] = current[tile].astype(BF16)
        return summed

    for r in range(ROWS_AT_ONCE):
        for _ in transport(r):
            pass
    lit_tile = jnp.concatenate([lit] * LEVELS_AT_ONCE, axis=1)

    def rows(group, sides):
        places = [
            (level, group * ROWS_AT_ONCE + extra)
            for extra in range(ROWS_AT_ONCE)
            for level in range(0, n_levels, LEVELS_AT_ONCE)
        ]

        def tile_at(level, r):
            return jnp.concatenate(
                [diffused[level + extra, r] for extra in range(LEVELS_AT_ONCE)], axis=1
            )

        rounded = [tile_at(*place).astype(BF16) for place in places]
        ahead = itertools.chain(
            *[transport((group + 1) * ROWS_AT_ONCE + extra) for extra in range(ROWS_AT_ONCE)]
        )
        steps = (2 * n_levels - 1) * ROWS_AT_ONCE
        share = -(-steps // (SUBSTEPS * len(places) - 1))

        def beside():
            for _ in itertools.islice(ahead, share):
                pass

        changes = increments(rounded, beside)
        for _ in ahead:
            pass
        for (level, r), change in zip(places, changes):
            tile = tile_at(level, r) + jnp.where(lit_tile, change, 0.0)
            for half in range(LEVELS_AT_ONCE):
                value = tile[:, half * n_cols : (half + 1) * n_cols]
                at = (level + half) * n_rows + r
                if last:
                    diffused[level + half, r] = value
                else:
                    refs[0][level + half, r] = value
                    speed = east_c[level + half, pl.ds(r, 1), :]
                    side = jnp.where(
                        lanes == 0, jnp.minimum(speed, 0.0), jnp.maximum(speed, 0.0)
                    )
                    sides = pack_sides(value, side, at, *sides)
        return sides

    n_groups = n_rows // ROWS_AT_ONCE
    if last:
        copies = []
        for half in range(2):
            lax.fori_loop(half * n_groups // 2, (half + 1) * n_groups // 2, rows, 0)
            within = slice(half * half_rows, (half + 1) * half_rows)
            for level in range(n_levels):
                staged[half, level] = jnp.transpose(diffused[level, within], (1, 0, 2))
                copies.append(
                    pltpu.make_async_copy(
                        staged.at[half, level],
                        refs[0].at[:, level, within],
                        sems.at[half, level],
                    )
                )
                copies[-1].start()
        for copy in copies:
            copy.wait()
        return
    out, lon_a, lon_b, lat_a, lat_b = refs[:5]
    zeros = jnp.zeros((n_species, n_cols), F32)
    west, east = lax.fori_loop(0, n_groups, rows, (zeros, zeros))
    by_parity("lon", east, west, lon_a, lon_b)
    for level in range(n_levels):
        south = (out[level, 0] * coefs[SOUTH, level, :1]).astype(BF16)
        north = (out[level, n_rows - 1] * coefs[NORTH, level, n_rows - 1 :]).astype(BF16)
        by_parity("lat", north, south, lat_a.at[level], lat_b.at[level])


def vmem(count):
    return [pl.BlockSpec(memory_space=pltpu.VMEM)] * count


def exchanged(lon_a, lon_b, lat_a, lat_b):
    def swapped(array, axis, first):
        size = lax.axis_size(axis)
        pairs = [(i % size, (i + 1) % size) for i in range(first, size + first, 2)]
        return lax.ppermute(array, axis, pairs + [(j, i) for i, j in pairs])

    lon_b, lon_a = swapped(lon_b, "lon", 1), swapped(lon_a, "lon", 0)
    lat_b, lat_a = swapped(lat_b, "lat", 1), swapped(lat_a, "lat", 0)
    return lon_a, lon_b, lat_a, lat_b


def on_device(
    latent_field,
    east_courant,
    north_courant,
    mixing,
    sunlit,
    decode_w,
    react_a,
    react_b,
    stoich,
    encode_w,
    rate_const,
):
    n_species, n_levels, n_rows, n_cols = latent_field.shape
    layered = jax.ShapeDtypeStruct((n_levels, n_rows, n_species, n_cols), F32)
    side = jax.ShapeDtypeStruct((n_species, n_cols), F32)
    edge = jax.ShapeDtypeStruct((n_levels, n_species, n_cols), BF16)
    params = pltpu.CompilerParams(vmem_limit_bytes=VMEM_BYTES)
    smem = pl.BlockSpec(memory_space=pltpu.SMEM)
    hbm = pl.BlockSpec(memory_space=pltpu.HBM)
    n_reactions = react_a.shape[0]
    edges = pl.pallas_call(
        first_kernel,
        out_shape=(side, side, edge, edge),
        in_specs=[hbm] * 3,
        out_specs=tuple(vmem(4)),
        scratch_shapes=[
            pltpu.VMEM((n_levels, n_species, n_rows, n_cols), F32),
            pltpu.VMEM((n_levels, n_rows, n_cols), F32),
            pltpu.VMEM((n_levels, n_rows, n_cols), F32),
            pltpu.SemaphoreType.DMA((n_levels + 2,)),
        ],
        compiler_params=pltpu.CompilerParams(vmem_limit_bytes=FIRST_VMEM_BYTES),
        name="first_sends",
        cost_estimate=pl.CostEstimate(flops=4_000_000_000, bytes_accessed=2_000_000, transcendentals=0),
    )(latent_field, east_courant, north_courant)
    weights = (decode_w.T, react_a.T, react_b.T, stoich, encode_w, rate_const[None])
    folded = (
        jax.ShapeDtypeStruct((2 * n_reactions, n_species), BF16),
        jax.ShapeDtypeStruct((n_species, n_reactions), BF16),
    )
    field = latent_field
    for step in range(STEPS):
        first, last = step == 0, step == STEPS - 1
        halos = exchanged(*edges)
        scratch = [pltpu.VMEM(layered.shape, F32)] if first else []
        if last:
            scratch += [
                pltpu.VMEM((2, n_levels, n_species, n_rows // 2, n_cols), F32),
                pltpu.SemaphoreType.DMA((2, n_levels)),
            ]
        scratch += [pltpu.VMEM(array.shape, array.dtype) for array in (edge, edge, side, side)]
        scratch += [
            pltpu.VMEM((8, n_levels, n_rows, n_cols), F32),
            pltpu.VMEM((n_levels, n_rows + ROWS_AT_ONCE, n_species, n_cols), F32),
        ]
        outs = pl.pallas_call(
            functools.partial(step_kernel, n_levels, n_rows, first, last),
            out_shape=(jax.ShapeDtypeStruct(latent_field.shape, F32),)
            if last
            else (layered, side, side, edge, edge, *folded),
            in_specs=[smem] + vmem(8 + len(weights)),
            out_specs=(hbm,) if last else tuple(vmem(7)),
            scratch_shapes=scratch,
            compiler_params=params,
            name="splitting_step",
            cost_estimate=pl.CostEstimate(flops=20_000_000_000, bytes_accessed=1, transcendentals=0),
        )(sunlit, field, east_courant, north_courant, mixing, *halos, *weights)
        field, edges, weights = outs[0], outs[1:5], outs[5:]
    return field


def solution(mesh):
    placed = (
        P(None, None, "lat", "lon"),
        P(None, "lat", "lon"),
        P(None, "lat", "lon"),
        P(None, "lat", "lon"),
        P("lat", "lon"),
        P(),
        P(),
        P(),
        P(),
        P(),
        P(),
    )
    return jax.shard_map(
        on_device,
        mesh=mesh,
        in_specs=placed,
        out_specs=P(None, None, "lat", "lon"),
        check_vma=False,
    )
```

```python
import functools
import itertools

import jax
import jax.numpy as jnp
from jax import lax
from jax.experimental import pallas as pl
from jax.experimental.pallas import tpu as pltpu
from jax.sharding import PartitionSpec as P

BLOCK = 16
SUBSTEPS = 2
STEPS = 2
GROUP = 16
ROWS_AT_ONCE = 8
ROWS_IN_FLIGHT = 2
LEVELS_AT_ONCE = 4
LAG = 1

F32 = jnp.float32
BF16 = jnp.bfloat16
VMEM_BYTES = 48 * 1024 * 1024
FIRST_VMEM_BYTES = 56 * 1024 * 1024


def lane_ids(shape):
    return lax.broadcasted_iota(jnp.int32, shape, len(shape) - 1)


def fold_weights(decode_t, react_a_t, react_b_t, stoich, encode, rate, linear_out, encode_out):
    n_reactions = react_a_t.shape[1]
    contract = (((0,), (1,)), ((), ()))
    for part, react in enumerate((react_a_t, react_b_t)):
        product = lax.dot_general(
            react[...], decode_t[...], contract, preferred_element_type=F32
        )
        for group in range(n_reactions // GROUP):
            at = (2 * group + part) * GROUP
            linear_out[at : at + GROUP, :] = product[
                group * GROUP : (group + 1) * GROUP
            ].astype(BF16)
    folded = jnp.dot(encode[...], stoich[...], preferred_element_type=F32)
    encode_out[...] = (folded * rate[...]).astype(BF16)


def at_ends():
    index = lax.axis_index("lat")
    return index == 0, index == lax.axis_size("lat") - 1


def is_even(axis):
    return lax.axis_index(axis) % 2 == 0


def by_parity(axis, up, down, into_first, into_second):
    even = is_even(axis)
    into_first[...] = jnp.where(even, up, down)
    into_second[...] = jnp.where(even, down, up)


def pack_sides(value, coef, at, west, east):
    lanes = lane_ids(value.shape)
    size = value.shape[-1]
    turned = pltpu.roll(value * coef, at, 1)
    west = jnp.where(lanes == at, turned, west)
    east = jnp.where(lanes == (at + size - 1) % size, turned, east)
    return west, east


def first_kernel(latent, east_c, north_c, lon_a, lon_b, lat_a, lat_b, *scratch):
    tiles, east_v, north_v, sems = scratch
    n_levels, n_species, n_rows, n_cols = tiles.shape
    lanes = lane_ids((1, n_cols))
    is_first, is_last = at_ends()
    copies = [
        pltpu.make_async_copy(east_c, east_v, sems.at[n_levels]),
        pltpu.make_async_copy(north_c, north_v, sems.at[n_levels + 1]),
    ]
    levels = [
        pltpu.make_async_copy(latent.at[:, level], tiles.at[level], sems.at[level])
        for level in range(n_levels)
    ]
    for copy in copies + levels:
        copy.start()
    for copy in copies:
        copy.wait()
    sides = (jnp.zeros((n_species, n_cols), F32),) * 2
    for level in range(n_levels):
        levels[level].wait()
        tile = jnp.transpose(tiles[level], (1, 0, 2))
        for r in range(n_rows):
            at = level * n_rows + r
            value = tile[r]
            speed = east_v[level, r : r + 1, :]
            coef = jnp.where(lanes == 0, jnp.minimum(speed, 0.0), jnp.maximum(speed, 0.0))
            sides = pack_sides(value, coef, at, *sides)
        ends = []
        for r, closed, clip in ((0, is_first, jnp.minimum), (n_rows - 1, is_last, jnp.maximum)):
            speed = clip(north_v[level, r : r + 1, :], 0.0)
            ends.append((tile[r] * jnp.where(closed, 0.0, speed)).astype(BF16))
        by_parity("lat", ends[1], ends[0], lat_a.at[level], lat_b.at[level])
    by_parity("lon", sides[1], sides[0], lon_a, lon_b)


def step_kernel(
    n_levels,
    n_rows,
    first,
    last,
    sun,
    field,
    east_c,
    north_c,
    mixing,
    lon_a_in,
    lon_b_in,
    lat_a_in,
    lat_b_in,
    *refs,
):
    if first:
        weights, refs = refs[:6], refs[6:]
        linear, encode = refs[5:7]
    else:
        (linear, encode), refs = refs[:2], refs[2:]
    half_rows = n_rows // 2
    south_in, north_in, west_in, east_in, coefs, diffused = refs[-6:]
    if last:
        staged, sems = refs[-8:-6]
    by_parity("lon", lon_a_in[...], lon_b_in[...], east_in, west_in)
    by_parity("lat", lat_a_in[...], lat_b_in[...], north_in, south_in)
    n_species, n_cols = west_in.shape
    n_reactions = encode.shape[1]
    cells = n_levels * n_rows
    lanes = lane_ids((1, n_cols))
    row_ids = lax.broadcasted_iota(jnp.int32, (n_rows, n_cols), 0)
    is_first, is_last = at_ends()
    if first:
        latent, field = field, refs[-7]
        fold_weights(*weights, linear, encode)
        for level in range(n_levels):
            field[level] = jnp.transpose(latent[:, level], (1, 0, 2))
    CENTRE, EAST, WEST, NORTH, SOUTH, SCALE, LOWER, UPPER = range(8)

    upper = None
    for level in range(n_levels):
        ce, cn = east_c[level], north_c[level]
        east, west = jnp.maximum(ce, 0.0), jnp.minimum(ce, 0.0)
        north = jnp.where((row_ids == n_rows - 1) & is_last, 0.0, jnp.maximum(cn, 0.0))
        south = jnp.where((row_ids == 0) & is_first, 0.0, jnp.minimum(cn, 0.0))
        coefs[CENTRE, level] = 1.0 - east + west - north + south
        coefs[EAST, level] = east
        coefs[WEST, level] = west
        coefs[NORTH, level] = north
        coefs[SOUTH, level] = south
        pivot = 1.0
        if level > 0:
            below = mixing[level - 1]
            pivot = pivot + below - below * upper
        if level < n_levels - 1:
            pivot = pivot + mixing[level]
        scale = 1.0 / pivot
        coefs[SCALE, level] = scale
        if level > 0:
            coefs[LOWER, level] = below * scale
        if level < n_levels - 1:
            upper = mixing[level] * scale
            coefs[UPPER, level] = upper

    lit = jnp.zeros((1, n_cols), jnp.int32)
    for block in range(n_cols // BLOCK):
        lit = jnp.where(lanes // BLOCK == block, sun[0, block], lit)
    lit = lit > 0

    def coef(kind, level, r):
        return coefs[kind, level, pl.ds(r, 1), :]

    def transport(slot):
        r = jnp.minimum(slot, n_rows - 1)
        before, after = jnp.maximum(r - 1, 0), jnp.minimum(r + 1, n_rows - 1)
        right = None
        for level in range(n_levels):
            at = level * n_rows + r
            value = field[level, r]
            from_west = jnp.where(
                lanes == 0,
                pltpu.roll(west_in[...], (n_cols + 1 - at) % n_cols, 1),
                pltpu.roll(value * coef(EAST, level, r), 1, 1),
            )
            from_east = jnp.where(
                lanes == n_cols - 1,
                pltpu.roll(east_in[...], n_cols - 1 - at, 1),
                pltpu.roll(value * coef(WEST, level, r), n_cols - 1, 1),
            )
            from_south = jnp.where(
                r == 0,
                south_in[level].astype(F32),
                field[level, before] * coef(NORTH, level, before),
            )
            from_north = jnp.where(
                r == n_rows - 1,
                north_in[level].astype(F32),
                field[level, after] * coef(SOUTH, level, after),
            )
            moved = value * coef(CENTRE, level, r) + (from_west - from_east) + (from_south - from_north)
            scaled = moved * coef(SCALE, level, r)
            right = scaled if level == 0 else scaled + coef(LOWER, level, r) * right
            diffused[level, slot] = right
            yield
        for level in range(n_levels - 2, -1, -1):
            right = diffused[level, slot] + coef(UPPER, level, r) * right
            diffused[level, slot] = right
            yield

    def product_of(rounded):
        both = jnp.dot(linear[...], rounded, preferred_element_type=F32)
        parts = [
            both[at : at + GROUP] * both[at + GROUP : at + 2 * GROUP]
            for at in range(0, 2 * n_reactions, 2 * GROUP)
        ]
        return jnp.concatenate(parts, axis=0).astype(BF16)

    for r in range(ROWS_IN_FLIGHT):
        for _ in transport(r):
            pass
    lit_tile = jnp.concatenate([lit] * LEVELS_AT_ONCE, axis=1)

    def tile_at(level, r):
        return jnp.concatenate(
            [diffused[level + extra, r] for extra in range(LEVELS_AT_ONCE)], axis=1
        )

    def rows(turn, sides):
        units, ahead = [], {}
        for first_row in range(0, ROWS_AT_ONCE, ROWS_IN_FLIGHT):
            in_flight = [turn * ROWS_AT_ONCE + first_row + extra for extra in range(ROWS_IN_FLIGHT)]
            places = [
                (level, r) for r in in_flight for level in range(0, n_levels, LEVELS_AT_ONCE)
            ]
            steps = itertools.chain(*[transport(r + ROWS_IN_FLIGHT) for r in in_flight])
            share = -(-(2 * n_levels - 1) * ROWS_IN_FLIGHT // (SUBSTEPS * len(places)))
            for substep in range(SUBSTEPS):
                for place in places:
                    ahead[len(units)] = (steps, share)
                    units.append((substep, place))
        rounded, rates = {}, {}
        for at in range(len(units) + LAG):
            if at < len(units):
                substep, (level, r) = units[at]
                if substep == 0:
                    rounded[at] = tile_at(level, r).astype(BF16)
                rates[at] = product_of(rounded.pop(at))
                steps, share = ahead[at]
                for _ in itertools.islice(steps, share):
                    pass
            if at >= LAG:
                done = at - LAG
                substep, (level, r) = units[done]
                change = jnp.dot(encode[...], rates.pop(done), preferred_element_type=F32)
                tile = tile_at(level, r)
                value = tile + jnp.where(lit_tile, change, 0.0)
                if substep < SUBSTEPS - 1:
                    later = done + ROWS_IN_FLIGHT * (n_levels // LEVELS_AT_ONCE)
                    rounded[later] = (tile.astype(BF16).astype(F32) + change).astype(BF16)
                for extra in range(LEVELS_AT_ONCE):
                    part = value[:, extra * n_cols : (extra + 1) * n_cols]
                    at_level = level + extra
                    if last or substep < SUBSTEPS - 1:
                        diffused[at_level, r] = part
                    else:
                        refs[0][at_level, r] = part
                        speed = east_c[at_level, pl.ds(r, 1), :]
                        side = jnp.where(
                            lanes == 0, jnp.minimum(speed, 0.0), jnp.maximum(speed, 0.0)
                        )
                        sides = pack_sides(part, side, at_level * n_rows + r, *sides)
        return sides

    if last:

        def sends(half):
            within = pl.ds(pl.multiple_of(half * half_rows, half_rows), half_rows)
            return [
                pltpu.make_async_copy(
                    staged.at[half, level], refs[0].at[:, level, within], sems.at[half, level]
                )
                for level in range(n_levels)
            ]

        def half_done(half, carry):
            for turn in range(half_rows // ROWS_AT_ONCE):
                rows(half * (half_rows // ROWS_AT_ONCE) + turn, None)
            for level, copy in enumerate(sends(half)):
                within = pl.ds(half * half_rows, half_rows)
                staged[half, level] = jnp.transpose(diffused[level, within], (1, 0, 2))
                copy.start()
            return carry

        lax.fori_loop(0, 2, half_done, 0)
        for half in range(2):
            for copy in sends(half):
                copy.wait()
        return
    out, lon_a, lon_b, lat_a, lat_b = refs[:5]
    zeros = jnp.zeros((n_species, n_cols), F32)
    west, east = lax.fori_loop(0, n_rows // ROWS_AT_ONCE, rows, (zeros, zeros))
    by_parity("lon", east, west, lon_a, lon_b)
    for level in range(n_levels):
        south = (out[level, 0] * coefs[SOUTH, level, :1]).astype(BF16)
        north = (out[level, n_rows - 1] * coefs[NORTH, level, n_rows - 1 :]).astype(BF16)
        by_parity("lat", north, south, lat_a.at[level], lat_b.at[level])


def vmem(count):
    return [pl.BlockSpec(memory_space=pltpu.VMEM)] * count


def exchanged(lon_a, lon_b, lat_a, lat_b):
    def swapped(array, axis, first):
        size = lax.axis_size(axis)
        pairs = [(i % size, (i + 1) % size) for i in range(first, size + first, 2)]
        return lax.ppermute(array, axis, pairs + [(j, i) for i, j in pairs])

    lon_b, lon_a = swapped(lon_b, "lon", 1), swapped(lon_a, "lon", 0)
    lat_b, lat_a = swapped(lat_b, "lat", 1), swapped(lat_a, "lat", 0)
    return lon_a, lon_b, lat_a, lat_b


def on_device(
    latent_field,
    east_courant,
    north_courant,
    mixing,
    sunlit,
    decode_w,
    react_a,
    react_b,
    stoich,
    encode_w,
    rate_const,
):
    n_species, n_levels, n_rows, n_cols = latent_field.shape
    layered = jax.ShapeDtypeStruct((n_levels, n_rows, n_species, n_cols), F32)
    side = jax.ShapeDtypeStruct((n_species, n_cols), F32)
    edge = jax.ShapeDtypeStruct((n_levels, n_species, n_cols), BF16)
    params = pltpu.CompilerParams(vmem_limit_bytes=VMEM_BYTES)
    smem = pl.BlockSpec(memory_space=pltpu.SMEM)
    hbm = pl.BlockSpec(memory_space=pltpu.HBM)
    n_reactions = react_a.shape[0]
    edges = pl.pallas_call(
        first_kernel,
        out_shape=(side, side, edge, edge),
        in_specs=[hbm] * 3,
        out_specs=tuple(vmem(4)),
        scratch_shapes=[
            pltpu.VMEM((n_levels, n_species, n_rows, n_cols), F32),
            pltpu.VMEM((n_levels, n_rows, n_cols), F32),
            pltpu.VMEM((n_levels, n_rows, n_cols), F32),
            pltpu.SemaphoreType.DMA((n_levels + 2,)),
        ],
        compiler_params=pltpu.CompilerParams(vmem_limit_bytes=FIRST_VMEM_BYTES),
        name="first_sends",
        cost_estimate=pl.CostEstimate(flops=4_000_000_000, bytes_accessed=2_000_000, transcendentals=0),
    )(latent_field, east_courant, north_courant)
    weights = (decode_w.T, react_a.T, react_b.T, stoich, encode_w, rate_const[None])
    folded = (
        jax.ShapeDtypeStruct((2 * n_reactions, n_species), BF16),
        jax.ShapeDtypeStruct((n_species, n_reactions), BF16),
    )
    field = latent_field
    for step in range(STEPS):
        first, last = step == 0, step == STEPS - 1
        halos = exchanged(*edges)
        scratch = [pltpu.VMEM(layered.shape, F32)] if first else []
        if last:
            scratch += [
                pltpu.VMEM((2, n_levels, n_species, n_rows // 2, n_cols), F32),
                pltpu.SemaphoreType.DMA((2, n_levels)),
            ]
        scratch += [pltpu.VMEM(array.shape, array.dtype) for array in (edge, edge, side, side)]
        scratch += [
            pltpu.VMEM((8, n_levels, n_rows, n_cols), F32),
            pltpu.VMEM((n_levels, n_rows + ROWS_IN_FLIGHT, n_species, n_cols), F32),
        ]
        outs = pl.pallas_call(
            functools.partial(step_kernel, n_levels, n_rows, first, last),
            out_shape=(jax.ShapeDtypeStruct(latent_field.shape, F32),)
            if last
            else (layered, side, side, edge, edge, *folded),
            in_specs=[smem] + vmem(8 + len(weights)),
            out_specs=(hbm,) if last else tuple(vmem(7)),
            scratch_shapes=scratch,
            compiler_params=params,
            name="splitting_step",
            cost_estimate=pl.CostEstimate(flops=20_000_000_000, bytes_accessed=1, transcendentals=0),
        )(sunlit, field, east_courant, north_courant, mixing, *halos, *weights)
        field, edges, weights = outs[0], outs[1:5], outs[5:]
    return field


def solution(mesh):
    placed = (
        P(None, None, "lat", "lon"),
        P(None, "lat", "lon"),
        P(None, "lat", "lon"),
        P(None, "lat", "lon"),
        P("lat", "lon"),
        P(),
        P(),
        P(),
        P(),
        P(),
        P(),
    )
    return jax.shard_map(
        on_device,
        mesh=mesh,
        in_specs=placed,
        out_specs=P(None, None, "lat", "lon"),
        check_vma=False,
    )
```

```python
import functools
import itertools

import jax
import jax.numpy as jnp
from jax import lax
from jax.experimental import pallas as pl
from jax.experimental.pallas import tpu as pltpu
from jax.sharding import PartitionSpec as P

BLOCK = 16
SUBSTEPS = 2
STEPS = 2
GROUP = 16
ROWS_AT_ONCE = 8
ROWS_IN_FLIGHT = 2
LEVELS_AT_ONCE = 4
LAG = 1

F32 = jnp.float32
BF16 = jnp.bfloat16
VMEM_BYTES = 48 * 1024 * 1024
FIRST_VMEM_BYTES = 56 * 1024 * 1024


def lane_ids(shape):
    return lax.broadcasted_iota(jnp.int32, shape, len(shape) - 1)


def fold_weights(decode_t, react_a_t, react_b_t, stoich, encode, rate, linear_out, encode_out):
    n_reactions = react_a_t.shape[1]
    contract = (((0,), (1,)), ((), ()))
    for part, react in enumerate((react_a_t, react_b_t)):
        product = lax.dot_general(
            react[...], decode_t[...], contract, preferred_element_type=F32
        )
        for group in range(n_reactions // GROUP):
            at = (2 * group + part) * GROUP
            linear_out[at : at + GROUP, :] = product[
                group * GROUP : (group + 1) * GROUP
            ].astype(BF16)
    folded = jnp.dot(encode[...], stoich[...], preferred_element_type=F32)
    encode_out[...] = (folded * rate[...]).astype(BF16)


def at_ends():
    index = lax.axis_index("lat")
    return index == 0, index == lax.axis_size("lat") - 1


def is_even(axis):
    return lax.axis_index(axis) % 2 == 0


def by_parity(axis, up, down, into_first, into_second):
    even = is_even(axis)
    into_first[...] = jnp.where(even, up, down)
    into_second[...] = jnp.where(even, down, up)


COLUMN_ROWS = 40
EAST_ROW, NORTH_ROW, MIXING_ROW, LIT_ROW = 32, 33, 34, 35


def first_kernel(sun, latent, east_c, north_c, mixing, lon_a, lon_b, lat_a, lat_b, *scratch):
    tiles, east_v, north_v, mixing_v, sems = scratch
    n_levels, n_species, n_rows, n_cols = tiles.shape
    lanes = lane_ids((1, n_cols))
    is_first, is_last = at_ends()
    copies = [
        pltpu.make_async_copy(source, held, sems.at[n_levels + at])
        for at, (source, held) in enumerate(
            ((east_c, east_v), (north_c, north_v), (mixing, mixing_v))
        )
    ]
    levels = [
        pltpu.make_async_copy(latent.at[:, level], tiles.at[level], sems.at[level])
        for level in range(n_levels)
    ]
    for copy in copies + levels:
        copy.start()
    for copy in copies:
        copy.wait()
    turns = (0, 1, -2, -1)
    columns = [jnp.zeros((COLUMN_ROWS, n_cols), F32) for _ in turns]
    for level in range(n_levels):
        levels[level].wait()
        extra = [east_v[level], north_v[level]]
        if level < n_levels - 1:
            extra.append(mixing_v[level])
        extra += [jnp.zeros((n_rows, n_cols), F32)] * (COLUMN_ROWS - n_species - len(extra))
        tile = jnp.transpose(
            jnp.concatenate([tiles[level]] + [plane[None] for plane in extra], axis=0), (1, 0, 2)
        )
        for r in range(n_rows):
            at = level * n_rows + r
            turned = pltpu.roll(tile[r], at, 1)
            columns = [
                jnp.where(lanes == (at + turn) % n_cols, turned, column)
                for turn, column in zip(turns, columns)
            ]
        ends = []
        for r, closed, clip in ((0, is_first, jnp.minimum), (n_rows - 1, is_last, jnp.maximum)):
            speed = clip(north_v[level, r : r + 1, :], 0.0)
            ends.append((tile[r, :n_species] * jnp.where(closed, 0.0, speed)).astype(BF16))
        by_parity("lat", ends[1], ends[0], lat_a.at[level], lat_b.at[level])
    columns = [
        column if turn == 0 else pltpu.roll(column, -turn % n_cols, 1)
        for turn, column in zip(turns, columns)
    ]
    kinds = lax.broadcasted_iota(jnp.int32, (COLUMN_ROWS, n_cols), 0)
    lit_west = sun[0, 0].astype(F32)
    lit_east = sun[0, n_cols // BLOCK - 1].astype(F32)
    west = [jnp.where(kinds == LIT_ROW, lit_west, columns[at]) for at in (0, 1)]
    east = [jnp.where(kinds == LIT_ROW, lit_east, columns[at]) for at in (3, 2)]
    by_parity("lon", jnp.concatenate(east, axis=0), jnp.concatenate(west, axis=0), lon_a, lon_b)


def split_columns(message):
    return message[:COLUMN_ROWS], message[COLUMN_ROWS:]


def inflow(column, n_species, clip):
    return column[:n_species] * clip(column[EAST_ROW : EAST_ROW + 1], 0.0)


def lat_inflow(column, n_species, clip):
    return column[:n_species] * clip(column[NORTH_ROW : NORTH_ROW + 1], 0.0)


def diffused_column(column, west, east, south, north, n_species, n_levels, n_rows, ends):
    n_cols = column.shape[1]
    lanes = lane_ids((1, n_cols))
    levels, rows = lanes // n_rows, lanes % n_rows
    is_first, is_last = ends
    speed = column[EAST_ROW : EAST_ROW + 1]
    lat_speed = column[NORTH_ROW : NORTH_ROW + 1]
    up = jnp.where((rows == n_rows - 1) & is_last, 0.0, jnp.maximum(lat_speed, 0.0))
    down = jnp.where((rows == 0) & is_first, 0.0, jnp.minimum(lat_speed, 0.0))
    value = column[:n_species]
    from_south = jnp.where(rows == 0, south, pltpu.roll(value * up, 1, 1))
    from_north = jnp.where(rows == n_rows - 1, north, pltpu.roll(value * down, n_cols - 1, 1))
    centre = 1.0 - jnp.abs(speed) - up + down
    moved = value * centre + (west - east) + (from_south - from_north)
    above = column[MIXING_ROW : MIXING_ROW + 1]
    below = jnp.where(levels == 0, 0.0, pltpu.roll(above, n_rows, 1))
    upper = jnp.zeros((1, n_cols), F32)
    scale = upper
    for level in range(n_levels):
        pivot = 1.0 + below + above - below * pltpu.roll(upper, n_rows, 1)
        scale = jnp.where(levels == level, 1.0 / pivot, scale)
        upper = above * scale
    solved = jnp.zeros_like(moved)
    for level in range(n_levels):
        swept = (moved + below * pltpu.roll(solved, n_rows, 1)) * scale
        solved = jnp.where(levels == level, swept, solved)
    for level in range(n_levels - 2, -1, -1):
        swept = solved + upper * pltpu.roll(solved, n_cols - n_rows, 1)
        solved = jnp.where(levels == level, swept, solved)
    return solved


def step_kernel(
    n_levels,
    n_rows,
    first,
    last,
    sun,
    field,
    east_c,
    north_c,
    mixing,
    lon_a_in,
    lon_b_in,
    lat_a_in,
    lat_b_in,
    *refs,
):
    if first:
        weights, refs = refs[:6], refs[6:]
        linear, encode = refs[3:5]
    else:
        (lon_a_own, lon_b_own, linear, encode), refs = refs[:4], refs[4:]
    half_rows = n_rows // 2
    south_in, north_in, west_in, east_in, coefs, diffused = refs[-6:]
    if last:
        staged, sems = refs[-8:-6]
    by_parity("lat", lat_a_in[...], lat_b_in[...], north_in, south_in)
    n_species, n_cols = west_in.shape
    n_reactions = encode.shape[1]
    cells = n_levels * n_rows
    lanes = lane_ids((1, n_cols))
    row_ids = lax.broadcasted_iota(jnp.int32, (n_rows, n_cols), 0)
    is_first, is_last = at_ends()
    if first:
        latent, field = field, refs[-7]
        fold_weights(*weights, linear, encode)
        for level in range(n_levels):
            field[level] = jnp.transpose(latent[:, level], (1, 0, 2))
    CENTRE, EAST, WEST, NORTH, SOUTH, SCALE, LOWER, UPPER = range(8)

    upper = None
    for level in range(n_levels):
        ce, cn = east_c[level], north_c[level]
        east, west = jnp.maximum(ce, 0.0), jnp.minimum(ce, 0.0)
        north = jnp.where((row_ids == n_rows - 1) & is_last, 0.0, jnp.maximum(cn, 0.0))
        south = jnp.where((row_ids == 0) & is_first, 0.0, jnp.minimum(cn, 0.0))
        coefs[CENTRE, level] = 1.0 - east + west - north + south
        coefs[EAST, level] = east
        coefs[WEST, level] = west
        coefs[NORTH, level] = north
        coefs[SOUTH, level] = south
        pivot = 1.0
        if level > 0:
            below = mixing[level - 1]
            pivot = pivot + below - below * upper
        if level < n_levels - 1:
            pivot = pivot + mixing[level]
        scale = 1.0 / pivot
        coefs[SCALE, level] = scale
        if level > 0:
            coefs[LOWER, level] = below * scale
        if level < n_levels - 1:
            upper = mixing[level] * scale
            coefs[UPPER, level] = upper

    even = is_even("lon")
    west_near, west_far = split_columns(jnp.where(even, lon_b_in[...], lon_a_in[...]))
    east_near, east_far = split_columns(jnp.where(even, lon_a_in[...], lon_b_in[...]))

    lit = jnp.zeros((1, n_cols), jnp.int32)
    for block in range(n_cols // BLOCK):
        lit = jnp.where(lanes // BLOCK == block, sun[0, block], lit)
    lit = lit > 0

    def coef(kind, level, r):
        return coefs[kind, level, pl.ds(r, 1), :]

    def transport(slot):
        r = jnp.minimum(slot, n_rows - 1)
        before, after = jnp.maximum(r - 1, 0), jnp.minimum(r + 1, n_rows - 1)
        right = None
        for level in range(n_levels):
            at = level * n_rows + r
            value = field[level, r]
            from_west = jnp.where(
                lanes == 0,
                pltpu.roll(west_in[...], (n_cols - at) % n_cols, 1),
                pltpu.roll(value * coef(EAST, level, r), 1, 1),
            )
            from_east = jnp.where(
                lanes == n_cols - 1,
                pltpu.roll(east_in[...], n_cols - 1 - at, 1),
                pltpu.roll(value * coef(WEST, level, r), n_cols - 1, 1),
            )
            from_south = jnp.where(
                r == 0,
                south_in[level].astype(F32),
                field[level, before] * coef(NORTH, level, before),
            )
            from_north = jnp.where(
                r == n_rows - 1,
                north_in[level].astype(F32),
                field[level, after] * coef(SOUTH, level, after),
            )
            moved = value * coef(CENTRE, level, r) + (from_west - from_east) + (from_south - from_north)
            scaled = moved * coef(SCALE, level, r)
            right = scaled if level == 0 else scaled + coef(LOWER, level, r) * right
            diffused[level, slot] = right
            yield
        for level in range(n_levels - 2, -1, -1):
            right = diffused[level, slot] + coef(UPPER, level, r) * right
            diffused[level, slot] = right
            yield

    def product_of(rounded):
        both = jnp.dot(linear[...], rounded, preferred_element_type=F32)
        parts = [
            both[at : at + GROUP] * both[at + GROUP : at + 2 * GROUP]
            for at in range(0, 2 * n_reactions, 2 * GROUP)
        ]
        return jnp.concatenate(parts, axis=0).astype(BF16)

    if first:
        west_in[...] = inflow(west_near, n_species, jnp.maximum)
        east_in[...] = inflow(east_near, n_species, jnp.minimum)
    else:
        own_west, _ = split_columns(jnp.where(even, lon_b_own[...], lon_a_own[...]))
        own_east, _ = split_columns(jnp.where(even, lon_a_own[...], lon_b_own[...]))
        ends = is_first, is_last

        def corner(edge, at, turn):
            return pltpu.roll(edge[n_levels + at].astype(F32), turn, 1)

        def column_after(at, near, west, east):
            return diffused_column(
                near,
                inflow(west, n_species, jnp.maximum),
                inflow(east, n_species, jnp.minimum),
                corner(south_in, at, n_cols - (n_rows - 1)),
                corner(north_in, at, n_rows - 1),
                n_species,
                n_levels,
                n_rows,
                ends,
            )

        pair = jnp.concatenate(
            [
                column_after(0, west_near, west_far, own_west),
                column_after(1, east_near, own_east, east_far),
            ],
            axis=1,
        )
        rounded = pair.astype(BF16)
        current, summed = rounded.astype(F32), None
        for substep in range(SUBSTEPS):
            change = jnp.dot(encode[...], product_of(rounded), preferred_element_type=F32)
            summed = change if summed is None else summed + change
            current = current + change
            rounded = current.astype(BF16)
        pair_lit = jnp.concatenate(
            [near[LIT_ROW : LIT_ROW + 1] for near in (west_near, east_near)], axis=1
        )
        pair = pair + jnp.where(pair_lit > 0.0, summed, 0.0)
        west_speed = west_near[EAST_ROW : EAST_ROW + 1]
        east_speed = east_near[EAST_ROW : EAST_ROW + 1]
        west_in[...] = pair[:, :n_cols] * jnp.maximum(west_speed, 0.0)
        east_in[...] = pair[:, n_cols:] * jnp.minimum(east_speed, 0.0)

    for r in range(ROWS_IN_FLIGHT):
        for _ in transport(r):
            pass
    lit_tile = jnp.concatenate([lit] * LEVELS_AT_ONCE, axis=1)

    def tile_at(level, r):
        return jnp.concatenate(
            [diffused[level + extra, r] for extra in range(LEVELS_AT_ONCE)], axis=1
        )

    def rows(turn, carry):
        units, ahead = [], {}
        for first_row in range(0, ROWS_AT_ONCE, ROWS_IN_FLIGHT):
            in_flight = [turn * ROWS_AT_ONCE + first_row + extra for extra in range(ROWS_IN_FLIGHT)]
            places = [
                (level, r) for r in in_flight for level in range(0, n_levels, LEVELS_AT_ONCE)
            ]
            steps = itertools.chain(*[transport(r + ROWS_IN_FLIGHT) for r in in_flight])
            share = -(-(2 * n_levels - 1) * ROWS_IN_FLIGHT // (SUBSTEPS * len(places)))
            for substep in range(SUBSTEPS):
                for place in places:
                    ahead[len(units)] = (steps, share)
                    units.append((substep, place))
        rounded, rates = {}, {}
        for at in range(len(units) + LAG):
            if at < len(units):
                substep, (level, r) = units[at]
                if substep == 0:
                    rounded[at] = tile_at(level, r).astype(BF16)
                rates[at] = product_of(rounded.pop(at))
                steps, share = ahead[at]
                for _ in itertools.islice(steps, share):
                    pass
            if at >= LAG:
                done = at - LAG
                substep, (level, r) = units[done]
                change = jnp.dot(encode[...], rates.pop(done), preferred_element_type=F32)
                tile = tile_at(level, r)
                value = tile + jnp.where(lit_tile, change, 0.0)
                if substep < SUBSTEPS - 1:
                    later = done + ROWS_IN_FLIGHT * (n_levels // LEVELS_AT_ONCE)
                    rounded[later] = (tile.astype(BF16).astype(F32) + change).astype(BF16)
                for extra in range(LEVELS_AT_ONCE):
                    part = value[:, extra * n_cols : (extra + 1) * n_cols]
                    at_level = level + extra
                    if last or substep < SUBSTEPS - 1:
                        diffused[at_level, r] = part
                    else:
                        refs[0][at_level, r] = part
        return carry

    if last:

        def sends(half):
            within = pl.ds(pl.multiple_of(half * half_rows, half_rows), half_rows)
            return [
                pltpu.make_async_copy(
                    staged.at[half, level], refs[0].at[:, level, within], sems.at[half, level]
                )
                for level in range(n_levels)
            ]

        def half_done(half, carry):
            for turn in range(half_rows // ROWS_AT_ONCE):
                rows(half * (half_rows // ROWS_AT_ONCE) + turn, None)
            for level, copy in enumerate(sends(half)):
                within = pl.ds(half * half_rows, half_rows)
                staged[half, level] = jnp.transpose(diffused[level, within], (1, 0, 2))
                copy.start()
            return carry

        lax.fori_loop(0, 2, half_done, 0)
        for half in range(2):
            for copy in sends(half):
                copy.wait()
        return
    out, lat_a, lat_b = refs[:3]
    lax.fori_loop(0, n_rows // ROWS_AT_ONCE, rows, 0)
    for level in range(n_levels):
        south = (out[level, 0] * coefs[SOUTH, level, :1]).astype(BF16)
        north = (out[level, n_rows - 1] * coefs[NORTH, level, n_rows - 1 :]).astype(BF16)
        by_parity("lat", north, south, lat_a.at[level], lat_b.at[level])
    for at, near in enumerate((west_near, east_near)):
        south = jnp.where(is_first, 0.0, lat_inflow(near, n_species, jnp.minimum)).astype(BF16)
        north = jnp.where(is_last, 0.0, lat_inflow(near, n_species, jnp.maximum)).astype(BF16)
        by_parity("lat", north, south, lat_a.at[n_levels + at], lat_b.at[n_levels + at])


def vmem(count):
    return [pl.BlockSpec(memory_space=pltpu.VMEM)] * count


def swapped(array, axis, first):
    size = lax.axis_size(axis)
    pairs = [(i % size, (i + 1) % size) for i in range(first, size + first, 2)]
    return lax.ppermute(array, axis, pairs + [(j, i) for i, j in pairs])


def on_device(
    latent_field,
    east_courant,
    north_courant,
    mixing,
    sunlit,
    decode_w,
    react_a,
    react_b,
    stoich,
    encode_w,
    rate_const,
):
    n_species, n_levels, n_rows, n_cols = latent_field.shape
    layered = jax.ShapeDtypeStruct((n_levels, n_rows, n_species, n_cols), F32)
    column = jax.ShapeDtypeStruct((2 * COLUMN_ROWS, n_cols), F32)
    side = jax.ShapeDtypeStruct((n_species, n_cols), F32)
    edge = jax.ShapeDtypeStruct((n_levels, n_species, n_cols), BF16)
    cornered = jax.ShapeDtypeStruct((n_levels + 2, n_species, n_cols), BF16)
    params = pltpu.CompilerParams(vmem_limit_bytes=VMEM_BYTES)
    smem = pl.BlockSpec(memory_space=pltpu.SMEM)
    hbm = pl.BlockSpec(memory_space=pltpu.HBM)
    n_reactions = react_a.shape[0]
    lon_a, lon_b, lat_a, lat_b = pl.pallas_call(
        first_kernel,
        out_shape=(column, column, edge, edge),
        in_specs=[smem] + [hbm] * 4,
        out_specs=tuple(vmem(4)),
        scratch_shapes=[
            pltpu.VMEM((n_levels, n_species, n_rows, n_cols), F32),
            pltpu.VMEM(east_courant.shape, F32),
            pltpu.VMEM(north_courant.shape, F32),
            pltpu.VMEM(mixing.shape, F32),
            pltpu.SemaphoreType.DMA((n_levels + 3,)),
        ],
        compiler_params=pltpu.CompilerParams(vmem_limit_bytes=FIRST_VMEM_BYTES),
        name="first_sends",
        cost_estimate=pl.CostEstimate(flops=4_000_000_000, bytes_accessed=2_000_000, transcendentals=0),
    )(sunlit, latent_field, east_courant, north_courant, mixing)
    weights = (decode_w.T, react_a.T, react_b.T, stoich, encode_w, rate_const[None])
    folded = (
        jax.ShapeDtypeStruct((2 * n_reactions, n_species), BF16),
        jax.ShapeDtypeStruct((n_species, n_reactions), BF16),
    )
    lon_halos = swapped(lon_a, "lon", 0), swapped(lon_b, "lon", 1)
    field = latent_field
    for step in range(STEPS):
        first, last = step == 0, step == STEPS - 1
        lat_halos = swapped(lat_a, "lat", 0), swapped(lat_b, "lat", 1)
        scratch = [pltpu.VMEM(layered.shape, F32)] if first else []
        if last:
            scratch += [
                pltpu.VMEM((2, n_levels, n_species, n_rows // 2, n_cols), F32),
                pltpu.SemaphoreType.DMA((2, n_levels)),
            ]
        scratch += [pltpu.VMEM(array.shape, array.dtype) for array in (*lat_halos, side, side)]
        scratch += [
            pltpu.VMEM((8, n_levels, n_rows, n_cols), F32),
            pltpu.VMEM((n_levels, n_rows + ROWS_IN_FLIGHT, n_species, n_cols), F32),
        ]
        operands = weights if first else (lon_a, lon_b, *weights)
        outs = pl.pallas_call(
            functools.partial(step_kernel, n_levels, n_rows, first, last),
            out_shape=(jax.ShapeDtypeStruct(latent_field.shape, F32),)
            if last
            else (layered, cornered, cornered, *folded),
            in_specs=[smem] + vmem(8 + len(operands)),
            out_specs=(hbm,) if last else tuple(vmem(5)),
            scratch_shapes=scratch,
            compiler_params=params,
            name="splitting_step",
            cost_estimate=pl.CostEstimate(flops=20_000_000_000, bytes_accessed=1, transcendentals=0),
        )(sunlit, field, east_courant, north_courant, mixing, *lon_halos, *lat_halos, *operands)
        if not last:
            field, lat_a, lat_b, *weights = outs
    return outs[0]


def solution(mesh):
    placed = (
        P(None, None, "lat", "lon"),
        P(None, "lat", "lon"),
        P(None, "lat", "lon"),
        P(None, "lat", "lon"),
        P("lat", "lon"),
        P(),
        P(),
        P(),
        P(),
        P(),
        P(),
    )
    return jax.shard_map(
        on_device,
        mesh=mesh,
        in_specs=placed,
        out_specs=P(None, None, "lat", "lon"),
        check_vma=False,
    )
```

```python
import functools
import itertools

import jax
import jax.numpy as jnp
from jax import lax
from jax.experimental import pallas as pl
from jax.experimental.pallas import tpu as pltpu
from jax.sharding import PartitionSpec as P

BLOCK = 16
SUBSTEPS = 2
STEPS = 2
GROUP = 16
ROWS_AT_ONCE = 8
ROWS_IN_FLIGHT = 2
LEVELS_AT_ONCE = 4
LAG = 1

F32 = jnp.float32
BF16 = jnp.bfloat16
VMEM_BYTES = 48 * 1024 * 1024
FIRST_VMEM_BYTES = 56 * 1024 * 1024


def lane_ids(shape):
    return lax.broadcasted_iota(jnp.int32, shape, len(shape) - 1)


def fold_weights(decode_t, react_a_t, react_b_t, stoich, encode, rate, linear_out, encode_out):
    n_reactions = react_a_t.shape[1]
    contract = (((0,), (1,)), ((), ()))
    for part, react in enumerate((react_a_t, react_b_t)):
        product = lax.dot_general(
            react[...], decode_t[...], contract, preferred_element_type=F32
        )
        for group in range(n_reactions // GROUP):
            at = (2 * group + part) * GROUP
            linear_out[at : at + GROUP, :] = product[
                group * GROUP : (group + 1) * GROUP
            ].astype(BF16)
    folded = jnp.dot(encode[...], stoich[...], preferred_element_type=F32)
    encode_out[...] = (folded * rate[...]).astype(BF16)


def at_ends():
    index = lax.axis_index("lat")
    return index == 0, index == lax.axis_size("lat") - 1


def is_even(axis):
    return lax.axis_index(axis) % 2 == 0


def by_parity(axis, up, down, into_first, into_second):
    even = is_even(axis)
    into_first[...] = jnp.where(even, up, down)
    into_second[...] = jnp.where(even, down, up)


COLUMN_ROWS = 40
EAST_ROW, NORTH_ROW, MIXING_ROW, LIT_ROW = 32, 33, 34, 35


def first_kernel(sun, latent, east_c, north_c, mixing, lon_a, lon_b, lat_a, lat_b, *scratch):
    tiles, east_v, north_v, mixing_v, sems = scratch
    n_levels, n_species, n_rows, n_cols = tiles.shape
    lanes = lane_ids((1, n_cols))
    is_first, is_last = at_ends()
    copies = [
        pltpu.make_async_copy(source, held, sems.at[n_levels + at])
        for at, (source, held) in enumerate(
            ((east_c, east_v), (north_c, north_v), (mixing, mixing_v))
        )
    ]
    levels = [
        pltpu.make_async_copy(latent.at[:, level], tiles.at[level], sems.at[level])
        for level in range(n_levels)
    ]
    for copy in copies + levels:
        copy.start()
    for copy in copies:
        copy.wait()
    gathered = [jnp.zeros((COLUMN_ROWS, n_cols), F32) for _ in range(4)]
    for level in range(n_levels):
        levels[level].wait()
        extra = [east_v[level], north_v[level]]
        if level < n_levels - 1:
            extra.append(mixing_v[level])
        extra += [jnp.zeros((n_rows, n_cols), F32)] * (COLUMN_ROWS - n_species - len(extra))
        tile = jnp.transpose(
            jnp.concatenate([tiles[level]] + [plane[None] for plane in extra], axis=0), (1, 0, 2)
        )
        for r in range(n_rows):
            at = level * n_rows + r
            turned = pltpu.roll(tile[r], at // 4 * 4 + 2, 1)
            gathered[at % 4] = jnp.where(lanes // 4 == at // 4, turned, gathered[at % 4])
        ends = []
        for r, closed, clip in ((0, is_first, jnp.minimum), (n_rows - 1, is_last, jnp.maximum)):
            speed = clip(north_v[level, r : r + 1, :], 0.0)
            ends.append((tile[r, :n_species] * jnp.where(closed, 0.0, speed)).astype(BF16))
        by_parity("lat", ends[1], ends[0], lat_a.at[level], lat_b.at[level])
    columns = []
    for slot in range(4):
        column = gathered[0]
        for place, part in enumerate(gathered):
            part = pltpu.roll(part, (place - slot) % n_cols, 1) if place != slot else part
            column = part if place == 0 else jnp.where(lanes % 4 == place, part, column)
        columns.append(column)
    kinds = lax.broadcasted_iota(jnp.int32, (COLUMN_ROWS, n_cols), 0)
    lit_west = sun[0, 0].astype(F32)
    lit_east = sun[0, n_cols // BLOCK - 1].astype(F32)
    west = [jnp.where(kinds == LIT_ROW, lit_west, columns[at]) for at in (2, 3)]
    east = [jnp.where(kinds == LIT_ROW, lit_east, columns[at]) for at in (1, 0)]
    by_parity("lon", jnp.concatenate(east, axis=0), jnp.concatenate(west, axis=0), lon_a, lon_b)


def split_columns(message):
    return message[:COLUMN_ROWS], message[COLUMN_ROWS:]


def inflow(column, n_species, clip):
    return column[:n_species] * clip(column[EAST_ROW : EAST_ROW + 1], 0.0)


def lat_inflow(column, n_species, clip):
    return column[:n_species] * clip(column[NORTH_ROW : NORTH_ROW + 1], 0.0)


def moved_column(column, west, east, south, north, n_species, n_rows, ends):
    n_cols = column.shape[1]
    rows = lane_ids((1, n_cols)) % n_rows
    is_first, is_last = ends
    speed = column[EAST_ROW : EAST_ROW + 1]
    lat_speed = column[NORTH_ROW : NORTH_ROW + 1]
    up = jnp.where((rows == n_rows - 1) & is_last, 0.0, jnp.maximum(lat_speed, 0.0))
    down = jnp.where((rows == 0) & is_first, 0.0, jnp.minimum(lat_speed, 0.0))
    value = column[:n_species]
    from_south = jnp.where(rows == 0, south, pltpu.roll(value * up, 1, 1))
    from_north = jnp.where(rows == n_rows - 1, north, pltpu.roll(value * down, n_cols - 1, 1))
    centre = 1.0 - jnp.abs(speed) - up + down
    return value * centre + (west - east) + (from_south - from_north)


def by_level(west, east, n_levels, n_rows):
    n_cols = west.shape[1]
    of_west = lane_ids((1, n_cols)) < n_rows
    return [
        jnp.where(
            of_west,
            pltpu.roll(west, (n_cols - level * n_rows) % n_cols, 1),
            pltpu.roll(east, (n_cols - (level - 1) * n_rows) % n_cols, 1),
        )
        for level in range(n_levels)
    ]


def joined(levels, n_rows):
    n_cols = levels[0].shape[1]
    width = 2 * n_rows
    lanes = lane_ids((1, n_cols))
    arrays = []
    for at, array in enumerate(levels):
        turn = at * width % n_cols
        if turn == 0:
            arrays.append(array)
        else:
            arrays[-1] = jnp.where(lanes // width == turn // width, pltpu.roll(array, turn, 1), arrays[-1])
    return arrays


def diffused_columns(moved, mixing):
    upper, swept = None, []
    uppers = []
    for level, value in enumerate(moved):
        pivot = 1.0
        if level > 0:
            below = mixing[level - 1]
            pivot = pivot + below - below * upper
            value = value + below * swept[-1]
        if level < len(moved) - 1:
            pivot = pivot + mixing[level]
        scale = 1.0 / pivot
        if level < len(moved) - 1:
            upper = mixing[level] * scale
            uppers.append(upper)
        swept.append(value * scale)
    for level in range(len(moved) - 2, -1, -1):
        swept[level] = swept[level] + uppers[level] * swept[level + 1]
    return swept


def step_kernel(
    n_levels,
    n_rows,
    first,
    last,
    sun,
    field,
    east_c,
    north_c,
    mixing,
    lon_a_in,
    lon_b_in,
    lat_a_in,
    lat_b_in,
    *refs,
):
    if first:
        weights, refs = refs[:6], refs[6:]
        linear, encode = refs[3:5]
    else:
        (lon_a_own, lon_b_own, linear, encode), refs = refs[:4], refs[4:]
    half_rows = n_rows // 2
    south_in, north_in, lon_in, coefs, diffused = refs[-5:]
    if last:
        staged, sems = refs[-7:-5]
    by_parity("lat", lat_a_in[...], lat_b_in[...], north_in, south_in)
    _, n_species, n_cols = lon_in.shape
    n_reactions = encode.shape[1]
    cells = n_levels * n_rows
    lanes = lane_ids((1, n_cols))
    row_ids = lax.broadcasted_iota(jnp.int32, (n_rows, n_cols), 0)
    is_first, is_last = at_ends()
    if first:
        latent, field = field, refs[-6]
        fold_weights(*weights, linear, encode)
        for level in range(n_levels):
            field[level] = jnp.transpose(latent[:, level], (1, 0, 2))
    CENTRE, EAST, WEST, NORTH, SOUTH, SCALE, LOWER, UPPER = range(8)

    upper = None
    for level in range(n_levels):
        ce, cn = east_c[level], north_c[level]
        east, west = jnp.maximum(ce, 0.0), jnp.minimum(ce, 0.0)
        north = jnp.where((row_ids == n_rows - 1) & is_last, 0.0, jnp.maximum(cn, 0.0))
        south = jnp.where((row_ids == 0) & is_first, 0.0, jnp.minimum(cn, 0.0))
        coefs[CENTRE, level] = 1.0 - east + west - north + south
        coefs[EAST, level] = east
        coefs[WEST, level] = west
        coefs[NORTH, level] = north
        coefs[SOUTH, level] = south
        pivot = 1.0
        if level > 0:
            below = mixing[level - 1]
            pivot = pivot + below - below * upper
        if level < n_levels - 1:
            pivot = pivot + mixing[level]
        scale = 1.0 / pivot
        coefs[SCALE, level] = scale
        if level > 0:
            coefs[LOWER, level] = below * scale
        if level < n_levels - 1:
            upper = mixing[level] * scale
            coefs[UPPER, level] = upper

    even = is_even("lon")
    west_near, west_far = split_columns(jnp.where(even, lon_b_in[...], lon_a_in[...]))
    east_near, east_far = split_columns(jnp.where(even, lon_a_in[...], lon_b_in[...]))

    lit = jnp.zeros((1, n_cols), jnp.int32)
    for block in range(n_cols // BLOCK):
        lit = jnp.where(lanes // BLOCK == block, sun[0, block], lit)
    lit = lit > 0

    def coef(kind, level, r):
        return coefs[kind, level, pl.ds(r, 1), :]

    def transport(slot):
        r = jnp.minimum(slot, n_rows - 1)
        before, after = jnp.maximum(r - 1, 0), jnp.minimum(r + 1, n_rows - 1)
        right = None
        for level in range(n_levels):
            value = field[level, r]
            spot = level * 2 * n_rows % n_cols
            halo = lon_in[level * 2 * n_rows // n_cols]
            from_west = jnp.where(
                lanes == 0,
                pltpu.roll(halo, (n_cols - spot - r) % n_cols, 1),
                pltpu.roll(value * coef(EAST, level, r), 1, 1),
            )
            from_east = jnp.where(
                lanes == n_cols - 1,
                pltpu.roll(halo, n_cols - 1 - spot - n_rows - r, 1),
                pltpu.roll(value * coef(WEST, level, r), n_cols - 1, 1),
            )
            from_south = jnp.where(
                r == 0,
                south_in[level].astype(F32),
                field[level, before] * coef(NORTH, level, before),
            )
            from_north = jnp.where(
                r == n_rows - 1,
                north_in[level].astype(F32),
                field[level, after] * coef(SOUTH, level, after),
            )
            moved = value * coef(CENTRE, level, r) + (from_west - from_east) + (from_south - from_north)
            scaled = moved * coef(SCALE, level, r)
            right = scaled if level == 0 else scaled + coef(LOWER, level, r) * right
            diffused[level, slot] = right
            yield
        for level in range(n_levels - 2, -1, -1):
            right = diffused[level, slot] + coef(UPPER, level, r) * right
            diffused[level, slot] = right
            yield

    def product_of(rounded):
        both = jnp.dot(linear[...], rounded, preferred_element_type=F32)
        parts = [
            both[at : at + GROUP] * both[at + GROUP : at + 2 * GROUP]
            for at in range(0, 2 * n_reactions, 2 * GROUP)
        ]
        return jnp.concatenate(parts, axis=0).astype(BF16)

    def levels_of(west, east):
        return by_level(west, east, n_levels, n_rows)

    def kind_of(kind):
        return levels_of(west_near[kind : kind + 1], east_near[kind : kind + 1])

    if first:
        halos = joined(
            levels_of(
                inflow(west_near, n_species, jnp.maximum), inflow(east_near, n_species, jnp.minimum)
            ),
            n_rows,
        )
    else:
        own_west, _ = split_columns(jnp.where(even, lon_b_own[...], lon_a_own[...]))
        own_east, _ = split_columns(jnp.where(even, lon_a_own[...], lon_b_own[...]))

        def corner(edge, at, turn):
            return pltpu.roll(edge[n_levels + at].astype(F32), turn, 1)

        def column_after(at, near, west, east):
            return moved_column(
                near,
                inflow(west, n_species, jnp.maximum),
                inflow(east, n_species, jnp.minimum),
                corner(south_in, at, n_cols - (n_rows - 1)),
                corner(north_in, at, n_rows - 1),
                n_species,
                n_rows,
                (is_first, is_last),
            )

        moved = levels_of(
            column_after(0, west_near, west_far, own_west),
            column_after(1, east_near, own_east, east_far),
        )
        pair = joined(diffused_columns(moved, kind_of(MIXING_ROW)), n_rows)
        pair = jnp.concatenate(pair, axis=1)
        rounded = pair.astype(BF16)
        current, summed = rounded.astype(F32), None
        for substep in range(SUBSTEPS):
            change = jnp.dot(encode[...], product_of(rounded), preferred_element_type=F32)
            summed = change if summed is None else summed + change
            current = current + change
            rounded = current.astype(BF16)
        pair_lit = jnp.concatenate(joined(kind_of(LIT_ROW), n_rows), axis=1)
        pair = pair + jnp.where(pair_lit > 0.0, summed, 0.0)
        halos = []
        for at, speed in enumerate(joined(kind_of(EAST_ROW), n_rows)):
            clipped = jnp.where(
                lanes // n_rows % 2 == 0, jnp.maximum(speed, 0.0), jnp.minimum(speed, 0.0)
            )
            halos.append(pair[:, at * n_cols : (at + 1) * n_cols] * clipped)
    for at, halo in enumerate(halos):
        lon_in[at] = halo

    for r in range(ROWS_IN_FLIGHT):
        for _ in transport(r):
            pass
    lit_tile = jnp.concatenate([lit] * LEVELS_AT_ONCE, axis=1)

    def tile_at(level, r):
        return jnp.concatenate(
            [diffused[level + extra, r] for extra in range(LEVELS_AT_ONCE)], axis=1
        )

    def rows(turn, carry):
        units, ahead = [], {}
        for first_row in range(0, ROWS_AT_ONCE, ROWS_IN_FLIGHT):
            in_flight = [turn * ROWS_AT_ONCE + first_row + extra for extra in range(ROWS_IN_FLIGHT)]
            places = [
                (level, r) for r in in_flight for level in range(0, n_levels, LEVELS_AT_ONCE)
            ]
            steps = itertools.chain(*[transport(r + ROWS_IN_FLIGHT) for r in in_flight])
            share = -(-(2 * n_levels - 1) * ROWS_IN_FLIGHT // (SUBSTEPS * len(places)))
            for substep in range(SUBSTEPS):
                for place in places:
                    ahead[len(units)] = (steps, share)
                    units.append((substep, place))
        rounded, rates = {}, {}
        for at in range(len(units) + LAG):
            if at < len(units):
                substep, (level, r) = units[at]
                if substep == 0:
                    rounded[at] = tile_at(level, r).astype(BF16)
                rates[at] = product_of(rounded.pop(at))
                steps, share = ahead[at]
                for _ in itertools.islice(steps, share):
                    pass
            if at >= LAG:
                done = at - LAG
                substep, (level, r) = units[done]
                change = jnp.dot(encode[...], rates.pop(done), preferred_element_type=F32)
                tile = tile_at(level, r)
                value = tile + jnp.where(lit_tile, change, 0.0)
                if substep < SUBSTEPS - 1:
                    later = done + ROWS_IN_FLIGHT * (n_levels // LEVELS_AT_ONCE)
                    rounded[later] = (tile.astype(BF16).astype(F32) + change).astype(BF16)
                for extra in range(LEVELS_AT_ONCE):
                    part = value[:, extra * n_cols : (extra + 1) * n_cols]
                    at_level = level + extra
                    if last or substep < SUBSTEPS - 1:
                        diffused[at_level, r] = part
                    else:
                        refs[0][at_level, r] = part
        return carry

    if last:

        def sends(half):
            within = pl.ds(pl.multiple_of(half * half_rows, half_rows), half_rows)
            return [
                pltpu.make_async_copy(
                    staged.at[half, level], refs[0].at[:, level, within], sems.at[half, level]
                )
                for level in range(n_levels)
            ]

        def half_done(half, carry):
            for turn in range(half_rows // ROWS_AT_ONCE):
                rows(half * (half_rows // ROWS_AT_ONCE) + turn, None)
            for level, copy in enumerate(sends(half)):
                within = pl.ds(half * half_rows, half_rows)
                staged[half, level] = jnp.transpose(diffused[level, within], (1, 0, 2))
                copy.start()
            return carry

        lax.fori_loop(0, 2, half_done, 0)
        for half in range(2):
            for copy in sends(half):
                copy.wait()
        return
    out, lat_a, lat_b = refs[:3]
    lax.fori_loop(0, n_rows // ROWS_AT_ONCE, rows, 0)
    for level in range(n_levels):
        south = (out[level, 0] * coefs[SOUTH, level, :1]).astype(BF16)
        north = (out[level, n_rows - 1] * coefs[NORTH, level, n_rows - 1 :]).astype(BF16)
        by_parity("lat", north, south, lat_a.at[level], lat_b.at[level])
    for at, near in enumerate((west_near, east_near)):
        south = jnp.where(is_first, 0.0, lat_inflow(near, n_species, jnp.minimum)).astype(BF16)
        north = jnp.where(is_last, 0.0, lat_inflow(near, n_species, jnp.maximum)).astype(BF16)
        by_parity("lat", north, south, lat_a.at[n_levels + at], lat_b.at[n_levels + at])


def vmem(count):
    return [pl.BlockSpec(memory_space=pltpu.VMEM)] * count


def swapped(array, axis, first, closed=False):
    size = lax.axis_size(axis)
    pairs = [(i % size, (i + 1) % size) for i in range(first, size + first - closed, 2)]
    return lax.ppermute(array, axis, pairs + [(j, i) for i, j in pairs])


def on_device(
    latent_field,
    east_courant,
    north_courant,
    mixing,
    sunlit,
    decode_w,
    react_a,
    react_b,
    stoich,
    encode_w,
    rate_const,
):
    n_species, n_levels, n_rows, n_cols = latent_field.shape
    layered = jax.ShapeDtypeStruct((n_levels, n_rows, n_species, n_cols), F32)
    column = jax.ShapeDtypeStruct((2 * COLUMN_ROWS, n_cols), F32)
    edge = jax.ShapeDtypeStruct((n_levels, n_species, n_cols), BF16)
    cornered = jax.ShapeDtypeStruct((n_levels + 2, n_species, n_cols), BF16)
    params = pltpu.CompilerParams(vmem_limit_bytes=VMEM_BYTES)
    smem = pl.BlockSpec(memory_space=pltpu.SMEM)
    hbm = pl.BlockSpec(memory_space=pltpu.HBM)
    n_reactions = react_a.shape[0]
    lon_a, lon_b, lat_a, lat_b = pl.pallas_call(
        first_kernel,
        out_shape=(column, column, edge, edge),
        in_specs=[smem] + [hbm] * 4,
        out_specs=tuple(vmem(4)),
        scratch_shapes=[
            pltpu.VMEM((n_levels, n_species, n_rows, n_cols), F32),
            pltpu.VMEM(east_courant.shape, F32),
            pltpu.VMEM(north_courant.shape, F32),
            pltpu.VMEM(mixing.shape, F32),
            pltpu.SemaphoreType.DMA((n_levels + 3,)),
        ],
        compiler_params=pltpu.CompilerParams(vmem_limit_bytes=FIRST_VMEM_BYTES),
        name="first_sends",
        cost_estimate=pl.CostEstimate(flops=4_000_000_000, bytes_accessed=2_000_000, transcendentals=0),
    )(sunlit, latent_field, east_courant, north_courant, mixing)
    weights = (decode_w.T, react_a.T, react_b.T, stoich, encode_w, rate_const[None])
    folded = (
        jax.ShapeDtypeStruct((2 * n_reactions, n_species), BF16),
        jax.ShapeDtypeStruct((n_species, n_reactions), BF16),
    )
    lon_halos = swapped(lon_a, "lon", 0), swapped(lon_b, "lon", 1)
    field = latent_field
    for step in range(STEPS):
        first, last = step == 0, step == STEPS - 1
        lat_halos = swapped(lat_a, "lat", 0), swapped(lat_b, "lat", 1, closed=True)
        scratch = [pltpu.VMEM(layered.shape, F32)] if first else []
        if last:
            scratch += [
                pltpu.VMEM((2, n_levels, n_species, n_rows // 2, n_cols), F32),
                pltpu.SemaphoreType.DMA((2, n_levels)),
            ]
        scratch += [pltpu.VMEM(array.shape, array.dtype) for array in lat_halos]
        scratch += [
            pltpu.VMEM((2 * n_levels * n_rows // n_cols, n_species, n_cols), F32),
            pltpu.VMEM((8, n_levels, n_rows, n_cols), F32),
            pltpu.VMEM((n_levels, n_rows + ROWS_IN_FLIGHT, n_species, n_cols), F32),
        ]
        operands = weights if first else (lon_a, lon_b, *weights)
        outs = pl.pallas_call(
            functools.partial(step_kernel, n_levels, n_rows, first, last),
            out_shape=(jax.ShapeDtypeStruct(latent_field.shape, F32),)
            if last
            else (layered, cornered, cornered, *folded),
            in_specs=[smem] + vmem(8 + len(operands)),
            out_specs=(hbm,) if last else tuple(vmem(5)),
            scratch_shapes=scratch,
            compiler_params=params,
            name="splitting_step",
            cost_estimate=pl.CostEstimate(flops=20_000_000_000, bytes_accessed=1, transcendentals=0),
        )(sunlit, field, east_courant, north_courant, mixing, *lon_halos, *lat_halos, *operands)
        if not last:
            field, lat_a, lat_b, *weights = outs
    return outs[0]


def solution(mesh):
    placed = (
        P(None, None, "lat", "lon"),
        P(None, "lat", "lon"),
        P(None, "lat", "lon"),
        P(None, "lat", "lon"),
        P("lat", "lon"),
        P(),
        P(),
        P(),
        P(),
        P(),
        P(),
    )
    return jax.shard_map(
        on_device,
        mesh=mesh,
        in_specs=placed,
        out_specs=P(None, None, "lat", "lon"),
        check_vma=False,
    )
```

```python
import functools
import itertools

import jax
import jax.numpy as jnp
from jax import lax
from jax.experimental import pallas as pl
from jax.experimental.pallas import tpu as pltpu
from jax.sharding import PartitionSpec as P

BLOCK = 16
SUBSTEPS = 2
STEPS = 2
GROUP = 16
ROWS_AT_ONCE = 8
ROWS_IN_FLIGHT = 2
LEVELS_AT_ONCE = 4
LAG = 1

F32 = jnp.float32
BF16 = jnp.bfloat16
VMEM_BYTES = 48 * 1024 * 1024
FIRST_VMEM_BYTES = 56 * 1024 * 1024


def lane_ids(shape):
    return lax.broadcasted_iota(jnp.int32, shape, len(shape) - 1)


def fold_weights(decode_t, react_a_t, react_b_t, stoich, encode, rate, linear_out, encode_out):
    n_reactions = react_a_t.shape[1]
    contract = (((0,), (1,)), ((), ()))
    for part, react in enumerate((react_a_t, react_b_t)):
        product = lax.dot_general(
            react[...], decode_t[...], contract, preferred_element_type=F32
        )
        for group in range(n_reactions // GROUP):
            at = (2 * group + part) * GROUP
            linear_out[at : at + GROUP, :] = product[
                group * GROUP : (group + 1) * GROUP
            ].astype(BF16)
    folded = jnp.dot(encode[...], stoich[...], preferred_element_type=F32)
    encode_out[...] = (folded * rate[...]).astype(BF16)


def at_ends():
    index = lax.axis_index("lat")
    return index == 0, index == lax.axis_size("lat") - 1


def is_even(axis):
    return lax.axis_index(axis) % 2 == 0


def by_parity(axis, up, down, into_first, into_second):
    even = is_even(axis)
    into_first[...] = jnp.where(even, up, down)
    into_second[...] = jnp.where(even, down, up)


COLUMN_ROWS = 40
EAST_ROW, NORTH_ROW, MIXING_ROW, LIT_ROW = 32, 33, 34, 35


def first_kernel(sun, latent, east_c, north_c, mixing, lon_a, lon_b, lat_a, lat_b, *scratch):
    tiles, east_v, north_v, mixing_v, faces, turned_faces, sems = scratch
    n_levels, n_species, n_rows, n_cols = tiles.shape
    lanes = lane_ids((1, n_cols))
    is_first, is_last = at_ends()
    copies = [
        pltpu.make_async_copy(source, held, sems.at[n_levels + at])
        for at, (source, held) in enumerate(
            ((east_c, east_v), (north_c, north_v), (mixing, mixing_v))
        )
    ]
    levels = [
        pltpu.make_async_copy(latent.at[:, level], tiles.at[level], sems.at[level])
        for level in range(n_levels)
    ]
    for copy in copies + levels:
        copy.start()
    for copy in copies:
        copy.wait()
    def face_lanes(planes):
        packed = None
        for at, plane in enumerate(planes):
            turned = pltpu.roll(plane, (4 * at + 2) % n_cols, 1)
            packed = turned if packed is None else jnp.where(lanes // 4 == at, turned, packed)
        return packed

    for level in range(n_levels):
        levels[level].wait()
        within = slice(level * n_rows, (level + 1) * n_rows)
        faces[0, within] = face_lanes([tiles[level, at] for at in range(n_species)])
        planes = [east_v[level], north_v[level]]
        if level < n_levels - 1:
            planes.append(mixing_v[level])
        zero = jnp.zeros((n_rows, n_cols), F32)
        faces[1, within] = face_lanes(planes + [zero] * (COLUMN_ROWS - n_species - len(planes)))
        rows = tiles.at[level].reshape(n_species * n_rows, n_cols)
        ends = []
        for r, closed, clip in ((0, is_first, jnp.minimum), (n_rows - 1, is_last, jnp.maximum)):
            speed = clip(north_v[level, r : r + 1, :], 0.0)
            value = rows[pl.ds(r, n_species, stride=n_rows), :]
            ends.append((value * jnp.where(closed, 0.0, speed)).astype(BF16))
        by_parity("lat", ends[1], ends[0], lat_a.at[level], lat_b.at[level])
    turned_faces[0] = faces[0].T
    turned_faces[1] = faces[1].T
    columns = [
        jnp.concatenate(
            [
                turned_faces[0, pl.ds(slot, n_species, stride=4), :],
                turned_faces[1, pl.ds(slot, COLUMN_ROWS - n_species, stride=4), :],
            ],
            axis=0,
        )
        for slot in range(4)
    ]
    kinds = lax.broadcasted_iota(jnp.int32, (COLUMN_ROWS, n_cols), 0)
    lit_west = sun[0, 0].astype(F32)
    lit_east = sun[0, n_cols // BLOCK - 1].astype(F32)
    west = [jnp.where(kinds == LIT_ROW, lit_west, columns[at]) for at in (2, 3)]
    east = [jnp.where(kinds == LIT_ROW, lit_east, columns[at]) for at in (1, 0)]
    by_parity("lon", jnp.concatenate(east, axis=0), jnp.concatenate(west, axis=0), lon_a, lon_b)


def split_columns(message):
    return message[:COLUMN_ROWS], message[COLUMN_ROWS:]


def inflow(column, n_species, clip):
    return column[:n_species] * clip(column[EAST_ROW : EAST_ROW + 1], 0.0)


def lat_inflow(column, n_species, clip):
    return column[:n_species] * clip(column[NORTH_ROW : NORTH_ROW + 1], 0.0)


def moved_column(column, west, east, south, north, n_species, n_rows, ends):
    n_cols = column.shape[1]
    rows = lane_ids((1, n_cols)) % n_rows
    is_first, is_last = ends
    speed = column[EAST_ROW : EAST_ROW + 1]
    lat_speed = column[NORTH_ROW : NORTH_ROW + 1]
    up = jnp.where((rows == n_rows - 1) & is_last, 0.0, jnp.maximum(lat_speed, 0.0))
    down = jnp.where((rows == 0) & is_first, 0.0, jnp.minimum(lat_speed, 0.0))
    value = column[:n_species]
    from_south = jnp.where(rows == 0, south, pltpu.roll(value * up, 1, 1))
    from_north = jnp.where(rows == n_rows - 1, north, pltpu.roll(value * down, n_cols - 1, 1))
    centre = 1.0 - jnp.abs(speed) - up + down
    return value * centre + (west - east) + (from_south - from_north)


def by_level(west, east, n_levels, n_rows):
    n_cols = west.shape[1]
    of_west = lane_ids((1, n_cols)) < n_rows
    return [
        jnp.where(
            of_west,
            pltpu.roll(west, (n_cols - level * n_rows) % n_cols, 1),
            pltpu.roll(east, (n_cols - (level - 1) * n_rows) % n_cols, 1),
        )
        for level in range(n_levels)
    ]


def joined(levels, n_rows):
    n_cols = levels[0].shape[1]
    width = 2 * n_rows
    lanes = lane_ids((1, n_cols))
    arrays = []
    for at, array in enumerate(levels):
        turn = at * width % n_cols
        if turn == 0:
            arrays.append(array)
        else:
            arrays[-1] = jnp.where(lanes // width == turn // width, pltpu.roll(array, turn, 1), arrays[-1])
    return arrays


def diffused_columns(moved, mixing):
    upper, swept = None, []
    uppers = []
    for level, value in enumerate(moved):
        pivot = 1.0
        if level > 0:
            below = mixing[level - 1]
            pivot = pivot + below - below * upper
            value = value + below * swept[-1]
        if level < len(moved) - 1:
            pivot = pivot + mixing[level]
        scale = 1.0 / pivot
        if level < len(moved) - 1:
            upper = mixing[level] * scale
            uppers.append(upper)
        swept.append(value * scale)
    for level in range(len(moved) - 2, -1, -1):
        swept[level] = swept[level] + uppers[level] * swept[level + 1]
    return swept


def step_kernel(
    n_levels,
    n_rows,
    first,
    last,
    sun,
    field,
    east_c,
    north_c,
    mixing,
    lon_a_in,
    lon_b_in,
    lat_a_in,
    lat_b_in,
    *refs,
):
    if first:
        weights, refs = refs[:6], refs[6:]
        linear, encode = refs[3:5]
    else:
        (lon_a_own, lon_b_own, linear, encode), refs = refs[:4], refs[4:]
    half_rows = n_rows // 2
    south_in, north_in, lon_in, coefs, diffused = refs[-5:]
    if last:
        staged, sems = refs[-7:-5]
    by_parity("lat", lat_a_in[...], lat_b_in[...], north_in, south_in)
    _, n_species, n_cols = lon_in.shape
    n_reactions = encode.shape[1]
    cells = n_levels * n_rows
    lanes = lane_ids((1, n_cols))
    row_ids = lax.broadcasted_iota(jnp.int32, (n_rows, n_cols), 0)
    is_first, is_last = at_ends()
    if first:
        latent, field = field, refs[-6]
        fold_weights(*weights, linear, encode)
        for level in range(n_levels):
            field[level] = jnp.transpose(latent[:, level], (1, 0, 2))
    CENTRE, EAST, WEST, NORTH, SOUTH, SCALE, LOWER, UPPER = range(8)

    upper = None
    for level in range(n_levels):
        ce, cn = east_c[level], north_c[level]
        east, west = jnp.maximum(ce, 0.0), jnp.minimum(ce, 0.0)
        north = jnp.where((row_ids == n_rows - 1) & is_last, 0.0, jnp.maximum(cn, 0.0))
        south = jnp.where((row_ids == 0) & is_first, 0.0, jnp.minimum(cn, 0.0))
        coefs[CENTRE, level] = 1.0 - east + west - north + south
        coefs[EAST, level] = east
        coefs[WEST, level] = west
        coefs[NORTH, level] = north
        coefs[SOUTH, level] = south
        pivot = 1.0
        if level > 0:
            below = mixing[level - 1]
            pivot = pivot + below - below * upper
        if level < n_levels - 1:
            pivot = pivot + mixing[level]
        scale = 1.0 / pivot
        coefs[SCALE, level] = scale
        if level > 0:
            coefs[LOWER, level] = below * scale
        if level < n_levels - 1:
            upper = mixing[level] * scale
            coefs[UPPER, level] = upper

    even = is_even("lon")
    west_near, west_far = split_columns(jnp.where(even, lon_b_in[...], lon_a_in[...]))
    east_near, east_far = split_columns(jnp.where(even, lon_a_in[...], lon_b_in[...]))

    lit = jnp.zeros((1, n_cols), jnp.int32)
    for block in range(n_cols // BLOCK):
        lit = jnp.where(lanes // BLOCK == block, sun[0, block], lit)
    lit = lit > 0

    def coef(kind, level, r):
        return coefs[kind, level, pl.ds(r, 1), :]

    def transport(slot):
        r = jnp.minimum(slot, n_rows - 1)
        before, after = jnp.maximum(r - 1, 0), jnp.minimum(r + 1, n_rows - 1)
        right = None
        for level in range(n_levels):
            value = field[level, r]
            spot = level * 2 * n_rows % n_cols
            halo = lon_in[level * 2 * n_rows // n_cols]
            from_west = jnp.where(
                lanes == 0,
                pltpu.roll(halo, (n_cols - spot - r) % n_cols, 1),
                pltpu.roll(value * coef(EAST, level, r), 1, 1),
            )
            from_east = jnp.where(
                lanes == n_cols - 1,
                pltpu.roll(halo, n_cols - 1 - spot - n_rows - r, 1),
                pltpu.roll(value * coef(WEST, level, r), n_cols - 1, 1),
            )
            from_south = jnp.where(
                r == 0,
                south_in[level].astype(F32),
                field[level, before] * coef(NORTH, level, before),
            )
            from_north = jnp.where(
                r == n_rows - 1,
                north_in[level].astype(F32),
                field[level, after] * coef(SOUTH, level, after),
            )
            moved = value * coef(CENTRE, level, r) + (from_west - from_east) + (from_south - from_north)
            scaled = moved * coef(SCALE, level, r)
            right = scaled if level == 0 else scaled + coef(LOWER, level, r) * right
            diffused[level, slot] = right
            yield
        for level in range(n_levels - 2, -1, -1):
            right = diffused[level, slot] + coef(UPPER, level, r) * right
            diffused[level, slot] = right
            yield

    def product_of(rounded):
        both = jnp.dot(linear[...], rounded, preferred_element_type=F32)
        parts = [
            both[at : at + GROUP] * both[at + GROUP : at + 2 * GROUP]
            for at in range(0, 2 * n_reactions, 2 * GROUP)
        ]
        return jnp.concatenate(parts, axis=0).astype(BF16)

    def levels_of(west, east):
        return by_level(west, east, n_levels, n_rows)

    def kind_of(kind):
        return levels_of(west_near[kind : kind + 1], east_near[kind : kind + 1])

    if first:
        halos = joined(
            levels_of(
                inflow(west_near, n_species, jnp.maximum), inflow(east_near, n_species, jnp.minimum)
            ),
            n_rows,
        )
    else:
        own_west, _ = split_columns(jnp.where(even, lon_b_own[...], lon_a_own[...]))
        own_east, _ = split_columns(jnp.where(even, lon_a_own[...], lon_b_own[...]))

        def corner(edge, at, turn):
            return pltpu.roll(edge[n_levels + at].astype(F32), turn, 1)

        def column_after(at, near, west, east):
            return moved_column(
                near,
                inflow(west, n_species, jnp.maximum),
                inflow(east, n_species, jnp.minimum),
                corner(south_in, at, n_cols - (n_rows - 1)),
                corner(north_in, at, n_rows - 1),
                n_species,
                n_rows,
                (is_first, is_last),
            )

        moved = levels_of(
            column_after(0, west_near, west_far, own_west),
            column_after(1, east_near, own_east, east_far),
        )
        pair = joined(diffused_columns(moved, kind_of(MIXING_ROW)), n_rows)
        pair = jnp.concatenate(pair, axis=1)
        rounded = pair.astype(BF16)
        current, summed = rounded.astype(F32), None
        for substep in range(SUBSTEPS):
            change = jnp.dot(encode[...], product_of(rounded), preferred_element_type=F32)
            summed = change if summed is None else summed + change
            current = current + change
            rounded = current.astype(BF16)
        pair_lit = jnp.concatenate(joined(kind_of(LIT_ROW), n_rows), axis=1)
        pair = pair + jnp.where(pair_lit > 0.0, summed, 0.0)
        halos = []
        for at, speed in enumerate(joined(kind_of(EAST_ROW), n_rows)):
            clipped = jnp.where(
                lanes // n_rows % 2 == 0, jnp.maximum(speed, 0.0), jnp.minimum(speed, 0.0)
            )
            halos.append(pair[:, at * n_cols : (at + 1) * n_cols] * clipped)
    for at, halo in enumerate(halos):
        lon_in[at] = halo

    for r in range(ROWS_IN_FLIGHT):
        for _ in transport(r):
            pass
    lit_tile = jnp.concatenate([lit] * LEVELS_AT_ONCE, axis=1)

    def tile_at(level, r):
        return jnp.concatenate(
            [diffused[level + extra, r] for extra in range(LEVELS_AT_ONCE)], axis=1
        )

    def rows(turn, carry):
        units, ahead = [], {}
        for first_row in range(0, ROWS_AT_ONCE, ROWS_IN_FLIGHT):
            in_flight = [turn * ROWS_AT_ONCE + first_row + extra for extra in range(ROWS_IN_FLIGHT)]
            places = [
                (level, r) for r in in_flight for level in range(0, n_levels, LEVELS_AT_ONCE)
            ]
            steps = itertools.chain(*[transport(r + ROWS_IN_FLIGHT) for r in in_flight])
            share = -(-(2 * n_levels - 1) * ROWS_IN_FLIGHT // (SUBSTEPS * len(places)))
            for substep in range(SUBSTEPS):
                for place in places:
                    ahead[len(units)] = (steps, share)
                    units.append((substep, place))
        rounded, rates = {}, {}
        for at in range(len(units) + LAG):
            if at < len(units):
                substep, (level, r) = units[at]
                if substep == 0:
                    rounded[at] = tile_at(level, r).astype(BF16)
                rates[at] = product_of(rounded.pop(at))
                steps, share = ahead[at]
                for _ in itertools.islice(steps, share):
                    pass
            if at >= LAG:
                done = at - LAG
                substep, (level, r) = units[done]
                change = jnp.dot(encode[...], rates.pop(done), preferred_element_type=F32)
                tile = tile_at(level, r)
                value = tile + jnp.where(lit_tile, change, 0.0)
                if substep < SUBSTEPS - 1:
                    later = done + ROWS_IN_FLIGHT * (n_levels // LEVELS_AT_ONCE)
                    rounded[later] = (tile.astype(BF16).astype(F32) + change).astype(BF16)
                for extra in range(LEVELS_AT_ONCE):
                    part = value[:, extra * n_cols : (extra + 1) * n_cols]
                    at_level = level + extra
                    if last or substep < SUBSTEPS - 1:
                        diffused[at_level, r] = part
                    else:
                        refs[0][at_level, r] = part
        return carry

    if last:

        def sends(half):
            within = pl.ds(pl.multiple_of(half * half_rows, half_rows), half_rows)
            return [
                pltpu.make_async_copy(
                    staged.at[half, level], refs[0].at[:, level, within], sems.at[half, level]
                )
                for level in range(n_levels)
            ]

        def half_done(half, carry):
            for turn in range(half_rows // ROWS_AT_ONCE):
                rows(half * (half_rows // ROWS_AT_ONCE) + turn, None)
            for level, copy in enumerate(sends(half)):
                within = pl.ds(half * half_rows, half_rows)
                staged[half, level] = jnp.transpose(diffused[level, within], (1, 0, 2))
                copy.start()
            return carry

        lax.fori_loop(0, 2, half_done, 0)
        for half in range(2):
            for copy in sends(half):
                copy.wait()
        return
    out, lat_a, lat_b = refs[:3]
    lax.fori_loop(0, n_rows // ROWS_AT_ONCE, rows, 0)
    for level in range(n_levels):
        south = (out[level, 0] * coefs[SOUTH, level, :1]).astype(BF16)
        north = (out[level, n_rows - 1] * coefs[NORTH, level, n_rows - 1 :]).astype(BF16)
        by_parity("lat", north, south, lat_a.at[level], lat_b.at[level])
    for at, near in enumerate((west_near, east_near)):
        south = jnp.where(is_first, 0.0, lat_inflow(near, n_species, jnp.minimum)).astype(BF16)
        north = jnp.where(is_last, 0.0, lat_inflow(near, n_species, jnp.maximum)).astype(BF16)
        by_parity("lat", north, south, lat_a.at[n_levels + at], lat_b.at[n_levels + at])


def vmem(count):
    return [pl.BlockSpec(memory_space=pltpu.VMEM)] * count


def swapped(array, axis, first, closed=False):
    size = lax.axis_size(axis)
    pairs = [(i % size, (i + 1) % size) for i in range(first, size + first - 2 * closed, 2)]
    return lax.ppermute(array, axis, pairs + [(j, i) for i, j in pairs])


def on_device(
    latent_field,
    east_courant,
    north_courant,
    mixing,
    sunlit,
    decode_w,
    react_a,
    react_b,
    stoich,
    encode_w,
    rate_const,
):
    n_species, n_levels, n_rows, n_cols = latent_field.shape
    layered = jax.ShapeDtypeStruct((n_levels, n_rows, n_species, n_cols), F32)
    column = jax.ShapeDtypeStruct((2 * COLUMN_ROWS, n_cols), F32)
    edge = jax.ShapeDtypeStruct((n_levels, n_species, n_cols), BF16)
    cornered = jax.ShapeDtypeStruct((n_levels + 2, n_species, n_cols), BF16)
    params = pltpu.CompilerParams(vmem_limit_bytes=VMEM_BYTES)
    smem = pl.BlockSpec(memory_space=pltpu.SMEM)
    hbm = pl.BlockSpec(memory_space=pltpu.HBM)
    n_reactions = react_a.shape[0]
    lon_a, lon_b, lat_a, lat_b = pl.pallas_call(
        first_kernel,
        out_shape=(column, column, edge, edge),
        in_specs=[smem] + [hbm] * 4,
        out_specs=tuple(vmem(4)),
        scratch_shapes=[
            pltpu.VMEM((n_levels, n_species, n_rows, n_cols), F32),
            pltpu.VMEM(east_courant.shape, F32),
            pltpu.VMEM(north_courant.shape, F32),
            pltpu.VMEM(mixing.shape, F32),
            pltpu.VMEM((2, n_levels * n_rows, n_cols), F32),
            pltpu.VMEM((2, n_cols, n_levels * n_rows), F32),
            pltpu.SemaphoreType.DMA((n_levels + 3,)),
        ],
        compiler_params=pltpu.CompilerParams(vmem_limit_bytes=FIRST_VMEM_BYTES),
        name="first_sends",
        cost_estimate=pl.CostEstimate(flops=4_000_000_000, bytes_accessed=2_000_000, transcendentals=0),
    )(sunlit, latent_field, east_courant, north_courant, mixing)
    weights = (decode_w.T, react_a.T, react_b.T, stoich, encode_w, rate_const[None])
    folded = (
        jax.ShapeDtypeStruct((2 * n_reactions, n_species), BF16),
        jax.ShapeDtypeStruct((n_species, n_reactions), BF16),
    )
    lon_halos = swapped(lon_a, "lon", 0), swapped(lon_b, "lon", 1)
    field = latent_field
    for step in range(STEPS):
        first, last = step == 0, step == STEPS - 1
        lat_halos = swapped(lat_a, "lat", 0), swapped(lat_b, "lat", 1, closed=True)
        scratch = [pltpu.VMEM(layered.shape, F32)] if first else []
        if last:
            scratch += [
                pltpu.VMEM((2, n_levels, n_species, n_rows // 2, n_cols), F32),
                pltpu.SemaphoreType.DMA((2, n_levels)),
            ]
        scratch += [pltpu.VMEM(array.shape, array.dtype) for array in lat_halos]
        scratch += [
            pltpu.VMEM((2 * n_levels * n_rows // n_cols, n_species, n_cols), F32),
            pltpu.VMEM((8, n_levels, n_rows, n_cols), F32),
            pltpu.VMEM((n_levels, n_rows + ROWS_IN_FLIGHT, n_species, n_cols), F32),
        ]
        operands = weights if first else (lon_a, lon_b, *weights)
        outs = pl.pallas_call(
            functools.partial(step_kernel, n_levels, n_rows, first, last),
            out_shape=(jax.ShapeDtypeStruct(latent_field.shape, F32),)
            if last
            else (layered, cornered, cornered, *folded),
            in_specs=[smem] + vmem(8 + len(operands)),
            out_specs=(hbm,) if last else tuple(vmem(5)),
            scratch_shapes=scratch,
            compiler_params=params,
            name="splitting_step",
            cost_estimate=pl.CostEstimate(flops=20_000_000_000, bytes_accessed=1, transcendentals=0),
        )(sunlit, field, east_courant, north_courant, mixing, *lon_halos, *lat_halos, *operands)
        if not last:
            field, lat_a, lat_b, *weights = outs
    return outs[0]


def solution(mesh):
    placed = (
        P(None, None, "lat", "lon"),
        P(None, "lat", "lon"),
        P(None, "lat", "lon"),
        P(None, "lat", "lon"),
        P("lat", "lon"),
        P(),
        P(),
        P(),
        P(),
        P(),
        P(),
    )
    return jax.shard_map(
        on_device,
        mesh=mesh,
        in_specs=placed,
        out_specs=P(None, None, "lat", "lon"),
        check_vma=False,
    )
```

```python
import functools
import itertools

import jax
import jax.numpy as jnp
from jax import lax
from jax.experimental import pallas as pl
from jax.experimental.pallas import tpu as pltpu
from jax.sharding import PartitionSpec as P

BLOCK = 16
SUBSTEPS = 2
STEPS = 2
GROUP = 16
ROWS_IN_FLIGHT = 2
LEVELS_AT_ONCE = 4
LAG = 1

F32 = jnp.float32
BF16 = jnp.bfloat16
VMEM_BYTES = 48 * 1024 * 1024
FIRST_VMEM_BYTES = 56 * 1024 * 1024


def lane_ids(shape):
    return lax.broadcasted_iota(jnp.int32, shape, len(shape) - 1)


def fold_weights(decode_t, react_a_t, react_b_t, stoich, encode, rate, linear_out, encode_out):
    n_reactions = react_a_t.shape[1]
    contract = (((0,), (1,)), ((), ()))
    for part, react in enumerate((react_a_t, react_b_t)):
        product = lax.dot_general(
            react[...], decode_t[...], contract, preferred_element_type=F32
        )
        for group in range(n_reactions // GROUP):
            at = (2 * group + part) * GROUP
            linear_out[at : at + GROUP, :] = product[
                group * GROUP : (group + 1) * GROUP
            ].astype(BF16)
    folded = jnp.dot(encode[...], stoich[...], preferred_element_type=F32)
    encode_out[...] = (folded * rate[...]).astype(BF16)


def at_ends():
    index = lax.axis_index("lat")
    return index == 0, index == lax.axis_size("lat") - 1


def is_even(axis):
    return lax.axis_index(axis) % 2 == 0


def by_parity(axis, up, down, into_first, into_second):
    even = is_even(axis)
    into_first[...] = jnp.where(even, up, down)
    into_second[...] = jnp.where(even, down, up)


COLUMN_ROWS = 40
EAST_ROW, NORTH_ROW, MIXING_ROW, LIT_ROW = 32, 33, 34, 35


def first_kernel(sun, latent, east_c, north_c, mixing, lon_a, lon_b, lat_a, lat_b, *scratch):
    tiles, sun_v, east_v, north_v, mixing_v, faces, turned_faces, sems = scratch
    n_levels, n_species, n_rows, n_cols = tiles.shape
    lanes = lane_ids((1, n_cols))
    is_first, is_last = at_ends()
    copies = [
        pltpu.make_async_copy(source, held, sems.at[n_levels + at])
        for at, (source, held) in enumerate(
            ((sun, sun_v), (east_c, east_v), (north_c, north_v), (mixing, mixing_v))
        )
    ]
    levels = [
        pltpu.make_async_copy(latent.at[:, level], tiles.at[level], sems.at[level])
        for level in range(n_levels)
    ]
    for copy in copies + levels:
        copy.start()
    for copy in copies:
        copy.wait()
    def face_lanes(planes):
        packed = None
        for at, plane in enumerate(planes):
            turned = pltpu.roll(plane, (4 * at + 2) % n_cols, 1)
            packed = turned if packed is None else jnp.where(lanes // 4 == at, turned, packed)
        return packed

    for level in range(n_levels):
        levels[level].wait()
        within = slice(level * n_rows, (level + 1) * n_rows)
        faces[0, within] = face_lanes([tiles[level, at] for at in range(n_species)])
        planes = [east_v[level], north_v[level]]
        if level < n_levels - 1:
            planes.append(mixing_v[level])
        zero = jnp.zeros((n_rows, n_cols), F32)
        faces[1, within] = face_lanes(planes + [zero] * (COLUMN_ROWS - n_species - len(planes)))
        rows = tiles.at[level].reshape(n_species * n_rows, n_cols)
        ends = []
        for r, closed, clip in ((0, is_first, jnp.minimum), (n_rows - 1, is_last, jnp.maximum)):
            speed = clip(north_v[level, r : r + 1, :], 0.0)
            value = rows[pl.ds(r, n_species, stride=n_rows), :]
            ends.append((value * jnp.where(closed, 0.0, speed)).astype(BF16))
        by_parity("lat", ends[1], ends[0], lat_a.at[level], lat_b.at[level])
    turned_faces[0] = faces[0].T
    turned_faces[1] = faces[1].T
    columns = [
        jnp.concatenate(
            [
                turned_faces[0, pl.ds(slot, n_species, stride=4), :],
                turned_faces[1, pl.ds(slot, COLUMN_ROWS - n_species, stride=4), :],
            ],
            axis=0,
        )
        for slot in range(4)
    ]
    kinds = lax.broadcasted_iota(jnp.int32, (COLUMN_ROWS, n_cols), 0)
    lit_west = sun_v[:, :1].astype(F32)
    lit_east = sun_v[:, n_cols // BLOCK - 1 :].astype(F32)
    west = [jnp.where(kinds == LIT_ROW, lit_west, columns[at]) for at in (2, 3)]
    east = [jnp.where(kinds == LIT_ROW, lit_east, columns[at]) for at in (1, 0)]
    by_parity("lon", jnp.concatenate(east, axis=0), jnp.concatenate(west, axis=0), lon_a, lon_b)


def split_columns(message):
    return message[:COLUMN_ROWS], message[COLUMN_ROWS:]


def inflow(column, n_species, clip):
    return column[:n_species] * clip(column[EAST_ROW : EAST_ROW + 1], 0.0)


def lat_inflow(column, n_species, clip):
    return column[:n_species] * clip(column[NORTH_ROW : NORTH_ROW + 1], 0.0)


def moved_column(column, west, east, south, north, n_species, n_rows, ends):
    n_cols = column.shape[1]
    rows = lane_ids((1, n_cols)) % n_rows
    is_first, is_last = ends
    speed = column[EAST_ROW : EAST_ROW + 1]
    lat_speed = column[NORTH_ROW : NORTH_ROW + 1]
    up = jnp.where((rows == n_rows - 1) & is_last, 0.0, jnp.maximum(lat_speed, 0.0))
    down = jnp.where((rows == 0) & is_first, 0.0, jnp.minimum(lat_speed, 0.0))
    value = column[:n_species]
    from_south = jnp.where(rows == 0, south, pltpu.roll(value * up, 1, 1))
    from_north = jnp.where(rows == n_rows - 1, north, pltpu.roll(value * down, n_cols - 1, 1))
    centre = 1.0 - jnp.abs(speed) - up + down
    return value * centre + (west - east) + (from_south - from_north)


def by_level(west, east, n_levels, n_rows):
    n_cols = west.shape[1]
    of_west = lane_ids((1, n_cols)) < n_rows
    return [
        jnp.where(
            of_west,
            pltpu.roll(west, (n_cols - level * n_rows) % n_cols, 1),
            pltpu.roll(east, (n_cols - (level - 1) * n_rows) % n_cols, 1),
        )
        for level in range(n_levels)
    ]


def joined(levels, n_rows):
    n_cols = levels[0].shape[1]
    width = 2 * n_rows
    lanes = lane_ids((1, n_cols))
    arrays = []
    for at, array in enumerate(levels):
        turn = at * width % n_cols
        if turn == 0:
            arrays.append(array)
        else:
            arrays[-1] = jnp.where(lanes // width == turn // width, pltpu.roll(array, turn, 1), arrays[-1])
    return arrays


def diffused_columns(moved, mixing):
    upper, swept = None, []
    uppers = []
    for level, value in enumerate(moved):
        pivot = 1.0
        if level > 0:
            below = mixing[level - 1]
            pivot = pivot + below - below * upper
            value = value + below * swept[-1]
        if level < len(moved) - 1:
            pivot = pivot + mixing[level]
        scale = 1.0 / pivot
        if level < len(moved) - 1:
            upper = mixing[level] * scale
            uppers.append(upper)
        swept.append(value * scale)
    for level in range(len(moved) - 2, -1, -1):
        swept[level] = swept[level] + uppers[level] * swept[level + 1]
    return swept


def step_kernel(
    n_levels,
    n_rows,
    first,
    last,
    sun,
    field,
    east_c,
    north_c,
    mixing,
    lon_a_in,
    lon_b_in,
    lat_a_in,
    lat_b_in,
    *refs,
):
    if first:
        weights, refs = refs[:6], refs[6:]
        linear, encode = refs[3:5]
    else:
        (lon_a_own, lon_b_own, linear, encode), refs = refs[:4], refs[4:]
    half_rows = n_rows // 2
    south_in, north_in, lon_in, coefs, diffused = refs[-5:]
    if last:
        staged, sems = refs[-7:-5]
    by_parity("lat", lat_a_in[...], lat_b_in[...], north_in, south_in)
    _, n_species, n_cols = lon_in.shape
    n_reactions = encode.shape[1]
    cells = n_levels * n_rows
    lanes = lane_ids((1, n_cols))
    row_ids = lax.broadcasted_iota(jnp.int32, (n_rows, n_cols), 0)
    is_first, is_last = at_ends()
    if first:
        latent, field = field, refs[-6]
        fold_weights(*weights, linear, encode)

        def gather(half):
            within = slice(half * half_rows, (half + 1) * half_rows)
            for level in range(n_levels):
                field[level, within] = jnp.transpose(latent[:, level, within], (1, 0, 2))
                yield

        for _ in gather(0):
            pass
    CENTRE, EAST, WEST, NORTH, SOUTH, SCALE, LOWER, UPPER = range(8)

    upper = None
    for level in range(n_levels):
        ce, cn = east_c[level], north_c[level]
        east, west = jnp.maximum(ce, 0.0), jnp.minimum(ce, 0.0)
        north = jnp.where((row_ids == n_rows - 1) & is_last, 0.0, jnp.maximum(cn, 0.0))
        south = jnp.where((row_ids == 0) & is_first, 0.0, jnp.minimum(cn, 0.0))
        coefs[CENTRE, level] = 1.0 - east + west - north + south
        coefs[EAST, level] = east
        coefs[WEST, level] = west
        coefs[NORTH, level] = north
        coefs[SOUTH, level] = south
        pivot = 1.0
        if level > 0:
            below = mixing[level - 1]
            pivot = pivot + below - below * upper
        if level < n_levels - 1:
            pivot = pivot + mixing[level]
        scale = 1.0 / pivot
        coefs[SCALE, level] = scale
        if level > 0:
            coefs[LOWER, level] = below * scale
        if level < n_levels - 1:
            upper = mixing[level] * scale
            coefs[UPPER, level] = upper

    even = is_even("lon")
    west_near, west_far = split_columns(jnp.where(even, lon_b_in[...], lon_a_in[...]))
    east_near, east_far = split_columns(jnp.where(even, lon_a_in[...], lon_b_in[...]))

    lit = jnp.zeros((1, n_cols), jnp.int32)
    for block in range(n_cols // BLOCK):
        lit = jnp.where(lanes // BLOCK == block, sun[:, block : block + 1], lit)
    lit = lit > 0

    def coef(kind, level, r):
        return coefs[kind, level, r : r + 1, :]

    def transport(r):
        before, after = max(r - 1, 0), min(r + 1, n_rows - 1)
        right = None
        for level in range(n_levels):
            value = field[level, r]
            spot = level * 2 * n_rows % n_cols
            halo = lon_in[level * 2 * n_rows // n_cols]
            from_west = jnp.where(
                lanes == 0,
                pltpu.roll(halo, (n_cols - spot - r) % n_cols, 1),
                pltpu.roll(value * coef(EAST, level, r), 1, 1),
            )
            from_east = jnp.where(
                lanes == n_cols - 1,
                pltpu.roll(halo, n_cols - 1 - spot - n_rows - r, 1),
                pltpu.roll(value * coef(WEST, level, r), n_cols - 1, 1),
            )
            if r == 0:
                from_south = south_in[level].astype(F32)
            else:
                from_south = field[level, before] * coef(NORTH, level, before)
            if r == n_rows - 1:
                from_north = north_in[level].astype(F32)
            else:
                from_north = field[level, after] * coef(SOUTH, level, after)
            moved = value * coef(CENTRE, level, r) + (from_west - from_east) + (from_south - from_north)
            scaled = moved * coef(SCALE, level, r)
            right = scaled if level == 0 else scaled + coef(LOWER, level, r) * right
            diffused[level, r] = right
            yield
        for level in range(n_levels - 2, -1, -1):
            right = diffused[level, r] + coef(UPPER, level, r) * right
            diffused[level, r] = right
            yield

    def product_of(rounded):
        both = jnp.dot(linear[...], rounded, preferred_element_type=F32)
        parts = [
            both[at : at + GROUP] * both[at + GROUP : at + 2 * GROUP]
            for at in range(0, 2 * n_reactions, 2 * GROUP)
        ]
        return jnp.concatenate(parts, axis=0).astype(BF16)

    def levels_of(west, east):
        return by_level(west, east, n_levels, n_rows)

    def kind_of(kind):
        return levels_of(west_near[kind : kind + 1], east_near[kind : kind + 1])

    if first:
        halos = joined(
            levels_of(
                inflow(west_near, n_species, jnp.maximum), inflow(east_near, n_species, jnp.minimum)
            ),
            n_rows,
        )
    else:
        own_west, _ = split_columns(jnp.where(even, lon_b_own[...], lon_a_own[...]))
        own_east, _ = split_columns(jnp.where(even, lon_a_own[...], lon_b_own[...]))

        def corner(edge, at, turn):
            return pltpu.roll(edge[n_levels + at].astype(F32), turn, 1)

        def column_after(at, near, west, east):
            return moved_column(
                near,
                inflow(west, n_species, jnp.maximum),
                inflow(east, n_species, jnp.minimum),
                corner(south_in, at, n_cols - (n_rows - 1)),
                corner(north_in, at, n_rows - 1),
                n_species,
                n_rows,
                (is_first, is_last),
            )

        moved = levels_of(
            column_after(0, west_near, west_far, own_west),
            column_after(1, east_near, own_east, east_far),
        )
        pair = joined(diffused_columns(moved, kind_of(MIXING_ROW)), n_rows)
        pair = jnp.concatenate(pair, axis=1)
        rounded = pair.astype(BF16)
        current, summed = rounded.astype(F32), None
        for substep in range(SUBSTEPS):
            change = jnp.dot(encode[...], product_of(rounded), preferred_element_type=F32)
            summed = change if summed is None else summed + change
            current = current + change
            rounded = current.astype(BF16)
        pair_lit = jnp.concatenate(joined(kind_of(LIT_ROW), n_rows), axis=1)
        pair = pair + jnp.where(pair_lit > 0.0, summed, 0.0)
        halos = []
        for at, speed in enumerate(joined(kind_of(EAST_ROW), n_rows)):
            clipped = jnp.where(
                lanes // n_rows % 2 == 0, jnp.maximum(speed, 0.0), jnp.minimum(speed, 0.0)
            )
            halos.append(pair[:, at * n_cols : (at + 1) * n_cols] * clipped)
    for at, halo in enumerate(halos):
        lon_in[at] = halo

    for r in range(ROWS_IN_FLIGHT):
        for _ in transport(r):
            pass
    lit_tile = jnp.concatenate([lit] * LEVELS_AT_ONCE, axis=1)

    def tile_at(level, r):
        return jnp.concatenate(
            [diffused[level + extra, r] for extra in range(LEVELS_AT_ONCE)], axis=1
        )

    def send(half):
        within = slice(half * half_rows, (half + 1) * half_rows)
        for level in range(n_levels):
            staged[half, level] = jnp.transpose(diffused[level, within], (1, 0, 2))
            copy = pltpu.make_async_copy(
                staged.at[half, level], refs[0].at[:, level, within], sems.at[half, level]
            )
            copy.start()
            copies.append(copy)
            yield

    units, beside, copies = [], [], []
    for first_row in range(0, n_rows, ROWS_IN_FLIGHT):
        in_flight = range(first_row, first_row + ROWS_IN_FLIGHT)
        places = [(level, r) for r in in_flight for level in range(0, n_levels, LEVELS_AT_ONCE)]
        steps = itertools.chain(
            *[transport(r + ROWS_IN_FLIGHT) for r in in_flight if r + ROWS_IN_FLIGHT < n_rows]
        )
        share = -(-(2 * n_levels - 1) * ROWS_IN_FLIGHT // (SUBSTEPS * len(places)))
        for substep in range(SUBSTEPS):
            for place in places:
                beside.append((steps, share))
                units.append((substep, place))
    period = len(units) * ROWS_IN_FLIGHT // n_rows
    passage, passage_from = iter(()), 0
    if first:
        passage = gather(1)
    elif last:
        passage, passage_from = send(0), len(units) // 2 + LAG + 1
    rounded, rates = {}, {}
    for at in range(len(units) + LAG):
        if at < len(units):
            substep, (level, r) = units[at]
            if substep == 0:
                rounded[at] = tile_at(level, r).astype(BF16)
            rates[at] = product_of(rounded.pop(at))
            if at >= passage_from:
                next(passage, None)
            for _ in itertools.islice(*beside[at]):
                pass
        if at >= LAG:
            done = at - LAG
            substep, (level, r) = units[done]
            change = jnp.dot(encode[...], rates.pop(done), preferred_element_type=F32)
            tile = tile_at(level, r)
            value = tile + jnp.where(lit_tile, change, 0.0)
            if substep < SUBSTEPS - 1:
                later = done + period // SUBSTEPS
                rounded[later] = (tile.astype(BF16).astype(F32) + change).astype(BF16)
            for extra in range(LEVELS_AT_ONCE):
                part = value[:, extra * n_cols : (extra + 1) * n_cols]
                if last or substep < SUBSTEPS - 1:
                    diffused[level + extra, r] = part
                else:
                    refs[0][level + extra, r] = part
    if last:
        for _ in send(1):
            pass
        for copy in copies:
            copy.wait()
        return
    out, lat_a, lat_b = refs[:3]
    for level in range(n_levels):
        south = (out[level, 0] * coefs[SOUTH, level, :1]).astype(BF16)
        north = (out[level, n_rows - 1] * coefs[NORTH, level, n_rows - 1 :]).astype(BF16)
        by_parity("lat", north, south, lat_a.at[level], lat_b.at[level])
    for at, near in enumerate((west_near, east_near)):
        south = jnp.where(is_first, 0.0, lat_inflow(near, n_species, jnp.minimum)).astype(BF16)
        north = jnp.where(is_last, 0.0, lat_inflow(near, n_species, jnp.maximum)).astype(BF16)
        by_parity("lat", north, south, lat_a.at[n_levels + at], lat_b.at[n_levels + at])


def vmem(count):
    return [pl.BlockSpec(memory_space=pltpu.VMEM)] * count


def swapped(array, axis, first, closed=False):
    size = lax.axis_size(axis)
    pairs = [(i % size, (i + 1) % size) for i in range(first, size + first - 2 * closed, 2)]
    pairs += [(j, i) for i, j in pairs]
    if closed:
        pairs += [(0, 0), (size - 1, size - 1)]
    return lax.ppermute(array, axis, pairs)


def on_device(
    latent_field,
    east_courant,
    north_courant,
    mixing,
    sunlit,
    decode_w,
    react_a,
    react_b,
    stoich,
    encode_w,
    rate_const,
):
    n_species, n_levels, n_rows, n_cols = latent_field.shape
    layered = jax.ShapeDtypeStruct((n_levels, n_rows, n_species, n_cols), F32)
    column = jax.ShapeDtypeStruct((2 * COLUMN_ROWS, n_cols), F32)
    edge = jax.ShapeDtypeStruct((n_levels, n_species, n_cols), BF16)
    cornered = jax.ShapeDtypeStruct((n_levels + 2, n_species, n_cols), BF16)
    params = pltpu.CompilerParams(vmem_limit_bytes=VMEM_BYTES)
    hbm = pl.BlockSpec(memory_space=pltpu.HBM)
    n_reactions = react_a.shape[0]
    lon_a, lon_b, lat_a, lat_b = pl.pallas_call(
        first_kernel,
        out_shape=(column, column, edge, edge),
        in_specs=[hbm] * 5,
        out_specs=tuple(vmem(4)),
        scratch_shapes=[
            pltpu.VMEM((n_levels, n_species, n_rows, n_cols), F32),
            pltpu.VMEM(sunlit.shape, sunlit.dtype),
            pltpu.VMEM(east_courant.shape, F32),
            pltpu.VMEM(north_courant.shape, F32),
            pltpu.VMEM(mixing.shape, F32),
            pltpu.VMEM((2, n_levels * n_rows, n_cols), F32),
            pltpu.VMEM((2, n_cols, n_levels * n_rows), F32),
            pltpu.SemaphoreType.DMA((n_levels + 4,)),
        ],
        compiler_params=pltpu.CompilerParams(vmem_limit_bytes=FIRST_VMEM_BYTES),
        name="first_sends",
        cost_estimate=pl.CostEstimate(flops=4_000_000_000, bytes_accessed=2_000_000, transcendentals=0),
    )(sunlit, latent_field, east_courant, north_courant, mixing)
    weights = (decode_w.T, react_a.T, react_b.T, stoich, encode_w, rate_const[None])
    folded = (
        jax.ShapeDtypeStruct((2 * n_reactions, n_species), BF16),
        jax.ShapeDtypeStruct((n_species, n_reactions), BF16),
    )
    lon_halos = swapped(lon_a, "lon", 0), swapped(lon_b, "lon", 1)
    field = latent_field
    for step in range(STEPS):
        first, last = step == 0, step == STEPS - 1
        lat_halos = swapped(lat_a, "lat", 0), swapped(lat_b, "lat", 1, closed=True)
        scratch = [pltpu.VMEM(layered.shape, F32)] if first else []
        if last:
            scratch += [
                pltpu.VMEM((2, n_levels, n_species, n_rows // 2, n_cols), F32),
                pltpu.SemaphoreType.DMA((2, n_levels)),
            ]
        scratch += [pltpu.VMEM(array.shape, array.dtype) for array in lat_halos]
        scratch += [
            pltpu.VMEM((2 * n_levels * n_rows // n_cols, n_species, n_cols), F32),
            pltpu.VMEM((8, n_levels, n_rows, n_cols), F32),
            pltpu.VMEM((n_levels, n_rows, n_species, n_cols), F32),
        ]
        operands = weights if first else (lon_a, lon_b, *weights)
        outs = pl.pallas_call(
            functools.partial(step_kernel, n_levels, n_rows, first, last),
            out_shape=(jax.ShapeDtypeStruct(latent_field.shape, F32),)
            if last
            else (layered, cornered, cornered, *folded),
            in_specs=vmem(9 + len(operands)),
            out_specs=(hbm,) if last else tuple(vmem(5)),
            scratch_shapes=scratch,
            compiler_params=params,
            name="splitting_step",
            cost_estimate=pl.CostEstimate(flops=20_000_000_000, bytes_accessed=1, transcendentals=0),
        )(sunlit, field, east_courant, north_courant, mixing, *lon_halos, *lat_halos, *operands)
        if not last:
            field, lat_a, lat_b, *weights = outs
    return outs[0]


def solution(mesh):
    placed = (
        P(None, None, "lat", "lon"),
        P(None, "lat", "lon"),
        P(None, "lat", "lon"),
        P(None, "lat", "lon"),
        P("lat", "lon"),
        P(),
        P(),
        P(),
        P(),
        P(),
        P(),
    )
    return jax.shard_map(
        on_device,
        mesh=mesh,
        in_specs=placed,
        out_specs=P(None, None, "lat", "lon"),
        check_vma=False,
    )
```

```python
import functools
import itertools

import jax
import jax.numpy as jnp
from jax import lax
from jax.experimental import pallas as pl
from jax.experimental.pallas import tpu as pltpu
from jax.sharding import PartitionSpec as P

BLOCK = 16
SUBSTEPS = 2
GROUP = 16
ROWS_IN_FLIGHT = 2
LEVELS_AT_ONCE = 4
LAG = 1

F32 = jnp.float32
BF16 = jnp.bfloat16
VMEM_BYTES = 48 * 1024 * 1024
FIRST_VMEM_BYTES = 56 * 1024 * 1024


def lane_ids(shape):
    return lax.broadcasted_iota(jnp.int32, shape, len(shape) - 1)


def fold_weights(decode_t, react_a_t, react_b_t, stoich, encode, rate, linear_out, encode_out):
    n_reactions = react_a_t.shape[1]
    contract = (((0,), (1,)), ((), ()))
    for part, react in enumerate((react_a_t, react_b_t)):
        product = lax.dot_general(
            react[...], decode_t[...], contract, preferred_element_type=F32
        )
        for group in range(n_reactions // GROUP):
            at = (2 * group + part) * GROUP
            linear_out[at : at + GROUP, :] = product[
                group * GROUP : (group + 1) * GROUP
            ].astype(BF16)
    folded = jnp.dot(encode[...], stoich[...], preferred_element_type=F32)
    encode_out[...] = (folded * rate[...]).astype(BF16)


def at_ends():
    index = lax.axis_index("lat")
    return index == 0, index == lax.axis_size("lat") - 1


def is_even(axis):
    return lax.axis_index(axis) % 2 == 0


def by_parity(axis, up, down, into_first, into_second):
    even = is_even(axis)
    into_first[...] = jnp.where(even, up, down)
    into_second[...] = jnp.where(even, down, up)


COLUMN_ROWS = 40
EAST_ROW, NORTH_ROW, MIXING_ROW, LIT_ROW = 32, 33, 34, 35


def first_kernel(sun, latent, east_c, north_c, mixing, lon_a, lon_b, lat_a, lat_b, *scratch):
    tiles, sun_v, east_v, north_v, mixing_v, faces, turned_faces, sems = scratch
    n_levels, n_species, n_rows, n_cols = tiles.shape
    lanes = lane_ids((1, n_cols))
    is_first, is_last = at_ends()
    copies = [
        pltpu.make_async_copy(source, held, sems.at[n_levels + at])
        for at, (source, held) in enumerate(
            ((sun, sun_v), (east_c, east_v), (north_c, north_v), (mixing, mixing_v))
        )
    ]
    levels = [
        pltpu.make_async_copy(latent.at[:, level], tiles.at[level], sems.at[level])
        for level in range(n_levels)
    ]
    for copy in copies + levels:
        copy.start()
    for copy in copies:
        copy.wait()
    def face_lanes(planes):
        packed = None
        for at, plane in enumerate(planes):
            turned = pltpu.roll(plane, (4 * at + 2) % n_cols, 1)
            packed = turned if packed is None else jnp.where(lanes // 4 == at, turned, packed)
        return packed

    for level in range(n_levels):
        levels[level].wait()
        within = slice(level * n_rows, (level + 1) * n_rows)
        faces[0, within] = face_lanes([tiles[level, at] for at in range(n_species)])
        planes = [east_v[level], north_v[level]]
        if level < n_levels - 1:
            planes.append(mixing_v[level])
        zero = jnp.zeros((n_rows, n_cols), F32)
        faces[1, within] = face_lanes(planes + [zero] * (COLUMN_ROWS - n_species - len(planes)))
        rows = tiles.at[level].reshape(n_species * n_rows, n_cols)
        ends = []
        for r, closed, clip in ((0, is_first, jnp.minimum), (n_rows - 1, is_last, jnp.maximum)):
            speed = clip(north_v[level, r : r + 1, :], 0.0)
            value = rows[pl.ds(r, n_species, stride=n_rows), :]
            ends.append((value * jnp.where(closed, 0.0, speed)).astype(BF16))
        by_parity("lat", ends[1], ends[0], lat_a.at[level], lat_b.at[level])
    turned_faces[0] = faces[0].T
    turned_faces[1] = faces[1].T
    columns = [
        jnp.concatenate(
            [
                turned_faces[0, pl.ds(slot, n_species, stride=4), :],
                turned_faces[1, pl.ds(slot, COLUMN_ROWS - n_species, stride=4), :],
            ],
            axis=0,
        )
        for slot in range(4)
    ]
    kinds = lax.broadcasted_iota(jnp.int32, (COLUMN_ROWS, n_cols), 0)
    lit_west = sun_v[:, :1].astype(F32)
    lit_east = sun_v[:, n_cols // BLOCK - 1 :].astype(F32)
    west = [jnp.where(kinds == LIT_ROW, lit_west, columns[at]) for at in (2, 3)]
    east = [jnp.where(kinds == LIT_ROW, lit_east, columns[at]) for at in (1, 0)]
    by_parity("lon", jnp.concatenate(east, axis=0), jnp.concatenate(west, axis=0), lon_a, lon_b)


def split_columns(message):
    return message[:COLUMN_ROWS], message[COLUMN_ROWS:]


def inflow(column, n_species, clip):
    return column[:n_species] * clip(column[EAST_ROW : EAST_ROW + 1], 0.0)


def lat_inflow(column, n_species, clip):
    return column[:n_species] * clip(column[NORTH_ROW : NORTH_ROW + 1], 0.0)


def moved_column(column, west, east, south, north, n_species, n_rows, ends):
    n_cols = column.shape[1]
    rows = lane_ids((1, n_cols)) % n_rows
    is_first, is_last = ends
    speed = column[EAST_ROW : EAST_ROW + 1]
    lat_speed = column[NORTH_ROW : NORTH_ROW + 1]
    up = jnp.where((rows == n_rows - 1) & is_last, 0.0, jnp.maximum(lat_speed, 0.0))
    down = jnp.where((rows == 0) & is_first, 0.0, jnp.minimum(lat_speed, 0.0))
    value = column[:n_species]
    from_south = jnp.where(rows == 0, south, pltpu.roll(value * up, 1, 1))
    from_north = jnp.where(rows == n_rows - 1, north, pltpu.roll(value * down, n_cols - 1, 1))
    centre = 1.0 - jnp.abs(speed) - up + down
    return value * centre + (west - east) + (from_south - from_north)


def by_level(west, east, n_levels, n_rows):
    n_cols = west.shape[1]
    of_west = lane_ids((1, n_cols)) < n_rows
    return [
        jnp.where(
            of_west,
            pltpu.roll(west, (n_cols - level * n_rows) % n_cols, 1),
            pltpu.roll(east, (n_cols - (level - 1) * n_rows) % n_cols, 1),
        )
        for level in range(n_levels)
    ]


def joined(levels, n_rows):
    n_cols = levels[0].shape[1]
    width = 2 * n_rows
    lanes = lane_ids((1, n_cols))
    arrays = []
    for at, array in enumerate(levels):
        turn = at * width % n_cols
        if turn == 0:
            arrays.append(array)
        else:
            arrays[-1] = jnp.where(lanes // width == turn // width, pltpu.roll(array, turn, 1), arrays[-1])
    return arrays


def diffused_columns(moved, mixing):
    upper, swept = None, []
    uppers = []
    for level, value in enumerate(moved):
        pivot = 1.0
        if level > 0:
            below = mixing[level - 1]
            pivot = pivot + below - below * upper
            value = value + below * swept[-1]
        if level < len(moved) - 1:
            pivot = pivot + mixing[level]
        scale = 1.0 / pivot
        if level < len(moved) - 1:
            upper = mixing[level] * scale
            uppers.append(upper)
        swept.append(value * scale)
    for level in range(len(moved) - 2, -1, -1):
        swept[level] = swept[level] + uppers[level] * swept[level + 1]
    return swept


COEFFICIENTS = CENTRE, EAST, WEST, NORTH, SOUTH, SCALE, LOWER, UPPER = range(8)


def prepare_kernel(latent, east_c, north_c, mixing, *refs):
    weights, (field, coefs, linear, encode) = refs[:6], refs[6:]
    n_levels, n_rows, _, n_cols = field.shape
    fold_weights(*weights, linear, encode)
    is_first, is_last = at_ends()
    row_ids = lax.broadcasted_iota(jnp.int32, (n_rows, n_cols), 0)
    upper = None
    for level in range(n_levels):
        field[level] = jnp.transpose(latent[:, level], (1, 0, 2))
        ce, cn = east_c[level], north_c[level]
        east, west = jnp.maximum(ce, 0.0), jnp.minimum(ce, 0.0)
        north = jnp.where((row_ids == n_rows - 1) & is_last, 0.0, jnp.maximum(cn, 0.0))
        south = jnp.where((row_ids == 0) & is_first, 0.0, jnp.minimum(cn, 0.0))
        coefs[CENTRE, level] = 1.0 - east + west - north + south
        coefs[EAST, level] = east
        coefs[WEST, level] = west
        coefs[NORTH, level] = north
        coefs[SOUTH, level] = south
        pivot = 1.0
        if level > 0:
            below = mixing[level - 1]
            pivot = pivot + below - below * upper
        if level < n_levels - 1:
            pivot = pivot + mixing[level]
        scale = 1.0 / pivot
        coefs[SCALE, level] = scale
        if level > 0:
            coefs[LOWER, level] = below * scale
        if level < n_levels - 1:
            upper = mixing[level] * scale
            coefs[UPPER, level] = upper


def product_of(linear, rounded):
    n_reactions = linear.shape[0] // 2
    both = jnp.dot(linear[...], rounded, preferred_element_type=F32)
    parts = [
        both[at : at + GROUP] * both[at + GROUP : at + 2 * GROUP]
        for at in range(0, 2 * n_reactions, 2 * GROUP)
    ]
    return jnp.concatenate(parts, axis=0).astype(BF16)


def lit_lanes(sun, n_cols):
    lanes = lane_ids((1, n_cols))
    lit = jnp.zeros((1, n_cols), jnp.int32)
    for block in range(n_cols // BLOCK):
        lit = jnp.where(lanes // BLOCK == block, sun[:, block : block + 1], lit)
    return lit > 0


def step_rows(order, sun, field, coefs, linear, encode, lon_in, south_in, north_in, diffused, finish, passage=None):
    n_levels, n_rows, _, n_cols = field.shape
    lanes = lane_ids((1, n_cols))

    def coef(kind, level, r):
        return coefs[kind, level, r : r + 1, :]

    def transport(r):
        right = None
        for level in range(n_levels):
            value = field[level, r]
            spot = level * 2 * n_rows % n_cols
            halo = lon_in[level * 2 * n_rows // n_cols]
            from_west = jnp.where(
                lanes == 0,
                pltpu.roll(halo, (n_cols - spot - r) % n_cols, 1),
                pltpu.roll(value * coef(EAST, level, r), 1, 1),
            )
            from_east = jnp.where(
                lanes == n_cols - 1,
                pltpu.roll(halo, n_cols - 1 - spot - n_rows - r, 1),
                pltpu.roll(value * coef(WEST, level, r), n_cols - 1, 1),
            )
            if r == 0:
                from_south = south_in[level].astype(F32)
            else:
                from_south = field[level, r - 1] * coef(NORTH, level, r - 1)
            if r == n_rows - 1:
                from_north = north_in[level].astype(F32)
            else:
                from_north = field[level, r + 1] * coef(SOUTH, level, r + 1)
            moved = value * coef(CENTRE, level, r) + (from_west - from_east) + (from_south - from_north)
            scaled = moved * coef(SCALE, level, r)
            right = scaled if level == 0 else scaled + coef(LOWER, level, r) * right
            diffused[level, r] = right
            yield
        for level in range(n_levels - 2, -1, -1):
            right = diffused[level, r] + coef(UPPER, level, r) * right
            diffused[level, r] = right
            yield

    def tile_at(level, r):
        return jnp.concatenate(
            [diffused[level + extra, r] for extra in range(LEVELS_AT_ONCE)], axis=1
        )

    lit_tile = jnp.concatenate([lit_lanes(sun, n_cols)] * LEVELS_AT_ONCE, axis=1)
    for r in order[:ROWS_IN_FLIGHT]:
        for _ in transport(r):
            pass
    units, beside = [], []
    for first in range(0, len(order), ROWS_IN_FLIGHT):
        in_flight = order[first : first + ROWS_IN_FLIGHT]
        places = [(level, r) for r in in_flight for level in range(0, n_levels, LEVELS_AT_ONCE)]
        ahead = order[first + ROWS_IN_FLIGHT : first + 2 * ROWS_IN_FLIGHT]
        steps = itertools.chain(*[transport(r) for r in ahead])
        share = -(-(2 * n_levels - 1) * ROWS_IN_FLIGHT // (SUBSTEPS * len(places)))
        for substep in range(SUBSTEPS):
            for place in places:
                beside.append((steps, share))
                units.append((substep, place))
    later_by = ROWS_IN_FLIGHT * (n_levels // LEVELS_AT_ONCE)
    rounded, rates = {}, {}
    for at in range(len(units) + LAG):
        if at < len(units):
            substep, (level, r) = units[at]
            if substep == 0:
                rounded[at] = tile_at(level, r).astype(BF16)
            rates[at] = product_of(linear, rounded.pop(at))
            if passage is not None and at > len(units) // 2 + LAG:
                next(passage, None)
            for _ in itertools.islice(*beside[at]):
                pass
        if at >= LAG:
            done = at - LAG
            substep, (level, r) = units[done]
            change = jnp.dot(encode[...], rates.pop(done), preferred_element_type=F32)
            tile = tile_at(level, r)
            value = tile + jnp.where(lit_tile, change, 0.0)
            if substep < SUBSTEPS - 1:
                rounded[done + later_by] = (tile.astype(BF16).astype(F32) + change).astype(BF16)
            for extra in range(LEVELS_AT_ONCE):
                part = value[:, extra * n_cols : (extra + 1) * n_cols]
                if substep < SUBSTEPS - 1:
                    diffused[level + extra, r] = part
                else:
                    finish(level + extra, r, part)


def near_and_far(lon_b_in, lon_a_in):
    even = is_even("lon")
    west = split_columns(jnp.where(even, lon_b_in[...], lon_a_in[...]))
    east = split_columns(jnp.where(even, lon_a_in[...], lon_b_in[...]))
    return west, east


def edge_rows_kernel(
    sun, field, coefs, linear, encode, lat_b_in, lat_a_in, lon_b_in, lon_a_in,
    done, lat_a, lat_b, lon_in, south_in, north_in, diffused,
):
    n_levels, n_rows, n_species, n_cols = field.shape
    lanes = lane_ids((1, n_cols))
    is_first, is_last = at_ends()
    by_parity("lat", lat_a_in[...], lat_b_in[...], north_in, south_in)
    (west_near, _), (east_near, _) = near_and_far(lon_b_in, lon_a_in)
    halos = by_level(
        inflow(west_near, n_species, jnp.maximum),
        inflow(east_near, n_species, jnp.minimum),
        n_levels,
        n_rows,
    )
    for at, halo in enumerate(joined(halos, n_rows)):
        lon_in[at] = halo
    order = [0, n_rows - 1]

    def finish(level, r, value):
        done[level, order.index(r)] = value

    step_rows(order, sun, field, coefs, linear, encode, lon_in, south_in, north_in, diffused, finish)
    for level in range(n_levels):
        south = (done[level, 0] * coefs[SOUTH, level, :1]).astype(BF16)
        north = (done[level, 1] * coefs[NORTH, level, n_rows - 1 :]).astype(BF16)
        by_parity("lat", north, south, lat_a.at[level], lat_b.at[level])
    rows_of = lanes % n_rows
    corners = []
    for closed, clip, turn, row in (
        (is_first, jnp.minimum, 1, 0),
        (is_last, jnp.maximum, n_cols - 1, n_rows - 1),
    ):
        of_west = lat_inflow(west_near, n_species, clip)
        of_east = pltpu.roll(lat_inflow(east_near, n_species, clip), turn, 1)
        corners.append(jnp.where(closed, 0.0, jnp.where(rows_of == row, of_west, of_east)))
    south, north = (value.astype(BF16) for value in corners)
    by_parity("lat", north, south, lat_a.at[n_levels], lat_b.at[n_levels])


def inner_rows_kernel(sun, field, coefs, linear, encode, done, lon_in, out, diffused):
    n_levels, n_rows, _, _ = field.shape
    for level in range(n_levels):
        out[level, 0] = done[level, 0]
        out[level, n_rows - 1] = done[level, 1]

    def finish(level, r, value):
        out[level, r] = value

    order = list(range(1, n_rows - 1))
    step_rows(order, sun, field, coefs, linear, encode, lon_in, None, None, diffused, finish)


def last_step_kernel(
    sun, field, coefs, linear, encode, lat_b_in, lat_a_in, lon_b_in, lon_a_in, lon_a_own, lon_b_own,
    out, staged, sems, south_in, north_in, lon_in, diffused,
):
    n_levels, n_rows, n_species, n_cols = field.shape
    half_rows = n_rows // 2
    lanes = lane_ids((1, n_cols))
    ends = at_ends()
    by_parity("lat", lat_a_in[...], lat_b_in[...], north_in, south_in)
    (west_near, west_far), (east_near, east_far) = near_and_far(lon_b_in, lon_a_in)
    even = is_even("lon")
    own_west, _ = split_columns(jnp.where(even, lon_b_own[...], lon_a_own[...]))
    own_east, _ = split_columns(jnp.where(even, lon_a_own[...], lon_b_own[...]))

    def levels_of(west, east):
        return by_level(west, east, n_levels, n_rows)

    def kind_of(kind):
        return levels_of(west_near[kind : kind + 1], east_near[kind : kind + 1])

    def corner(edge, at, turn):
        shift = turn if at == 0 else (turn + (1 if turn > n_rows else n_cols - 1)) % n_cols
        return pltpu.roll(edge[n_levels].astype(F32), shift, 1)

    def column_after(at, near, west, east):
        return moved_column(
            near,
            inflow(west, n_species, jnp.maximum),
            inflow(east, n_species, jnp.minimum),
            corner(south_in, at, n_cols - (n_rows - 1)),
            corner(north_in, at, n_rows - 1),
            n_species,
            n_rows,
            ends,
        )

    moved = levels_of(
        column_after(0, west_near, west_far, own_west),
        column_after(1, east_near, own_east, east_far),
    )
    pair = jnp.concatenate(joined(diffused_columns(moved, kind_of(MIXING_ROW)), n_rows), axis=1)
    rounded = pair.astype(BF16)
    current, summed = rounded.astype(F32), None
    for substep in range(SUBSTEPS):
        change = jnp.dot(encode[...], product_of(linear, rounded), preferred_element_type=F32)
        summed = change if summed is None else summed + change
        current = current + change
        rounded = current.astype(BF16)
    pair_lit = jnp.concatenate(joined(kind_of(LIT_ROW), n_rows), axis=1)
    pair = pair + jnp.where(pair_lit > 0.0, summed, 0.0)
    for at, speed in enumerate(joined(kind_of(EAST_ROW), n_rows)):
        clipped = jnp.where(
            lanes // n_rows % 2 == 0, jnp.maximum(speed, 0.0), jnp.minimum(speed, 0.0)
        )
        lon_in[at] = pair[:, at * n_cols : (at + 1) * n_cols] * clipped

    copies = []

    def send(half):
        within = slice(half * half_rows, (half + 1) * half_rows)
        for level in range(n_levels):
            staged[half, level] = jnp.transpose(diffused[level, within], (1, 0, 2))
            copy = pltpu.make_async_copy(
                staged.at[half, level], out.at[:, level, within], sems.at[half, level]
            )
            copy.start()
            copies.append(copy)
            yield

    def finish(level, r, value):
        diffused[level, r] = value

    step_rows(
        list(range(n_rows)), sun, field, coefs, linear, encode, lon_in, south_in, north_in, diffused,
        finish, send(0),
    )
    for _ in send(1):
        pass
    for copy in copies:
        copy.wait()


def vmem(count):
    return [pl.BlockSpec(memory_space=pltpu.VMEM)] * count


def swapped(array, axis, first):
    size = lax.axis_size(axis)
    pairs = [(i % size, (i + 1) % size) for i in range(first, size + first, 2)]
    return lax.ppermute(array, axis, pairs + [(j, i) for i, j in pairs])


def on_device(
    latent_field,
    east_courant,
    north_courant,
    mixing,
    sunlit,
    decode_w,
    react_a,
    react_b,
    stoich,
    encode_w,
    rate_const,
):
    n_species, n_levels, n_rows, n_cols = latent_field.shape
    layered = jax.ShapeDtypeStruct((n_levels, n_rows, n_species, n_cols), F32)
    column = jax.ShapeDtypeStruct((2 * COLUMN_ROWS, n_cols), F32)
    edge = jax.ShapeDtypeStruct((n_levels, n_species, n_cols), BF16)
    cornered = jax.ShapeDtypeStruct((n_levels + 1, n_species, n_cols), BF16)
    params = pltpu.CompilerParams(vmem_limit_bytes=VMEM_BYTES)
    hbm = pl.BlockSpec(memory_space=pltpu.HBM)
    n_reactions = react_a.shape[0]
    lon_a, lon_b, lat_a, lat_b = pl.pallas_call(
        first_kernel,
        out_shape=(column, column, edge, edge),
        in_specs=[hbm] * 5,
        out_specs=tuple(vmem(4)),
        scratch_shapes=[
            pltpu.VMEM((n_levels, n_species, n_rows, n_cols), F32),
            pltpu.VMEM(sunlit.shape, sunlit.dtype),
            pltpu.VMEM(east_courant.shape, F32),
            pltpu.VMEM(north_courant.shape, F32),
            pltpu.VMEM(mixing.shape, F32),
            pltpu.VMEM((2, n_levels * n_rows, n_cols), F32),
            pltpu.VMEM((2, n_cols, n_levels * n_rows), F32),
            pltpu.SemaphoreType.DMA((n_levels + 4,)),
        ],
        compiler_params=pltpu.CompilerParams(vmem_limit_bytes=FIRST_VMEM_BYTES),
        name="first_sends",
        cost_estimate=pl.CostEstimate(flops=4_000_000_000, bytes_accessed=2_000_000, transcendentals=0),
    )(sunlit, latent_field, east_courant, north_courant, mixing)
    weights = (decode_w.T, react_a.T, react_b.T, stoich, encode_w, rate_const[None])
    field, coefs, linear, encode = pl.pallas_call(
        prepare_kernel,
        out_shape=(
            layered,
            jax.ShapeDtypeStruct((len(COEFFICIENTS), n_levels, n_rows, n_cols), F32),
            jax.ShapeDtypeStruct((2 * n_reactions, n_species), BF16),
            jax.ShapeDtypeStruct((n_species, n_reactions), BF16),
        ),
        in_specs=vmem(4 + len(weights)),
        out_specs=tuple(vmem(4)),
        compiler_params=params,
        name="prepare",
        cost_estimate=pl.CostEstimate(flops=4_000_000_000, bytes_accessed=1, transcendentals=0),
    )(latent_field, east_courant, north_courant, mixing, *weights)
    lon_halos = swapped(lon_b, "lon", 1), swapped(lon_a, "lon", 0)
    hint = pl.CostEstimate(flops=20_000_000_000, bytes_accessed=1, transcendentals=0)
    halo = jax.ShapeDtypeStruct((2 * n_levels * n_rows // n_cols, n_species, n_cols), F32)

    def call(kernel, name, operands, out_shape, out_specs, *scratch):
        return pl.pallas_call(
            kernel,
            out_shape=out_shape,
            in_specs=vmem(len(operands)),
            out_specs=out_specs,
            scratch_shapes=[
                pltpu.VMEM(a.shape, a.dtype) if isinstance(a, jax.ShapeDtypeStruct) else a
                for a in scratch
            ],
            compiler_params=params,
            name=name,
            cost_estimate=hint,
        )(*operands)

    lat_halos = swapped(lat_b, "lat", 1), swapped(lat_a, "lat", 0)
    shared = sunlit, field, coefs, linear, encode
    done, lat_a, lat_b, lon_in = call(
        edge_rows_kernel,
        "edge_rows",
        (*shared, *lat_halos, *lon_halos),
        (jax.ShapeDtypeStruct((n_levels, 2, n_species, n_cols), F32), cornered, cornered, halo),
        tuple(vmem(4)),
        edge,
        edge,
        layered,
    )
    lat_halos = swapped(lat_b, "lat", 1), swapped(lat_a, "lat", 0)
    (field,) = call(
        inner_rows_kernel, "inner_rows", (*shared, done, lon_in), (layered,), tuple(vmem(1)), layered
    )
    (advanced,) = call(
        last_step_kernel,
        "last_step",
        (sunlit, field, coefs, linear, encode, *lat_halos, *lon_halos, lon_a, lon_b),
        (jax.ShapeDtypeStruct(latent_field.shape, F32),),
        (hbm,),
        pltpu.VMEM((2, n_levels, n_species, n_rows // 2, n_cols), F32),
        pltpu.SemaphoreType.DMA((2, n_levels)),
        cornered,
        cornered,
        halo,
        layered,
    )
    return advanced


def solution(mesh):
    placed = (
        P(None, None, "lat", "lon"),
        P(None, "lat", "lon"),
        P(None, "lat", "lon"),
        P(None, "lat", "lon"),
        P("lat", "lon"),
        P(),
        P(),
        P(),
        P(),
        P(),
        P(),
    )
    return jax.shard_map(
        on_device,
        mesh=mesh,
        in_specs=placed,
        out_specs=P(None, None, "lat", "lon"),
        check_vma=False,
    )
```

```python
import functools
import itertools

import jax
import jax.numpy as jnp
from jax import lax
from jax.experimental import pallas as pl
from jax.experimental.pallas import tpu as pltpu
from jax.sharding import PartitionSpec as P

BLOCK = 16
SUBSTEPS = 2
GROUP = 8
ROWS_IN_FLIGHT = 2
LEVELS_AT_ONCE = 4
LAG = 1

F32 = jnp.float32
BF16 = jnp.bfloat16
VMEM_BYTES = 48 * 1024 * 1024
FIRST_VMEM_BYTES = 56 * 1024 * 1024
PREPARE_VMEM_BYTES = 50 * 1024 * 1024


def lane_ids(shape):
    return lax.broadcasted_iota(jnp.int32, shape, len(shape) - 1)


def fold_weights(decode_t, react_a_t, react_b_t, stoich, encode, rate, linear_out, encode_out):
    n_reactions = react_a_t.shape[1]
    contract = (((0,), (1,)), ((), ()))
    products = [
        lax.dot_general(react[...], decode_t[...], contract, preferred_element_type=F32)
        for react in (react_a_t, react_b_t)
    ]
    linear_out[...] = jnp.concatenate(
        [
            product[at : at + GROUP]
            for at in range(0, n_reactions, GROUP)
            for product in products
        ],
        axis=0,
    ).astype(BF16)
    folded = jnp.dot(encode[...], stoich[...], preferred_element_type=F32)
    encode_out[...] = (folded * rate[...]).astype(BF16)


def at_ends():
    index = lax.axis_index("lat")
    return index == 0, index == lax.axis_size("lat") - 1


def is_even(axis):
    return lax.axis_index(axis) % 2 == 0


def by_parity(axis, up, down, into_first, into_second):
    even = is_even(axis)
    into_first[...] = jnp.where(even, up, down)
    into_second[...] = jnp.where(even, down, up)


COLUMN_ROWS = 40
EAST_ROW, NORTH_ROW, MIXING_ROW, LIT_ROW = 32, 33, 34, 35


def first_kernel(sun, latent, east_c, north_c, mixing, lon_a, lon_b, lat_a, lat_b, *scratch):
    tiles, sun_v, east_v, north_v, mixing_v, faces, turned_faces, sems = scratch
    n_levels, n_species, n_rows, n_cols = tiles.shape
    lanes = lane_ids((1, n_cols))
    is_first, is_last = at_ends()
    copies = [
        pltpu.make_async_copy(source, held, sems.at[n_levels + at])
        for at, (source, held) in enumerate(
            ((sun, sun_v), (east_c, east_v), (north_c, north_v), (mixing, mixing_v))
        )
    ]
    levels = [
        pltpu.make_async_copy(latent.at[:, level], tiles.at[level], sems.at[level])
        for level in range(n_levels)
    ]
    for copy in copies + levels:
        copy.start()
    for copy in copies:
        copy.wait()
    def face_lanes(planes):
        packed = None
        for at, plane in enumerate(planes):
            turned = pltpu.roll(plane, (4 * at + 2) % n_cols, 1)
            packed = turned if packed is None else jnp.where(lanes // 4 == at, turned, packed)
        return packed

    for level in range(n_levels):
        levels[level].wait()
        within = slice(level * n_rows, (level + 1) * n_rows)
        faces[0, within] = face_lanes([tiles[level, at] for at in range(n_species)])
        planes = [east_v[level], north_v[level]]
        if level < n_levels - 1:
            planes.append(mixing_v[level])
        zero = jnp.zeros((n_rows, n_cols), F32)
        faces[1, within] = face_lanes(planes + [zero] * (COLUMN_ROWS - n_species - len(planes)))
        rows = tiles.at[level].reshape(n_species * n_rows, n_cols)
        ends = []
        for r, closed, clip in ((0, is_first, jnp.minimum), (n_rows - 1, is_last, jnp.maximum)):
            speed = clip(north_v[level, r : r + 1, :], 0.0)
            value = rows[pl.ds(r, n_species, stride=n_rows), :]
            ends.append((value * jnp.where(closed, 0.0, speed)).astype(BF16))
        by_parity("lat", ends[1], ends[0], lat_a.at[level], lat_b.at[level])
    turned_faces[0] = faces[0].T
    turned_faces[1] = faces[1].T
    columns = [
        jnp.concatenate(
            [
                turned_faces[0, pl.ds(slot, n_species, stride=4), :],
                turned_faces[1, pl.ds(slot, COLUMN_ROWS - n_species, stride=4), :],
            ],
            axis=0,
        )
        for slot in range(4)
    ]
    kinds = lax.broadcasted_iota(jnp.int32, (COLUMN_ROWS, n_cols), 0)
    lit_west = sun_v[:, :1].astype(F32)
    lit_east = sun_v[:, n_cols // BLOCK - 1 :].astype(F32)
    west = [jnp.where(kinds == LIT_ROW, lit_west, columns[at]) for at in (2, 3)]
    east = [jnp.where(kinds == LIT_ROW, lit_east, columns[at]) for at in (1, 0)]
    by_parity("lon", jnp.concatenate(east, axis=0), jnp.concatenate(west, axis=0), lon_a, lon_b)


def split_columns(message):
    return message[:COLUMN_ROWS], message[COLUMN_ROWS:]


def inflow(column, n_species, clip):
    return column[:n_species] * clip(column[EAST_ROW : EAST_ROW + 1], 0.0)


def lat_inflow(column, n_species, clip):
    return column[:n_species] * clip(column[NORTH_ROW : NORTH_ROW + 1], 0.0)


def moved_column(column, west, east, south, north, n_species, n_rows, ends):
    n_cols = column.shape[1]
    rows = lane_ids((1, n_cols)) % n_rows
    is_first, is_last = ends
    speed = column[EAST_ROW : EAST_ROW + 1]
    lat_speed = column[NORTH_ROW : NORTH_ROW + 1]
    up = jnp.where((rows == n_rows - 1) & is_last, 0.0, jnp.maximum(lat_speed, 0.0))
    down = jnp.where((rows == 0) & is_first, 0.0, jnp.minimum(lat_speed, 0.0))
    value = column[:n_species]
    from_south = jnp.where(rows == 0, south, pltpu.roll(value * up, 1, 1))
    from_north = jnp.where(rows == n_rows - 1, north, pltpu.roll(value * down, n_cols - 1, 1))
    centre = 1.0 - jnp.abs(speed) - up + down
    return value * centre + (west - east) + (from_south - from_north)


def by_level(west, east, n_levels, n_rows):
    n_cols = west.shape[1]
    of_west = lane_ids((1, n_cols)) < n_rows
    return [
        jnp.where(
            of_west,
            pltpu.roll(west, (n_cols - level * n_rows) % n_cols, 1),
            pltpu.roll(east, (n_cols - (level - 1) * n_rows) % n_cols, 1),
        )
        for level in range(n_levels)
    ]


def joined(levels, n_rows):
    n_cols = levels[0].shape[1]
    width = 2 * n_rows
    lanes = lane_ids((1, n_cols))
    arrays = []
    for at, array in enumerate(levels):
        turn = at * width % n_cols
        if turn == 0:
            arrays.append(array)
        else:
            arrays[-1] = jnp.where(lanes // width == turn // width, pltpu.roll(array, turn, 1), arrays[-1])
    return arrays


def diffused_columns(moved, mixing):
    upper, swept = None, []
    uppers = []
    for level, value in enumerate(moved):
        pivot = 1.0
        if level > 0:
            below = mixing[level - 1]
            pivot = pivot + below - below * upper
            value = value + below * swept[-1]
        if level < len(moved) - 1:
            pivot = pivot + mixing[level]
        scale = 1.0 / pivot
        if level < len(moved) - 1:
            upper = mixing[level] * scale
            uppers.append(upper)
        swept.append(value * scale)
    for level in range(len(moved) - 2, -1, -1):
        swept[level] = swept[level] + uppers[level] * swept[level + 1]
    return swept


COEFFICIENTS = CENTRE, EAST, WEST, NORTH, SOUTH, SCALE, LOWER, UPPER = range(8)


def prepare_kernel(latent, east_c, north_c, mixing, *refs):
    weights, (field, coefs, linear, encode, tiles, sems) = refs[:6], refs[6:]
    n_levels, n_rows, _, n_cols = field.shape
    copies = [
        pltpu.make_async_copy(latent.at[:, level], tiles.at[level], sems.at[level])
        for level in range(n_levels)
    ]
    for copy in copies:
        copy.start()
    fold_weights(*weights, linear, encode)
    is_first, is_last = at_ends()
    row_ids = lax.broadcasted_iota(jnp.int32, (n_rows, n_cols), 0)
    upper = None
    for level in range(n_levels):
        copies[level].wait()
        field[level] = jnp.transpose(tiles[level], (1, 0, 2))
        ce, cn = east_c[level], north_c[level]
        east, west = jnp.maximum(ce, 0.0), jnp.minimum(ce, 0.0)
        north = jnp.where((row_ids == n_rows - 1) & is_last, 0.0, jnp.maximum(cn, 0.0))
        south = jnp.where((row_ids == 0) & is_first, 0.0, jnp.minimum(cn, 0.0))
        coefs[CENTRE, level] = 1.0 - east + west - north + south
        coefs[EAST, level] = east
        coefs[WEST, level] = west
        coefs[NORTH, level] = north
        coefs[SOUTH, level] = south
        pivot = 1.0
        if level > 0:
            below = mixing[level - 1]
            pivot = pivot + below - below * upper
        if level < n_levels - 1:
            pivot = pivot + mixing[level]
        scale = 1.0 / pivot
        coefs[SCALE, level] = scale
        if level > 0:
            coefs[LOWER, level] = below * scale
        if level < n_levels - 1:
            upper = mixing[level] * scale
            coefs[UPPER, level] = upper


def product_of(linear, rounded):
    n_reactions = linear.shape[0] // 2
    both = jnp.dot(linear[...], rounded, preferred_element_type=F32)
    parts = [
        both[at : at + GROUP] * both[at + GROUP : at + 2 * GROUP]
        for at in range(0, 2 * n_reactions, 2 * GROUP)
    ]
    return jnp.concatenate(parts, axis=0).astype(BF16)


def lit_lanes(sun, n_cols):
    lanes = lane_ids((1, n_cols))
    lit = jnp.zeros((1, n_cols), jnp.int32)
    for block in range(n_cols // BLOCK):
        lit = jnp.where(lanes // BLOCK == block, sun[:, block : block + 1], lit)
    return lit > 0


def step_rows(order, sun, field, coefs, linear, encode, lon_in, south_in, north_in, diffused, finish, passage=None):
    n_levels, n_rows, _, n_cols = field.shape
    lanes = lane_ids((1, n_cols))

    def coef(kind, level, r):
        return coefs[kind, level, r : r + 1, :]

    def transport(r):
        right = None
        for level in range(n_levels):
            value = field[level, r]
            spot = level * 2 * n_rows % n_cols
            halo = lon_in[level * 2 * n_rows // n_cols]
            from_west = jnp.where(
                lanes == 0,
                pltpu.roll(halo, (n_cols - spot - r) % n_cols, 1),
                pltpu.roll(value * coef(EAST, level, r), 1, 1),
            )
            from_east = jnp.where(
                lanes == n_cols - 1,
                pltpu.roll(halo, n_cols - 1 - spot - n_rows - r, 1),
                pltpu.roll(value * coef(WEST, level, r), n_cols - 1, 1),
            )
            if r == 0:
                from_south = south_in[level].astype(F32)
            else:
                from_south = field[level, r - 1] * coef(NORTH, level, r - 1)
            if r == n_rows - 1:
                from_north = north_in[level].astype(F32)
            else:
                from_north = field[level, r + 1] * coef(SOUTH, level, r + 1)
            moved = value * coef(CENTRE, level, r) + (from_west - from_east) + (from_south - from_north)
            scaled = moved * coef(SCALE, level, r)
            right = scaled if level == 0 else scaled + coef(LOWER, level, r) * right
            diffused[level, r] = right
            yield
        for level in range(n_levels - 2, -1, -1):
            right = diffused[level, r] + coef(UPPER, level, r) * right
            diffused[level, r] = right
            yield

    def tile_at(level, r):
        return jnp.concatenate(
            [diffused[level + extra, r] for extra in range(LEVELS_AT_ONCE)], axis=1
        )

    lit_tile = jnp.concatenate([lit_lanes(sun, n_cols)] * LEVELS_AT_ONCE, axis=1)
    for r in order[:ROWS_IN_FLIGHT]:
        for _ in transport(r):
            pass
    units, beside = [], []
    for first in range(0, len(order), ROWS_IN_FLIGHT):
        in_flight = order[first : first + ROWS_IN_FLIGHT]
        places = [(level, r) for r in in_flight for level in range(0, n_levels, LEVELS_AT_ONCE)]
        ahead = order[first + ROWS_IN_FLIGHT : first + 2 * ROWS_IN_FLIGHT]
        steps = itertools.chain(*[transport(r) for r in ahead])
        share = -(-(2 * n_levels - 1) * ROWS_IN_FLIGHT // (SUBSTEPS * len(places)))
        for substep in range(SUBSTEPS):
            for place in places:
                beside.append((steps, share))
                units.append((substep, place))
    later_by = ROWS_IN_FLIGHT * (n_levels // LEVELS_AT_ONCE)
    rounded, rates = {}, {}
    for at in range(len(units) + LAG):
        if at < len(units):
            substep, (level, r) = units[at]
            if substep == 0:
                rounded[at] = tile_at(level, r).astype(BF16)
            rates[at] = product_of(linear, rounded.pop(at))
            if passage is not None and at > len(units) // 2 + LAG:
                next(passage, None)
            for _ in itertools.islice(*beside[at]):
                pass
        if at >= LAG:
            done = at - LAG
            substep, (level, r) = units[done]
            change = jnp.dot(encode[...], rates.pop(done), preferred_element_type=F32)
            tile = tile_at(level, r)
            value = tile + jnp.where(lit_tile, change, 0.0)
            if substep < SUBSTEPS - 1:
                rounded[done + later_by] = (tile.astype(BF16).astype(F32) + change).astype(BF16)
            for extra in range(LEVELS_AT_ONCE):
                part = value[:, extra * n_cols : (extra + 1) * n_cols]
                if substep < SUBSTEPS - 1:
                    diffused[level + extra, r] = part
                else:
                    finish(level + extra, r, part)


def near_and_far(lon_b_in, lon_a_in):
    even = is_even("lon")
    west = split_columns(jnp.where(even, lon_b_in[...], lon_a_in[...]))
    east = split_columns(jnp.where(even, lon_a_in[...], lon_b_in[...]))
    return west, east


def edge_rows_kernel(
    sun, field, coefs, linear, encode, lat_b_in, lat_a_in, lon_b_in, lon_a_in,
    done, lat_a, lat_b, lon_in, south_in, north_in, diffused,
):
    n_levels, n_rows, n_species, n_cols = field.shape
    lanes = lane_ids((1, n_cols))
    is_first, is_last = at_ends()
    by_parity("lat", lat_a_in[...], lat_b_in[...], north_in, south_in)
    (west_near, _), (east_near, _) = near_and_far(lon_b_in, lon_a_in)
    halos = by_level(
        inflow(west_near, n_species, jnp.maximum),
        inflow(east_near, n_species, jnp.minimum),
        n_levels,
        n_rows,
    )
    for at, halo in enumerate(joined(halos, n_rows)):
        lon_in[at] = halo
    order = [0, n_rows - 1]

    def finish(level, r, value):
        done[level, order.index(r)] = value

    step_rows(order, sun, field, coefs, linear, encode, lon_in, south_in, north_in, diffused, finish)
    for level in range(n_levels):
        south = (done[level, 0] * coefs[SOUTH, level, :1]).astype(BF16)
        north = (done[level, 1] * coefs[NORTH, level, n_rows - 1 :]).astype(BF16)
        by_parity("lat", north, south, lat_a.at[level], lat_b.at[level])
    rows_of = lanes % n_rows
    corners = []
    for closed, clip, turn, row in (
        (is_first, jnp.minimum, 1, 0),
        (is_last, jnp.maximum, n_cols - 1, n_rows - 1),
    ):
        of_west = lat_inflow(west_near, n_species, clip)
        of_east = pltpu.roll(lat_inflow(east_near, n_species, clip), turn, 1)
        corners.append(jnp.where(closed, 0.0, jnp.where(rows_of == row, of_west, of_east)))
    south, north = (value.astype(BF16) for value in corners)
    by_parity("lat", north, south, lat_a.at[n_levels], lat_b.at[n_levels])


def inner_rows_kernel(sun, field, coefs, linear, encode, done, lon_in, out, diffused):
    n_levels, n_rows, _, _ = field.shape
    for level in range(n_levels):
        out[level, 0] = done[level, 0]
        out[level, n_rows - 1] = done[level, 1]

    def finish(level, r, value):
        out[level, r] = value

    order = list(range(1, n_rows - 1))
    step_rows(order, sun, field, coefs, linear, encode, lon_in, None, None, diffused, finish)


def last_step_kernel(
    sun, field, coefs, linear, encode, lat_b_in, lat_a_in, lon_b_in, lon_a_in, lon_a_own, lon_b_own,
    out, staged, sems, south_in, north_in, lon_in, diffused,
):
    n_levels, n_rows, n_species, n_cols = field.shape
    half_rows = n_rows // 2
    lanes = lane_ids((1, n_cols))
    ends = at_ends()
    by_parity("lat", lat_a_in[...], lat_b_in[...], north_in, south_in)
    (west_near, west_far), (east_near, east_far) = near_and_far(lon_b_in, lon_a_in)
    even = is_even("lon")
    own_west, _ = split_columns(jnp.where(even, lon_b_own[...], lon_a_own[...]))
    own_east, _ = split_columns(jnp.where(even, lon_a_own[...], lon_b_own[...]))

    def levels_of(west, east):
        return by_level(west, east, n_levels, n_rows)

    def kind_of(kind):
        return levels_of(west_near[kind : kind + 1], east_near[kind : kind + 1])

    def corner(edge, at, turn):
        shift = turn if at == 0 else (turn + (1 if turn > n_rows else n_cols - 1)) % n_cols
        return pltpu.roll(edge[n_levels].astype(F32), shift, 1)

    def column_after(at, near, west, east):
        return moved_column(
            near,
            inflow(west, n_species, jnp.maximum),
            inflow(east, n_species, jnp.minimum),
            corner(south_in, at, n_cols - (n_rows - 1)),
            corner(north_in, at, n_rows - 1),
            n_species,
            n_rows,
            ends,
        )

    moved = levels_of(
        column_after(0, west_near, west_far, own_west),
        column_after(1, east_near, own_east, east_far),
    )
    pair = jnp.concatenate(joined(diffused_columns(moved, kind_of(MIXING_ROW)), n_rows), axis=1)
    rounded = pair.astype(BF16)
    current, summed = rounded.astype(F32), None
    for substep in range(SUBSTEPS):
        change = jnp.dot(encode[...], product_of(linear, rounded), preferred_element_type=F32)
        summed = change if summed is None else summed + change
        current = current + change
        rounded = current.astype(BF16)
    pair_lit = jnp.concatenate(joined(kind_of(LIT_ROW), n_rows), axis=1)
    pair = pair + jnp.where(pair_lit > 0.0, summed, 0.0)
    for at, speed in enumerate(joined(kind_of(EAST_ROW), n_rows)):
        clipped = jnp.where(
            lanes // n_rows % 2 == 0, jnp.maximum(speed, 0.0), jnp.minimum(speed, 0.0)
        )
        lon_in[at] = pair[:, at * n_cols : (at + 1) * n_cols] * clipped

    copies = []

    def send(half):
        within = slice(half * half_rows, (half + 1) * half_rows)
        for level in range(n_levels):
            staged[half, level] = jnp.transpose(diffused[level, within], (1, 0, 2))
            copy = pltpu.make_async_copy(
                staged.at[half, level], out.at[:, level, within], sems.at[half, level]
            )
            copy.start()
            copies.append(copy)
            yield

    def finish(level, r, value):
        diffused[level, r] = value

    step_rows(
        list(range(n_rows)), sun, field, coefs, linear, encode, lon_in, south_in, north_in, diffused,
        finish, send(0),
    )
    for _ in send(1):
        pass
    for copy in copies:
        copy.wait()


def vmem(count):
    return [pl.BlockSpec(memory_space=pltpu.VMEM)] * count


def swapped(array, axis, first):
    size = lax.axis_size(axis)
    pairs = [(i % size, (i + 1) % size) for i in range(first, size + first, 2)]
    return lax.ppermute(array, axis, pairs + [(j, i) for i, j in pairs])


def on_device(
    latent_field,
    east_courant,
    north_courant,
    mixing,
    sunlit,
    decode_w,
    react_a,
    react_b,
    stoich,
    encode_w,
    rate_const,
):
    n_species, n_levels, n_rows, n_cols = latent_field.shape
    layered = jax.ShapeDtypeStruct((n_levels, n_rows, n_species, n_cols), F32)
    column = jax.ShapeDtypeStruct((2 * COLUMN_ROWS, n_cols), F32)
    edge = jax.ShapeDtypeStruct((n_levels, n_species, n_cols), BF16)
    cornered = jax.ShapeDtypeStruct((n_levels + 1, n_species, n_cols), BF16)
    params = pltpu.CompilerParams(vmem_limit_bytes=VMEM_BYTES)
    hbm = pl.BlockSpec(memory_space=pltpu.HBM)
    n_reactions = react_a.shape[0]
    lon_a, lon_b, lat_a, lat_b = pl.pallas_call(
        first_kernel,
        out_shape=(column, column, edge, edge),
        in_specs=[hbm] * 5,
        out_specs=tuple(vmem(4)),
        scratch_shapes=[
            pltpu.VMEM((n_levels, n_species, n_rows, n_cols), F32),
            pltpu.VMEM(sunlit.shape, sunlit.dtype),
            pltpu.VMEM(east_courant.shape, F32),
            pltpu.VMEM(north_courant.shape, F32),
            pltpu.VMEM(mixing.shape, F32),
            pltpu.VMEM((2, n_levels * n_rows, n_cols), F32),
            pltpu.VMEM((2, n_cols, n_levels * n_rows), F32),
            pltpu.SemaphoreType.DMA((n_levels + 4,)),
        ],
        compiler_params=pltpu.CompilerParams(vmem_limit_bytes=FIRST_VMEM_BYTES),
        name="first_sends",
        cost_estimate=pl.CostEstimate(flops=4_000_000_000, bytes_accessed=2_000_000, transcendentals=0),
    )(sunlit, latent_field, east_courant, north_courant, mixing)
    weights = (decode_w.T, react_a.T, react_b.T, stoich, encode_w, rate_const[None])
    field, coefs, linear, encode = pl.pallas_call(
        prepare_kernel,
        out_shape=(
            layered,
            jax.ShapeDtypeStruct((len(COEFFICIENTS), n_levels, n_rows, n_cols), F32),
            jax.ShapeDtypeStruct((2 * n_reactions, n_species), BF16),
            jax.ShapeDtypeStruct((n_species, n_reactions), BF16),
        ),
        in_specs=[hbm] + vmem(3 + len(weights)),
        out_specs=tuple(vmem(4)),
        scratch_shapes=[
            pltpu.VMEM((n_levels, n_species, n_rows, n_cols), F32),
            pltpu.SemaphoreType.DMA((n_levels,)),
        ],
        compiler_params=pltpu.CompilerParams(vmem_limit_bytes=PREPARE_VMEM_BYTES),
        name="prepare",
        cost_estimate=pl.CostEstimate(flops=4_000_000_000, bytes_accessed=1, transcendentals=0),
    )(latent_field, east_courant, north_courant, mixing, *weights)
    lon_halos = swapped(lon_b, "lon", 1), swapped(lon_a, "lon", 0)
    hint = pl.CostEstimate(flops=20_000_000_000, bytes_accessed=1, transcendentals=0)
    halo = jax.ShapeDtypeStruct((2 * n_levels * n_rows // n_cols, n_species, n_cols), F32)

    def call(kernel, name, operands, out_shape, out_specs, *scratch):
        return pl.pallas_call(
            kernel,
            out_shape=out_shape,
            in_specs=vmem(len(operands)),
            out_specs=out_specs,
            scratch_shapes=[
                pltpu.VMEM(a.shape, a.dtype) if isinstance(a, jax.ShapeDtypeStruct) else a
                for a in scratch
            ],
            compiler_params=params,
            name=name,
            cost_estimate=hint,
        )(*operands)

    lat_halos = swapped(lat_b, "lat", 1), swapped(lat_a, "lat", 0)
    shared = sunlit, field, coefs, linear, encode
    done, lat_a, lat_b, lon_in = call(
        edge_rows_kernel,
        "edge_rows",
        (*shared, *lat_halos, *lon_halos),
        (jax.ShapeDtypeStruct((n_levels, 2, n_species, n_cols), F32), cornered, cornered, halo),
        tuple(vmem(4)),
        edge,
        edge,
        layered,
    )
    lat_halos = swapped(lat_b, "lat", 1), swapped(lat_a, "lat", 0)
    (field,) = call(
        inner_rows_kernel, "inner_rows", (*shared, done, lon_in), (layered,), tuple(vmem(1)), layered
    )
    (advanced,) = call(
        last_step_kernel,
        "last_step",
        (sunlit, field, coefs, linear, encode, *lat_halos, *lon_halos, lon_a, lon_b),
        (jax.ShapeDtypeStruct(latent_field.shape, F32),),
        (hbm,),
        pltpu.VMEM((2, n_levels, n_species, n_rows // 2, n_cols), F32),
        pltpu.SemaphoreType.DMA((2, n_levels)),
        cornered,
        cornered,
        halo,
        layered,
    )
    return advanced


def solution(mesh):
    placed = (
        P(None, None, "lat", "lon"),
        P(None, "lat", "lon"),
        P(None, "lat", "lon"),
        P(None, "lat", "lon"),
        P("lat", "lon"),
        P(),
        P(),
        P(),
        P(),
        P(),
        P(),
    )
    return jax.shard_map(
        on_device,
        mesh=mesh,
        in_specs=placed,
        out_specs=P(None, None, "lat", "lon"),
        check_vma=False,
    )
```

```python
import functools
import itertools

import jax
import jax.numpy as jnp
from jax import lax
from jax.experimental import pallas as pl
from jax.experimental.pallas import tpu as pltpu
from jax.sharding import PartitionSpec as P

BLOCK = 16
SUBSTEPS = 2
GROUP = 8
ROWS_IN_FLIGHT = 2
LEVELS_AT_ONCE = 4
LAG = 1

F32 = jnp.float32
BF16 = jnp.bfloat16
VMEM_BYTES = 48 * 1024 * 1024
FIRST_VMEM_BYTES = 56 * 1024 * 1024
PREPARE_VMEM_BYTES = 50 * 1024 * 1024


def lane_ids(shape):
    return lax.broadcasted_iota(jnp.int32, shape, len(shape) - 1)


def fold_weights(decode_t, react_a_t, react_b_t, stoich, encode, rate, linear_out, encode_out):
    n_reactions = react_a_t.shape[1]
    contract = (((0,), (1,)), ((), ()))
    products = [
        lax.dot_general(react[...], decode_t[...], contract, preferred_element_type=F32)
        for react in (react_a_t, react_b_t)
    ]
    linear_out[...] = jnp.concatenate(
        [
            product[at : at + GROUP]
            for at in range(0, n_reactions, GROUP)
            for product in products
        ],
        axis=0,
    ).astype(BF16)
    folded = jnp.dot(encode[...], stoich[...], preferred_element_type=F32)
    encode_out[...] = (folded * rate[...]).astype(BF16)


def at_ends():
    index = lax.axis_index("lat")
    return index == 0, index == lax.axis_size("lat") - 1


def is_even(axis):
    return lax.axis_index(axis) % 2 == 0


def by_parity(axis, up, down, into_first, into_second):
    even = is_even(axis)
    into_first[...] = jnp.where(even, up, down)
    into_second[...] = jnp.where(even, down, up)


COLUMN_ROWS = 40
EAST_ROW, NORTH_ROW, MIXING_ROW, LIT_ROW = 32, 33, 34, 35


def first_kernel(sun, latent, east_c, north_c, mixing, lon_a, lon_b, lat_a, lat_b, *scratch):
    tiles, sun_v, east_v, north_v, mixing_v, faces, turned_faces, sems = scratch
    n_levels, n_species, n_rows, n_cols = tiles.shape
    lanes = lane_ids((1, n_cols))
    is_first, is_last = at_ends()
    copies = [
        pltpu.make_async_copy(source, held, sems.at[n_levels + at])
        for at, (source, held) in enumerate(
            ((sun, sun_v), (east_c, east_v), (north_c, north_v), (mixing, mixing_v))
        )
    ]
    levels = [
        pltpu.make_async_copy(latent.at[:, level], tiles.at[level], sems.at[level])
        for level in range(n_levels)
    ]
    for copy in copies + levels:
        copy.start()
    for copy in copies:
        copy.wait()
    def face_lanes(planes):
        packed = None
        for at, plane in enumerate(planes):
            turned = pltpu.roll(plane, (4 * at + 2) % n_cols, 1)
            packed = turned if packed is None else jnp.where(lanes // 4 == at, turned, packed)
        return packed

    for level in range(n_levels):
        levels[level].wait()
        within = slice(level * n_rows, (level + 1) * n_rows)
        faces[0, within] = face_lanes([tiles[level, at] for at in range(n_species)])
        planes = [east_v[level], north_v[level]]
        if level < n_levels - 1:
            planes.append(mixing_v[level])
        zero = jnp.zeros((n_rows, n_cols), F32)
        faces[1, within] = face_lanes(planes + [zero] * (COLUMN_ROWS - n_species - len(planes)))
        rows = tiles.at[level].reshape(n_species * n_rows, n_cols)
        ends = []
        for r, closed, clip in ((0, is_first, jnp.minimum), (n_rows - 1, is_last, jnp.maximum)):
            speed = clip(north_v[level, r : r + 1, :], 0.0)
            value = rows[pl.ds(r, n_species, stride=n_rows), :]
            ends.append((value * jnp.where(closed, 0.0, speed)).astype(BF16))
        by_parity("lat", ends[1], ends[0], lat_a.at[level], lat_b.at[level])
    turned_faces[0] = faces[0].T
    turned_faces[1] = faces[1].T
    columns = [
        jnp.concatenate(
            [
                turned_faces[0, pl.ds(slot, n_species, stride=4), :],
                turned_faces[1, pl.ds(slot, COLUMN_ROWS - n_species, stride=4), :],
            ],
            axis=0,
        )
        for slot in range(4)
    ]
    kinds = lax.broadcasted_iota(jnp.int32, (COLUMN_ROWS, n_cols), 0)
    lit_west = sun_v[:, :1].astype(F32)
    lit_east = sun_v[:, n_cols // BLOCK - 1 :].astype(F32)
    west = [jnp.where(kinds == LIT_ROW, lit_west, columns[at]) for at in (2, 3)]
    east = [jnp.where(kinds == LIT_ROW, lit_east, columns[at]) for at in (1, 0)]
    by_parity("lon", jnp.concatenate(east, axis=0), jnp.concatenate(west, axis=0), lon_a, lon_b)


def split_columns(message):
    return message[:COLUMN_ROWS], message[COLUMN_ROWS:]


def inflow(column, n_species, clip):
    return column[:n_species] * clip(column[EAST_ROW : EAST_ROW + 1], 0.0)


def lat_inflow(column, n_species, clip):
    return column[:n_species] * clip(column[NORTH_ROW : NORTH_ROW + 1], 0.0)


def moved_column(column, west, east, south, north, n_species, n_rows, ends):
    n_cols = column.shape[1]
    rows = lane_ids((1, n_cols)) % n_rows
    is_first, is_last = ends
    speed = column[EAST_ROW : EAST_ROW + 1]
    lat_speed = column[NORTH_ROW : NORTH_ROW + 1]
    up = jnp.where((rows == n_rows - 1) & is_last, 0.0, jnp.maximum(lat_speed, 0.0))
    down = jnp.where((rows == 0) & is_first, 0.0, jnp.minimum(lat_speed, 0.0))
    value = column[:n_species]
    from_south = jnp.where(rows == 0, south, pltpu.roll(value * up, 1, 1))
    from_north = jnp.where(rows == n_rows - 1, north, pltpu.roll(value * down, n_cols - 1, 1))
    centre = 1.0 - jnp.abs(speed) - up + down
    return value * centre + (west - east) + (from_south - from_north)


def by_level(west, east, n_levels, n_rows):
    n_cols = west.shape[1]
    of_west = lane_ids((1, n_cols)) < n_rows
    return [
        jnp.where(
            of_west,
            pltpu.roll(west, (n_cols - level * n_rows) % n_cols, 1),
            pltpu.roll(east, (n_cols - (level - 1) * n_rows) % n_cols, 1),
        )
        for level in range(n_levels)
    ]


def joined(levels, n_rows):
    n_cols = levels[0].shape[1]
    width = 2 * n_rows
    lanes = lane_ids((1, n_cols))
    arrays = []
    for at, array in enumerate(levels):
        turn = at * width % n_cols
        if turn == 0:
            arrays.append(array)
        else:
            arrays[-1] = jnp.where(lanes // width == turn // width, pltpu.roll(array, turn, 1), arrays[-1])
    return arrays


def diffused_columns(moved, mixing):
    upper, swept = None, []
    uppers = []
    for level, value in enumerate(moved):
        pivot = 1.0
        if level > 0:
            below = mixing[level - 1]
            pivot = pivot + below - below * upper
            value = value + below * swept[-1]
        if level < len(moved) - 1:
            pivot = pivot + mixing[level]
        scale = 1.0 / pivot
        if level < len(moved) - 1:
            upper = mixing[level] * scale
            uppers.append(upper)
        swept.append(value * scale)
    for level in range(len(moved) - 2, -1, -1):
        swept[level] = swept[level] + uppers[level] * swept[level + 1]
    return swept


COEFFICIENTS = CENTRE, EAST, WEST, NORTH, SOUTH, SCALE, LOWER, UPPER = range(8)


def prepare_kernel(latent, east_c, north_c, mixing, *refs):
    weights, (field, coefs, linear, encode, tiles, sems) = refs[:6], refs[6:]
    n_levels, n_rows, _, n_cols = field.shape
    copies = [
        pltpu.make_async_copy(latent.at[:, level], tiles.at[level], sems.at[level])
        for level in range(n_levels)
    ]
    for copy in copies:
        copy.start()
    fold_weights(*weights, linear, encode)
    is_first, is_last = at_ends()
    row_ids = lax.broadcasted_iota(jnp.int32, (n_rows, n_cols), 0)
    upper = None
    for level in range(n_levels):
        copies[level].wait()
        field[level] = jnp.transpose(tiles[level], (1, 0, 2))
        ce, cn = east_c[level], north_c[level]
        east, west = jnp.maximum(ce, 0.0), jnp.minimum(ce, 0.0)
        north = jnp.where((row_ids == n_rows - 1) & is_last, 0.0, jnp.maximum(cn, 0.0))
        south = jnp.where((row_ids == 0) & is_first, 0.0, jnp.minimum(cn, 0.0))
        coefs[CENTRE, level] = 1.0 - east + west - north + south
        coefs[EAST, level] = east
        coefs[WEST, level] = west
        coefs[NORTH, level] = north
        coefs[SOUTH, level] = south
        pivot = 1.0
        if level > 0:
            below = mixing[level - 1]
            pivot = pivot + below - below * upper
        if level < n_levels - 1:
            pivot = pivot + mixing[level]
        scale = 1.0 / pivot
        coefs[SCALE, level] = scale
        if level > 0:
            coefs[LOWER, level] = below * scale
        if level < n_levels - 1:
            upper = mixing[level] * scale
            coefs[UPPER, level] = upper


def product_of(linear, rounded):
    n_reactions = linear.shape[0] // 2
    both = jnp.dot(linear[...], rounded, preferred_element_type=F32)
    parts = [
        both[at : at + GROUP] * both[at + GROUP : at + 2 * GROUP]
        for at in range(0, 2 * n_reactions, 2 * GROUP)
    ]
    return jnp.concatenate(parts, axis=0).astype(BF16)


def lit_lanes(sun, n_cols):
    lanes = lane_ids((1, n_cols))
    lit = jnp.zeros((1, n_cols), jnp.int32)
    for block in range(n_cols // BLOCK):
        lit = jnp.where(lanes // BLOCK == block, sun[:, block : block + 1], lit)
    return lit > 0


def step_rows(
    order, sun, field, coefs, linear, encode, lon_of, south_in, north_in, diffused, finish, early=None, passage=None
):
    n_levels, n_rows, _, n_cols = field.shape
    lanes = lane_ids((1, n_cols))

    def coef(kind, level, r):
        return coefs[kind, level, r : r + 1, :]

    def transport(r):
        right = None
        for level in range(n_levels):
            value = field[level, r]
            spot = level * 2 * n_rows % n_cols
            halo = lon_of(r)[level * 2 * n_rows // n_cols]
            from_west = jnp.where(
                lanes == 0,
                pltpu.roll(halo, (n_cols - spot - r) % n_cols, 1),
                pltpu.roll(value * coef(EAST, level, r), 1, 1),
            )
            from_east = jnp.where(
                lanes == n_cols - 1,
                pltpu.roll(halo, n_cols - 1 - spot - n_rows - r, 1),
                pltpu.roll(value * coef(WEST, level, r), n_cols - 1, 1),
            )
            if r == 0:
                from_south = south_in[level].astype(F32)
            else:
                from_south = field[level, r - 1] * coef(NORTH, level, r - 1)
            if r == n_rows - 1:
                from_north = north_in[level].astype(F32)
            else:
                from_north = field[level, r + 1] * coef(SOUTH, level, r + 1)
            moved = value * coef(CENTRE, level, r) + (from_west - from_east) + (from_south - from_north)
            scaled = moved * coef(SCALE, level, r)
            right = scaled if level == 0 else scaled + coef(LOWER, level, r) * right
            diffused[level, r] = right
            yield
        for level in range(n_levels - 2, -1, -1):
            right = diffused[level, r] + coef(UPPER, level, r) * right
            diffused[level, r] = right
            yield

    def tile_at(level, r):
        return jnp.concatenate(
            [diffused[level + extra, r] for extra in range(LEVELS_AT_ONCE)], axis=1
        )

    lit_tile = jnp.concatenate([lit_lanes(sun, n_cols)] * LEVELS_AT_ONCE, axis=1)
    for r in order[:ROWS_IN_FLIGHT]:
        for _ in transport(r):
            pass
    units, beside = [], []
    for first in range(0, len(order), ROWS_IN_FLIGHT):
        in_flight = order[first : first + ROWS_IN_FLIGHT]
        places = [(level, r) for r in in_flight for level in range(0, n_levels, LEVELS_AT_ONCE)]
        ahead = order[first + ROWS_IN_FLIGHT : first + 2 * ROWS_IN_FLIGHT]
        steps = itertools.chain(*[transport(r) for r in ahead])
        share = -(-(2 * n_levels - 1) * ROWS_IN_FLIGHT // (SUBSTEPS * len(places)))
        for substep in range(SUBSTEPS):
            for place in places:
                beside.append((steps, share))
                units.append((substep, place))
    later_by = ROWS_IN_FLIGHT * (n_levels // LEVELS_AT_ONCE)
    rounded, rates = {}, {}
    for at in range(len(units) + LAG):
        if at < len(units):
            substep, (level, r) = units[at]
            if substep == 0:
                rounded[at] = tile_at(level, r).astype(BF16)
            rates[at] = product_of(linear, rounded.pop(at))
            if early is not None:
                next(early, None)
            if passage is not None and at > len(units) // 2 + LAG:
                next(passage, None)
            for _ in itertools.islice(*beside[at]):
                pass
        if at >= LAG:
            done = at - LAG
            substep, (level, r) = units[done]
            change = jnp.dot(encode[...], rates.pop(done), preferred_element_type=F32)
            tile = tile_at(level, r)
            value = tile + jnp.where(lit_tile, change, 0.0)
            if substep < SUBSTEPS - 1:
                rounded[done + later_by] = (tile.astype(BF16).astype(F32) + change).astype(BF16)
            for extra in range(LEVELS_AT_ONCE):
                part = value[:, extra * n_cols : (extra + 1) * n_cols]
                if substep < SUBSTEPS - 1:
                    diffused[level + extra, r] = part
                else:
                    finish(level + extra, r, part)


def near_and_far(lon_b_in, lon_a_in):
    even = is_even("lon")
    west = split_columns(jnp.where(even, lon_b_in[...], lon_a_in[...]))
    east = split_columns(jnp.where(even, lon_a_in[...], lon_b_in[...]))
    return west, east


def edge_rows_kernel(
    sun, field, coefs, linear, encode, lat_b_in, lat_a_in, lon_b_in, lon_a_in,
    done, lat_a, lat_b, lon_in, south_in, north_in, diffused,
):
    n_levels, n_rows, n_species, n_cols = field.shape
    lanes = lane_ids((1, n_cols))
    is_first, is_last = at_ends()
    by_parity("lat", lat_a_in[...], lat_b_in[...], north_in, south_in)
    (west_near, _), (east_near, _) = near_and_far(lon_b_in, lon_a_in)
    halos = by_level(
        inflow(west_near, n_species, jnp.maximum),
        inflow(east_near, n_species, jnp.minimum),
        n_levels,
        n_rows,
    )
    for at, halo in enumerate(joined(halos, n_rows)):
        lon_in[at] = halo
    order = [0, n_rows - 1]

    def finish(level, r, value):
        done[level, order.index(r)] = value

    step_rows(
        order, sun, field, coefs, linear, encode, lambda r: lon_in, south_in, north_in, diffused, finish
    )
    for level in range(n_levels):
        south = (done[level, 0] * coefs[SOUTH, level, :1]).astype(BF16)
        north = (done[level, 1] * coefs[NORTH, level, n_rows - 1 :]).astype(BF16)
        by_parity("lat", north, south, lat_a.at[level], lat_b.at[level])
    rows_of = lanes % n_rows
    corners = []
    for closed, clip, turn, row in (
        (is_first, jnp.minimum, 1, 0),
        (is_last, jnp.maximum, n_cols - 1, n_rows - 1),
    ):
        of_west = lat_inflow(west_near, n_species, clip)
        of_east = pltpu.roll(lat_inflow(east_near, n_species, clip), turn, 1)
        corners.append(jnp.where(closed, 0.0, jnp.where(rows_of == row, of_west, of_east)))
    south, north = (value.astype(BF16) for value in corners)
    by_parity("lat", north, south, lat_a.at[n_levels], lat_b.at[n_levels])


def columns_ahead(
    n_levels, n_rows, n_species, linear, encode, received, own, south_in, north_in, lon_out
):
    (west_near, west_far), (east_near, east_far) = near_and_far(*received)
    (own_east, _), (own_west, _) = sent_columns(*own)
    n_cols = west_near.shape[1]
    lanes = lane_ids((1, n_cols))
    ends = at_ends()

    def levels_of(west, east):
        return by_level(west, east, n_levels, n_rows)

    def kind_of(kind):
        return levels_of(west_near[kind : kind + 1], east_near[kind : kind + 1])

    def corner(edge, at, turn):
        if edge is None:
            return 0.0
        shift = turn if at == 0 else (turn + (1 if turn > n_rows else n_cols - 1)) % n_cols
        return pltpu.roll(edge[n_levels].astype(F32), shift, 1)

    def column_after(at, near, west, east):
        return moved_column(
            near,
            inflow(west, n_species, jnp.maximum),
            inflow(east, n_species, jnp.minimum),
            corner(south_in, at, n_cols - (n_rows - 1)),
            corner(north_in, at, n_rows - 1),
            n_species,
            n_rows,
            ends,
        )

    west = column_after(0, west_near, west_far, own_west)
    yield
    east = column_after(1, east_near, own_east, east_far)
    yield
    moved = levels_of(west, east)
    mixing = kind_of(MIXING_ROW)
    yield
    pair = jnp.concatenate(joined(diffused_columns(moved, mixing), n_rows), axis=1)
    rounded = pair.astype(BF16)
    current, summed = rounded.astype(F32), None
    yield
    for substep in range(SUBSTEPS):
        rates = product_of(linear, rounded)
        yield
        change = jnp.dot(encode[...], rates, preferred_element_type=F32)
        summed = change if summed is None else summed + change
        current = current + change
        rounded = current.astype(BF16)
        yield
    pair_lit = jnp.concatenate(joined(kind_of(LIT_ROW), n_rows), axis=1)
    pair = pair + jnp.where(pair_lit > 0.0, summed, 0.0)
    for at, speed in enumerate(joined(kind_of(EAST_ROW), n_rows)):
        clipped = jnp.where(
            lanes // n_rows % 2 == 0, jnp.maximum(speed, 0.0), jnp.minimum(speed, 0.0)
        )
        lon_out[at] = pair[:, at * n_cols : (at + 1) * n_cols] * clipped


def sent_columns(lon_b_own, lon_a_own):
    even = is_even("lon")
    east = split_columns(jnp.where(even, lon_a_own[...], lon_b_own[...]))
    west = split_columns(jnp.where(even, lon_b_own[...], lon_a_own[...]))
    return east, west


def inner_rows_kernel(
    sun, field, coefs, linear, encode, lon_b_in, lon_a_in, lon_b_own, lon_a_own, done, lon_in,
    out, lon_out, diffused,
):
    n_levels, n_rows, n_species, _ = field.shape
    for level in range(n_levels):
        out[level, 0] = done[level, 0]
        out[level, n_rows - 1] = done[level, 1]

    def finish(level, r, value):
        out[level, r] = value

    early = columns_ahead(
        n_levels, n_rows, n_species, linear, encode,
        (lon_b_in, lon_a_in), (lon_b_own, lon_a_own), None, None, lon_out,
    )
    order = list(range(1, n_rows - 1))
    step_rows(
        order, sun, field, coefs, linear, encode, lambda r: lon_in, None, None, diffused, finish, early
    )


def last_step_kernel(
    sun, field, coefs, linear, encode, lon_b_in, lon_a_in, lon_b_own, lon_a_own, lon_in, lat_b_in, lat_a_in,
    out, staged, sems, south_in, north_in, lon_ends, diffused,
):
    n_levels, n_rows, n_species, _ = field.shape
    half_rows = n_rows // 2
    by_parity("lat", lat_a_in[...], lat_b_in[...], north_in, south_in)
    early = columns_ahead(
        n_levels, n_rows, n_species, linear, encode,
        (lon_b_in, lon_a_in), (lon_b_own, lon_a_own), south_in, north_in, lon_ends,
    )
    copies = []

    def send(half):
        within = slice(half * half_rows, (half + 1) * half_rows)
        for level in range(n_levels):
            staged[half, level] = jnp.transpose(diffused[level, within], (1, 0, 2))
            copy = pltpu.make_async_copy(
                staged.at[half, level], out.at[:, level, within], sems.at[half, level]
            )
            copy.start()
            copies.append(copy)
            yield

    def finish(level, r, value):
        diffused[level, r] = value

    order = list(range(1, half_rows)) + [0] + list(range(half_rows, n_rows))
    step_rows(
        order, sun, field, coefs, linear, encode,
        lambda r: lon_ends if r in (0, n_rows - 1) else lon_in,
        south_in, north_in, diffused, finish, early, send(0),
    )
    for _ in send(1):
        pass
    for copy in copies:
        copy.wait()


def vmem(count):
    return [pl.BlockSpec(memory_space=pltpu.VMEM)] * count


def swapped(array, axis, first):
    size = lax.axis_size(axis)
    pairs = [(i % size, (i + 1) % size) for i in range(first, size + first, 2)]
    return lax.ppermute(array, axis, pairs + [(j, i) for i, j in pairs])


def on_device(
    latent_field,
    east_courant,
    north_courant,
    mixing,
    sunlit,
    decode_w,
    react_a,
    react_b,
    stoich,
    encode_w,
    rate_const,
):
    n_species, n_levels, n_rows, n_cols = latent_field.shape
    layered = jax.ShapeDtypeStruct((n_levels, n_rows, n_species, n_cols), F32)
    column = jax.ShapeDtypeStruct((2 * COLUMN_ROWS, n_cols), F32)
    edge = jax.ShapeDtypeStruct((n_levels, n_species, n_cols), BF16)
    cornered = jax.ShapeDtypeStruct((n_levels + 1, n_species, n_cols), BF16)
    params = pltpu.CompilerParams(vmem_limit_bytes=VMEM_BYTES)
    hbm = pl.BlockSpec(memory_space=pltpu.HBM)
    n_reactions = react_a.shape[0]
    lon_a, lon_b, lat_a, lat_b = pl.pallas_call(
        first_kernel,
        out_shape=(column, column, edge, edge),
        in_specs=[hbm] * 5,
        out_specs=tuple(vmem(4)),
        scratch_shapes=[
            pltpu.VMEM((n_levels, n_species, n_rows, n_cols), F32),
            pltpu.VMEM(sunlit.shape, sunlit.dtype),
            pltpu.VMEM(east_courant.shape, F32),
            pltpu.VMEM(north_courant.shape, F32),
            pltpu.VMEM(mixing.shape, F32),
            pltpu.VMEM((2, n_levels * n_rows, n_cols), F32),
            pltpu.VMEM((2, n_cols, n_levels * n_rows), F32),
            pltpu.SemaphoreType.DMA((n_levels + 4,)),
        ],
        compiler_params=pltpu.CompilerParams(vmem_limit_bytes=FIRST_VMEM_BYTES),
        name="first_sends",
        cost_estimate=pl.CostEstimate(flops=4_000_000_000, bytes_accessed=2_000_000, transcendentals=0),
    )(sunlit, latent_field, east_courant, north_courant, mixing)
    weights = (decode_w.T, react_a.T, react_b.T, stoich, encode_w, rate_const[None])
    field, coefs, linear, encode = pl.pallas_call(
        prepare_kernel,
        out_shape=(
            layered,
            jax.ShapeDtypeStruct((len(COEFFICIENTS), n_levels, n_rows, n_cols), F32),
            jax.ShapeDtypeStruct((2 * n_reactions, n_species), BF16),
            jax.ShapeDtypeStruct((n_species, n_reactions), BF16),
        ),
        in_specs=[hbm] + vmem(3 + len(weights)),
        out_specs=tuple(vmem(4)),
        scratch_shapes=[
            pltpu.VMEM((n_levels, n_species, n_rows, n_cols), F32),
            pltpu.SemaphoreType.DMA((n_levels,)),
        ],
        compiler_params=pltpu.CompilerParams(vmem_limit_bytes=PREPARE_VMEM_BYTES),
        name="prepare",
        cost_estimate=pl.CostEstimate(flops=4_000_000_000, bytes_accessed=1, transcendentals=0),
    )(latent_field, east_courant, north_courant, mixing, *weights)
    lon_halos = swapped(lon_b, "lon", 1), swapped(lon_a, "lon", 0)
    hint = pl.CostEstimate(flops=20_000_000_000, bytes_accessed=1, transcendentals=0)
    halo = jax.ShapeDtypeStruct((2 * n_levels * n_rows // n_cols, n_species, n_cols), F32)

    def call(kernel, name, operands, out_shape, out_specs, *scratch):
        return pl.pallas_call(
            kernel,
            out_shape=out_shape,
            in_specs=vmem(len(operands)),
            out_specs=out_specs,
            scratch_shapes=[
                pltpu.VMEM(a.shape, a.dtype) if isinstance(a, jax.ShapeDtypeStruct) else a
                for a in scratch
            ],
            compiler_params=params,
            name=name,
            cost_estimate=hint,
        )(*operands)

    lat_halos = swapped(lat_b, "lat", 1), swapped(lat_a, "lat", 0)
    shared = sunlit, field, coefs, linear, encode
    done, lat_a, lat_b, lon_in = call(
        edge_rows_kernel,
        "edge_rows",
        (*shared, *lat_halos, *lon_halos),
        (jax.ShapeDtypeStruct((n_levels, 2, n_species, n_cols), F32), cornered, cornered, halo),
        tuple(vmem(4)),
        edge,
        edge,
        layered,
    )
    lat_halos = swapped(lat_b, "lat", 1), swapped(lat_a, "lat", 0)
    columns = *lon_halos, lon_b, lon_a
    field, lon_in = call(
        inner_rows_kernel,
        "inner_rows",
        (*shared, *columns, done, lon_in),
        (layered, halo),
        tuple(vmem(2)),
        layered,
    )
    (advanced,) = call(
        last_step_kernel,
        "last_step",
        (sunlit, field, coefs, linear, encode, *columns, lon_in, *lat_halos),
        (jax.ShapeDtypeStruct(latent_field.shape, F32),),
        (hbm,),
        pltpu.VMEM((2, n_levels, n_species, n_rows // 2, n_cols), F32),
        pltpu.SemaphoreType.DMA((2, n_levels)),
        cornered,
        cornered,
        halo,
        layered,
    )
    return advanced


def solution(mesh):
    placed = (
        P(None, None, "lat", "lon"),
        P(None, "lat", "lon"),
        P(None, "lat", "lon"),
        P(None, "lat", "lon"),
        P("lat", "lon"),
        P(),
        P(),
        P(),
        P(),
        P(),
        P(),
    )
    return jax.shard_map(
        on_device,
        mesh=mesh,
        in_specs=placed,
        out_specs=P(None, None, "lat", "lon"),
        check_vma=False,
    )
```

```python
import functools
import itertools

import jax
import jax.numpy as jnp
from jax import lax
from jax.experimental import pallas as pl
from jax.experimental.pallas import tpu as pltpu
from jax.sharding import PartitionSpec as P

BLOCK = 16
SUBSTEPS = 2
GROUP = 8
ROWS_IN_FLIGHT = 2
LEVELS_AT_ONCE = 4
LAG = 1
EARLY_UNITS = (0, 1, 2, 3, 8, 10, 12, 14, 15)

F32 = jnp.float32
BF16 = jnp.bfloat16
VMEM_BYTES = 48 * 1024 * 1024
FIRST_VMEM_BYTES = 56 * 1024 * 1024
PREPARE_VMEM_BYTES = 50 * 1024 * 1024


def lane_ids(shape):
    return lax.broadcasted_iota(jnp.int32, shape, len(shape) - 1)


def fold_weights(decode_t, react_a_t, react_b_t, stoich, encode, rate, linear_out, encode_out):
    n_reactions = react_a_t.shape[1]
    contract = (((0,), (1,)), ((), ()))
    products = [
        lax.dot_general(react[...], decode_t[...], contract, preferred_element_type=F32)
        for react in (react_a_t, react_b_t)
    ]
    linear_out[...] = jnp.concatenate(
        [
            product[at : at + GROUP]
            for at in range(0, n_reactions, GROUP)
            for product in products
        ],
        axis=0,
    ).astype(BF16)
    folded = jnp.dot(encode[...], stoich[...], preferred_element_type=F32)
    encode_out[...] = (folded * rate[...]).astype(BF16)


def at_ends():
    index = lax.axis_index("lat")
    return index == 0, index == lax.axis_size("lat") - 1


def is_even(axis):
    return lax.axis_index(axis) % 2 == 0


def by_parity(axis, up, down, into_first, into_second):
    even = is_even(axis)
    into_first[...] = jnp.where(even, up, down)
    into_second[...] = jnp.where(even, down, up)


COLUMN_ROWS = 40
EAST_ROW, NORTH_ROW, MIXING_ROW, LIT_ROW = 32, 33, 34, 35


def first_kernel(sun, latent, east_c, north_c, mixing, *refs):
    outs, scratch, results = refs[:4], refs[4:-5], refs[-5:-1]
    lon_a, lon_b, lat_a, lat_b = results
    tiles, sun_v, east_v, north_v, mixing_v, faces, turned_faces, sems = scratch
    sends = [
        pltpu.make_async_copy(result, out, refs[-1].at[at])
        for at, (result, out) in enumerate(zip(results, outs))
    ]
    n_levels, n_species, n_rows, n_cols = tiles.shape
    lanes = lane_ids((1, n_cols))
    is_first, is_last = at_ends()
    copies = [
        pltpu.make_async_copy(source, held, sems.at[n_levels + at])
        for at, (source, held) in enumerate(
            ((sun, sun_v), (east_c, east_v), (north_c, north_v), (mixing, mixing_v))
        )
    ]
    levels = [
        pltpu.make_async_copy(latent.at[:, level], tiles.at[level], sems.at[level])
        for level in range(n_levels)
    ]
    for copy in copies + levels:
        copy.start()
    for copy in copies:
        copy.wait()
    def face_lanes(planes):
        packed = None
        for at, plane in enumerate(planes):
            turned = pltpu.roll(plane, (4 * at + 2) % n_cols, 1)
            packed = turned if packed is None else jnp.where(lanes // 4 == at, turned, packed)
        return packed

    for level in range(n_levels):
        levels[level].wait()
        within = slice(level * n_rows, (level + 1) * n_rows)
        faces[0, within] = face_lanes([tiles[level, at] for at in range(n_species)])
        planes = [east_v[level], north_v[level]]
        if level < n_levels - 1:
            planes.append(mixing_v[level])
        zero = jnp.zeros((n_rows, n_cols), F32)
        faces[1, within] = face_lanes(planes + [zero] * (COLUMN_ROWS - n_species - len(planes)))
        rows = tiles.at[level].reshape(n_species * n_rows, n_cols)
        ends = []
        for r, closed, clip in ((0, is_first, jnp.minimum), (n_rows - 1, is_last, jnp.maximum)):
            speed = clip(north_v[level, r : r + 1, :], 0.0)
            value = rows[pl.ds(r, n_species, stride=n_rows), :]
            ends.append((value * jnp.where(closed, 0.0, speed)).astype(BF16))
        by_parity("lat", ends[1], ends[0], lat_a.at[level], lat_b.at[level])
    for copy in sends[2:]:
        copy.start()
    turned_faces[0] = faces[0].T
    turned_faces[1] = faces[1].T
    columns = [
        jnp.concatenate(
            [
                turned_faces[0, pl.ds(slot, n_species, stride=4), :],
                turned_faces[1, pl.ds(slot, COLUMN_ROWS - n_species, stride=4), :],
            ],
            axis=0,
        )
        for slot in range(4)
    ]
    kinds = lax.broadcasted_iota(jnp.int32, (COLUMN_ROWS, n_cols), 0)
    lit_west = sun_v[:, :1].astype(F32)
    lit_east = sun_v[:, n_cols // BLOCK - 1 :].astype(F32)
    west = [jnp.where(kinds == LIT_ROW, lit_west, columns[at]) for at in (2, 3)]
    east = [jnp.where(kinds == LIT_ROW, lit_east, columns[at]) for at in (1, 0)]
    by_parity("lon", jnp.concatenate(east, axis=0), jnp.concatenate(west, axis=0), lon_a, lon_b)
    for copy in sends[:2]:
        copy.start()
    for copy in sends:
        copy.wait()


def split_columns(message):
    return message[:COLUMN_ROWS], message[COLUMN_ROWS:]


def inflow(column, n_species, clip):
    return column[:n_species] * clip(column[EAST_ROW : EAST_ROW + 1], 0.0)


def lat_inflow(column, n_species, clip):
    return column[:n_species] * clip(column[NORTH_ROW : NORTH_ROW + 1], 0.0)


def moved_column(column, west, east, south, north, n_species, n_rows, ends):
    n_cols = column.shape[1]
    rows = lane_ids((1, n_cols)) % n_rows
    is_first, is_last = ends
    speed = column[EAST_ROW : EAST_ROW + 1]
    lat_speed = column[NORTH_ROW : NORTH_ROW + 1]
    up = jnp.where((rows == n_rows - 1) & is_last, 0.0, jnp.maximum(lat_speed, 0.0))
    down = jnp.where((rows == 0) & is_first, 0.0, jnp.minimum(lat_speed, 0.0))
    value = column[:n_species]
    from_south = jnp.where(rows == 0, south, pltpu.roll(value * up, 1, 1))
    from_north = jnp.where(rows == n_rows - 1, north, pltpu.roll(value * down, n_cols - 1, 1))
    centre = 1.0 - jnp.abs(speed) - up + down
    return value * centre + (west - east) + (from_south - from_north)


def by_level(west, east, n_levels, n_rows):
    n_cols = west.shape[1]
    of_west = lane_ids((1, n_cols)) < n_rows
    return [
        jnp.where(
            of_west,
            pltpu.roll(west, (n_cols - level * n_rows) % n_cols, 1),
            pltpu.roll(east, (n_cols - (level - 1) * n_rows) % n_cols, 1),
        )
        for level in range(n_levels)
    ]


def joined(levels, n_rows):
    n_cols = levels[0].shape[1]
    width = 2 * n_rows
    lanes = lane_ids((1, n_cols))
    arrays = []
    for at, array in enumerate(levels):
        turn = at * width % n_cols
        if turn == 0:
            arrays.append(array)
        else:
            arrays[-1] = jnp.where(lanes // width == turn // width, pltpu.roll(array, turn, 1), arrays[-1])
    return arrays


def diffused_columns(moved, mixing):
    upper, swept = None, []
    uppers = []
    for level, value in enumerate(moved):
        pivot = 1.0
        if level > 0:
            below = mixing[level - 1]
            pivot = pivot + below - below * upper
            value = value + below * swept[-1]
        if level < len(moved) - 1:
            pivot = pivot + mixing[level]
        scale = 1.0 / pivot
        if level < len(moved) - 1:
            upper = mixing[level] * scale
            uppers.append(upper)
        swept.append(value * scale)
    for level in range(len(moved) - 2, -1, -1):
        swept[level] = swept[level] + uppers[level] * swept[level + 1]
    return swept


COEFFICIENTS = CENTRE, EAST, WEST, NORTH, SOUTH, SCALE, LOWER, UPPER = range(8)


def prepare_kernel(latent, east_c, north_c, mixing, *refs):
    weights, (field, coefs, linear, encode, tiles, sems) = refs[:6], refs[6:]
    n_levels, n_rows, _, n_cols = field.shape
    copies = [
        pltpu.make_async_copy(latent.at[:, level], tiles.at[level], sems.at[level])
        for level in range(n_levels)
    ]
    for copy in copies:
        copy.start()
    fold_weights(*weights, linear, encode)
    is_first, is_last = at_ends()
    row_ids = lax.broadcasted_iota(jnp.int32, (n_rows, n_cols), 0)
    upper = None
    for level in range(n_levels):
        copies[level].wait()
        field[level] = jnp.transpose(tiles[level], (1, 0, 2))
        ce, cn = east_c[level], north_c[level]
        east, west = jnp.maximum(ce, 0.0), jnp.minimum(ce, 0.0)
        north = jnp.where((row_ids == n_rows - 1) & is_last, 0.0, jnp.maximum(cn, 0.0))
        south = jnp.where((row_ids == 0) & is_first, 0.0, jnp.minimum(cn, 0.0))
        coefs[CENTRE, level] = 1.0 - east + west - north + south
        coefs[EAST, level] = east
        coefs[WEST, level] = west
        coefs[NORTH, level] = north
        coefs[SOUTH, level] = south
        pivot = 1.0
        if level > 0:
            below = mixing[level - 1]
            pivot = pivot + below - below * upper
        if level < n_levels - 1:
            pivot = pivot + mixing[level]
        scale = 1.0 / pivot
        coefs[SCALE, level] = scale
        if level > 0:
            coefs[LOWER, level] = below * scale
        if level < n_levels - 1:
            upper = mixing[level] * scale
            coefs[UPPER, level] = upper


def product_of(linear, rounded):
    n_reactions = linear.shape[0] // 2
    both = jnp.dot(linear[...], rounded, preferred_element_type=F32)
    parts = [
        both[at : at + GROUP] * both[at + GROUP : at + 2 * GROUP]
        for at in range(0, 2 * n_reactions, 2 * GROUP)
    ]
    return jnp.concatenate(parts, axis=0).astype(BF16)


def lit_lanes(sun, n_cols):
    lanes = lane_ids((1, n_cols))
    lit = jnp.zeros((1, n_cols), jnp.int32)
    for block in range(n_cols // BLOCK):
        lit = jnp.where(lanes // BLOCK == block, sun[:, block : block + 1], lit)
    return lit > 0


def step_rows(
    order, sun, field, coefs, linear, encode, lon_of, south_in, north_in, diffused, finish, early=None, passage=None, tail=None
):
    n_levels, n_rows, _, n_cols = field.shape
    lanes = lane_ids((1, n_cols))

    def coef(kind, level, r):
        return coefs[kind, level, r : r + 1, :]

    def transport(r):
        right = None
        for level in range(n_levels):
            value = field[level, r]
            spot = level * 2 * n_rows % n_cols
            halo = lon_of(r)[level * 2 * n_rows // n_cols]
            from_west = jnp.where(
                lanes == 0,
                pltpu.roll(halo, (n_cols - spot - r) % n_cols, 1),
                pltpu.roll(value * coef(EAST, level, r), 1, 1),
            )
            from_east = jnp.where(
                lanes == n_cols - 1,
                pltpu.roll(halo, n_cols - 1 - spot - n_rows - r, 1),
                pltpu.roll(value * coef(WEST, level, r), n_cols - 1, 1),
            )
            if r == 0:
                from_south = south_in[level].astype(F32)
            else:
                from_south = field[level, r - 1] * coef(NORTH, level, r - 1)
            if r == n_rows - 1:
                from_north = north_in[level].astype(F32)
            else:
                from_north = field[level, r + 1] * coef(SOUTH, level, r + 1)
            moved = value * coef(CENTRE, level, r) + (from_west - from_east) + (from_south - from_north)
            scaled = moved * coef(SCALE, level, r)
            right = scaled if level == 0 else scaled + coef(LOWER, level, r) * right
            diffused[level, r] = right
            yield
        for level in range(n_levels - 2, -1, -1):
            right = diffused[level, r] + coef(UPPER, level, r) * right
            diffused[level, r] = right
            yield

    def tile_at(level, r):
        return jnp.concatenate(
            [diffused[level + extra, r] for extra in range(LEVELS_AT_ONCE)], axis=1
        )

    lit_tile = jnp.concatenate([lit_lanes(sun, n_cols)] * LEVELS_AT_ONCE, axis=1)
    for r in order[:ROWS_IN_FLIGHT]:
        for _ in transport(r):
            pass
    units, beside = [], []
    for first in range(0, len(order), ROWS_IN_FLIGHT):
        in_flight = order[first : first + ROWS_IN_FLIGHT]
        places = [(level, r) for level in range(0, n_levels, LEVELS_AT_ONCE) for r in in_flight]
        ahead = order[first + ROWS_IN_FLIGHT : first + 2 * ROWS_IN_FLIGHT]
        steps = itertools.chain(*[transport(r) for r in ahead])
        share = -(-(2 * n_levels - 1) * ROWS_IN_FLIGHT // (SUBSTEPS * len(places)))
        for substep in range(SUBSTEPS):
            for place in places:
                beside.append((steps, share))
                units.append((substep, place))
    later_by = ROWS_IN_FLIGHT * (n_levels // LEVELS_AT_ONCE)
    rounded, rates = {}, {}
    for at in range(len(units) + LAG):
        if at < len(units):
            substep, (level, r) = units[at]
            if substep == 0:
                rounded[at] = tile_at(level, r).astype(BF16)
            rates[at] = product_of(linear, rounded.pop(at))
            if early is not None and at in EARLY_UNITS:
                next(early, None)
            if passage is not None and at > len(units) // 2 + LAG:
                next(passage, None)
            for _ in itertools.islice(*beside[at]):
                pass
        if tail is not None and at >= len(units) - 1:
            for _ in itertools.islice(tail, LEVELS_AT_ONCE // 2):
                pass
        if at >= LAG:
            done = at - LAG
            substep, (level, r) = units[done]
            change = jnp.dot(encode[...], rates.pop(done), preferred_element_type=F32)
            tile = tile_at(level, r)
            value = tile + jnp.where(lit_tile, change, 0.0)
            if substep < SUBSTEPS - 1:
                rounded[done + later_by] = (tile.astype(BF16).astype(F32) + change).astype(BF16)
            for extra in range(LEVELS_AT_ONCE):
                part = value[:, extra * n_cols : (extra + 1) * n_cols]
                if substep < SUBSTEPS - 1:
                    diffused[level + extra, r] = part
                else:
                    finish(level + extra, r, part)


def near_and_far(lon_b_in, lon_a_in):
    even = is_even("lon")
    west = split_columns(jnp.where(even, lon_b_in[...], lon_a_in[...]))
    east = split_columns(jnp.where(even, lon_a_in[...], lon_b_in[...]))
    return west, east


def edge_rows_kernel(
    sun, field, coefs, linear, encode, lat_b_in, lat_a_in, lon_b_in, lon_a_in,
    done, lat_a, lat_b, lon_in, south_in, north_in, diffused,
):
    n_levels, n_rows, n_species, n_cols = field.shape
    lanes = lane_ids((1, n_cols))
    is_first, is_last = at_ends()
    by_parity("lat", lat_a_in[...], lat_b_in[...], north_in, south_in)
    (west_near, _), (east_near, _) = near_and_far(lon_b_in, lon_a_in)
    halos = by_level(
        inflow(west_near, n_species, jnp.maximum),
        inflow(east_near, n_species, jnp.minimum),
        n_levels,
        n_rows,
    )
    for at, halo in enumerate(joined(halos, n_rows)):
        lon_in[at] = halo
    order = [0, n_rows - 1]

    def finish(level, r, value):
        done[level, order.index(r)] = value

    step_rows(
        order, sun, field, coefs, linear, encode, lambda r: lon_in, south_in, north_in, diffused, finish
    )
    for level in range(n_levels):
        south = (done[level, 0] * coefs[SOUTH, level, :1]).astype(BF16)
        north = (done[level, 1] * coefs[NORTH, level, n_rows - 1 :]).astype(BF16)
        by_parity("lat", north, south, lat_a.at[level], lat_b.at[level])
    rows_of = lanes % n_rows
    corners = []
    for closed, clip, turn, row in (
        (is_first, jnp.minimum, 1, 0),
        (is_last, jnp.maximum, n_cols - 1, n_rows - 1),
    ):
        of_west = lat_inflow(west_near, n_species, clip)
        of_east = pltpu.roll(lat_inflow(east_near, n_species, clip), turn, 1)
        corners.append(jnp.where(closed, 0.0, jnp.where(rows_of == row, of_west, of_east)))
    south, north = (value.astype(BF16) for value in corners)
    by_parity("lat", north, south, lat_a.at[n_levels], lat_b.at[n_levels])


def columns_ahead(
    n_levels, n_rows, n_species, linear, encode, received, own, south_in, north_in, lon_out
):
    (west_near, west_far), (east_near, east_far) = near_and_far(*received)
    (own_east, _), (own_west, _) = sent_columns(*own)
    n_cols = west_near.shape[1]
    lanes = lane_ids((1, n_cols))
    ends = at_ends()

    def levels_of(west, east):
        return by_level(west, east, n_levels, n_rows)

    def kind_of(kind):
        return levels_of(west_near[kind : kind + 1], east_near[kind : kind + 1])

    def corner(edge, at, turn):
        if edge is None:
            return 0.0
        shift = turn if at == 0 else (turn + (1 if turn > n_rows else n_cols - 1)) % n_cols
        return pltpu.roll(edge[n_levels].astype(F32), shift, 1)

    def column_after(at, near, west, east):
        return moved_column(
            near,
            inflow(west, n_species, jnp.maximum),
            inflow(east, n_species, jnp.minimum),
            corner(south_in, at, n_cols - (n_rows - 1)),
            corner(north_in, at, n_rows - 1),
            n_species,
            n_rows,
            ends,
        )

    west = column_after(0, west_near, west_far, own_west)
    yield
    east = column_after(1, east_near, own_east, east_far)
    yield
    moved = levels_of(west, east)
    mixing = kind_of(MIXING_ROW)
    yield
    pair = jnp.concatenate(joined(diffused_columns(moved, mixing), n_rows), axis=1)
    rounded = pair.astype(BF16)
    current, summed = rounded.astype(F32), None
    yield
    for substep in range(SUBSTEPS):
        rates = product_of(linear, rounded)
        yield
        change = jnp.dot(encode[...], rates, preferred_element_type=F32)
        summed = change if summed is None else summed + change
        current = current + change
        rounded = current.astype(BF16)
        yield
    pair_lit = jnp.concatenate(joined(kind_of(LIT_ROW), n_rows), axis=1)
    pair = pair + jnp.where(pair_lit > 0.0, summed, 0.0)
    for at, speed in enumerate(joined(kind_of(EAST_ROW), n_rows)):
        clipped = jnp.where(
            lanes // n_rows % 2 == 0, jnp.maximum(speed, 0.0), jnp.minimum(speed, 0.0)
        )
        lon_out[at] = pair[:, at * n_cols : (at + 1) * n_cols] * clipped


def sent_columns(lon_b_own, lon_a_own):
    even = is_even("lon")
    east = split_columns(jnp.where(even, lon_a_own[...], lon_b_own[...]))
    west = split_columns(jnp.where(even, lon_b_own[...], lon_a_own[...]))
    return east, west


def inner_rows_kernel(
    sun, field, coefs, linear, encode, lon_b_in, lon_a_in, lon_b_own, lon_a_own, done, lon_in,
    out, lon_out, diffused,
):
    n_levels, n_rows, n_species, _ = field.shape
    for level in range(n_levels):
        out[level, 0] = done[level, 0]
        out[level, n_rows - 1] = done[level, 1]

    def finish(level, r, value):
        out[level, r] = value

    early = columns_ahead(
        n_levels, n_rows, n_species, linear, encode,
        (lon_b_in, lon_a_in), (lon_b_own, lon_a_own), None, None, lon_out,
    )
    order = list(range(1, n_rows - 1))
    step_rows(
        order, sun, field, coefs, linear, encode, lambda r: lon_in, None, None, diffused, finish, early
    )


def last_step_kernel(
    sun, field, coefs, linear, encode, lon_b_in, lon_a_in, lon_b_own, lon_a_own, lon_in, lat_b_in, lat_a_in,
    out, staged, sems, south_in, north_in, lon_ends, diffused,
):
    n_levels, n_rows, n_species, _ = field.shape
    half_rows = n_rows // 2
    by_parity("lat", lat_a_in[...], lat_b_in[...], north_in, south_in)
    early = columns_ahead(
        n_levels, n_rows, n_species, linear, encode,
        (lon_b_in, lon_a_in), (lon_b_own, lon_a_own), south_in, north_in, lon_ends,
    )
    copies = []

    def send(half):
        within = slice(half * half_rows, (half + 1) * half_rows)
        for level in range(n_levels):
            staged[half, level] = jnp.transpose(diffused[level, within], (1, 0, 2))
            copy = pltpu.make_async_copy(
                staged.at[half, level], out.at[:, level, within], sems.at[half, level]
            )
            copy.start()
            copies.append(copy)
            yield

    def finish(level, r, value):
        diffused[level, r] = value

    order = list(range(1, half_rows)) + [0] + list(range(half_rows, n_rows))
    tail = send(1)
    step_rows(
        order, sun, field, coefs, linear, encode,
        lambda r: lon_ends if r in (0, n_rows - 1) else lon_in,
        south_in, north_in, diffused, finish, early, send(0), tail,
    )
    for _ in tail:
        pass
    for copy in copies:
        copy.wait()


def vmem(count):
    return [pl.BlockSpec(memory_space=pltpu.VMEM)] * count


def swapped(array, axis, first):
    size = lax.axis_size(axis)
    pairs = [(i % size, (i + 1) % size) for i in range(first, size + first, 2)]
    return lax.ppermute(array, axis, pairs + [(j, i) for i, j in pairs])


def on_device(
    latent_field,
    east_courant,
    north_courant,
    mixing,
    sunlit,
    decode_w,
    react_a,
    react_b,
    stoich,
    encode_w,
    rate_const,
):
    n_species, n_levels, n_rows, n_cols = latent_field.shape
    layered = jax.ShapeDtypeStruct((n_levels, n_rows, n_species, n_cols), F32)
    column = jax.ShapeDtypeStruct((2 * COLUMN_ROWS, n_cols), F32)
    edge = jax.ShapeDtypeStruct((n_levels, n_species, n_cols), BF16)
    cornered = jax.ShapeDtypeStruct((n_levels + 1, n_species, n_cols), BF16)
    params = pltpu.CompilerParams(vmem_limit_bytes=VMEM_BYTES)
    hbm = pl.BlockSpec(memory_space=pltpu.HBM)
    n_reactions = react_a.shape[0]
    lon_a, lon_b, lat_a, lat_b = pl.pallas_call(
        first_kernel,
        out_shape=(column, column, edge, edge),
        in_specs=[hbm] * 5,
        out_specs=(hbm,) * 4,
        scratch_shapes=[
            pltpu.VMEM((n_levels, n_species, n_rows, n_cols), F32),
            pltpu.VMEM(sunlit.shape, sunlit.dtype),
            pltpu.VMEM(east_courant.shape, F32),
            pltpu.VMEM(north_courant.shape, F32),
            pltpu.VMEM(mixing.shape, F32),
            pltpu.VMEM((2, n_levels * n_rows, n_cols), F32),
            pltpu.VMEM((2, n_cols, n_levels * n_rows), F32),
            pltpu.SemaphoreType.DMA((n_levels + 4,)),
        ]
        + [pltpu.VMEM(result.shape, result.dtype) for result in (column, column, edge, edge)]
        + [pltpu.SemaphoreType.DMA((4,))],
        compiler_params=pltpu.CompilerParams(vmem_limit_bytes=FIRST_VMEM_BYTES),
        name="first_sends",
        cost_estimate=pl.CostEstimate(flops=4_000_000_000, bytes_accessed=2_000_000, transcendentals=0),
    )(sunlit, latent_field, east_courant, north_courant, mixing)
    weights = (decode_w.T, react_a.T, react_b.T, stoich, encode_w, rate_const[None])
    field, coefs, linear, encode = pl.pallas_call(
        prepare_kernel,
        out_shape=(
            layered,
            jax.ShapeDtypeStruct((len(COEFFICIENTS), n_levels, n_rows, n_cols), F32),
            jax.ShapeDtypeStruct((2 * n_reactions, n_species), BF16),
            jax.ShapeDtypeStruct((n_species, n_reactions), BF16),
        ),
        in_specs=[hbm] + vmem(3 + len(weights)),
        out_specs=tuple(vmem(4)),
        scratch_shapes=[
            pltpu.VMEM((n_levels, n_species, n_rows, n_cols), F32),
            pltpu.SemaphoreType.DMA((n_levels,)),
        ],
        compiler_params=pltpu.CompilerParams(vmem_limit_bytes=PREPARE_VMEM_BYTES),
        name="prepare",
        cost_estimate=pl.CostEstimate(flops=4_000_000_000, bytes_accessed=1, transcendentals=0),
    )(latent_field, east_courant, north_courant, mixing, *weights)
    lon_halos = swapped(lon_b, "lon", 1), swapped(lon_a, "lon", 0)
    hint = pl.CostEstimate(flops=20_000_000_000, bytes_accessed=1, transcendentals=0)
    halo = jax.ShapeDtypeStruct((2 * n_levels * n_rows // n_cols, n_species, n_cols), F32)

    def call(kernel, name, operands, out_shape, out_specs, *scratch):
        return pl.pallas_call(
            kernel,
            out_shape=out_shape,
            in_specs=vmem(len(operands)),
            out_specs=out_specs,
            scratch_shapes=[
                pltpu.VMEM(a.shape, a.dtype) if isinstance(a, jax.ShapeDtypeStruct) else a
                for a in scratch
            ],
            compiler_params=params,
            name=name,
            cost_estimate=hint,
        )(*operands)

    lat_halos = swapped(lat_b, "lat", 1), swapped(lat_a, "lat", 0)
    shared = sunlit, field, coefs, linear, encode
    done, lat_a, lat_b, lon_in = call(
        edge_rows_kernel,
        "edge_rows",
        (*shared, *lat_halos, *lon_halos),
        (jax.ShapeDtypeStruct((n_levels, 2, n_species, n_cols), F32), cornered, cornered, halo),
        tuple(vmem(4)),
        edge,
        edge,
        layered,
    )
    lat_halos = swapped(lat_b, "lat", 1), swapped(lat_a, "lat", 0)
    columns = *lon_halos, lon_b, lon_a
    field, lon_in = call(
        inner_rows_kernel,
        "inner_rows",
        (*shared, *columns, done, lon_in),
        (layered, halo),
        tuple(vmem(2)),
        layered,
    )
    (advanced,) = call(
        last_step_kernel,
        "last_step",
        (sunlit, field, coefs, linear, encode, *columns, lon_in, *lat_halos),
        (jax.ShapeDtypeStruct(latent_field.shape, F32),),
        (hbm,),
        pltpu.VMEM((2, n_levels, n_species, n_rows // 2, n_cols), F32),
        pltpu.SemaphoreType.DMA((2, n_levels)),
        cornered,
        cornered,
        halo,
        layered,
    )
    return advanced


def solution(mesh):
    placed = (
        P(None, None, "lat", "lon"),
        P(None, "lat", "lon"),
        P(None, "lat", "lon"),
        P(None, "lat", "lon"),
        P("lat", "lon"),
        P(),
        P(),
        P(),
        P(),
        P(),
        P(),
    )
    return jax.shard_map(
        on_device,
        mesh=mesh,
        in_specs=placed,
        out_specs=P(None, None, "lat", "lon"),
        check_vma=False,
    )
```

```python
import functools
import itertools

import jax
import jax.numpy as jnp
from jax import lax
from jax.experimental import pallas as pl
from jax.experimental.pallas import tpu as pltpu
from jax.sharding import PartitionSpec as P

BLOCK = 16
SUBSTEPS = 2
GROUP = 8
ROWS_IN_FLIGHT = 2
LEVELS_AT_ONCE = 4
LAG = 1

F32 = jnp.float32
BF16 = jnp.bfloat16
VMEM_BYTES = 48 * 1024 * 1024
FIRST_VMEM_BYTES = 56 * 1024 * 1024
PREPARE_VMEM_BYTES = 50 * 1024 * 1024


def lane_ids(shape):
    return lax.broadcasted_iota(jnp.int32, shape, len(shape) - 1)


def fold_weights(decode_t, react_a_t, react_b_t, stoich, encode, rate, linear_out, encode_out):
    n_reactions = react_a_t.shape[1]
    contract = (((0,), (1,)), ((), ()))
    products = [
        lax.dot_general(react[...], decode_t[...], contract, preferred_element_type=F32)
        for react in (react_a_t, react_b_t)
    ]
    linear_out[...] = jnp.concatenate(
        [
            product[at : at + GROUP]
            for at in range(0, n_reactions, GROUP)
            for product in products
        ],
        axis=0,
    ).astype(BF16)
    folded = jnp.dot(encode[...], stoich[...], preferred_element_type=F32)
    encode_out[...] = (folded * rate[...]).astype(BF16)


def at_ends():
    index = lax.axis_index("lat")
    return index == 0, index == lax.axis_size("lat") - 1


def is_even(axis):
    return lax.axis_index(axis) % 2 == 0


def by_parity(axis, up, down, into_first, into_second):
    even = is_even(axis)
    into_first[...] = jnp.where(even, up, down)
    into_second[...] = jnp.where(even, down, up)


COLUMN_ROWS = 40
EAST_ROW, NORTH_ROW, MIXING_ROW, LIT_ROW = 32, 33, 34, 35


def first_kernel(sun, latent, east_c, north_c, mixing, *refs):
    outs, scratch, results = refs[:4], refs[4:-5], refs[-5:-1]
    lon_a, lon_b, lat_a, lat_b = results
    tiles, sun_v, east_v, north_v, mixing_v, faces, spread, turned_faces, sems = scratch
    sends = [
        pltpu.make_async_copy(result, out, refs[-1].at[at])
        for at, (result, out) in enumerate(zip(results, outs))
    ]
    n_levels, n_species, n_rows, n_cols = tiles.shape
    lanes = lane_ids((1, n_cols))
    is_first, is_last = at_ends()
    copies = [
        pltpu.make_async_copy(source, held, sems.at[n_levels + at])
        for at, (source, held) in enumerate(
            ((sun, sun_v), (east_c, east_v), (north_c, north_v), (mixing, mixing_v))
        )
    ]
    levels = [
        pltpu.make_async_copy(latent.at[:, level], tiles.at[level], sems.at[level])
        for level in range(n_levels)
    ]
    for copy in copies + levels:
        copy.start()
    for copy in copies:
        copy.wait()
    def face_lanes(planes):
        packed = None
        for at, plane in enumerate(planes):
            turned = pltpu.roll(plane, (4 * at + 2) % n_cols, 1)
            packed = turned if packed is None else jnp.where(lanes // 4 == at, turned, packed)
        return packed

    for level in range(n_levels):
        levels[level].wait()
        within = slice(level * n_rows, (level + 1) * n_rows)
        faces[0, within] = face_lanes([tiles[level, at] for at in range(n_species)])
        planes = [east_v[level], north_v[level]]
        if level < n_levels - 1:
            planes.append(mixing_v[level])
        zero = jnp.zeros((n_rows, n_cols), F32)
        faces[1, within] = face_lanes(planes + [zero] * (COLUMN_ROWS - n_species - len(planes)))
        rows = tiles.at[level].reshape(n_species * n_rows, n_cols)
        ends = []
        for r, closed, clip in ((0, is_first, jnp.minimum), (n_rows - 1, is_last, jnp.maximum)):
            speed = clip(north_v[level, r : r + 1, :], 0.0)
            value = rows[pl.ds(r, n_species, stride=n_rows), :]
            ends.append((value * jnp.where(closed, 0.0, speed)).astype(BF16))
        by_parity("lat", ends[1], ends[0], lat_a.at[level], lat_b.at[level])
    for copy in sends[2:]:
        copy.start()
    half_cells = n_levels * n_rows // 2
    odd = lanes % 2 == 1
    kinds = lax.broadcasted_iota(jnp.int32, (COLUMN_ROWS, n_cols), 0)
    lit_west = sun_v[:, :1].astype(F32)
    lit_east = sun_v[:, n_cols // BLOCK - 1 :].astype(F32)
    west, east = [], []
    for half in range(2):
        for kind in range(2):
            part = faces[kind, half * half_cells : (half + 1) * half_cells]
            for lane in range(2):
                spread[kind, pl.ds(lane, half_cells, stride=2), :] = part
            turned_faces[kind] = spread[kind].T
        columns = [
            jnp.concatenate(
                [
                    turned_faces[0, pl.ds(slot, n_species, stride=4), :],
                    turned_faces[1, pl.ds(slot, COLUMN_ROWS - n_species, stride=4), :],
                ],
                axis=0,
            )
            for slot in range(4)
        ]
        east.append(jnp.where(kinds == LIT_ROW, lit_east, jnp.where(odd, columns[1], columns[0])))
        west.append(jnp.where(kinds == LIT_ROW, lit_west, jnp.where(odd, columns[3], columns[2])))
    by_parity("lon", jnp.concatenate(east, axis=0), jnp.concatenate(west, axis=0), lon_a, lon_b)
    for copy in sends[:2]:
        copy.start()
    for copy in sends:
        copy.wait()


def split_halves(message):
    return message[:COLUMN_ROWS], message[COLUMN_ROWS:]


def is_odd(n_cols):
    return lane_ids((1, n_cols)) % 2 == 1


def clipped(speed):
    return jnp.where(is_odd(speed.shape[-1]), jnp.maximum(speed, 0.0), jnp.minimum(speed, 0.0))


def halo_columns(lon_b_in, lon_a_in):
    even = is_even("lon")
    from_west = split_halves(jnp.where(even, lon_b_in[...], lon_a_in[...]))
    from_east = split_halves(jnp.where(even, lon_a_in[...], lon_b_in[...]))
    odd = is_odd(lon_a_in.shape[1])
    near = [jnp.where(odd, w, e) for w, e in zip(from_west, from_east)]
    return near, from_west, from_east


def beside(odd_lanes, even_lanes):
    n_cols = odd_lanes.shape[1]
    return jnp.where(
        is_odd(n_cols), pltpu.roll(odd_lanes, 1, 1), pltpu.roll(even_lanes, n_cols - 1, 1)
    )


def inflow(column, n_species, clip):
    return column[:n_species] * clip(column[EAST_ROW : EAST_ROW + 1], 0.0)


def lat_inflow(column, n_species, clip):
    return column[:n_species] * clip(column[NORTH_ROW : NORTH_ROW + 1], 0.0)


def moved_column(column, west, east, south, north, n_species, n_rows, ends):
    n_cols = column.shape[1]
    rows = lane_ids((1, n_cols)) // 2 % n_rows
    is_first, is_last = ends
    speed = column[EAST_ROW : EAST_ROW + 1]
    lat_speed = column[NORTH_ROW : NORTH_ROW + 1]
    up = jnp.where((rows == n_rows - 1) & is_last, 0.0, jnp.maximum(lat_speed, 0.0))
    down = jnp.where((rows == 0) & is_first, 0.0, jnp.minimum(lat_speed, 0.0))
    value = column[:n_species]
    from_south = jnp.where(rows == 0, south, pltpu.roll(value * up, 2, 1))
    from_north = jnp.where(rows == n_rows - 1, north, pltpu.roll(value * down, n_cols - 2, 1))
    centre = 1.0 - jnp.abs(speed) - up + down
    return value * centre + (west - east) + (from_south - from_north)


def by_level(halves, n_levels, n_rows):
    n_cols = halves[0].shape[1]
    levels = []
    for level in range(n_levels):
        at = level * 2 * n_rows
        half = halves[at // n_cols]
        levels.append(half if at % n_cols == 0 else pltpu.roll(half, n_cols - at % n_cols, 1))
    return levels


def joined(levels, n_rows):
    n_cols = levels[0].shape[1]
    width = 2 * n_rows
    lanes = lane_ids((1, n_cols))
    arrays = []
    for at, array in enumerate(levels):
        turn = at * width % n_cols
        if turn == 0:
            arrays.append(array)
        else:
            arrays[-1] = jnp.where(lanes // width == turn // width, pltpu.roll(array, turn, 1), arrays[-1])
    return arrays


def diffused_columns(moved, mixing):
    upper, swept = None, []
    uppers = []
    for level, value in enumerate(moved):
        pivot = 1.0
        if level > 0:
            below = mixing[level - 1]
            pivot = pivot + below - below * upper
            value = value + below * swept[-1]
        if level < len(moved) - 1:
            pivot = pivot + mixing[level]
        scale = 1.0 / pivot
        if level < len(moved) - 1:
            upper = mixing[level] * scale
            uppers.append(upper)
        swept.append(value * scale)
    for level in range(len(moved) - 2, -1, -1):
        swept[level] = swept[level] + uppers[level] * swept[level + 1]
    return swept


COEFFICIENTS = CENTRE, EAST, WEST, NORTH, SOUTH, SCALE, LOWER, UPPER = range(8)


def prepare_kernel(latent, east_c, north_c, mixing, *refs):
    weights, (field, coefs, linear, encode, tiles, sems) = refs[:6], refs[6:]
    n_levels, n_rows, _, n_cols = field.shape
    copies = [
        pltpu.make_async_copy(latent.at[:, level], tiles.at[level], sems.at[level])
        for level in range(n_levels)
    ]
    for copy in copies:
        copy.start()
    fold_weights(*weights, linear, encode)
    is_first, is_last = at_ends()
    row_ids = lax.broadcasted_iota(jnp.int32, (n_rows, n_cols), 0)
    upper = None
    for level in range(n_levels):
        copies[level].wait()
        field[level] = jnp.transpose(tiles[level], (1, 0, 2))
        ce, cn = east_c[level], north_c[level]
        east, west = jnp.maximum(ce, 0.0), jnp.minimum(ce, 0.0)
        north = jnp.where((row_ids == n_rows - 1) & is_last, 0.0, jnp.maximum(cn, 0.0))
        south = jnp.where((row_ids == 0) & is_first, 0.0, jnp.minimum(cn, 0.0))
        coefs[CENTRE, level] = 1.0 - east + west - north + south
        coefs[EAST, level] = east
        coefs[WEST, level] = west
        coefs[NORTH, level] = north
        coefs[SOUTH, level] = south
        pivot = 1.0
        if level > 0:
            below = mixing[level - 1]
            pivot = pivot + below - below * upper
        if level < n_levels - 1:
            pivot = pivot + mixing[level]
        scale = 1.0 / pivot
        coefs[SCALE, level] = scale
        if level > 0:
            coefs[LOWER, level] = below * scale
        if level < n_levels - 1:
            upper = mixing[level] * scale
            coefs[UPPER, level] = upper


def product_of(linear, rounded):
    n_reactions = linear.shape[0] // 2
    both = jnp.dot(linear[...], rounded, preferred_element_type=F32)
    parts = [
        both[at : at + GROUP] * both[at + GROUP : at + 2 * GROUP]
        for at in range(0, 2 * n_reactions, 2 * GROUP)
    ]
    return jnp.concatenate(parts, axis=0).astype(BF16)


def lit_lanes(sun, n_cols):
    lanes = lane_ids((1, n_cols))
    lit = jnp.zeros((1, n_cols), jnp.int32)
    for block in range(n_cols // BLOCK):
        lit = jnp.where(lanes // BLOCK == block, sun[:, block : block + 1], lit)
    return lit > 0


def step_rows(
    order, sun, field, coefs, linear, encode, lon_in, south_in, north_in, diffused, finish, passage=None, tail=None
):
    n_levels, n_rows, _, n_cols = field.shape
    lanes = lane_ids((1, n_cols))

    def coef(kind, level, r):
        return coefs[kind, level, r : r + 1, :]

    def transport(r):
        right = None
        for level in range(n_levels):
            value = field[level, r]
            spot = level * 2 * n_rows + 2 * r + 1
            halo = pltpu.roll(lon_in[spot // n_cols], n_cols - spot % n_cols, 1)
            from_west = jnp.where(lanes == 0, halo, pltpu.roll(value * coef(EAST, level, r), 1, 1))
            from_east = jnp.where(
                lanes == n_cols - 1, halo, pltpu.roll(value * coef(WEST, level, r), n_cols - 1, 1)
            )
            if r == 0:
                from_south = south_in[level].astype(F32)
            else:
                from_south = field[level, r - 1] * coef(NORTH, level, r - 1)
            if r == n_rows - 1:
                from_north = north_in[level].astype(F32)
            else:
                from_north = field[level, r + 1] * coef(SOUTH, level, r + 1)
            moved = value * coef(CENTRE, level, r) + (from_west - from_east) + (from_south - from_north)
            scaled = moved * coef(SCALE, level, r)
            right = scaled if level == 0 else scaled + coef(LOWER, level, r) * right
            diffused[level, r] = right
            yield
        for level in range(n_levels - 2, -1, -1):
            right = diffused[level, r] + coef(UPPER, level, r) * right
            diffused[level, r] = right
            yield

    def tile_at(level, r):
        return jnp.concatenate(
            [diffused[level + extra, r] for extra in range(LEVELS_AT_ONCE)], axis=1
        )

    lit_tile = jnp.concatenate([lit_lanes(sun, n_cols)] * LEVELS_AT_ONCE, axis=1)
    for r in order[:ROWS_IN_FLIGHT]:
        for _ in transport(r):
            pass
    units, background = [], []
    for first in range(0, len(order), ROWS_IN_FLIGHT):
        in_flight = order[first : first + ROWS_IN_FLIGHT]
        places = [(level, r) for level in range(0, n_levels, LEVELS_AT_ONCE) for r in in_flight]
        ahead = order[first + ROWS_IN_FLIGHT : first + 2 * ROWS_IN_FLIGHT]
        steps = itertools.chain(*[transport(r) for r in ahead])
        share = -(-(2 * n_levels - 1) * ROWS_IN_FLIGHT // (SUBSTEPS * len(places)))
        for substep in range(SUBSTEPS):
            for place in places:
                background.append((steps, share))
                units.append((substep, place))
    later_by = ROWS_IN_FLIGHT * (n_levels // LEVELS_AT_ONCE)
    rounded, rates = {}, {}
    for at in range(len(units) + LAG):
        if at < len(units):
            substep, (level, r) = units[at]
            if substep == 0:
                rounded[at] = tile_at(level, r).astype(BF16)
            rates[at] = product_of(linear, rounded.pop(at))
            if passage is not None and at > len(units) // 2 + LAG:
                next(passage, None)
            for _ in itertools.islice(*background[at]):
                pass
        if tail is not None and at >= len(units) - 1:
            for _ in itertools.islice(tail, LEVELS_AT_ONCE // 2):
                pass
        if at >= LAG:
            done = at - LAG
            substep, (level, r) = units[done]
            change = jnp.dot(encode[...], rates.pop(done), preferred_element_type=F32)
            tile = tile_at(level, r)
            value = tile + jnp.where(lit_tile, change, 0.0)
            if substep < SUBSTEPS - 1:
                rounded[done + later_by] = (tile.astype(BF16).astype(F32) + change).astype(BF16)
            for extra in range(LEVELS_AT_ONCE):
                part = value[:, extra * n_cols : (extra + 1) * n_cols]
                if substep < SUBSTEPS - 1:
                    diffused[level + extra, r] = part
                else:
                    finish(level + extra, r, part)


def edge_rows_kernel(
    sun, field, coefs, linear, encode, lat_b_in, lat_a_in, lon_b_in, lon_a_in,
    done, lat_a, lat_b, lon_in, south_in, north_in, diffused,
):
    n_levels, n_rows, n_species, n_cols = field.shape
    lanes = lane_ids((1, n_cols))
    is_first, is_last = at_ends()
    by_parity("lat", lat_a_in[...], lat_b_in[...], north_in, south_in)
    near, _, _ = halo_columns(lon_b_in, lon_a_in)
    for half, column in enumerate(near):
        lon_in[half] = column[:n_species] * clipped(column[EAST_ROW : EAST_ROW + 1])
    order = [0, n_rows - 1]

    def finish(level, r, value):
        done[level, order.index(r)] = value

    step_rows(
        order, sun, field, coefs, linear, encode, lon_in, south_in, north_in, diffused, finish
    )
    for level in range(n_levels):
        south = (done[level, 0] * coefs[SOUTH, level, :1]).astype(BF16)
        north = (done[level, 1] * coefs[NORTH, level, n_rows - 1 :]).astype(BF16)
        by_parity("lat", north, south, lat_a.at[level], lat_b.at[level])
    rows_of = lanes // 2 % n_rows
    corners = []
    for closed, clip, turn, row in (
        (is_first, jnp.minimum, 2, 0),
        (is_last, jnp.maximum, n_cols - 2, n_rows - 1),
    ):
        lower, upper = (lat_inflow(column, n_species, clip) for column in near)
        both = jnp.where(rows_of == row, lower, pltpu.roll(upper, turn, 1))
        corners.append(jnp.where(closed, 0.0, both))
    south, north = (value.astype(BF16) for value in corners)
    by_parity("lat", north, south, lat_a.at[n_levels], lat_b.at[n_levels])


def columns_ahead(
    n_levels, n_rows, n_species, linear, encode, received, own, south_in, north_in, lon_out
):
    near, from_west, from_east = halo_columns(*received)
    lon_b_own, lon_a_own = own
    even = is_even("lon")
    own_east = split_halves(jnp.where(even, lon_a_own[...], lon_b_own[...]))
    own_west = split_halves(jnp.where(even, lon_b_own[...], lon_a_own[...]))
    n_cols = near[0].shape[1]
    odd = is_odd(n_cols)
    moved = []
    for half in range(2):
        far = beside(from_west[half], from_east[half])
        inner = beside(own_west[half], own_east[half])
        shift = 2 * (n_rows - 1 - half)
        moved.append(
            moved_column(
                near[half],
                inflow(jnp.where(odd, far, inner), n_species, jnp.maximum),
                inflow(jnp.where(odd, inner, far), n_species, jnp.minimum),
                pltpu.roll(south_in[n_levels].astype(F32), n_cols - shift, 1),
                pltpu.roll(north_in[n_levels].astype(F32), shift, 1),
                n_species,
                n_rows,
                at_ends(),
            )
        )
    mixing = by_level([column[MIXING_ROW : MIXING_ROW + 1] for column in near], n_levels, n_rows)
    solved = diffused_columns(by_level(moved, n_levels, n_rows), mixing)
    pair = jnp.concatenate(joined(solved, n_rows), axis=1)
    rounded = pair.astype(BF16)
    current, summed = rounded.astype(F32), None
    for substep in range(SUBSTEPS):
        rates = product_of(linear, rounded)
        change = jnp.dot(encode[...], rates, preferred_element_type=F32)
        summed = change if summed is None else summed + change
        current = current + change
        rounded = current.astype(BF16)
    for half, column in enumerate(near):
        within = slice(half * n_cols, (half + 1) * n_cols)
        lit = column[LIT_ROW : LIT_ROW + 1] > 0.0
        value = pair[:, within] + jnp.where(lit, summed[:, within], 0.0)
        lon_out[half] = value * clipped(column[EAST_ROW : EAST_ROW + 1])


def inner_rows_kernel(sun, field, coefs, linear, encode, done, lon_in, out, diffused):
    n_levels, n_rows, _, _ = field.shape
    for level in range(n_levels):
        out[level, 0] = done[level, 0]
        out[level, n_rows - 1] = done[level, 1]

    def finish(level, r, value):
        out[level, r] = value

    order = list(range(1, n_rows - 1))
    step_rows(order, sun, field, coefs, linear, encode, lon_in, None, None, diffused, finish)


def last_step_kernel(
    sun, field, coefs, linear, encode, lon_b_in, lon_a_in, lon_b_own, lon_a_own, lat_b_in, lat_a_in,
    out, staged, sems, south_in, north_in, lon_in, diffused,
):
    n_levels, n_rows, n_species, _ = field.shape
    half_rows = n_rows // 2
    by_parity("lat", lat_a_in[...], lat_b_in[...], north_in, south_in)
    columns_ahead(
        n_levels, n_rows, n_species, linear, encode,
        (lon_b_in, lon_a_in), (lon_b_own, lon_a_own), south_in, north_in, lon_in,
    )
    copies = []

    def send(half):
        within = slice(half * half_rows, (half + 1) * half_rows)
        for level in range(n_levels):
            staged[half, level] = jnp.transpose(diffused[level, within], (1, 0, 2))
            copy = pltpu.make_async_copy(
                staged.at[half, level], out.at[:, level, within], sems.at[half, level]
            )
            copy.start()
            copies.append(copy)
            yield

    def finish(level, r, value):
        diffused[level, r] = value

    order = list(range(n_rows))
    tail = send(1)
    step_rows(
        order, sun, field, coefs, linear, encode,
        lon_in, south_in, north_in, diffused, finish, send(0), tail,
    )
    for _ in tail:
        pass
    for copy in copies:
        copy.wait()


def vmem(count):
    return [pl.BlockSpec(memory_space=pltpu.VMEM)] * count


def swapped(array, axis, first):
    size = lax.axis_size(axis)
    pairs = [(i % size, (i + 1) % size) for i in range(first, size + first, 2)]
    return lax.ppermute(array, axis, pairs + [(j, i) for i, j in pairs])


def on_device(
    latent_field,
    east_courant,
    north_courant,
    mixing,
    sunlit,
    decode_w,
    react_a,
    react_b,
    stoich,
    encode_w,
    rate_const,
):
    n_species, n_levels, n_rows, n_cols = latent_field.shape
    layered = jax.ShapeDtypeStruct((n_levels, n_rows, n_species, n_cols), F32)
    column = jax.ShapeDtypeStruct((2 * COLUMN_ROWS, n_cols), F32)
    edge = jax.ShapeDtypeStruct((n_levels, n_species, n_cols), BF16)
    cornered = jax.ShapeDtypeStruct((n_levels + 1, n_species, n_cols), BF16)
    params = pltpu.CompilerParams(vmem_limit_bytes=VMEM_BYTES)
    hbm = pl.BlockSpec(memory_space=pltpu.HBM)
    n_reactions = react_a.shape[0]
    lon_a, lon_b, lat_a, lat_b = pl.pallas_call(
        first_kernel,
        out_shape=(column, column, edge, edge),
        in_specs=[hbm] * 5,
        out_specs=(hbm,) * 4,
        scratch_shapes=[
            pltpu.VMEM((n_levels, n_species, n_rows, n_cols), F32),
            pltpu.VMEM(sunlit.shape, sunlit.dtype),
            pltpu.VMEM(east_courant.shape, F32),
            pltpu.VMEM(north_courant.shape, F32),
            pltpu.VMEM(mixing.shape, F32),
            pltpu.VMEM((2, n_levels * n_rows, n_cols), F32),
            pltpu.VMEM((2, n_levels * n_rows, n_cols), F32),
            pltpu.VMEM((2, n_cols, n_levels * n_rows), F32),
            pltpu.SemaphoreType.DMA((n_levels + 4,)),
        ]
        + [pltpu.VMEM(result.shape, result.dtype) for result in (column, column, edge, edge)]
        + [pltpu.SemaphoreType.DMA((4,))],
        compiler_params=pltpu.CompilerParams(vmem_limit_bytes=FIRST_VMEM_BYTES),
        name="first_sends",
        cost_estimate=pl.CostEstimate(flops=4_000_000_000, bytes_accessed=2_000_000, transcendentals=0),
    )(sunlit, latent_field, east_courant, north_courant, mixing)
    weights = (decode_w.T, react_a.T, react_b.T, stoich, encode_w, rate_const[None])
    field, coefs, linear, encode = pl.pallas_call(
        prepare_kernel,
        out_shape=(
            layered,
            jax.ShapeDtypeStruct((len(COEFFICIENTS), n_levels, n_rows, n_cols), F32),
            jax.ShapeDtypeStruct((2 * n_reactions, n_species), BF16),
            jax.ShapeDtypeStruct((n_species, n_reactions), BF16),
        ),
        in_specs=[hbm] + vmem(3 + len(weights)),
        out_specs=tuple(vmem(4)),
        scratch_shapes=[
            pltpu.VMEM((n_levels, n_species, n_rows, n_cols), F32),
            pltpu.SemaphoreType.DMA((n_levels,)),
        ],
        compiler_params=pltpu.CompilerParams(vmem_limit_bytes=PREPARE_VMEM_BYTES),
        name="prepare",
        cost_estimate=pl.CostEstimate(flops=4_000_000_000, bytes_accessed=1, transcendentals=0),
    )(latent_field, east_courant, north_courant, mixing, *weights)
    lon_halos = swapped(lon_b, "lon", 1), swapped(lon_a, "lon", 0)
    hint = pl.CostEstimate(flops=20_000_000_000, bytes_accessed=1, transcendentals=0)
    halo = jax.ShapeDtypeStruct((2 * n_levels * n_rows // n_cols, n_species, n_cols), F32)

    def call(kernel, name, operands, out_shape, out_specs, *scratch):
        return pl.pallas_call(
            kernel,
            out_shape=out_shape,
            in_specs=vmem(len(operands)),
            out_specs=out_specs,
            scratch_shapes=[
                pltpu.VMEM(a.shape, a.dtype) if isinstance(a, jax.ShapeDtypeStruct) else a
                for a in scratch
            ],
            compiler_params=params,
            name=name,
            cost_estimate=hint,
        )(*operands)

    lat_halos = swapped(lat_b, "lat", 1), swapped(lat_a, "lat", 0)
    shared = sunlit, field, coefs, linear, encode
    done, lat_a, lat_b, lon_in = call(
        edge_rows_kernel,
        "edge_rows",
        (*shared, *lat_halos, *lon_halos),
        (jax.ShapeDtypeStruct((n_levels, 2, n_species, n_cols), F32), cornered, cornered, halo),
        tuple(vmem(4)),
        edge,
        edge,
        layered,
    )
    lat_halos = swapped(lat_b, "lat", 1), swapped(lat_a, "lat", 0)
    columns = *lon_halos, lon_b, lon_a
    (field,) = call(
        inner_rows_kernel, "inner_rows", (*shared, done, lon_in), (layered,), tuple(vmem(1)), layered
    )
    (advanced,) = call(
        last_step_kernel,
        "last_step",
        (sunlit, field, coefs, linear, encode, *columns, *lat_halos),
        (jax.ShapeDtypeStruct(latent_field.shape, F32),),
        (hbm,),
        pltpu.VMEM((2, n_levels, n_species, n_rows // 2, n_cols), F32),
        pltpu.SemaphoreType.DMA((2, n_levels)),
        cornered,
        cornered,
        halo,
        layered,
    )
    return advanced


def solution(mesh):
    placed = (
        P(None, None, "lat", "lon"),
        P(None, "lat", "lon"),
        P(None, "lat", "lon"),
        P(None, "lat", "lon"),
        P("lat", "lon"),
        P(),
        P(),
        P(),
        P(),
        P(),
        P(),
    )
    return jax.shard_map(
        on_device,
        mesh=mesh,
        in_specs=placed,
        out_specs=P(None, None, "lat", "lon"),
        check_vma=False,
    )
```

```python
import functools
import itertools

import jax
import jax.numpy as jnp
from jax import lax
from jax.experimental import pallas as pl
from jax.experimental.pallas import tpu as pltpu
from jax.sharding import PartitionSpec as P

BLOCK = 16
SUBSTEPS = 2
GROUP = 8
ROWS_IN_FLIGHT = 2
LEVELS_AT_ONCE = 4
LAG = 2
SPECIES_AT_ONCE = 8

F32 = jnp.float32
BF16 = jnp.bfloat16
VMEM_BYTES = 48 * 1024 * 1024
FIRST_VMEM_BYTES = 56 * 1024 * 1024
PREPARE_VMEM_BYTES = 50 * 1024 * 1024


def lane_ids(shape):
    return lax.broadcasted_iota(jnp.int32, shape, len(shape) - 1)


def fold_weights(decode_t, react_a_t, react_b_t, stoich, encode, rate, linear_out, encode_out):
    n_reactions = react_a_t.shape[1]
    contract = (((0,), (1,)), ((), ()))
    products = [
        lax.dot_general(react[...], decode_t[...], contract, preferred_element_type=F32)
        for react in (react_a_t, react_b_t)
    ]
    linear_out[...] = jnp.concatenate(
        [
            product[at : at + GROUP]
            for at in range(0, n_reactions, GROUP)
            for product in products
        ],
        axis=0,
    ).astype(BF16)
    folded = jnp.dot(encode[...], stoich[...], preferred_element_type=F32)
    encode_out[...] = (folded * rate[...]).astype(BF16)


def at_ends():
    index = lax.axis_index("lat")
    return index == 0, index == lax.axis_size("lat") - 1


def is_even(axis):
    return lax.axis_index(axis) % 2 == 0


def by_parity(axis, up, down, into_first, into_second):
    even = is_even(axis)
    into_first[...] = jnp.where(even, up, down)
    into_second[...] = jnp.where(even, down, up)


COLUMN_ROWS = 40
EAST_ROW, NORTH_ROW, MIXING_ROW, LIT_ROW = 32, 33, 34, 35


def first_kernel(sun, latent, east_c, north_c, mixing, *refs):
    outs, scratch, results = refs[:4], refs[4:-5], refs[-5:-1]
    lon_a, lon_b, lat_a, lat_b = results
    tiles, sun_v, east_v, north_v, mixing_v, faces, spread, turned_faces, sems = scratch
    sends = [
        pltpu.make_async_copy(result, out, refs[-1].at[at])
        for at, (result, out) in enumerate(zip(results, outs))
    ]
    n_species, n_levels, n_rows, n_cols = tiles.shape
    lanes = lane_ids((1, n_cols))
    is_first, is_last = at_ends()
    copies = [
        pltpu.make_async_copy(source, held, sems.at[n_levels + at])
        for at, (source, held) in enumerate(
            ((sun, sun_v), (east_c, east_v), (north_c, north_v), (mixing, mixing_v))
        )
    ]
    groups = [
        pltpu.make_async_copy(
            latent.at[at : at + SPECIES_AT_ONCE],
            tiles.at[at : at + SPECIES_AT_ONCE],
            sems.at[at // SPECIES_AT_ONCE],
        )
        for at in range(0, n_species, SPECIES_AT_ONCE)
    ]
    for copy in copies + groups:
        copy.start()
    for copy in copies:
        copy.wait()
    def with_plane(packed, plane, at):
        turned = pltpu.roll(plane, (4 * at + 2) % n_cols, 1)
        return turned if packed is None else jnp.where(lanes // 4 == at, turned, packed)

    for level in range(n_levels):
        planes = [east_v[level], north_v[level]]
        if level < n_levels - 1:
            planes.append(mixing_v[level])
        zero = jnp.zeros((n_rows, n_cols), F32)
        packed = None
        for at, plane in enumerate(planes + [zero] * (COLUMN_ROWS - n_species - len(planes))):
            packed = with_plane(packed, plane, at)
        faces[1, level * n_rows : (level + 1) * n_rows] = packed
    packed = [None] * n_levels
    for group, copy in enumerate(groups):
        copy.wait()
        for at in range(group * SPECIES_AT_ONCE, (group + 1) * SPECIES_AT_ONCE):
            packed = [
                with_plane(value, tiles[at, level], at) for level, value in enumerate(packed)
            ]
    rows = tiles.reshape(n_species * n_levels * n_rows, n_cols)
    for level in range(n_levels):
        faces[0, level * n_rows : (level + 1) * n_rows] = packed[level]
        ends = []
        for r, closed, clip in ((0, is_first, jnp.minimum), (n_rows - 1, is_last, jnp.maximum)):
            speed = clip(north_v[level, r : r + 1, :], 0.0)
            value = rows[pl.ds(level * n_rows + r, n_species, stride=n_levels * n_rows), :]
            ends.append((value * jnp.where(closed, 0.0, speed)).astype(BF16))
        by_parity("lat", ends[1], ends[0], lat_a.at[level], lat_b.at[level])
    for copy in sends[2:]:
        copy.start()
    half_cells = n_levels * n_rows // 2
    odd = lanes % 2 == 1
    kinds = lax.broadcasted_iota(jnp.int32, (COLUMN_ROWS, n_cols), 0)
    lit_west = sun_v[:, :1].astype(F32)
    lit_east = sun_v[:, n_cols // BLOCK - 1 :].astype(F32)
    west, east = [], []
    for half in range(2):
        for kind in range(2):
            part = faces[kind, half * half_cells : (half + 1) * half_cells]
            for lane in range(2):
                spread[kind, pl.ds(lane, half_cells, stride=2), :] = part
            turned_faces[kind] = spread[kind].T
        columns = [
            jnp.concatenate(
                [
                    turned_faces[0, pl.ds(slot, n_species, stride=4), :],
                    turned_faces[1, pl.ds(slot, COLUMN_ROWS - n_species, stride=4), :],
                ],
                axis=0,
            )
            for slot in range(4)
        ]
        east.append(jnp.where(kinds == LIT_ROW, lit_east, jnp.where(odd, columns[1], columns[0])))
        west.append(jnp.where(kinds == LIT_ROW, lit_west, jnp.where(odd, columns[3], columns[2])))
    by_parity("lon", jnp.concatenate(east, axis=0), jnp.concatenate(west, axis=0), lon_a, lon_b)
    for copy in sends[:2]:
        copy.start()
    for copy in sends:
        copy.wait()


def split_halves(message):
    return message[:COLUMN_ROWS], message[COLUMN_ROWS:]


def is_odd(n_cols):
    return lane_ids((1, n_cols)) % 2 == 1


def clipped(speed):
    return jnp.where(is_odd(speed.shape[-1]), jnp.maximum(speed, 0.0), jnp.minimum(speed, 0.0))


def halo_columns(lon_b_in, lon_a_in):
    even = is_even("lon")
    from_west = split_halves(jnp.where(even, lon_b_in[...], lon_a_in[...]))
    from_east = split_halves(jnp.where(even, lon_a_in[...], lon_b_in[...]))
    odd = is_odd(lon_a_in.shape[1])
    near = [jnp.where(odd, w, e) for w, e in zip(from_west, from_east)]
    return near, from_west, from_east


def beside(odd_lanes, even_lanes):
    n_cols = odd_lanes.shape[1]
    return jnp.where(
        is_odd(n_cols), pltpu.roll(odd_lanes, 1, 1), pltpu.roll(even_lanes, n_cols - 1, 1)
    )


def inflow(column, n_species, clip):
    return column[:n_species] * clip(column[EAST_ROW : EAST_ROW + 1], 0.0)


def lat_inflow(column, n_species, clip):
    return column[:n_species] * clip(column[NORTH_ROW : NORTH_ROW + 1], 0.0)


def moved_column(column, west, east, south, north, n_species, n_rows, ends):
    n_cols = column.shape[1]
    rows = lane_ids((1, n_cols)) // 2 % n_rows
    is_first, is_last = ends
    speed = column[EAST_ROW : EAST_ROW + 1]
    lat_speed = column[NORTH_ROW : NORTH_ROW + 1]
    up = jnp.where((rows == n_rows - 1) & is_last, 0.0, jnp.maximum(lat_speed, 0.0))
    down = jnp.where((rows == 0) & is_first, 0.0, jnp.minimum(lat_speed, 0.0))
    value = column[:n_species]
    from_south = jnp.where(rows == 0, south, pltpu.roll(value * up, 2, 1))
    from_north = jnp.where(rows == n_rows - 1, north, pltpu.roll(value * down, n_cols - 2, 1))
    centre = 1.0 - jnp.abs(speed) - up + down
    return value * centre + (west - east) + (from_south - from_north)


def by_level(halves, n_levels, n_rows):
    n_cols = halves[0].shape[1]
    levels = []
    for level in range(n_levels):
        at = level * 2 * n_rows
        half = halves[at // n_cols]
        levels.append(half if at % n_cols == 0 else pltpu.roll(half, n_cols - at % n_cols, 1))
    return levels


def joined(levels, n_rows):
    n_cols = levels[0].shape[1]
    width = 2 * n_rows
    lanes = lane_ids((1, n_cols))
    arrays = []
    for at, array in enumerate(levels):
        turn = at * width % n_cols
        if turn == 0:
            arrays.append(array)
        else:
            arrays[-1] = jnp.where(lanes // width == turn // width, pltpu.roll(array, turn, 1), arrays[-1])
    return arrays


def diffused_columns(moved, mixing):
    upper, swept = None, []
    uppers = []
    for level, value in enumerate(moved):
        pivot = 1.0
        if level > 0:
            below = mixing[level - 1]
            pivot = pivot + below - below * upper
            value = value + below * swept[-1]
        if level < len(moved) - 1:
            pivot = pivot + mixing[level]
        scale = 1.0 / pivot
        if level < len(moved) - 1:
            upper = mixing[level] * scale
            uppers.append(upper)
        swept.append(value * scale)
    for level in range(len(moved) - 2, -1, -1):
        swept[level] = swept[level] + uppers[level] * swept[level + 1]
    return swept


COEFFICIENTS = CENTRE, EAST, WEST, NORTH, SOUTH, SCALE, LOWER, UPPER = range(8)


def prepare_kernel(latent, east_c, north_c, mixing, *refs):
    weights, (field, coefs, linear, encode, tiles, sems) = refs[:6], refs[6:]
    n_levels, n_rows, _, n_cols = field.shape
    copies = [
        pltpu.make_async_copy(latent.at[:, level], tiles.at[level], sems.at[level])
        for level in range(n_levels)
    ]
    for copy in copies:
        copy.start()
    fold_weights(*weights, linear, encode)
    is_first, is_last = at_ends()
    row_ids = lax.broadcasted_iota(jnp.int32, (n_rows, n_cols), 0)
    upper = None
    for level in range(n_levels):
        copies[level].wait()
        field[level] = jnp.transpose(tiles[level], (1, 0, 2))
        ce, cn = east_c[level], north_c[level]
        east, west = jnp.maximum(ce, 0.0), jnp.minimum(ce, 0.0)
        north = jnp.where((row_ids == n_rows - 1) & is_last, 0.0, jnp.maximum(cn, 0.0))
        south = jnp.where((row_ids == 0) & is_first, 0.0, jnp.minimum(cn, 0.0))
        coefs[CENTRE, level] = 1.0 - east + west - north + south
        coefs[EAST, level] = east
        coefs[WEST, level] = west
        coefs[NORTH, level] = north
        coefs[SOUTH, level] = south
        pivot = 1.0
        if level > 0:
            below = mixing[level - 1]
            pivot = pivot + below - below * upper
        if level < n_levels - 1:
            pivot = pivot + mixing[level]
        scale = 1.0 / pivot
        coefs[SCALE, level] = scale
        if level > 0:
            coefs[LOWER, level] = below * scale
        if level < n_levels - 1:
            upper = mixing[level] * scale
            coefs[UPPER, level] = upper


def product_of(linear, rounded):
    n_reactions = linear.shape[0] // 2
    both = jnp.dot(linear[...], rounded, preferred_element_type=F32)
    parts = [
        both[at : at + GROUP] * both[at + GROUP : at + 2 * GROUP]
        for at in range(0, 2 * n_reactions, 2 * GROUP)
    ]
    return jnp.concatenate(parts, axis=0).astype(BF16)


def lit_lanes(sun, n_cols):
    lanes = lane_ids((1, n_cols))
    lit = jnp.zeros((1, n_cols), jnp.int32)
    for block in range(n_cols // BLOCK):
        lit = jnp.where(lanes // BLOCK == block, sun[:, block : block + 1], lit)
    return lit > 0


def step_rows(
    order, sun, field, coefs, linear, encode, lon_in, south_in, north_in, diffused, finish, passage=None, tail=None
):
    n_levels, n_rows, _, n_cols = field.shape
    lanes = lane_ids((1, n_cols))

    def coef(kind, level, r):
        return coefs[kind, level, r : r + 1, :]

    def transport(r):
        right = None
        for level in range(n_levels):
            value = field[level, r]
            spot = level * 2 * n_rows + 2 * r + 1
            halo = pltpu.roll(lon_in[spot // n_cols], n_cols - spot % n_cols, 1)
            from_west = jnp.where(lanes == 0, halo, pltpu.roll(value * coef(EAST, level, r), 1, 1))
            from_east = jnp.where(
                lanes == n_cols - 1, halo, pltpu.roll(value * coef(WEST, level, r), n_cols - 1, 1)
            )
            if r == 0:
                from_south = south_in[level].astype(F32)
            else:
                from_south = field[level, r - 1] * coef(NORTH, level, r - 1)
            if r == n_rows - 1:
                from_north = north_in[level].astype(F32)
            else:
                from_north = field[level, r + 1] * coef(SOUTH, level, r + 1)
            moved = value * coef(CENTRE, level, r) + (from_west - from_east) + (from_south - from_north)
            scaled = moved * coef(SCALE, level, r)
            right = scaled if level == 0 else scaled + coef(LOWER, level, r) * right
            diffused[level, r] = right
            yield
        for level in range(n_levels - 2, -1, -1):
            right = diffused[level, r] + coef(UPPER, level, r) * right
            diffused[level, r] = right
            yield

    def tile_at(level, r):
        return jnp.concatenate(
            [diffused[level + extra, r] for extra in range(LEVELS_AT_ONCE)], axis=1
        )

    lit_tile = jnp.concatenate([lit_lanes(sun, n_cols)] * LEVELS_AT_ONCE, axis=1)
    for r in order[:ROWS_IN_FLIGHT]:
        for _ in transport(r):
            pass
    units, background = [], []
    for first in range(0, len(order), ROWS_IN_FLIGHT):
        in_flight = order[first : first + ROWS_IN_FLIGHT]
        places = [(level, r) for level in range(0, n_levels, LEVELS_AT_ONCE) for r in in_flight]
        ahead = order[first + ROWS_IN_FLIGHT : first + 2 * ROWS_IN_FLIGHT]
        steps = itertools.chain(*[transport(r) for r in ahead])
        share = -(-(2 * n_levels - 1) * ROWS_IN_FLIGHT // (SUBSTEPS * len(places)))
        for substep in range(SUBSTEPS):
            for place in places:
                background.append((steps, share))
                units.append((substep, place))
    later_by = ROWS_IN_FLIGHT * (n_levels // LEVELS_AT_ONCE)
    rounded, rates = {}, {}
    for at in range(len(units) + LAG):
        if at < len(units):
            substep, (level, r) = units[at]
            if substep == 0:
                rounded[at] = tile_at(level, r).astype(BF16)
            rates[at] = product_of(linear, rounded.pop(at))
            if passage is not None and at > len(units) // 2 + LAG:
                next(passage, None)
            for _ in itertools.islice(*background[at]):
                pass
        if tail is not None and at >= len(units) + LAG - 2:
            for _ in itertools.islice(tail, LEVELS_AT_ONCE // 2):
                pass
        if at >= LAG:
            done = at - LAG
            substep, (level, r) = units[done]
            change = jnp.dot(encode[...], rates.pop(done), preferred_element_type=F32)
            tile = tile_at(level, r)
            value = tile + jnp.where(lit_tile, change, 0.0)
            if substep < SUBSTEPS - 1:
                rounded[done + later_by] = (tile.astype(BF16).astype(F32) + change).astype(BF16)
            for extra in range(LEVELS_AT_ONCE):
                part = value[:, extra * n_cols : (extra + 1) * n_cols]
                if substep < SUBSTEPS - 1:
                    diffused[level + extra, r] = part
                else:
                    finish(level + extra, r, part)


def edge_rows_kernel(
    sun, field, coefs, linear, encode, lat_b_in, lat_a_in, lon_b_in, lon_a_in,
    done, lat_a, lat_b, lon_in, south_in, north_in, diffused,
):
    n_levels, n_rows, n_species, n_cols = field.shape
    lanes = lane_ids((1, n_cols))
    is_first, is_last = at_ends()
    by_parity("lat", lat_a_in[...], lat_b_in[...], north_in, south_in)
    near, _, _ = halo_columns(lon_b_in, lon_a_in)
    for half, column in enumerate(near):
        lon_in[half] = column[:n_species] * clipped(column[EAST_ROW : EAST_ROW + 1])
    order = [0, n_rows - 1]

    def finish(level, r, value):
        done[level, order.index(r)] = value

    step_rows(
        order, sun, field, coefs, linear, encode, lon_in, south_in, north_in, diffused, finish
    )
    for level in range(n_levels):
        south = (done[level, 0] * coefs[SOUTH, level, :1]).astype(BF16)
        north = (done[level, 1] * coefs[NORTH, level, n_rows - 1 :]).astype(BF16)
        by_parity("lat", north, south, lat_a.at[level], lat_b.at[level])
    rows_of = lanes // 2 % n_rows
    corners = []
    for closed, clip, turn, row in (
        (is_first, jnp.minimum, 2, 0),
        (is_last, jnp.maximum, n_cols - 2, n_rows - 1),
    ):
        lower, upper = (lat_inflow(column, n_species, clip) for column in near)
        both = jnp.where(rows_of == row, lower, pltpu.roll(upper, turn, 1))
        corners.append(jnp.where(closed, 0.0, both))
    south, north = (value.astype(BF16) for value in corners)
    by_parity("lat", north, south, lat_a.at[n_levels], lat_b.at[n_levels])


def columns_ahead(
    n_levels, n_rows, n_species, linear, encode, received, own, south_in, north_in, lon_out
):
    near, from_west, from_east = halo_columns(*received)
    lon_b_own, lon_a_own = own
    even = is_even("lon")
    own_east = split_halves(jnp.where(even, lon_a_own[...], lon_b_own[...]))
    own_west = split_halves(jnp.where(even, lon_b_own[...], lon_a_own[...]))
    n_cols = near[0].shape[1]
    odd = is_odd(n_cols)
    moved = []
    for half in range(2):
        far = beside(from_west[half], from_east[half])
        inner = beside(own_west[half], own_east[half])
        shift = 2 * (n_rows - 1 - half)
        moved.append(
            moved_column(
                near[half],
                inflow(jnp.where(odd, far, inner), n_species, jnp.maximum),
                inflow(jnp.where(odd, inner, far), n_species, jnp.minimum),
                pltpu.roll(south_in[n_levels].astype(F32), n_cols - shift, 1),
                pltpu.roll(north_in[n_levels].astype(F32), shift, 1),
                n_species,
                n_rows,
                at_ends(),
            )
        )
    mixing = by_level([column[MIXING_ROW : MIXING_ROW + 1] for column in near], n_levels, n_rows)
    solved = diffused_columns(by_level(moved, n_levels, n_rows), mixing)
    pair = jnp.concatenate(joined(solved, n_rows), axis=1)
    rounded = pair.astype(BF16)
    current, summed = rounded.astype(F32), None
    for substep in range(SUBSTEPS):
        rates = product_of(linear, rounded)
        change = jnp.dot(encode[...], rates, preferred_element_type=F32)
        summed = change if summed is None else summed + change
        current = current + change
        rounded = current.astype(BF16)
    for half, column in enumerate(near):
        within = slice(half * n_cols, (half + 1) * n_cols)
        lit = column[LIT_ROW : LIT_ROW + 1] > 0.0
        value = pair[:, within] + jnp.where(lit, summed[:, within], 0.0)
        lon_out[half] = value * clipped(column[EAST_ROW : EAST_ROW + 1])


def inner_rows_kernel(sun, field, coefs, linear, encode, done, lon_in, out, diffused):
    n_levels, n_rows, _, _ = field.shape
    for level in range(n_levels):
        out[level, 0] = done[level, 0]
        out[level, n_rows - 1] = done[level, 1]

    def finish(level, r, value):
        out[level, r] = value

    order = list(range(1, n_rows - 1))
    step_rows(order, sun, field, coefs, linear, encode, lon_in, None, None, diffused, finish)


def last_step_kernel(
    sun, field, coefs, linear, encode, lon_b_in, lon_a_in, lon_b_own, lon_a_own, lat_b_in, lat_a_in,
    out, staged, sems, south_in, north_in, lon_in, diffused,
):
    n_levels, n_rows, n_species, _ = field.shape
    half_rows = n_rows // 2
    by_parity("lat", lat_a_in[...], lat_b_in[...], north_in, south_in)
    columns_ahead(
        n_levels, n_rows, n_species, linear, encode,
        (lon_b_in, lon_a_in), (lon_b_own, lon_a_own), south_in, north_in, lon_in,
    )
    copies = []

    def send(half):
        within = slice(half * half_rows, (half + 1) * half_rows)
        for level in range(n_levels):
            staged[half, level] = jnp.transpose(diffused[level, within], (1, 0, 2))
            copy = pltpu.make_async_copy(
                staged.at[half, level], out.at[:, level, within], sems.at[half, level]
            )
            copy.start()
            copies.append(copy)
            yield

    def finish(level, r, value):
        diffused[level, r] = value

    order = list(range(n_rows))
    tail = send(1)
    step_rows(
        order, sun, field, coefs, linear, encode,
        lon_in, south_in, north_in, diffused, finish, send(0), tail,
    )
    for _ in tail:
        pass
    for copy in copies:
        copy.wait()


def vmem(count):
    return [pl.BlockSpec(memory_space=pltpu.VMEM)] * count


def swapped(array, axis, first):
    size = lax.axis_size(axis)
    pairs = [(i % size, (i + 1) % size) for i in range(first, size + first, 2)]
    return lax.ppermute(array, axis, pairs + [(j, i) for i, j in pairs])


def on_device(
    latent_field,
    east_courant,
    north_courant,
    mixing,
    sunlit,
    decode_w,
    react_a,
    react_b,
    stoich,
    encode_w,
    rate_const,
):
    n_species, n_levels, n_rows, n_cols = latent_field.shape
    layered = jax.ShapeDtypeStruct((n_levels, n_rows, n_species, n_cols), F32)
    column = jax.ShapeDtypeStruct((2 * COLUMN_ROWS, n_cols), F32)
    edge = jax.ShapeDtypeStruct((n_levels, n_species, n_cols), BF16)
    cornered = jax.ShapeDtypeStruct((n_levels + 1, n_species, n_cols), BF16)
    params = pltpu.CompilerParams(vmem_limit_bytes=VMEM_BYTES)
    hbm = pl.BlockSpec(memory_space=pltpu.HBM)
    n_reactions = react_a.shape[0]
    lon_a, lon_b, lat_a, lat_b = pl.pallas_call(
        first_kernel,
        out_shape=(column, column, edge, edge),
        in_specs=[hbm] * 5,
        out_specs=(hbm,) * 4,
        scratch_shapes=[
            pltpu.VMEM(latent_field.shape, F32),
            pltpu.VMEM(sunlit.shape, sunlit.dtype),
            pltpu.VMEM(east_courant.shape, F32),
            pltpu.VMEM(north_courant.shape, F32),
            pltpu.VMEM(mixing.shape, F32),
            pltpu.VMEM((2, n_levels * n_rows, n_cols), F32),
            pltpu.VMEM((2, n_levels * n_rows, n_cols), F32),
            pltpu.VMEM((2, n_cols, n_levels * n_rows), F32),
            pltpu.SemaphoreType.DMA((n_levels + 4,)),
        ]
        + [pltpu.VMEM(result.shape, result.dtype) for result in (column, column, edge, edge)]
        + [pltpu.SemaphoreType.DMA((4,))],
        compiler_params=pltpu.CompilerParams(vmem_limit_bytes=FIRST_VMEM_BYTES),
        name="first_sends",
        cost_estimate=pl.CostEstimate(flops=4_000_000_000, bytes_accessed=2_000_000, transcendentals=0),
    )(sunlit, latent_field, east_courant, north_courant, mixing)
    weights = (decode_w.T, react_a.T, react_b.T, stoich, encode_w, rate_const[None])
    field, coefs, linear, encode = pl.pallas_call(
        prepare_kernel,
        out_shape=(
            layered,
            jax.ShapeDtypeStruct((len(COEFFICIENTS), n_levels, n_rows, n_cols), F32),
            jax.ShapeDtypeStruct((2 * n_reactions, n_species), BF16),
            jax.ShapeDtypeStruct((n_species, n_reactions), BF16),
        ),
        in_specs=[hbm] + vmem(3 + len(weights)),
        out_specs=tuple(vmem(4)),
        scratch_shapes=[
            pltpu.VMEM((n_levels, n_species, n_rows, n_cols), F32),
            pltpu.SemaphoreType.DMA((n_levels,)),
        ],
        compiler_params=pltpu.CompilerParams(vmem_limit_bytes=PREPARE_VMEM_BYTES),
        name="prepare",
        cost_estimate=pl.CostEstimate(flops=4_000_000_000, bytes_accessed=1, transcendentals=0),
    )(latent_field, east_courant, north_courant, mixing, *weights)
    lon_halos = swapped(lon_b, "lon", 1), swapped(lon_a, "lon", 0)
    hint = pl.CostEstimate(flops=20_000_000_000, bytes_accessed=1, transcendentals=0)
    halo = jax.ShapeDtypeStruct((2 * n_levels * n_rows // n_cols, n_species, n_cols), F32)

    def call(kernel, name, operands, out_shape, out_specs, *scratch):
        return pl.pallas_call(
            kernel,
            out_shape=out_shape,
            in_specs=vmem(len(operands)),
            out_specs=out_specs,
            scratch_shapes=[
                pltpu.VMEM(a.shape, a.dtype) if isinstance(a, jax.ShapeDtypeStruct) else a
                for a in scratch
            ],
            compiler_params=params,
            name=name,
            cost_estimate=hint,
        )(*operands)

    lat_halos = swapped(lat_b, "lat", 1), swapped(lat_a, "lat", 0)
    shared = sunlit, field, coefs, linear, encode
    done, lat_a, lat_b, lon_in = call(
        edge_rows_kernel,
        "edge_rows",
        (*shared, *lat_halos, *lon_halos),
        (jax.ShapeDtypeStruct((n_levels, 2, n_species, n_cols), F32), cornered, cornered, halo),
        tuple(vmem(4)),
        edge,
        edge,
        layered,
    )
    lat_halos = swapped(lat_b, "lat", 1), swapped(lat_a, "lat", 0)
    columns = *lon_halos, lon_b, lon_a
    (field,) = call(
        inner_rows_kernel, "inner_rows", (*shared, done, lon_in), (layered,), tuple(vmem(1)), layered
    )
    (advanced,) = call(
        last_step_kernel,
        "last_step",
        (sunlit, field, coefs, linear, encode, *columns, *lat_halos),
        (jax.ShapeDtypeStruct(latent_field.shape, F32),),
        (hbm,),
        pltpu.VMEM((2, n_levels, n_species, n_rows // 2, n_cols), F32),
        pltpu.SemaphoreType.DMA((2, n_levels)),
        cornered,
        cornered,
        halo,
        layered,
    )
    return advanced


def solution(mesh):
    placed = (
        P(None, None, "lat", "lon"),
        P(None, "lat", "lon"),
        P(None, "lat", "lon"),
        P(None, "lat", "lon"),
        P("lat", "lon"),
        P(),
        P(),
        P(),
        P(),
        P(),
        P(),
    )
    return jax.shard_map(
        on_device,
        mesh=mesh,
        in_specs=placed,
        out_specs=P(None, None, "lat", "lon"),
        check_vma=False,
    )
```

```python
import functools
import itertools

import jax
import jax.numpy as jnp
from jax import lax
from jax.experimental import pallas as pl
from jax.experimental.pallas import tpu as pltpu
from jax.sharding import PartitionSpec as P

BLOCK = 16
SUBSTEPS = 2
GROUP = 8
ROWS_IN_FLIGHT = 2
LEVELS_AT_ONCE = 4
LAG = 1

F32 = jnp.float32
BF16 = jnp.bfloat16
VMEM_BYTES = 48 * 1024 * 1024
FIRST_VMEM_BYTES = 56 * 1024 * 1024
PREPARE_VMEM_BYTES = 50 * 1024 * 1024


def lane_ids(shape):
    return lax.broadcasted_iota(jnp.int32, shape, len(shape) - 1)


def fold_weights(decode_t, react_a_t, react_b_t, stoich, encode, rate, linear_out, encode_out):
    n_reactions = react_a_t.shape[1]
    contract = (((0,), (1,)), ((), ()))
    products = [
        lax.dot_general(react[...], decode_t[...], contract, preferred_element_type=F32)
        for react in (react_a_t, react_b_t)
    ]
    linear_out[...] = jnp.concatenate(
        [
            product[at : at + GROUP]
            for at in range(0, n_reactions, GROUP)
            for product in products
        ],
        axis=0,
    ).astype(BF16)
    folded = jnp.dot(encode[...], stoich[...], preferred_element_type=F32)
    encode_out[...] = (folded * rate[...]).astype(BF16)


def at_ends():
    index = lax.axis_index("lat")
    return index == 0, index == lax.axis_size("lat") - 1


def is_even(axis):
    return lax.axis_index(axis) % 2 == 0


def by_parity(axis, up, down, into_first, into_second):
    even = is_even(axis)
    into_first[...] = jnp.where(even, up, down)
    into_second[...] = jnp.where(even, down, up)


COLUMN_ROWS = 40
EAST_ROW, NORTH_ROW, MIXING_ROW, LIT_ROW = 32, 33, 34, 35


def first_kernel(sun, latent, east_c, north_c, mixing, *refs):
    outs, scratch, results = refs[:4], refs[4:-5], refs[-5:-1]
    lon_a, lon_b, lat_a, lat_b = results
    tiles, sun_v, east_v, north_v, mixing_v, faces, spread, turned_faces, sems = scratch
    sends = [
        pltpu.make_async_copy(result, out, refs[-1].at[at])
        for at, (result, out) in enumerate(zip(results, outs))
    ]
    n_levels, n_species, n_rows, n_cols = tiles.shape
    lanes = lane_ids((1, n_cols))
    is_first, is_last = at_ends()
    copies = [
        pltpu.make_async_copy(source, held, sems.at[n_levels + at])
        for at, (source, held) in enumerate(
            ((sun, sun_v), (east_c, east_v), (north_c, north_v), (mixing, mixing_v))
        )
    ]
    levels = [
        pltpu.make_async_copy(latent.at[:, level], tiles.at[level], sems.at[level])
        for level in range(n_levels)
    ]
    for copy in copies + levels:
        copy.start()
    for copy in copies:
        copy.wait()
    def face_lanes(planes):
        packed = None
        for at, plane in enumerate(planes):
            turned = pltpu.roll(plane, (4 * at + 2) % n_cols, 1)
            packed = turned if packed is None else jnp.where(lanes // 4 == at, turned, packed)
        return packed

    for level in range(n_levels):
        levels[level].wait()
        within = slice(level * n_rows, (level + 1) * n_rows)
        faces[0, within] = face_lanes([tiles[level, at] for at in range(n_species)])
        planes = [east_v[level], north_v[level]]
        if level < n_levels - 1:
            planes.append(mixing_v[level])
        zero = jnp.zeros((n_rows, n_cols), F32)
        faces[1, within] = face_lanes(planes + [zero] * (COLUMN_ROWS - n_species - len(planes)))
        rows = tiles.at[level].reshape(n_species * n_rows, n_cols)
        ends = []
        for r, closed, clip in ((0, is_first, jnp.minimum), (n_rows - 1, is_last, jnp.maximum)):
            speed = clip(north_v[level, r : r + 1, :], 0.0)
            value = rows[pl.ds(r, n_species, stride=n_rows), :]
            ends.append((value * jnp.where(closed, 0.0, speed)).astype(BF16))
        by_parity("lat", ends[1], ends[0], lat_a.at[level], lat_b.at[level])
    for copy in sends[2:]:
        copy.start()
    half_cells = n_levels * n_rows // 2
    odd = lanes % 2 == 1
    kinds = lax.broadcasted_iota(jnp.int32, (COLUMN_ROWS, n_cols), 0)
    lit_west = sun_v[:, :1].astype(F32)
    lit_east = sun_v[:, n_cols // BLOCK - 1 :].astype(F32)
    west, east = [], []
    for half in range(2):
        for kind in range(2):
            part = faces[kind, half * half_cells : (half + 1) * half_cells]
            for lane in range(2):
                spread[kind, pl.ds(lane, half_cells, stride=2), :] = part
            turned_faces[kind] = spread[kind].T
        columns = [
            jnp.concatenate(
                [
                    turned_faces[0, pl.ds(slot, n_species, stride=4), :],
                    turned_faces[1, pl.ds(slot, COLUMN_ROWS - n_species, stride=4), :],
                ],
                axis=0,
            )
            for slot in range(4)
        ]
        east.append(jnp.where(kinds == LIT_ROW, lit_east, jnp.where(odd, columns[1], columns[0])))
        west.append(jnp.where(kinds == LIT_ROW, lit_west, jnp.where(odd, columns[3], columns[2])))
    east, west = (jnp.concatenate(parts, axis=0).astype(BF16) for parts in (east, west))
    by_parity("lon", east, west, lon_a, lon_b)
    for copy in sends[:2]:
        copy.start()
    for copy in sends:
        copy.wait()


def split_halves(message):
    message = message.astype(F32)
    return message[:COLUMN_ROWS], message[COLUMN_ROWS:]


def is_odd(n_cols):
    return lane_ids((1, n_cols)) % 2 == 1


def clipped(speed):
    return jnp.where(is_odd(speed.shape[-1]), jnp.maximum(speed, 0.0), jnp.minimum(speed, 0.0))


def halo_columns(lon_b_in, lon_a_in):
    even = is_even("lon")
    from_west = split_halves(jnp.where(even, lon_b_in[...], lon_a_in[...]))
    from_east = split_halves(jnp.where(even, lon_a_in[...], lon_b_in[...]))
    odd = is_odd(lon_a_in.shape[1])
    near = [jnp.where(odd, w, e) for w, e in zip(from_west, from_east)]
    return near, from_west, from_east


def beside(odd_lanes, even_lanes):
    n_cols = odd_lanes.shape[1]
    return jnp.where(
        is_odd(n_cols), pltpu.roll(odd_lanes, 1, 1), pltpu.roll(even_lanes, n_cols - 1, 1)
    )


def inflow(column, n_species, clip):
    return column[:n_species] * clip(column[EAST_ROW : EAST_ROW + 1], 0.0)


def lat_inflow(column, n_species, clip):
    return column[:n_species] * clip(column[NORTH_ROW : NORTH_ROW + 1], 0.0)


def moved_column(column, west, east, south, north, n_species, n_rows, ends):
    n_cols = column.shape[1]
    rows = lane_ids((1, n_cols)) // 2 % n_rows
    is_first, is_last = ends
    speed = column[EAST_ROW : EAST_ROW + 1]
    lat_speed = column[NORTH_ROW : NORTH_ROW + 1]
    up = jnp.where((rows == n_rows - 1) & is_last, 0.0, jnp.maximum(lat_speed, 0.0))
    down = jnp.where((rows == 0) & is_first, 0.0, jnp.minimum(lat_speed, 0.0))
    value = column[:n_species]
    from_south = jnp.where(rows == 0, south, pltpu.roll(value * up, 2, 1))
    from_north = jnp.where(rows == n_rows - 1, north, pltpu.roll(value * down, n_cols - 2, 1))
    centre = 1.0 - jnp.abs(speed) - up + down
    return value * centre + (west - east) + (from_south - from_north)


def by_level(halves, n_levels, n_rows):
    n_cols = halves[0].shape[1]
    levels = []
    for level in range(n_levels):
        at = level * 2 * n_rows
        half = halves[at // n_cols]
        levels.append(half if at % n_cols == 0 else pltpu.roll(half, n_cols - at % n_cols, 1))
    return levels


def joined(levels, n_rows):
    n_cols = levels[0].shape[1]
    width = 2 * n_rows
    lanes = lane_ids((1, n_cols))
    arrays = []
    for at, array in enumerate(levels):
        turn = at * width % n_cols
        if turn == 0:
            arrays.append(array)
        else:
            arrays[-1] = jnp.where(lanes // width == turn // width, pltpu.roll(array, turn, 1), arrays[-1])
    return arrays


def diffused_columns(moved, mixing):
    upper, swept = None, []
    uppers = []
    for level, value in enumerate(moved):
        pivot = 1.0
        if level > 0:
            below = mixing[level - 1]
            pivot = pivot + below - below * upper
            value = value + below * swept[-1]
        if level < len(moved) - 1:
            pivot = pivot + mixing[level]
        scale = 1.0 / pivot
        if level < len(moved) - 1:
            upper = mixing[level] * scale
            uppers.append(upper)
        swept.append(value * scale)
    for level in range(len(moved) - 2, -1, -1):
        swept[level] = swept[level] + uppers[level] * swept[level + 1]
    return swept


COEFFICIENTS = CENTRE, EAST, WEST, NORTH, SOUTH, SCALE, LOWER, UPPER = range(8)


def prepare_kernel(latent, east_c, north_c, mixing, *refs):
    weights, (field, coefs, linear, encode, tiles, sems) = refs[:6], refs[6:]
    n_levels, n_rows, _, n_cols = field.shape
    copies = [
        pltpu.make_async_copy(latent.at[:, level], tiles.at[level], sems.at[level])
        for level in range(n_levels)
    ]
    for copy in copies:
        copy.start()
    fold_weights(*weights, linear, encode)
    is_first, is_last = at_ends()
    row_ids = lax.broadcasted_iota(jnp.int32, (n_rows, n_cols), 0)
    upper = None
    for level in range(n_levels):
        copies[level].wait()
        field[level] = jnp.transpose(tiles[level], (1, 0, 2))
        ce, cn = east_c[level], north_c[level]
        east, west = jnp.maximum(ce, 0.0), jnp.minimum(ce, 0.0)
        north = jnp.where((row_ids == n_rows - 1) & is_last, 0.0, jnp.maximum(cn, 0.0))
        south = jnp.where((row_ids == 0) & is_first, 0.0, jnp.minimum(cn, 0.0))
        coefs[CENTRE, level] = 1.0 - east + west - north + south
        coefs[EAST, level] = east
        coefs[WEST, level] = west
        coefs[NORTH, level] = north
        coefs[SOUTH, level] = south
        pivot = 1.0
        if level > 0:
            below = mixing[level - 1]
            pivot = pivot + below - below * upper
        if level < n_levels - 1:
            pivot = pivot + mixing[level]
        scale = 1.0 / pivot
        coefs[SCALE, level] = scale
        if level > 0:
            coefs[LOWER, level] = below * scale
        if level < n_levels - 1:
            upper = mixing[level] * scale
            coefs[UPPER, level] = upper


def product_of(linear, rounded):
    n_reactions = linear.shape[0] // 2
    both = jnp.dot(linear[...], rounded, preferred_element_type=F32)
    parts = [
        both[at : at + GROUP] * both[at + GROUP : at + 2 * GROUP]
        for at in range(0, 2 * n_reactions, 2 * GROUP)
    ]
    return jnp.concatenate(parts, axis=0).astype(BF16)


def lit_lanes(sun, n_cols):
    lanes = lane_ids((1, n_cols))
    lit = jnp.zeros((1, n_cols), jnp.int32)
    for block in range(n_cols // BLOCK):
        lit = jnp.where(lanes // BLOCK == block, sun[:, block : block + 1], lit)
    return lit > 0


def step_rows(
    order, sun, field, coefs, linear, encode, lon_in, south_in, north_in, diffused, finish, passage=None, tail=None
):
    n_levels, n_rows, _, n_cols = field.shape
    lanes = lane_ids((1, n_cols))

    def coef(kind, level, r):
        return coefs[kind, level, r : r + 1, :]

    def transport(r):
        right = None
        for level in range(n_levels):
            value = field[level, r]
            spot = level * 2 * n_rows + 2 * r + 1
            halo = pltpu.roll(lon_in[spot // n_cols], n_cols - spot % n_cols, 1)
            from_west = jnp.where(lanes == 0, halo, pltpu.roll(value * coef(EAST, level, r), 1, 1))
            from_east = jnp.where(
                lanes == n_cols - 1, halo, pltpu.roll(value * coef(WEST, level, r), n_cols - 1, 1)
            )
            if r == 0:
                from_south = south_in[level].astype(F32)
            else:
                from_south = field[level, r - 1] * coef(NORTH, level, r - 1)
            if r == n_rows - 1:
                from_north = north_in[level].astype(F32)
            else:
                from_north = field[level, r + 1] * coef(SOUTH, level, r + 1)
            moved = value * coef(CENTRE, level, r) + (from_west - from_east) + (from_south - from_north)
            scaled = moved * coef(SCALE, level, r)
            right = scaled if level == 0 else scaled + coef(LOWER, level, r) * right
            diffused[level, r] = right
            yield
        for level in range(n_levels - 2, -1, -1):
            right = diffused[level, r] + coef(UPPER, level, r) * right
            diffused[level, r] = right
            yield

    def tile_at(level, r):
        return jnp.concatenate(
            [diffused[level + extra, r] for extra in range(LEVELS_AT_ONCE)], axis=1
        )

    lit_tile = jnp.concatenate([lit_lanes(sun, n_cols)] * LEVELS_AT_ONCE, axis=1)
    for r in order[:ROWS_IN_FLIGHT]:
        for _ in transport(r):
            pass
    units, background = [], []
    for first in range(0, len(order), ROWS_IN_FLIGHT):
        in_flight = order[first : first + ROWS_IN_FLIGHT]
        places = [(level, r) for level in range(0, n_levels, LEVELS_AT_ONCE) for r in in_flight]
        ahead = order[first + ROWS_IN_FLIGHT : first + 2 * ROWS_IN_FLIGHT]
        steps = itertools.chain(*[transport(r) for r in ahead])
        share = -(-(2 * n_levels - 1) * ROWS_IN_FLIGHT // (SUBSTEPS * len(places)))
        for substep in range(SUBSTEPS):
            for place in places:
                background.append((steps, share))
                units.append((substep, place))
    later_by = ROWS_IN_FLIGHT * (n_levels // LEVELS_AT_ONCE)
    rounded, rates = {}, {}
    for at in range(len(units) + LAG):
        if at < len(units):
            substep, (level, r) = units[at]
            if substep == 0:
                rounded[at] = tile_at(level, r).astype(BF16)
            rates[at] = product_of(linear, rounded.pop(at))
            if passage is not None and at > len(units) // 2 + LAG:
                next(passage, None)
            for _ in itertools.islice(*background[at]):
                pass
        if tail is not None and at >= len(units) - 1:
            for _ in itertools.islice(tail, LEVELS_AT_ONCE // 2):
                pass
        if at >= LAG:
            done = at - LAG
            substep, (level, r) = units[done]
            change = jnp.dot(encode[...], rates.pop(done), preferred_element_type=F32)
            tile = tile_at(level, r)
            value = tile + jnp.where(lit_tile, change, 0.0)
            if substep < SUBSTEPS - 1:
                rounded[done + later_by] = (tile.astype(BF16).astype(F32) + change).astype(BF16)
            for extra in range(LEVELS_AT_ONCE):
                part = value[:, extra * n_cols : (extra + 1) * n_cols]
                if substep < SUBSTEPS - 1:
                    diffused[level + extra, r] = part
                else:
                    finish(level + extra, r, part)


def edge_rows_kernel(
    sun, field, coefs, linear, encode, lat_b_in, lat_a_in, lon_b_in, lon_a_in,
    done, lat_a, lat_b, lon_in, south_in, north_in, diffused,
):
    n_levels, n_rows, n_species, n_cols = field.shape
    lanes = lane_ids((1, n_cols))
    is_first, is_last = at_ends()
    by_parity("lat", lat_a_in[...], lat_b_in[...], north_in, south_in)
    near, _, _ = halo_columns(lon_b_in, lon_a_in)
    for half, column in enumerate(near):
        lon_in[half] = column[:n_species] * clipped(column[EAST_ROW : EAST_ROW + 1])
    order = [0, n_rows - 1]

    def finish(level, r, value):
        done[level, order.index(r)] = value

    step_rows(
        order, sun, field, coefs, linear, encode, lon_in, south_in, north_in, diffused, finish
    )
    for level in range(n_levels):
        south = (done[level, 0] * coefs[SOUTH, level, :1]).astype(BF16)
        north = (done[level, 1] * coefs[NORTH, level, n_rows - 1 :]).astype(BF16)
        by_parity("lat", north, south, lat_a.at[level], lat_b.at[level])
    rows_of = lanes // 2 % n_rows
    corners = []
    for closed, clip, turn, row in (
        (is_first, jnp.minimum, 2, 0),
        (is_last, jnp.maximum, n_cols - 2, n_rows - 1),
    ):
        lower, upper = (lat_inflow(column, n_species, clip) for column in near)
        both = jnp.where(rows_of == row, lower, pltpu.roll(upper, turn, 1))
        corners.append(jnp.where(closed, 0.0, both))
    south, north = (value.astype(BF16) for value in corners)
    by_parity("lat", north, south, lat_a.at[n_levels], lat_b.at[n_levels])


def columns_ahead(
    n_levels, n_rows, n_species, linear, encode, received, own, south_in, north_in, lon_out
):
    near, from_west, from_east = halo_columns(*received)
    lon_b_own, lon_a_own = own
    even = is_even("lon")
    own_east = split_halves(jnp.where(even, lon_a_own[...], lon_b_own[...]))
    own_west = split_halves(jnp.where(even, lon_b_own[...], lon_a_own[...]))
    n_cols = near[0].shape[1]
    odd = is_odd(n_cols)
    moved = []
    for half in range(2):
        far = beside(from_west[half], from_east[half])
        inner = beside(own_west[half], own_east[half])
        shift = 2 * (n_rows - 1 - half)
        moved.append(
            moved_column(
                near[half],
                inflow(jnp.where(odd, far, inner), n_species, jnp.maximum),
                inflow(jnp.where(odd, inner, far), n_species, jnp.minimum),
                pltpu.roll(south_in[n_levels].astype(F32), n_cols - shift, 1),
                pltpu.roll(north_in[n_levels].astype(F32), shift, 1),
                n_species,
                n_rows,
                at_ends(),
            )
        )
    mixing = by_level([column[MIXING_ROW : MIXING_ROW + 1] for column in near], n_levels, n_rows)
    solved = diffused_columns(by_level(moved, n_levels, n_rows), mixing)
    pair = jnp.concatenate(joined(solved, n_rows), axis=1)
    rounded = pair.astype(BF16)
    current, summed = rounded.astype(F32), None
    for substep in range(SUBSTEPS):
        rates = product_of(linear, rounded)
        change = jnp.dot(encode[...], rates, preferred_element_type=F32)
        summed = change if summed is None else summed + change
        current = current + change
        rounded = current.astype(BF16)
    for half, column in enumerate(near):
        within = slice(half * n_cols, (half + 1) * n_cols)
        lit = column[LIT_ROW : LIT_ROW + 1] > 0.0
        value = pair[:, within] + jnp.where(lit, summed[:, within], 0.0)
        lon_out[half] = value * clipped(column[EAST_ROW : EAST_ROW + 1])


def inner_rows_kernel(sun, field, coefs, linear, encode, done, lon_in, out, diffused):
    n_levels, n_rows, _, _ = field.shape
    for level in range(n_levels):
        out[level, 0] = done[level, 0]
        out[level, n_rows - 1] = done[level, 1]

    def finish(level, r, value):
        out[level, r] = value

    order = list(range(1, n_rows - 1))
    step_rows(order, sun, field, coefs, linear, encode, lon_in, None, None, diffused, finish)


def last_step_kernel(
    sun, field, coefs, linear, encode, lon_b_in, lon_a_in, lon_b_own, lon_a_own, lat_b_in, lat_a_in,
    out, staged, sems, south_in, north_in, lon_in, diffused,
):
    n_levels, n_rows, n_species, _ = field.shape
    half_rows = n_rows // 2
    by_parity("lat", lat_a_in[...], lat_b_in[...], north_in, south_in)
    columns_ahead(
        n_levels, n_rows, n_species, linear, encode,
        (lon_b_in, lon_a_in), (lon_b_own, lon_a_own), south_in, north_in, lon_in,
    )
    copies = []

    def send(half):
        within = slice(half * half_rows, (half + 1) * half_rows)
        for level in range(n_levels):
            staged[half, level] = jnp.transpose(diffused[level, within], (1, 0, 2))
            copy = pltpu.make_async_copy(
                staged.at[half, level], out.at[:, level, within], sems.at[half, level]
            )
            copy.start()
            copies.append(copy)
            yield

    def finish(level, r, value):
        diffused[level, r] = value

    order = list(range(n_rows))
    tail = send(1)
    step_rows(
        order, sun, field, coefs, linear, encode,
        lon_in, south_in, north_in, diffused, finish, send(0), tail,
    )
    for _ in tail:
        pass
    for copy in copies:
        copy.wait()


def vmem(count):
    return [pl.BlockSpec(memory_space=pltpu.VMEM)] * count


def swapped(array, axis, first):
    size = lax.axis_size(axis)
    pairs = [(i % size, (i + 1) % size) for i in range(first, size + first, 2)]
    return lax.ppermute(array, axis, pairs + [(j, i) for i, j in pairs])


def on_device(
    latent_field,
    east_courant,
    north_courant,
    mixing,
    sunlit,
    decode_w,
    react_a,
    react_b,
    stoich,
    encode_w,
    rate_const,
):
    n_species, n_levels, n_rows, n_cols = latent_field.shape
    layered = jax.ShapeDtypeStruct((n_levels, n_rows, n_species, n_cols), F32)
    column = jax.ShapeDtypeStruct((2 * COLUMN_ROWS, n_cols), BF16)
    edge = jax.ShapeDtypeStruct((n_levels, n_species, n_cols), BF16)
    cornered = jax.ShapeDtypeStruct((n_levels + 1, n_species, n_cols), BF16)
    params = pltpu.CompilerParams(vmem_limit_bytes=VMEM_BYTES)
    hbm = pl.BlockSpec(memory_space=pltpu.HBM)
    n_reactions = react_a.shape[0]
    lon_a, lon_b, lat_a, lat_b = pl.pallas_call(
        first_kernel,
        out_shape=(column, column, edge, edge),
        in_specs=[hbm] * 5,
        out_specs=(hbm,) * 4,
        scratch_shapes=[
            pltpu.VMEM((n_levels, n_species, n_rows, n_cols), F32),
            pltpu.VMEM(sunlit.shape, sunlit.dtype),
            pltpu.VMEM(east_courant.shape, F32),
            pltpu.VMEM(north_courant.shape, F32),
            pltpu.VMEM(mixing.shape, F32),
            pltpu.VMEM((2, n_levels * n_rows, n_cols), F32),
            pltpu.VMEM((2, n_levels * n_rows, n_cols), F32),
            pltpu.VMEM((2, n_cols, n_levels * n_rows), F32),
            pltpu.SemaphoreType.DMA((n_levels + 4,)),
        ]
        + [pltpu.VMEM(result.shape, result.dtype) for result in (column, column, edge, edge)]
        + [pltpu.SemaphoreType.DMA((4,))],
        compiler_params=pltpu.CompilerParams(vmem_limit_bytes=FIRST_VMEM_BYTES),
        name="first_sends",
        cost_estimate=pl.CostEstimate(flops=4_000_000_000, bytes_accessed=2_000_000, transcendentals=0),
    )(sunlit, latent_field, east_courant, north_courant, mixing)
    weights = (decode_w.T, react_a.T, react_b.T, stoich, encode_w, rate_const[None])
    field, coefs, linear, encode = pl.pallas_call(
        prepare_kernel,
        out_shape=(
            layered,
            jax.ShapeDtypeStruct((len(COEFFICIENTS), n_levels, n_rows, n_cols), F32),
            jax.ShapeDtypeStruct((2 * n_reactions, n_species), BF16),
            jax.ShapeDtypeStruct((n_species, n_reactions), BF16),
        ),
        in_specs=[hbm] + vmem(3 + len(weights)),
        out_specs=tuple(vmem(4)),
        scratch_shapes=[
            pltpu.VMEM((n_levels, n_species, n_rows, n_cols), F32),
            pltpu.SemaphoreType.DMA((n_levels,)),
        ],
        compiler_params=pltpu.CompilerParams(vmem_limit_bytes=PREPARE_VMEM_BYTES),
        name="prepare",
        cost_estimate=pl.CostEstimate(flops=4_000_000_000, bytes_accessed=1, transcendentals=0),
    )(latent_field, east_courant, north_courant, mixing, *weights)
    lon_halos = swapped(lon_b, "lon", 1), swapped(lon_a, "lon", 0)
    hint = pl.CostEstimate(flops=20_000_000_000, bytes_accessed=1, transcendentals=0)
    halo = jax.ShapeDtypeStruct((2 * n_levels * n_rows // n_cols, n_species, n_cols), F32)

    def call(kernel, name, operands, out_shape, out_specs, *scratch):
        return pl.pallas_call(
            kernel,
            out_shape=out_shape,
            in_specs=vmem(len(operands)),
            out_specs=out_specs,
            scratch_shapes=[
                pltpu.VMEM(a.shape, a.dtype) if isinstance(a, jax.ShapeDtypeStruct) else a
                for a in scratch
            ],
            compiler_params=params,
            name=name,
            cost_estimate=hint,
        )(*operands)

    lat_halos = swapped(lat_b, "lat", 1), swapped(lat_a, "lat", 0)
    shared = sunlit, field, coefs, linear, encode
    done, lat_a, lat_b, lon_in = call(
        edge_rows_kernel,
        "edge_rows",
        (*shared, *lat_halos, *lon_halos),
        (jax.ShapeDtypeStruct((n_levels, 2, n_species, n_cols), F32), cornered, cornered, halo),
        tuple(vmem(4)),
        edge,
        edge,
        layered,
    )
    lat_halos = swapped(lat_b, "lat", 1), swapped(lat_a, "lat", 0)
    columns = *lon_halos, lon_b, lon_a
    (field,) = call(
        inner_rows_kernel, "inner_rows", (*shared, done, lon_in), (layered,), tuple(vmem(1)), layered
    )
    (advanced,) = call(
        last_step_kernel,
        "last_step",
        (sunlit, field, coefs, linear, encode, *columns, *lat_halos),
        (jax.ShapeDtypeStruct(latent_field.shape, F32),),
        (hbm,),
        pltpu.VMEM((2, n_levels, n_species, n_rows // 2, n_cols), F32),
        pltpu.SemaphoreType.DMA((2, n_levels)),
        cornered,
        cornered,
        halo,
        layered,
    )
    return advanced


def solution(mesh):
    placed = (
        P(None, None, "lat", "lon"),
        P(None, "lat", "lon"),
        P(None, "lat", "lon"),
        P(None, "lat", "lon"),
        P("lat", "lon"),
        P(),
        P(),
        P(),
        P(),
        P(),
        P(),
    )
    return jax.shard_map(
        on_device,
        mesh=mesh,
        in_specs=placed,
        out_specs=P(None, None, "lat", "lon"),
        check_vma=False,
    )
```
